32 devices in a mesh: groups: 2 (over x), mesh: 16 (over z, y, core).
Axes of the slice: x: 2, y: 2, z: 4, core: 2. Of those that a mesh axis runs over, the one named last changes fastest.
Arguments:
- tracers: float32 [2, 16, 32768], P(None, None, ('groups', 'mesh')), parts along dimension 2, may hold values from -6 to 6
- potential: float32 [16, 32768], P(None, ('groups', 'mesh')), parts along dimension 1, may hold values from -4 to 4
- surface_current: float32 [2, 32768], P(None, ('groups', 'mesh')), parts along dimension 1, may hold values from -4 to 4
- cell_neighbors: int32 [6, 16384], P(None, 'mesh'), may hold values from 0 to 16383, as said below
- cell_normal: float32 [6, 16384], P(None, 'mesh'), may hold values from -3.140625 to 3.140625
- cell_weight: float32 [6, 16384], P(None, 'mesh'), may hold values from 0.02 to 0.06
- spectra: float32 [50, 36, 4096], P(None, None, ('groups', 'mesh')), parts along dimension 2, may hold values from 0 to 10, as said below
- wind_velocity: float32 [2, 4096], P(None, ('groups', 'mesh')), parts along dimension 1, may hold values from -6 to 6
- node_neighbors: int32 [6, 2048], P(None, 'mesh'), may hold values from 0 to 2047, as said below
- node_normal: float32 [6, 2048], P(None, 'mesh'), may hold values from -3.140625 to 3.140625
- node_weight: float32 [6, 2048], P(None, 'mesh'), may hold values from 0.02 to 0.1
- send_rows: int32 [16, 16, 16], replicated, may hold values from 0 to 1023
- node_slot: int32 [2048], P('mesh'), may hold values from 0 to 255, as said below
Outputs:
- tracers_new: float32 [2, 16, 32768], P(None, None, ('groups', 'mesh')), parts along dimension 2
- spectra_new: float32 [50, 36, 4096], P(None, None, ('groups', 'mesh')), parts along dimension 2
The draws below stay inside these ranges and needn't reach their ends.
There are 2 independent parts, one for each index of `groups`. The reference program is written for one: setup_inputs(seed, part) draws one part's arguments, and reference() takes and returns one part's arrays. A program takes and returns all parts, laid end to end along the dimension named above; an argument that names none is the same for every part. Nothing has to cross between parts.
Inputs may be any that keep to these rules, and one draw needn't show every extreme that they name: `cell_neighbors`: entry [s, c] is a cell at most 128 places from c in the numbering; c itself marks a padded slot. `node_neighbors`: entry [s, n] is a node at most 64 places from n in the numbering; n itself marks a padded slot. `node_slot`: the nodes of one block use distinct slots; at most 16 nodes of one block take a given cell block, and in every draw one cell block serves exactly 16 nodes of every node block. `spectra`: positive spectral densities.
All inputs are finite; a program needn't handle non-finite values.
Results may differ from the reference program's by a relative error of at most 0.0003.
Values sent between devices are 32-bit elements; how exact they have to be, the bound alone decides.
No kernel may reach another device: no remote copies, remote signals or barrier semaphores. Data moves between devices by JAX's collectives and lax.ppermute only.
A program may use at most 128 MiB of HBM per device.

```python
import math
import jax
import jax.numpy as jnp
from jax import lax

TRACERS = 2
LAYERS = 16
CELL_DEV = 1024
EDGES = 6
CELL_HALO = 128
FREQS = 50
DIRS = 36
NODE_DEV = 128
NODE_HALO = 64
CELLS = 16384
NODES = 2048
CAP = 16
N_MESH = 16


def neighbor_table(key, total_count, reach_cells, slot_count):
    first, second, third = jax.random.split(key, 3)
    anchor = jnp.arange(total_count, dtype=jnp.int32)[None, :]
    offset = jax.random.randint(first, (slot_count, total_count), 1, reach_cells + 1)
    direction = 2 * jax.random.randint(second, (slot_count, total_count), 0, 2) - 1
    target = anchor + direction * offset
    edge_slot = jnp.arange(slot_count, dtype=jnp.int32)[:, None]
    target = jnp.where((edge_slot == 0) & (anchor % 7 == 0), anchor + reach_cells, target)
    padded = (edge_slot == slot_count - 1) & (jax.random.randint(third, (1, total_count), 0, 3) == 0)
    inside = (target >= 0) & (target < total_count)
    return jnp.where(inside & jnp.logical_not(padded), target, anchor).astype(jnp.int32)


def draw_cell_neighbors(key, part):
    key = jax.random.fold_in(key, 1)
    return neighbor_table(key, CELLS, CELL_HALO, EDGES)


def draw_node_neighbors(key, part):
    key = jax.random.fold_in(key, 2)
    return neighbor_table(key, NODES, NODE_HALO, EDGES)


def draw_spectra(key, part):
    key = jax.random.fold_in(key, 3)
    first, second, third = jax.random.split(key, 3)
    freq_scale = jnp.exp(jax.random.uniform(first, (FREQS, 1, 1), jnp.float32, math.log(0.3), math.log(3.0)))
    node_scale = jnp.exp(jax.random.uniform(second, (1, 1, NODES), jnp.float32, math.log(0.3), math.log(3.0)))
    element = jnp.exp(jax.random.uniform(third, (FREQS, DIRS, NODES), jnp.float32, math.log(0.01), 0.0))
    return (freq_scale * node_scale * element).astype(jnp.float32)


def draw_node_slot(key, part):
    key = jax.random.fold_in(key, 4)
    first, second = jax.random.split(key, 2)
    busy_owner = jax.random.randint(first, (), 0, N_MESH)

    def one_device(device_key):
        pick_key, order_key = jax.random.split(device_key, 2)
        chosen = jax.random.permutation(pick_key, (N_MESH - 1) * CAP)[:NODE_DEV - CAP]
        owner_index = chosen // CAP
        owner_index = owner_index + (owner_index >= busy_owner).astype(jnp.int32)
        slot_values = owner_index * CAP + chosen % CAP
        busy_slots = busy_owner * CAP + jnp.arange(CAP, dtype=jnp.int32)
        all_slots = jnp.concatenate([busy_slots, slot_values])
        return all_slots[jax.random.permutation(order_key, NODE_DEV)]
    device_keys = jax.random.split(second, N_MESH)
    return jax.vmap(one_device)(device_keys).reshape(-1).astype(jnp.int32)


def place_ends(array, key, least, high):
    spot = [jax.random.randint(jax.random.fold_in(key, axis), (), 0, length) for axis, length in enumerate(array.shape)]
    longest = array.shape.index(max(array.shape))
    neighbour = spot[:longest] + [(spot[longest] + 1) % array.shape[longest]] + spot[longest + 1:]
    return array.at[tuple(spot)].set(least).at[tuple(neighbour)].set(high)


def level_of(stream_key, extent, cuts, least, high):
    level = 1.0
    for dim, parts in cuts:
        draws = jax.random.uniform(jax.random.fold_in(jax.random.fold_in(stream_key, 6), dim), (parts,), jnp.float32, least / len(cuts), high / len(cuts))
        level = level * jnp.repeat(jnp.exp(draws), extent[dim] // parts).reshape((-1,) + (1,) * (len(extent) - 1 - dim))
    return level


def scatter_about(rng, dims, spread, bound, shards=(), held_as=jnp.bfloat16):
    gain = level_of(rng, dims, shards, -0.22, 0.18) if shards else 1.0
    values = jax.random.normal(rng, dims, jnp.float32) * spread * gain
    return jnp.minimum(jnp.maximum(values, -bound), bound).astype(held_as)


def setup_inputs(seed: int = 0, part: int = 0) -> dict:
    seeds = jax.random.split(jax.random.key(seed), 14)
    own_keys = jax.random.split(jax.random.fold_in(seeds[13], part), 14)
    tracers = scatter_about(own_keys[0], (TRACERS, LAYERS, CELLS), 1.0, 6.0, ((2, 16),), jnp.float32)
    potential = scatter_about(own_keys[1], (LAYERS, CELLS), 0.3, 4.0, ((1, 16),), jnp.float32)
    surface_current = scatter_about(own_keys[2], (2, CELLS), 0.3, 4.0, ((1, 16),), jnp.float32)
    cell_neighbors = draw_cell_neighbors(jax.random.fold_in(seeds[13], 71), part)
    cell_normal = jnp.clip(jax.random.uniform(seeds[4], (EDGES, CELLS), jnp.float32, -3.140625, 3.140625), -3.140625, 3.140625)
    cell_weight = jnp.clip(0.02 + 0.04 * jax.random.uniform(seeds[5], (EDGES, CELLS), jnp.float32) ** level_of(seeds[5], (EDGES, CELLS), ((1, 16),), -0.2, 0.2), 0.02, 0.06)
    spectra = draw_spectra(jax.random.fold_in(jax.random.fold_in(seeds[13], part), 71), part)
    wind_velocity = scatter_about(own_keys[7], (2, NODES), 1.5, 6.0, ((1, 16),), jnp.float32)
    node_neighbors = draw_node_neighbors(jax.random.fold_in(seeds[13], 71), part)
    node_normal = jnp.clip(jax.random.uniform(seeds[9], (EDGES, NODES), jnp.float32, -3.140625, 3.140625), -3.140625, 3.140625)
    node_weight = jnp.clip(0.02 + 0.08 * jax.random.uniform(seeds[10], (EDGES, NODES), jnp.float32) ** level_of(seeds[10], (EDGES, NODES), ((1, 16),), -0.2, 0.2), 0.02, 0.1)
    send_rows = place_ends(jax.random.randint(seeds[11], (N_MESH, N_MESH, CAP), 0, CELL_DEV), jax.random.fold_in(seeds[11], 1), 0, CELL_DEV - 1).astype(jnp.int32)
    node_slot = draw_node_slot(jax.random.fold_in(seeds[13], 71), part)
    return dict(tracers=tracers, potential=potential, surface_current=surface_current, cell_neighbors=cell_neighbors, cell_normal=cell_normal, cell_weight=cell_weight, spectra=spectra, wind_velocity=wind_velocity, node_neighbors=node_neighbors, node_normal=node_normal, node_weight=node_weight, send_rows=send_rows, node_slot=node_slot)


fct_floor = 1e-3


def wave_tables(freq_count, dir_count):
    freq_index = jnp.arange(freq_count, dtype=jnp.float32)
    angles = 2.0 * math.pi * jnp.arange(dir_count, dtype=jnp.float32) / dir_count
    group_speed = jnp.exp(-math.log(1.1) * freq_index)
    stokes_factor = (freq_index + 1.0) / freq_count
    return angles, group_speed, stokes_factor


def advect(energy, energy_ext, current, current_ext, neighbors, normal, weight):
    angles, group_speed, stokes_factor = wave_tables(energy.shape[0], energy.shape[1])
    speed_x = group_speed[:, None, None] * jnp.cos(angles)[None, :, None]
    speed_y = group_speed[:, None, None] * jnp.sin(angles)[None, :, None]
    outflow = jnp.zeros(energy.shape, jnp.float32)
    for edge_slot in range(neighbors.shape[0]):
        target = neighbors[edge_slot]
        beside = jnp.take(energy_ext, target, axis=2)
        beside_current = jnp.take(current_ext, target, axis=1)
        current_x = 0.5 * (current[0] + beside_current[0])
        current_y = 0.5 * (current[1] + beside_current[1])
        normal_speed = (speed_x + current_x) * jnp.cos(normal[edge_slot]) + (speed_y + current_y) * jnp.sin(normal[edge_slot])
        edge_flux = weight[edge_slot] * (jnp.maximum(normal_speed, 0.0) * energy + jnp.minimum(normal_speed, 0.0) * beside)
        outflow = outflow + edge_flux
    return energy - outflow


def source(advected, wind_velocity):
    angles, group_speed, stokes_factor = wave_tables(advected.shape[0], advected.shape[1])
    cosine = jnp.cos(angles)[:, None]
    sine = jnp.sin(angles)[:, None]
    forcing = jnp.maximum(wind_velocity[0][None, :] * cosine + wind_velocity[1][None, :] * sine, 0.0)
    growth = 0.25 * stokes_factor[:, None, None] * forcing[None]
    mean_energy = jnp.mean(advected, axis=(0, 1))
    damping = 2.0 * stokes_factor[:, None, None] * mean_energy[None, None, :]
    evolved = advected * jnp.exp(growth - damping)
    stokes_table = jnp.stack([stokes_factor[:, None] * jnp.cos(angles)[None, :], stokes_factor[:, None] * jnp.sin(angles)[None, :]]) / advected.shape[1]
    stokes = jnp.einsum("fdn,cfd->cn", evolved, stokes_table, precision=lax.Precision.HIGHEST)
    return evolved, stokes


def antidiffusion(tracers, tracers_ext, potential, potential_ext, cell_stokes, neighbors, normal, weight):
    layer_count = tracers.shape[1]
    beside = jnp.take(tracers_ext, neighbors, axis=2)
    beside_potential = jnp.take(potential_ext, neighbors, axis=1)
    layer_index = jnp.arange(layer_count, dtype=jnp.float32)
    depth_decay = jnp.exp(-3.0 * layer_index / layer_count)
    drift_normal = cell_stokes[0][None, :] * jnp.cos(normal) + cell_stokes[1][None, :] * jnp.sin(normal)
    velocity = beside_potential - potential[:, None, :] + depth_decay[:, None, None] * drift_normal[None]
    own_value = tracers[:, :, None, :]
    low_flux = weight * (jnp.maximum(velocity, 0.0) * own_value + jnp.minimum(velocity, 0.0) * beside)
    high_flux = weight * velocity * 0.5 * (own_value + beside)
    antiflux = high_flux - low_flux
    lowered = tracers - jnp.sum(low_flux, axis=2)
    upper_bound = jnp.maximum(tracers, jnp.max(beside, axis=2))
    lower_bound = jnp.minimum(tracers, jnp.min(beside, axis=2))
    inflow_sum = jnp.sum(jnp.maximum(-antiflux, 0.0), axis=2)
    outflow_sum = jnp.sum(jnp.maximum(antiflux, 0.0), axis=2)
    room_up = jnp.maximum(upper_bound - lowered, 0.0)
    room_down = jnp.maximum(lowered - lower_bound, 0.0)
    ratio_plus = jnp.minimum(1.0, room_up / (inflow_sum + fct_floor))
    ratio_minus = jnp.minimum(1.0, room_down / (outflow_sum + fct_floor))
    return antiflux, lowered, ratio_plus, ratio_minus


def limited(antiflux, lowered, ratio_plus, ratio_minus, plus_ext, minus_ext, neighbors):
    plus_beside = jnp.take(plus_ext, neighbors, axis=2)
    minus_beside = jnp.take(minus_ext, neighbors, axis=2)
    factor = jnp.where(antiflux >= 0.0, jnp.minimum(ratio_minus[:, :, None, :], plus_beside), jnp.minimum(ratio_plus[:, :, None, :], minus_beside))
    return lowered - jnp.sum(factor * antiflux, axis=2)


def reference(tracers, potential, surface_current, cell_neighbors, cell_normal, cell_weight, spectra, wind_velocity, node_neighbors, node_normal, node_weight, send_rows, node_slot):
    node_index = jnp.arange(NODES, dtype=jnp.int32)
    device_of = node_index // NODE_DEV
    owner_of = node_slot // CAP
    position = node_slot % CAP
    cell_of_node = owner_of * CELL_DEV + send_rows[owner_of, device_of, position]
    node_current = jnp.take(surface_current, cell_of_node, axis=1)
    advected = advect(spectra, spectra, node_current, node_current, node_neighbors, node_normal, node_weight)
    spectra_new, stokes = source(advected, wind_velocity)
    cell_stokes = jnp.zeros((2, CELLS), jnp.float32).at[:, cell_of_node].add(stokes)
    antiflux, lowered, ratio_plus, ratio_minus = antidiffusion(tracers, tracers, potential, potential, cell_stokes, cell_neighbors, cell_normal, cell_weight)
    tracers_new = limited(antiflux, lowered, ratio_plus, ratio_minus, ratio_plus, ratio_minus, cell_neighbors)
    return tracers_new, spectra_new
```

```python
import math

import jax
import jax.numpy as jnp
from jax import lax
from jax.experimental import pallas as pl
from jax.experimental.pallas import tpu as pltpu
from jax.sharding import PartitionSpec as P

LANES = 128
FCT_FLOOR = 0.001
TABLE_ROWS = 24
VMEM_LIMIT = 48 * 1024 * 1024


def lane_gather(values, index):
    return jnp.take_along_axis(values, index, axis=1, mode="promise_in_bounds")


def spread(row, count):
    return jnp.broadcast_to(row, (count, LANES))


def lane_iota(rows):
    return lax.broadcasted_iota(jnp.int32, (rows, LANES), 1)


def row_iota(rows):
    return lax.broadcasted_iota(jnp.int32, (rows, LANES), 0)


def slot_rows(send_rows, block):
    peers, capacity = send_rows.shape[1:]
    entry = send_rows[block]
    wide = jnp.concatenate([entry, jnp.zeros((peers, LANES - capacity), jnp.int32)], axis=1)
    wide = lane_gather(wide, lane_iota(peers) % capacity)
    owner = row_iota(peers)
    out = []
    for half in range(peers * capacity // LANES):
        wanted = (lane_iota(peers) + half * LANES) // capacity
        picked = jnp.where(owner == wanted, wide, 0).astype(jnp.float32)
        out.append(jnp.sum(picked, axis=0, keepdims=True).astype(jnp.int32))
    return out


def pack_kernel(
    spectra, tracers, potential, neighbors, normal, weight, current, send_rows, node_slot,
    tile, ahead, behind,
):
    me = lax.axis_index("mesh")
    freqs, dirs = spectra.shape[:2]
    layers, cells = potential.shape
    blocks = cells // LANES
    field_rows = (tracers.shape[0] + 1) * layers
    stacked = jnp.concatenate(
        [current[:, b * LANES : (b + 1) * LANES] for b in range(blocks)], axis=0
    )
    place = row_iota(2 * blocks)
    halves = slot_rows(send_rows, me)
    tile[...] = jnp.zeros(tile.shape, jnp.float32)
    for half, cell in enumerate(halves):
        found = lane_gather(stacked, spread(cell % LANES, 2 * blocks))
        for part in range(2):
            picked = jnp.where(place == 2 * (cell // LANES) + part, found, 0.0)
            row = part * len(halves) + half
            tile[row : row + 1, :] = jnp.sum(picked, axis=0, keepdims=True)
    row = 2 * len(halves)
    tile[row : row + 1, :] = node_slot[...].astype(jnp.float32)
    for out, first in ((ahead, blocks - 2), (behind, 0)):
        for b in range(2):
            lanes = slice((first + b) * LANES, (first + b + 1) * LANES)
            base = b * field_rows
            for t in range(tracers.shape[0]):
                out[base + t * layers : base + (t + 1) * layers, :] = tracers[t, :, lanes]
            out[base + field_rows - layers : base + field_rows, :] = potential[:, lanes]
    for out, b in ((ahead, blocks - 1), (behind, 0)):
        lanes = slice(b * LANES, (b + 1) * LANES)
        base = 2 * field_rows
        out[base : base + TABLE_ROWS, :] = jnp.zeros((TABLE_ROWS, LANES), jnp.float32)
        edges = neighbors.shape[0]
        out[base : base + edges, :] = neighbors[:, lanes].astype(jnp.float32)
        out[base + 8 : base + 8 + edges, :] = normal[:, lanes]
        out[base + 16 : base + 16 + edges, :] = weight[:, lanes]
    base = 2 * field_rows + TABLE_ROWS
    pairs = freqs // 2
    whole = dirs // 8 * 8
    rest = dirs - whole
    low = lane_iota(dirs) < LANES // 2
    for g in range(pairs):
        natural = spectra[g]
        turned = pltpu.roll(spectra[g + pairs], LANES // 2, 1)
        for out, mixed in (
            (ahead, jnp.where(low, turned, natural)),
            (behind, jnp.where(low, natural, turned)),
        ):
            at = base + g * whole
            out[at : at + whole, :] = mixed[:whole]
            at = base + pairs * whole + g * rest
            out[at : at + rest, :] = mixed[whole:]
    at = base + pairs * dirs
    if at < ahead.shape[0]:
        for out in (ahead, behind):
            out[at:, :] = jnp.zeros((ahead.shape[0] - at, LANES), jnp.float32)


def node_currents(table, slot, block, capacity):
    peers = table.shape[0]
    halves = peers * capacity // LANES
    owner = slot // capacity
    entry = block * capacity + slot % capacity
    lane = spread(entry % LANES, 8)
    owner8 = spread(owner, 8)
    found = jnp.zeros((8, LANES), jnp.float32)
    for p in range(peers):
        found = jnp.where(owner8 == p, lane_gather(table[p], lane), found)
    half = entry // LANES
    out = []
    for part in range(2):
        value = found[part * halves : part * halves + 1]
        for h in range(1, halves):
            row = part * halves + h
            value = jnp.where(half == h, found[row : row + 1], value)
        out.append(value)
    return out


def wave_kernel(
    spectra, before, after, table, node_slot, neighbors, normal, weight, wind, send_rows,
    spectra_new, tile, project, drift,
):
    me = lax.axis_index("mesh")
    freqs, dirs = spectra.shape[:2]
    edges = neighbors.shape[0]
    peers, _, capacity = send_rows.shape
    halves = peers * capacity // LANES
    pairs = freqs // 2
    whole = dirs // 8 * 8
    rest = dirs - whole
    base = before.shape[0] - (pairs * dirs + 7) // 8 * 8
    low1 = lane_iota(1) < LANES // 2

    slot = node_slot[...]
    row = 2 * halves
    previous = jnp.maximum(me - 1, 0)
    following = jnp.minimum(me + 1, peers - 1)
    beside_slot = jnp.where(
        low1, table[following][row : row + 1], table[previous][row : row + 1]
    ).astype(jnp.int32)
    beside_block = jnp.where(low1, following, previous)
    own_block = jnp.full((1, LANES), me, jnp.int32)
    own_x, own_y = node_currents(table, slot, own_block, capacity)
    halo_x, halo_y = node_currents(table, beside_slot, beside_block, capacity)

    target = neighbors[...]
    lane = target % LANES
    inside = target // LANES == me
    angle = normal[...]
    w = weight[...]
    cosine = w * jnp.cos(angle)
    sine = w * jnp.sin(angle)

    def beside(own, halo):
        a = lane_gather(spread(own, edges), lane)
        b = lane_gather(spread(halo, edges), lane)
        return jnp.where(inside, a, b)

    drift[0:edges, :] = (
        0.5 * (own_x + beside(own_x, halo_x)) * cosine
        + 0.5 * (own_y + beside(own_y, halo_y)) * sine
    )
    turn = 2.0 * math.pi / dirs * lax.broadcasted_iota(jnp.int32, (dirs, LANES), 0).astype(
        jnp.float32
    )
    cos_dir = jnp.cos(turn)
    sin_dir = jnp.sin(turn)
    for s in range(edges):
        project[s] = cos_dir * cosine[s : s + 1] + sin_dir * sine[s : s + 1]

    low = lane_iota(dirs) < LANES // 2
    straight = [spread(lane[s : s + 1], dirs) for s in range(edges)]
    swapped = [spread((lane[s : s + 1] + LANES // 2) % LANES, dirs) for s in range(edges)]
    within = [spread(target[s : s + 1] // LANES, dirs) == me for s in range(edges)]
    ratio = 1.0 / 1.1
    jump = ratio**pairs

    def pair(g, carry):
        speed, total = carry
        halo_parts = []
        for message in (before, after):
            at = pl.multiple_of(base + g * whole, 8)
            upper = message[pl.ds(at, whole), :]
            lower = message[pl.ds(base + pairs * whole + g * rest, rest), :]
            halo_parts.append(jnp.concatenate([upper, lower], axis=0))
        b, a = halo_parts
        for f, group_speed, halo, halo_lane in (
            (g, speed, jnp.where(low, a, b), straight),
            (g + pairs, speed * jump, jnp.where(low, b, a), swapped),
        ):
            own = spectra[f]
            out_speed = jnp.zeros((dirs, LANES), jnp.float32)
            inflow = jnp.zeros((dirs, LANES), jnp.float32)
            for s in range(edges):
                normal_speed = group_speed * project[s] + drift[s : s + 1]
                near = jnp.where(
                    within[s], lane_gather(own, straight[s]), lane_gather(halo, halo_lane[s])
                )
                out_speed = out_speed + jnp.maximum(normal_speed, 0.0)
                inflow = inflow + jnp.minimum(normal_speed, 0.0) * near
            advected = own - (out_speed * own + inflow)
            spectra_new[f] = advected
            total = total + advected
        return speed * ratio, total

    zero = jnp.zeros((dirs, LANES), jnp.float32)
    _, total = lax.fori_loop(0, pairs, pair, (jnp.float32(1.0), zero))
    mean = jnp.sum(total, axis=0, keepdims=True) * (1.0 / (freqs * dirs))
    forcing = jnp.maximum(wind[0:1, :] * cos_dir + wind[1:2, :] * sin_dir, 0.0)
    step = jnp.exp((0.25 * forcing - 2.0 * mean) * (1.0 / freqs))

    def grow(f, carry):
        factor, weighted = carry
        factor = factor * step
        evolved = spectra_new[f] * factor
        spectra_new[f] = evolved
        kappa = (f + 1).astype(jnp.float32) * (1.0 / freqs)
        return factor, weighted + kappa * evolved

    _, weighted = lax.fori_loop(0, freqs, grow, (zero + 1.0, zero))
    stokes = jnp.concatenate(
        [
            jnp.sum(weighted * cos_dir, axis=0, keepdims=True),
            jnp.sum(weighted * sin_dir, axis=0, keepdims=True),
        ],
        axis=0,
    ) * (1.0 / dirs)
    in_order = exact_dot(
        stokes, lax.broadcasted_iota(jnp.int32, (halves * LANES, LANES), 0) == slot
    )
    tile[...] = jnp.zeros(tile.shape, jnp.float32)
    for part in range(2):
        for half in range(halves):
            row = part * halves + half
            tile[row : row + 1, :] = in_order[
                part : part + 1, half * LANES : (half + 1) * LANES
            ]


def exact_dot(values, chosen):
    first = values.astype(jnp.bfloat16).astype(jnp.float32)
    left = values - first
    second = left.astype(jnp.bfloat16).astype(jnp.float32)
    third = left - second
    pad = jnp.zeros((10, values.shape[1]), jnp.float32)
    parts = jnp.concatenate([first, second, third, pad], axis=0).astype(jnp.bfloat16)
    picks = jnp.where(chosen, 1.0, 0.0).astype(jnp.bfloat16)
    out = lax.dot_general(
        parts, picks, (((1,), (1,)), ((), ())), preferred_element_type=jnp.float32
    )
    return out[0:2] + (out[2:4] + out[4:6])


def tracer_kernel(
    tracers, potential, before, after, table, neighbors, normal, weight, send_rows,
    tracers_new, fields, target, cosine, sine, scale, stokes, antiflux, lowered, ratios,
):
    me = lax.axis_index("mesh")
    peers, _, capacity = send_rows.shape
    halves = peers * capacity // LANES
    tracer_count, layers, cells = tracers.shape
    blocks = cells // LANES
    edges = neighbors.shape[0]
    field_rows = (tracer_count + 1) * layers
    groups = field_rows // 8
    layer_groups = layers // 8
    tracer_groups = tracer_count * layer_groups

    for b in range(2):
        fields[b] = before[b * field_rows : (b + 1) * field_rows, :]
        fields[blocks + 2 + b] = after[b * field_rows : (b + 1) * field_rows, :]
    for b in range(blocks):
        lanes = slice(b * LANES, (b + 1) * LANES)
        for t in range(tracer_count):
            fields[b + 2, t * layers : (t + 1) * layers, :] = tracers[t, :, lanes]
        fields[b + 2, field_rows - layers : field_rows, :] = potential[:, lanes]
    at = 2 * field_rows
    for b in range(blocks + 2):
        if b == 0 or b == blocks + 1:
            message = before if b == 0 else after
            near = message[at : at + edges, :].astype(jnp.int32)
            angle = message[at + 8 : at + 8 + edges, :]
            w = message[at + 16 : at + 16 + edges, :]
        else:
            lanes = slice((b - 1) * LANES, b * LANES)
            near = neighbors[:, lanes]
            angle = normal[:, lanes]
            w = weight[:, lanes]
        target[b, 0:edges, :] = near
        scale[b, 0:edges, :] = w
        cosine[b, 0:edges, :] = w * jnp.cos(angle)
        sine[b, 0:edges, :] = w * jnp.sin(angle)

    lane1 = lane_iota(1)
    lane8 = lane_iota(8)
    per_row = LANES // capacity
    for which in range(3):
        block = jnp.clip(me + which - 1, 0, peers - 1)
        cell = slot_rows(send_rows, block)
        first = block * capacity
        pick = (first % LANES) + lane8 % capacity
        found = [jnp.zeros((8, LANES), jnp.float32) for _ in range(halves)]
        for d in range(peers):
            half = d // per_row
            found[half] = jnp.where(
                lane8 // capacity == d % per_row, lane_gather(table[d], pick), found[half]
            )
        source_half = first // LANES
        values = []
        for part in range(2):
            row = []
            for half in range(halves):
                value = found[half][part * halves : part * halves + 1]
                for h in range(1, halves):
                    at_row = part * halves + h
                    value = jnp.where(source_half == h, found[half][at_row : at_row + 1], value)
                row.append(value)
            values.append(jnp.concatenate(row, axis=1))
        values = jnp.concatenate(values, axis=0)
        names = jnp.concatenate(cell, axis=1)
        count = cells if which == 1 else LANES
        start = cells - LANES if which == 0 else 0
        number = lax.broadcasted_iota(jnp.int32, (count, halves * LANES), 0) + start
        sums = exact_dot(values, number == names)
        if which == 1:
            for b in range(blocks):
                stokes[b + 1, 0:2, :] = sums[:, b * LANES : (b + 1) * LANES]
        else:
            stokes[0 if which == 0 else blocks + 1, 0:2, :] = sums

    decay = [
        jnp.exp(-3.0 / layers * (row_iota(8) + 8 * g).astype(jnp.float32))
        for g in range(layer_groups)
    ]

    def neighbour_of(near, b, s):
        row = spread(near[s : s + 1, :], 8)
        side = row // LANES - (me * blocks + b - 1)
        return row % LANES, side

    def low_order(b, carry):
        near = target[b]
        w = scale[b]
        slope = cosine[b] * stokes[b, 0:1, :] + sine[b] * stokes[b, 1:2, :]
        own = [fields[b + 1, 8 * g : 8 * g + 8, :] for g in range(groups)]
        zero = jnp.zeros((8, LANES), jnp.float32)
        out_speed = [zero] * layer_groups
        inflow = [zero] * tracer_groups
        upper = own[:tracer_groups]
        lower = own[:tracer_groups]
        positive = [zero] * tracer_groups
        negative = [zero] * tracer_groups
        for s in range(edges):
            lane, side = neighbour_of(near, b, s)
            w8 = spread(w[s : s + 1, :], 8)
            slope8 = spread(slope[s : s + 1, :], 8)
            beside = []
            for g in range(groups):
                rows = slice(8 * g, 8 * g + 8)
                middle = lane_gather(own[g], lane)
                left = lane_gather(fields[b, rows, :], lane)
                right = lane_gather(fields[b + 2, rows, :], lane)
                beside.append(jnp.where(side == 0, middle, jnp.where(side < 0, left, right)))
            for lg in range(layer_groups):
                k = tracer_groups + lg
                speed = w8 * (beside[k] - own[k]) + decay[lg] * slope8
                up = jnp.maximum(speed, 0.0)
                down = jnp.minimum(speed, 0.0)
                half = 0.5 * (up - down)
                out_speed[lg] = out_speed[lg] + up
                for t in range(tracer_count):
                    g = t * layer_groups + lg
                    q = beside[g]
                    flux = half * (q - own[g])
                    antiflux[b, s, 8 * g : 8 * g + 8, :] = flux
                    inflow[g] = inflow[g] + down * q
                    upper[g] = jnp.maximum(upper[g], q)
                    lower[g] = jnp.minimum(lower[g], q)
                    positive[g] = positive[g] + jnp.maximum(flux, 0.0)
                    negative[g] = negative[g] - jnp.minimum(flux, 0.0)
        for g in range(tracer_groups):
            rows = slice(8 * g, 8 * g + 8)
            value = own[g] - (out_speed[g % layer_groups] * own[g] + inflow[g])
            lowered[b, rows, :] = value
            plus = jnp.maximum(upper[g] - value, 0.0) / (negative[g] + FCT_FLOOR)
            minus = jnp.maximum(value - lower[g], 0.0) / (positive[g] + FCT_FLOOR)
            ratios[b, rows, :] = jnp.minimum(1.0, plus)
            at = 8 * (tracer_groups + g)
            ratios[b, at : at + 8, :] = jnp.minimum(1.0, minus)
        return carry

    lax.fori_loop(0, blocks + 2, low_order, 0)

    def limit(i, carry):
        b = i + 1
        near = target[b]
        out = [lowered[b, 8 * g : 8 * g + 8, :] for g in range(tracer_groups)]
        own = [ratios[b, 8 * g : 8 * g + 8, :] for g in range(2 * tracer_groups)]
        for s in range(edges):
            lane, side = neighbour_of(near, b, s)
            beside = []
            for g in range(2 * tracer_groups):
                rows = slice(8 * g, 8 * g + 8)
                middle = lane_gather(own[g], lane)
                left = lane_gather(ratios[b - 1, rows, :], lane)
                right = lane_gather(ratios[b + 1, rows, :], lane)
                beside.append(jnp.where(side == 0, middle, jnp.where(side < 0, left, right)))
            for g in range(tracer_groups):
                flux = antiflux[b, s, 8 * g : 8 * g + 8, :]
                m = g + tracer_groups
                factor = jnp.where(
                    flux >= 0.0,
                    jnp.minimum(own[m], beside[g]),
                    jnp.minimum(own[g], beside[m]),
                )
                out[g] = out[g] - factor * flux
        lanes = pl.ds(pl.multiple_of(i * LANES, LANES), LANES)
        for g in range(tracer_groups):
            t, lg = g // layer_groups, g % layer_groups
            tracers_new[t, 8 * lg : 8 * lg + 8, lanes] = out[g]
        return carry

    lax.fori_loop(0, blocks, limit, 0)


def whole_spec():
    return pl.BlockSpec(memory_space=pltpu.VMEM)


def local(
    tracers,
    potential,
    surface_current,
    cell_neighbors,
    cell_normal,
    cell_weight,
    spectra,
    wind_velocity,
    node_neighbors,
    node_normal,
    node_weight,
    send_rows,
    node_slot,
):
    peers = send_rows.shape[0]
    freqs, dirs, nodes = spectra.shape
    tracer_count, layers, cells = tracers.shape
    edges = cell_neighbors.shape[0]
    blocks = cells // LANES
    field_rows = (tracer_count + 1) * layers
    head_rows = 2 * field_rows + TABLE_ROWS
    message_rows = head_rows + (freqs // 2 * dirs + 7) // 8 * 8
    slots = node_slot.reshape(1, nodes)
    params = pltpu.CompilerParams(vmem_limit_bytes=VMEM_LIMIT)
    f32 = jnp.float32

    tile, ahead, behind = pl.pallas_call(
        pack_kernel,
        out_shape=(
            jax.ShapeDtypeStruct((8, LANES), f32),
            jax.ShapeDtypeStruct((message_rows, LANES), f32),
            jax.ShapeDtypeStruct((message_rows, LANES), f32),
        ),
        in_specs=[whole_spec()] * 9,
        out_specs=(whole_spec(),) * 3,
        compiler_params=params,
        name="pack",
    )(
        spectra, tracers, potential, cell_neighbors, cell_normal, cell_weight, surface_current,
        send_rows, slots,
    )
    up = [(i, i + 1) for i in range(peers - 1)]
    down = [(j, i) for i, j in up]
    before = lax.ppermute(ahead, "mesh", up)
    after = lax.ppermute(behind, "mesh", down)

    def everywhere(one):
        copies = jnp.broadcast_to(one[None], (peers,) + one.shape)
        return lax.all_to_all(copies, "mesh", 0, 0, tiled=True)

    currents = everywhere(tile)

    spectra_new, stokes_tile = pl.pallas_call(
        wave_kernel,
        out_shape=(
            jax.ShapeDtypeStruct(spectra.shape, f32),
            jax.ShapeDtypeStruct((8, LANES), f32),
        ),
        in_specs=[whole_spec()] * 10,
        out_specs=(whole_spec(),) * 2,
        scratch_shapes=[
            pltpu.VMEM((edges, dirs, LANES), f32),
            pltpu.VMEM((8, LANES), f32),
        ],
        compiler_params=params,
        name="wave",
    )(
        spectra, before, after, currents, slots, node_neighbors, node_normal, node_weight,
        wind_velocity, send_rows,
    )

    stokes_all = everywhere(stokes_tile)

    def head_spec():
        return pl.BlockSpec((head_rows, LANES), lambda i: (0, 0))

    def full_spec(x):
        zeros = (0,) * x.ndim
        return pl.BlockSpec(x.shape, lambda i: zeros)

    rows = tracer_count * layers
    tracers_new = pl.pallas_call(
        tracer_kernel,
        grid=(1,),
        out_shape=jax.ShapeDtypeStruct(tracers.shape, f32),
        in_specs=[
            full_spec(tracers),
            full_spec(potential),
            head_spec(),
            head_spec(),
            full_spec(stokes_all),
            full_spec(cell_neighbors),
            full_spec(cell_normal),
            full_spec(cell_weight),
            full_spec(send_rows),
        ],
        out_specs=full_spec(tracers),
        scratch_shapes=[
            pltpu.VMEM((blocks + 4, field_rows, LANES), f32),
            pltpu.VMEM((blocks + 2, 8, LANES), jnp.int32),
            pltpu.VMEM((blocks + 2, 8, LANES), f32),
            pltpu.VMEM((blocks + 2, 8, LANES), f32),
            pltpu.VMEM((blocks + 2, 8, LANES), f32),
            pltpu.VMEM((blocks + 2, 8, LANES), f32),
            pltpu.VMEM((blocks + 2, edges, rows, LANES), f32),
            pltpu.VMEM((blocks + 2, rows, LANES), f32),
            pltpu.VMEM((blocks + 2, 2 * rows, LANES), f32),
        ],
        compiler_params=params,
        name="tracer",
    )(
        tracers, potential, before, after, stokes_all, cell_neighbors, cell_normal, cell_weight,
        send_rows,
    )
    return tracers_new, spectra_new


def solution(mesh):
    return jax.shard_map(
        local,
        mesh=mesh,
        in_specs=(
            P(None, None, ("groups", "mesh")),
            P(None, ("groups", "mesh")),
            P(None, ("groups", "mesh")),
            P(None, "mesh"),
            P(None, "mesh"),
            P(None, "mesh"),
            P(None, None, ("groups", "mesh")),
            P(None, ("groups", "mesh")),
            P(None, "mesh"),
            P(None, "mesh"),
            P(None, "mesh"),
            P(),
            P("mesh"),
        ),
        out_specs=(P(None, None, ("groups", "mesh")), P(None, None, ("groups", "mesh"))),
        check_vma=False,
    )
```

```python
import math

import jax
import jax.numpy as jnp
from jax import lax
from jax.experimental import pallas as pl
from jax.experimental.pallas import tpu as pltpu
from jax.sharding import PartitionSpec as P

LANES = 128
FCT_FLOOR = 0.001
TABLE_ROWS = 24
VMEM_LIMIT = 48 * 1024 * 1024


def lane_gather(values, index):
    return jnp.take_along_axis(values, index, axis=1, mode="promise_in_bounds")


def spread(row, count):
    return jnp.broadcast_to(row, (count, LANES))


def lane_iota(rows):
    return lax.broadcasted_iota(jnp.int32, (rows, LANES), 1)


def row_iota(rows):
    return lax.broadcasted_iota(jnp.int32, (rows, LANES), 0)


def slot_rows(entry):
    peers, capacity = entry.shape
    wide = jnp.concatenate([entry, jnp.zeros((peers, LANES - capacity), jnp.int32)], axis=1)
    wide = lane_gather(wide, lane_iota(peers) % capacity)
    owner = row_iota(peers)
    out = []
    for half in range(peers * capacity // LANES):
        wanted = (lane_iota(peers) + half * LANES) // capacity
        picked = jnp.where(owner == wanted, wide, 0).astype(jnp.float32)
        out.append(jnp.sum(picked, axis=0, keepdims=True).astype(jnp.int32))
    return out


def half_mask(rows, lower):
    half = lane_iota(rows) // (LANES // 2)
    return half == jnp.where(lower, 0, 1)


def pack_kernel(
    spectra_in, tracers_in, potential_in, neighbors_in, normal_in, weight_in, current_in,
    send_rows, slot_in,
    tile, outer, inner, spectra,
    tracers, potential, neighbors, normal, weight, current, own_rows, node_slot, sems,
):
    me = lax.axis_index("mesh")
    copies = []
    for source, target in (
        (send_rows.at[me], own_rows),
        (current_in, current),
        (slot_in, node_slot),
        (spectra_in, spectra),
        (tracers_in, tracers),
        (potential_in, potential),
        (neighbors_in, neighbors),
        (normal_in, normal),
        (weight_in, weight),
    ):
        copy = pltpu.make_async_copy(source, target, sems.at[len(copies)])
        copy.start()
        copies.append(copy)
    for copy in copies[:3]:
        copy.wait()
    freqs, dirs = spectra.shape[:2]
    layers, cells = potential.shape
    blocks = cells // LANES
    field_rows = (tracers.shape[0] + 1) * layers
    stacked = jnp.concatenate(
        [current[:, b * LANES : (b + 1) * LANES] for b in range(blocks)], axis=0
    )
    place = row_iota(2 * blocks)
    halves = slot_rows(own_rows[...])
    tile[...] = jnp.zeros(tile.shape, jnp.float32)
    for half, cell in enumerate(halves):
        found = lane_gather(stacked, spread(cell % LANES, 2 * blocks))
        for part in range(2):
            picked = jnp.where(place == 2 * (cell // LANES) + part, found, 0.0)
            row = part * len(halves) + half
            tile[row : row + 1, :] = jnp.sum(picked, axis=0, keepdims=True)
    row = 2 * len(halves)
    tile[row : row + 1, :] = node_slot[...].astype(jnp.float32)
    for copy in copies[3:]:
        copy.wait()
    odd = me % 2 == 1
    for out, upward in ((outer, odd), (inner, jnp.logical_not(odd))):
        for b in range(2):
            high = slice((blocks - 2 + b) * LANES, (blocks - 1 + b) * LANES)
            low = slice(b * LANES, (b + 1) * LANES)
            base = b * field_rows
            for t in range(tracers.shape[0]):
                out[base + t * layers : base + (t + 1) * layers, :] = jnp.where(
                    upward, tracers[t, :, high], tracers[t, :, low]
                )
            out[base + field_rows - layers : base + field_rows, :] = jnp.where(
                upward, potential[:, high], potential[:, low]
            )
        high = slice((blocks - 1) * LANES, blocks * LANES)
        low = slice(0, LANES)
        base = 2 * field_rows
        out[base : base + TABLE_ROWS, :] = jnp.zeros((TABLE_ROWS, LANES), jnp.float32)
        edges = neighbors.shape[0]
        near = jnp.where(upward, neighbors[:, high], neighbors[:, low])
        out[base : base + edges, :] = near.astype(jnp.float32)
        out[base + 8 : base + 8 + edges, :] = jnp.where(upward, normal[:, high], normal[:, low])
        out[base + 16 : base + 16 + edges, :] = jnp.where(upward, weight[:, high], weight[:, low])
    base = 2 * field_rows + TABLE_ROWS
    pairs = freqs // 2
    whole = dirs // 8 * 8
    rest = dirs - whole
    turns = half_mask(dirs, odd)
    for g in range(pairs):
        natural = spectra[g]
        turned = pltpu.roll(spectra[g + pairs], LANES // 2, 1)
        for out, mixed in (
            (outer, jnp.where(turns, turned, natural)),
            (inner, jnp.where(turns, natural, turned)),
        ):
            at = base + g * whole
            out[at : at + whole, :] = mixed[:whole]
            at = base + pairs * whole + g * rest
            out[at : at + rest, :] = mixed[whole:]
    at = base + pairs * dirs
    if at < outer.shape[0]:
        for out in (outer, inner):
            out[at:, :] = jnp.zeros((outer.shape[0] - at, LANES), jnp.float32)


def node_currents(table, slot, block, capacity):
    peers = table.shape[0]
    halves = peers * capacity // LANES
    owner = slot // capacity
    entry = block * capacity + slot % capacity
    lane = spread(entry % LANES, 8)
    owner8 = spread(owner, 8)
    found = jnp.zeros((8, LANES), jnp.float32)
    for p in range(peers):
        found = jnp.where(owner8 == p, lane_gather(table[p], lane), found)
    half = entry // LANES
    out = []
    for part in range(2):
        value = found[part * halves : part * halves + 1]
        for h in range(1, halves):
            row = part * halves + h
            value = jnp.where(half == h, found[row : row + 1], value)
        out.append(value)
    return out


def wave_kernel(
    spectra, outer, inner, table, node_slot, neighbors, normal, weight, wind, send_rows,
    spectra_new, tile, project, drift,
):
    me = lax.axis_index("mesh")
    freqs, dirs = spectra.shape[:2]
    edges = neighbors.shape[0]
    peers, _, capacity = send_rows.shape
    halves = peers * capacity // LANES
    pairs = freqs // 2
    whole = dirs // 8 * 8
    rest = dirs - whole
    base = outer.shape[0] - (pairs * dirs + 7) // 8 * 8
    low1 = lane_iota(1) < LANES // 2

    slot = node_slot[...]
    row = 2 * halves
    previous = jnp.maximum(me - 1, 0)
    following = jnp.minimum(me + 1, peers - 1)
    beside_slot = jnp.where(
        low1, table[following][row : row + 1], table[previous][row : row + 1]
    ).astype(jnp.int32)
    beside_block = jnp.where(low1, following, previous)
    own_block = jnp.full((1, LANES), me, jnp.int32)
    own_x, own_y = node_currents(table, slot, own_block, capacity)
    halo_x, halo_y = node_currents(table, beside_slot, beside_block, capacity)

    target = neighbors[...]
    lane = target % LANES
    inside = target // LANES == me
    angle = normal[...]
    w = weight[...]
    cosine = w * jnp.cos(angle)
    sine = w * jnp.sin(angle)

    def beside(own, halo):
        a = lane_gather(spread(own, edges), lane)
        b = lane_gather(spread(halo, edges), lane)
        return jnp.where(inside, a, b)

    drift[0:edges, :] = (
        0.5 * (own_x + beside(own_x, halo_x)) * cosine
        + 0.5 * (own_y + beside(own_y, halo_y)) * sine
    )
    turn = 2.0 * math.pi / dirs * lax.broadcasted_iota(jnp.int32, (dirs, LANES), 0).astype(
        jnp.float32
    )
    cos_dir = jnp.cos(turn)
    sin_dir = jnp.sin(turn)
    for s in range(edges):
        project[s] = cos_dir * cosine[s : s + 1] + sin_dir * sine[s : s + 1]

    from_outer = half_mask(dirs, me % 2 == 1)
    straight = [spread(lane[s : s + 1], dirs) for s in range(edges)]
    swapped = [spread((lane[s : s + 1] + LANES // 2) % LANES, dirs) for s in range(edges)]
    within = [spread(target[s : s + 1] // LANES, dirs) == me for s in range(edges)]
    ratio = 1.0 / 1.1
    jump = ratio**pairs

    def pair(g, carry):
        speed, total = carry
        halo_parts = []
        for message in (outer, inner):
            at = pl.multiple_of(base + g * whole, 8)
            upper = message[pl.ds(at, whole), :]
            lower = message[pl.ds(base + pairs * whole + g * rest, rest), :]
            halo_parts.append(jnp.concatenate([upper, lower], axis=0))
        x, y = halo_parts
        for f, group_speed, halo, halo_lane in (
            (g, speed, jnp.where(from_outer, x, y), straight),
            (g + pairs, speed * jump, jnp.where(from_outer, y, x), swapped),
        ):
            own = spectra[f]
            out_speed = jnp.zeros((dirs, LANES), jnp.float32)
            inflow = jnp.zeros((dirs, LANES), jnp.float32)
            for s in range(edges):
                normal_speed = group_speed * project[s] + drift[s : s + 1]
                near = jnp.where(
                    within[s], lane_gather(own, straight[s]), lane_gather(halo, halo_lane[s])
                )
                out_speed = out_speed + jnp.maximum(normal_speed, 0.0)
                inflow = inflow + jnp.minimum(normal_speed, 0.0) * near
            advected = own - (out_speed * own + inflow)
            spectra_new[f] = advected
            total = total + advected
        return speed * ratio, total

    zero = jnp.zeros((dirs, LANES), jnp.float32)
    _, total = lax.fori_loop(0, pairs, pair, (jnp.float32(1.0), zero))
    mean = jnp.sum(total, axis=0, keepdims=True) * (1.0 / (freqs * dirs))
    forcing = jnp.maximum(wind[0:1, :] * cos_dir + wind[1:2, :] * sin_dir, 0.0)
    step = jnp.exp((0.25 * forcing - 2.0 * mean) * (1.0 / freqs))

    def grow(f, carry):
        factor, weighted = carry
        factor = factor * step
        evolved = spectra_new[f] * factor
        spectra_new[f] = evolved
        kappa = (f + 1).astype(jnp.float32) * (1.0 / freqs)
        return factor, weighted + kappa * evolved

    _, weighted = lax.fori_loop(0, freqs, grow, (zero + 1.0, zero))
    stokes = jnp.concatenate(
        [
            jnp.sum(weighted * cos_dir, axis=0, keepdims=True),
            jnp.sum(weighted * sin_dir, axis=0, keepdims=True),
        ],
        axis=0,
    ) * (1.0 / dirs)
    in_order = exact_dot(
        stokes, lax.broadcasted_iota(jnp.int32, (halves * LANES, LANES), 0) == slot
    )
    tile[...] = jnp.zeros(tile.shape, jnp.float32)
    for part in range(2):
        for half in range(halves):
            row = part * halves + half
            tile[row : row + 1, :] = in_order[
                part : part + 1, half * LANES : (half + 1) * LANES
            ]


def exact_dot(values, chosen):
    first = values.astype(jnp.bfloat16).astype(jnp.float32)
    left = values - first
    second = left.astype(jnp.bfloat16).astype(jnp.float32)
    third = left - second
    pad = jnp.zeros((10, values.shape[1]), jnp.float32)
    parts = jnp.concatenate([first, second, third, pad], axis=0).astype(jnp.bfloat16)
    picks = jnp.where(chosen, 1.0, 0.0).astype(jnp.bfloat16)
    out = lax.dot_general(
        parts, picks, (((1,), (1,)), ((), ())), preferred_element_type=jnp.float32
    )
    return out[0:2] + (out[2:4] + out[4:6])


def tracer_kernel(
    tracers, potential, outer, inner, table, neighbors, normal, weight, send_rows,
    tracers_new, fields, target, cosine, sine, scale, stokes, antiflux, lowered, ratios,
):
    me = lax.axis_index("mesh")
    peers, _, capacity = send_rows.shape
    halves = peers * capacity // LANES
    tracer_count, layers, cells = tracers.shape
    blocks = cells // LANES
    edges = neighbors.shape[0]
    field_rows = (tracer_count + 1) * layers
    groups = field_rows // 8
    layer_groups = layers // 8
    tracer_groups = tracer_count * layer_groups

    odd = me % 2 == 1
    for b in range(2):
        x = outer[b * field_rows : (b + 1) * field_rows, :]
        y = inner[b * field_rows : (b + 1) * field_rows, :]
        fields[b] = jnp.where(odd, y, x)
        fields[blocks + 2 + b] = jnp.where(odd, x, y)
    for b in range(blocks):
        lanes = slice(b * LANES, (b + 1) * LANES)
        for t in range(tracer_count):
            fields[b + 2, t * layers : (t + 1) * layers, :] = tracers[t, :, lanes]
        fields[b + 2, field_rows - layers : field_rows, :] = potential[:, lanes]
    at = 2 * field_rows
    for b in range(blocks + 2):
        if b == 0 or b == blocks + 1:
            x = outer[at : at + TABLE_ROWS, :]
            y = inner[at : at + TABLE_ROWS, :]
            table_rows = jnp.where(odd, y, x) if b == 0 else jnp.where(odd, x, y)
            near = table_rows[0:edges].astype(jnp.int32)
            angle = table_rows[8 : 8 + edges]
            w = table_rows[16 : 16 + edges]
        else:
            lanes = slice((b - 1) * LANES, b * LANES)
            near = neighbors[:, lanes]
            angle = normal[:, lanes]
            w = weight[:, lanes]
        target[b, 0:edges, :] = near
        scale[b, 0:edges, :] = w
        cosine[b, 0:edges, :] = w * jnp.cos(angle)
        sine[b, 0:edges, :] = w * jnp.sin(angle)

    lane1 = lane_iota(1)
    lane8 = lane_iota(8)
    per_row = LANES // capacity
    for which in range(3):
        block = jnp.clip(me + which - 1, 0, peers - 1)
        cell = slot_rows(send_rows[block])
        first = block * capacity
        pick = (first % LANES) + lane8 % capacity
        found = [jnp.zeros((8, LANES), jnp.float32) for _ in range(halves)]
        for d in range(peers):
            half = d // per_row
            found[half] = jnp.where(
                lane8 // capacity == d % per_row, lane_gather(table[d], pick), found[half]
            )
        source_half = first // LANES
        values = []
        for part in range(2):
            row = []
            for half in range(halves):
                value = found[half][part * halves : part * halves + 1]
                for h in range(1, halves):
                    at_row = part * halves + h
                    value = jnp.where(source_half == h, found[half][at_row : at_row + 1], value)
                row.append(value)
            values.append(jnp.concatenate(row, axis=1))
        values = jnp.concatenate(values, axis=0)
        names = jnp.concatenate(cell, axis=1)
        count = cells if which == 1 else LANES
        start = cells - LANES if which == 0 else 0
        number = lax.broadcasted_iota(jnp.int32, (count, halves * LANES), 0) + start
        sums = exact_dot(values, number == names)
        if which == 1:
            for b in range(blocks):
                stokes[b + 1, 0:2, :] = sums[:, b * LANES : (b + 1) * LANES]
        else:
            stokes[0 if which == 0 else blocks + 1, 0:2, :] = sums

    decay = [
        jnp.exp(-3.0 / layers * (row_iota(8) + 8 * g).astype(jnp.float32))
        for g in range(layer_groups)
    ]

    def neighbour_of(near, b, s):
        row = spread(near[s : s + 1, :], 8)
        side = row // LANES - (me * blocks + b - 1)
        return row % LANES, side

    def low_order(b, carry):
        near = target[b]
        w = scale[b]
        slope = cosine[b] * stokes[b, 0:1, :] + sine[b] * stokes[b, 1:2, :]
        own = [fields[b + 1, 8 * g : 8 * g + 8, :] for g in range(groups)]
        zero = jnp.zeros((8, LANES), jnp.float32)
        out_speed = [zero] * layer_groups
        inflow = [zero] * tracer_groups
        upper = own[:tracer_groups]
        lower = own[:tracer_groups]
        positive = [zero] * tracer_groups
        negative = [zero] * tracer_groups
        for s in range(edges):
            lane, side = neighbour_of(near, b, s)
            w8 = spread(w[s : s + 1, :], 8)
            slope8 = spread(slope[s : s + 1, :], 8)
            beside = []
            for g in range(groups):
                rows = slice(8 * g, 8 * g + 8)
                middle = lane_gather(own[g], lane)
                left = lane_gather(fields[b, rows, :], lane)
                right = lane_gather(fields[b + 2, rows, :], lane)
                beside.append(jnp.where(side == 0, middle, jnp.where(side < 0, left, right)))
            for lg in range(layer_groups):
                k = tracer_groups + lg
                speed = w8 * (beside[k] - own[k]) + decay[lg] * slope8
                up = jnp.maximum(speed, 0.0)
                down = jnp.minimum(speed, 0.0)
                half = 0.5 * (up - down)
                out_speed[lg] = out_speed[lg] + up
                for t in range(tracer_count):
                    g = t * layer_groups + lg
                    q = beside[g]
                    flux = half * (q - own[g])
                    antiflux[b, s, 8 * g : 8 * g + 8, :] = flux
                    inflow[g] = inflow[g] + down * q
                    upper[g] = jnp.maximum(upper[g], q)
                    lower[g] = jnp.minimum(lower[g], q)
                    positive[g] = positive[g] + jnp.maximum(flux, 0.0)
                    negative[g] = negative[g] - jnp.minimum(flux, 0.0)
        for g in range(tracer_groups):
            rows = slice(8 * g, 8 * g + 8)
            value = own[g] - (out_speed[g % layer_groups] * own[g] + inflow[g])
            lowered[b, rows, :] = value
            plus = jnp.maximum(upper[g] - value, 0.0) / (negative[g] + FCT_FLOOR)
            minus = jnp.maximum(value - lower[g], 0.0) / (positive[g] + FCT_FLOOR)
            ratios[b, rows, :] = jnp.minimum(1.0, plus)
            at = 8 * (tracer_groups + g)
            ratios[b, at : at + 8, :] = jnp.minimum(1.0, minus)
        return carry

    lax.fori_loop(0, blocks + 2, low_order, 0)

    def limit(i, carry):
        b = i + 1
        near = target[b]
        out = [lowered[b, 8 * g : 8 * g + 8, :] for g in range(tracer_groups)]
        own = [ratios[b, 8 * g : 8 * g + 8, :] for g in range(2 * tracer_groups)]
        for s in range(edges):
            lane, side = neighbour_of(near, b, s)
            beside = []
            for g in range(2 * tracer_groups):
                rows = slice(8 * g, 8 * g + 8)
                middle = lane_gather(own[g], lane)
                left = lane_gather(ratios[b - 1, rows, :], lane)
                right = lane_gather(ratios[b + 1, rows, :], lane)
                beside.append(jnp.where(side == 0, middle, jnp.where(side < 0, left, right)))
            for g in range(tracer_groups):
                flux = antiflux[b, s, 8 * g : 8 * g + 8, :]
                m = g + tracer_groups
                factor = jnp.where(
                    flux >= 0.0,
                    jnp.minimum(own[m], beside[g]),
                    jnp.minimum(own[g], beside[m]),
                )
                out[g] = out[g] - factor * flux
        lanes = pl.ds(pl.multiple_of(i * LANES, LANES), LANES)
        for g in range(tracer_groups):
            t, lg = g // layer_groups, g % layer_groups
            tracers_new[t, 8 * lg : 8 * lg + 8, lanes] = out[g]
        return carry

    lax.fori_loop(0, blocks, limit, 0)


def swap(message, first, peers):
    pairs = []
    for i in range(first, peers - 1, 2):
        pairs += [(i, i + 1), (i + 1, i)]
    return lax.ppermute(message, "mesh", pairs)


def whole_spec():
    return pl.BlockSpec(memory_space=pltpu.VMEM)


def local(
    tracers,
    potential,
    surface_current,
    cell_neighbors,
    cell_normal,
    cell_weight,
    spectra,
    wind_velocity,
    node_neighbors,
    node_normal,
    node_weight,
    send_rows,
    node_slot,
):
    peers = send_rows.shape[0]
    freqs, dirs, nodes = spectra.shape
    tracer_count, layers, cells = tracers.shape
    edges = cell_neighbors.shape[0]
    blocks = cells // LANES
    field_rows = (tracer_count + 1) * layers
    head_rows = 2 * field_rows + TABLE_ROWS
    message_rows = head_rows + (freqs // 2 * dirs + 7) // 8 * 8
    slots = node_slot.reshape(1, nodes)
    params = pltpu.CompilerParams(vmem_limit_bytes=VMEM_LIMIT)
    f32 = jnp.float32

    stored = pl.BlockSpec(memory_space=pltpu.HBM)
    tile, outer, inner, own_spectra = pl.pallas_call(
        pack_kernel,
        out_shape=(
            jax.ShapeDtypeStruct((8, LANES), f32),
            jax.ShapeDtypeStruct((message_rows, LANES), f32),
            jax.ShapeDtypeStruct((message_rows, LANES), f32),
            jax.ShapeDtypeStruct(spectra.shape, f32),
        ),
        in_specs=[stored] * 9,
        out_specs=(whole_spec(),) * 4,
        scratch_shapes=[
            pltpu.VMEM(tracers.shape, f32),
            pltpu.VMEM(potential.shape, f32),
            pltpu.VMEM(cell_neighbors.shape, jnp.int32),
            pltpu.VMEM(cell_normal.shape, f32),
            pltpu.VMEM(cell_weight.shape, f32),
            pltpu.VMEM(surface_current.shape, f32),
            pltpu.VMEM(send_rows.shape[1:], jnp.int32),
            pltpu.VMEM(slots.shape, jnp.int32),
            pltpu.SemaphoreType.DMA((9,)),
        ],
        compiler_params=params,
        name="pack",
    )(
        *(
            pltpu.with_memory_space_constraint(x, pltpu.HBM)
            for x in (
                spectra, tracers, potential, cell_neighbors, cell_normal, cell_weight,
                surface_current, send_rows, slots,
            )
        )
    )
    outer = swap(outer, 1, peers)
    inner = swap(inner, 0, peers)

    def everywhere(one):
        copies = jnp.broadcast_to(one[None], (peers,) + one.shape)
        return lax.all_to_all(copies, "mesh", 0, 0, tiled=True)

    currents = everywhere(tile)

    spectra_new, stokes_tile = pl.pallas_call(
        wave_kernel,
        out_shape=(
            jax.ShapeDtypeStruct(spectra.shape, f32),
            jax.ShapeDtypeStruct((8, LANES), f32),
        ),
        in_specs=[whole_spec()] * 10,
        out_specs=(whole_spec(),) * 2,
        scratch_shapes=[
            pltpu.VMEM((edges, dirs, LANES), f32),
            pltpu.VMEM((8, LANES), f32),
        ],
        compiler_params=params,
        name="wave",
    )(
        own_spectra, outer, inner, currents, slots, node_neighbors, node_normal, node_weight,
        wind_velocity, send_rows,
    )

    stokes_all = everywhere(stokes_tile)

    def head_spec():
        return pl.BlockSpec((head_rows, LANES), lambda i: (0, 0))

    def full_spec(x):
        zeros = (0,) * x.ndim
        return pl.BlockSpec(x.shape, lambda i: zeros)

    rows = tracer_count * layers
    tracers_new = pl.pallas_call(
        tracer_kernel,
        grid=(1,),
        out_shape=jax.ShapeDtypeStruct(tracers.shape, f32),
        in_specs=[
            full_spec(tracers),
            full_spec(potential),
            head_spec(),
            head_spec(),
            full_spec(stokes_all),
            full_spec(cell_neighbors),
            full_spec(cell_normal),
            full_spec(cell_weight),
            full_spec(send_rows),
        ],
        out_specs=full_spec(tracers),
        scratch_shapes=[
            pltpu.VMEM((blocks + 4, field_rows, LANES), f32),
            pltpu.VMEM((blocks + 2, 8, LANES), jnp.int32),
            pltpu.VMEM((blocks + 2, 8, LANES), f32),
            pltpu.VMEM((blocks + 2, 8, LANES), f32),
            pltpu.VMEM((blocks + 2, 8, LANES), f32),
            pltpu.VMEM((blocks + 2, 8, LANES), f32),
            pltpu.VMEM((blocks + 2, edges, rows, LANES), f32),
            pltpu.VMEM((blocks + 2, rows, LANES), f32),
            pltpu.VMEM((blocks + 2, 2 * rows, LANES), f32),
        ],
        compiler_params=params,
        name="tracer",
    )(
        tracers, potential, outer, inner, stokes_all, cell_neighbors, cell_normal, cell_weight,
        send_rows,
    )
    return tracers_new, spectra_new


def solution(mesh):
    return jax.shard_map(
        local,
        mesh=mesh,
        in_specs=(
            P(None, None, ("groups", "mesh")),
            P(None, ("groups", "mesh")),
            P(None, ("groups", "mesh")),
            P(None, "mesh"),
            P(None, "mesh"),
            P(None, "mesh"),
            P(None, None, ("groups", "mesh")),
            P(None, ("groups", "mesh")),
            P(None, "mesh"),
            P(None, "mesh"),
            P(None, "mesh"),
            P(),
            P("mesh"),
        ),
        out_specs=(P(None, None, ("groups", "mesh")), P(None, None, ("groups", "mesh"))),
        check_vma=False,
    )
```

```python
import math

import jax
import jax.numpy as jnp
from jax import lax
from jax.experimental import pallas as pl
from jax.experimental.pallas import tpu as pltpu
from jax.sharding import PartitionSpec as P

LANES = 128
FCT_FLOOR = 0.001
TABLE_ROWS = 24
VMEM_LIMIT = 48 * 1024 * 1024


def lane_gather(values, index):
    return jnp.take_along_axis(values, index, axis=1, mode="promise_in_bounds")


def spread(row, count):
    return jnp.broadcast_to(row, (count, LANES))


def lane_iota(rows):
    return lax.broadcasted_iota(jnp.int32, (rows, LANES), 1)


def row_iota(rows):
    return lax.broadcasted_iota(jnp.int32, (rows, LANES), 0)


def slot_rows(entry):
    peers, capacity = entry.shape
    wide = jnp.concatenate([entry, jnp.zeros((peers, LANES - capacity), jnp.int32)], axis=1)
    wide = lane_gather(wide, lane_iota(peers) % capacity)
    owner = row_iota(peers)
    out = []
    for half in range(peers * capacity // LANES):
        wanted = (lane_iota(peers) + half * LANES) // capacity
        picked = jnp.where(owner == wanted, wide, 0).astype(jnp.float32)
        out.append(jnp.sum(picked, axis=0, keepdims=True).astype(jnp.int32))
    return out


def half_mask(rows, lower):
    half = lane_iota(rows) // (LANES // 2)
    return half == jnp.where(lower, 0, 1)


def pack_kernel(
    spectra_in, tracers_in, potential_in, neighbors_in, normal_in, weight_in, current_in,
    send_rows, slot_in,
    tile, outer, inner, spectra,
    tracers, potential, neighbors, normal, weight, current, own_rows, node_slot, sems,
):
    me = lax.axis_index("mesh")
    copies = []
    for source, target in (
        (send_rows.at[me], own_rows),
        (current_in, current),
        (slot_in, node_slot),
        (spectra_in, spectra),
        (tracers_in, tracers),
        (potential_in, potential),
        (neighbors_in, neighbors),
        (normal_in, normal),
        (weight_in, weight),
    ):
        copy = pltpu.make_async_copy(source, target, sems.at[len(copies)])
        copy.start()
        copies.append(copy)
    for copy in copies[:3]:
        copy.wait()
    freqs, dirs = spectra.shape[:2]
    layers, cells = potential.shape
    blocks = cells // LANES
    field_rows = (tracers.shape[0] + 1) * layers
    stacked = jnp.concatenate(
        [current[:, b * LANES : (b + 1) * LANES] for b in range(blocks)], axis=0
    )
    place = row_iota(2 * blocks)
    halves = slot_rows(own_rows[...])
    tile[...] = jnp.zeros(tile.shape, jnp.float32)
    for half, cell in enumerate(halves):
        found = lane_gather(stacked, spread(cell % LANES, 2 * blocks))
        for part in range(2):
            picked = jnp.where(place == 2 * (cell // LANES) + part, found, 0.0)
            row = part * len(halves) + half
            tile[row : row + 1, :] = jnp.sum(picked, axis=0, keepdims=True)
    row = 2 * len(halves)
    tile[row : row + 1, :] = node_slot[...].astype(jnp.float32)
    for copy in copies[3:]:
        copy.wait()
    odd = me % 2 == 1
    for out, upward in ((outer, odd), (inner, jnp.logical_not(odd))):
        for b in range(2):
            high = slice((blocks - 2 + b) * LANES, (blocks - 1 + b) * LANES)
            low = slice(b * LANES, (b + 1) * LANES)
            base = b * field_rows
            for t in range(tracers.shape[0]):
                out[base + t * layers : base + (t + 1) * layers, :] = jnp.where(
                    upward, tracers[t, :, high], tracers[t, :, low]
                )
            out[base + field_rows - layers : base + field_rows, :] = jnp.where(
                upward, potential[:, high], potential[:, low]
            )
        high = slice((blocks - 1) * LANES, blocks * LANES)
        low = slice(0, LANES)
        base = 2 * field_rows
        out[base : base + TABLE_ROWS, :] = jnp.zeros((TABLE_ROWS, LANES), jnp.float32)
        edges = neighbors.shape[0]
        near = jnp.where(upward, neighbors[:, high], neighbors[:, low])
        out[base : base + edges, :] = near.astype(jnp.float32)
        out[base + 8 : base + 8 + edges, :] = jnp.where(upward, normal[:, high], normal[:, low])
        out[base + 16 : base + 16 + edges, :] = jnp.where(upward, weight[:, high], weight[:, low])
    base = 2 * field_rows + TABLE_ROWS
    pairs = freqs // 2
    whole = dirs // 8 * 8
    rest = dirs - whole
    turns = half_mask(dirs, odd)
    for g in range(pairs):
        natural = spectra[g]
        turned = pltpu.roll(spectra[g + pairs], LANES // 2, 1)
        for out, mixed in (
            (outer, jnp.where(turns, turned, natural)),
            (inner, jnp.where(turns, natural, turned)),
        ):
            at = base + g * whole
            out[at : at + whole, :] = mixed[:whole]
            at = base + pairs * whole + g * rest
            out[at : at + rest, :] = mixed[whole:]
    at = base + pairs * dirs
    if at < outer.shape[0]:
        for out in (outer, inner):
            out[at:, :] = jnp.zeros((outer.shape[0] - at, LANES), jnp.float32)


def node_currents(table, slot, block, capacity):
    peers = table.shape[0]
    halves = peers * capacity // LANES
    owner = slot // capacity
    entry = block * capacity + slot % capacity
    lane = spread(entry % LANES, 8)
    owner8 = spread(owner, 8)
    found = jnp.zeros((8, LANES), jnp.float32)
    for p in range(peers):
        found = jnp.where(owner8 == p, lane_gather(table[p], lane), found)
    half = entry // LANES
    out = []
    for part in range(2):
        value = found[part * halves : part * halves + 1]
        for h in range(1, halves):
            row = part * halves + h
            value = jnp.where(half == h, found[row : row + 1], value)
        out.append(value)
    return out


def wave_kernel(
    spectra, outer, inner, table, node_slot, neighbors, normal, weight, wind, send_rows,
    spectra_new, tile, project, drift,
):
    me = lax.axis_index("mesh")
    freqs, dirs = spectra.shape[:2]
    edges = neighbors.shape[0]
    peers, _, capacity = send_rows.shape
    halves = peers * capacity // LANES
    pairs = freqs // 2
    whole = dirs // 8 * 8
    rest = dirs - whole
    base = outer.shape[0] - (pairs * dirs + 7) // 8 * 8
    low1 = lane_iota(1) < LANES // 2

    slot = node_slot[...]
    row = 2 * halves
    previous = jnp.maximum(me - 1, 0)
    following = jnp.minimum(me + 1, peers - 1)
    beside_slot = jnp.where(
        low1, table[following][row : row + 1], table[previous][row : row + 1]
    ).astype(jnp.int32)
    beside_block = jnp.where(low1, following, previous)
    own_block = jnp.full((1, LANES), me, jnp.int32)
    own_x, own_y = node_currents(table, slot, own_block, capacity)
    halo_x, halo_y = node_currents(table, beside_slot, beside_block, capacity)

    target = neighbors[...]
    lane = target % LANES
    inside = target // LANES == me
    angle = normal[...]
    w = weight[...]
    cosine = w * jnp.cos(angle)
    sine = w * jnp.sin(angle)

    def beside(own, halo):
        a = lane_gather(spread(own, edges), lane)
        b = lane_gather(spread(halo, edges), lane)
        return jnp.where(inside, a, b)

    drift[0:edges, :] = (
        0.5 * (own_x + beside(own_x, halo_x)) * cosine
        + 0.5 * (own_y + beside(own_y, halo_y)) * sine
    )
    turn = 2.0 * math.pi / dirs * lax.broadcasted_iota(jnp.int32, (dirs, LANES), 0).astype(
        jnp.float32
    )
    cos_dir = jnp.cos(turn)
    sin_dir = jnp.sin(turn)
    for s in range(edges):
        project[s] = cos_dir * cosine[s : s + 1] + sin_dir * sine[s : s + 1]

    from_outer = half_mask(dirs, me % 2 == 1)
    straight = [spread(lane[s : s + 1], dirs) for s in range(edges)]
    swapped = [spread((lane[s : s + 1] + LANES // 2) % LANES, dirs) for s in range(edges)]
    within = [spread(target[s : s + 1] // LANES, dirs) == me for s in range(edges)]
    ratio = 1.0 / 1.1
    jump = ratio**pairs

    def pair(g, carry):
        speed, total = carry
        halo_parts = []
        for message in (outer, inner):
            at = pl.multiple_of(base + g * whole, 8)
            upper = message[pl.ds(at, whole), :]
            lower = message[pl.ds(base + pairs * whole + g * rest, rest), :]
            halo_parts.append(jnp.concatenate([upper, lower], axis=0))
        x, y = halo_parts
        for f, group_speed, halo, halo_lane in (
            (g, speed, jnp.where(from_outer, x, y), straight),
            (g + pairs, speed * jump, jnp.where(from_outer, y, x), swapped),
        ):
            own = spectra[f]
            out_speed = jnp.zeros((dirs, LANES), jnp.float32)
            inflow = jnp.zeros((dirs, LANES), jnp.float32)
            for s in range(edges):
                normal_speed = group_speed * project[s] + drift[s : s + 1]
                near = jnp.where(
                    within[s], lane_gather(own, straight[s]), lane_gather(halo, halo_lane[s])
                )
                out_speed = out_speed + jnp.maximum(normal_speed, 0.0)
                inflow = inflow + jnp.minimum(normal_speed, 0.0) * near
            advected = own - (out_speed * own + inflow)
            spectra_new[f] = advected
            total = total + advected
        return speed * ratio, total

    zero = jnp.zeros((dirs, LANES), jnp.float32)
    _, total = lax.fori_loop(0, pairs, pair, (jnp.float32(1.0), zero))
    mean = jnp.sum(total, axis=0, keepdims=True) * (1.0 / (freqs * dirs))
    forcing = jnp.maximum(wind[0:1, :] * cos_dir + wind[1:2, :] * sin_dir, 0.0)
    step = jnp.exp((0.25 * forcing - 2.0 * mean) * (1.0 / freqs))

    def grow(f, carry):
        factor, weighted = carry
        factor = factor * step
        evolved = spectra_new[f] * factor
        spectra_new[f] = evolved
        kappa = (f + 1).astype(jnp.float32) * (1.0 / freqs)
        return factor, weighted + kappa * evolved

    _, weighted = lax.fori_loop(0, freqs, grow, (zero + 1.0, zero))
    stokes = jnp.concatenate(
        [
            jnp.sum(weighted * cos_dir, axis=0, keepdims=True),
            jnp.sum(weighted * sin_dir, axis=0, keepdims=True),
        ],
        axis=0,
    ) * (1.0 / dirs)
    in_order = exact_dot(
        stokes, lax.broadcasted_iota(jnp.int32, (halves * LANES, LANES), 0) == slot
    )
    tile[...] = jnp.zeros(tile.shape, jnp.float32)
    for part in range(2):
        for half in range(halves):
            row = part * halves + half
            tile[row : row + 1, :] = in_order[
                part : part + 1, half * LANES : (half + 1) * LANES
            ]


def exact_dot(values, chosen):
    first = values.astype(jnp.bfloat16).astype(jnp.float32)
    left = values - first
    second = left.astype(jnp.bfloat16).astype(jnp.float32)
    third = left - second
    pad = jnp.zeros((10, values.shape[1]), jnp.float32)
    parts = jnp.concatenate([first, second, third, pad], axis=0).astype(jnp.bfloat16)
    picks = jnp.where(chosen, 1.0, 0.0).astype(jnp.bfloat16)
    out = lax.dot_general(
        parts, picks, (((1,), (1,)), ((), ())), preferred_element_type=jnp.float32
    )
    return out[0:2] + (out[2:4] + out[4:6])


def tracer_kernel(
    tracers, potential, outer, inner, table, neighbors, normal, weight, send_rows,
    tracers_new, fields, target, cosine, sine, scale, stokes, antiflux, lowered, ratios,
):
    me = lax.axis_index("mesh")
    peers, _, capacity = send_rows.shape
    halves = peers * capacity // LANES
    tracer_count, layers, cells = tracers.shape
    blocks = cells // LANES
    edges = neighbors.shape[0]
    field_rows = (tracer_count + 1) * layers
    groups = field_rows // 8
    layer_groups = layers // 8
    tracer_groups = tracer_count * layer_groups

    odd = me % 2 == 1
    for b in range(2):
        x = outer[b * field_rows : (b + 1) * field_rows, :]
        y = inner[b * field_rows : (b + 1) * field_rows, :]
        fields[b] = jnp.where(odd, y, x)
        fields[blocks + 2 + b] = jnp.where(odd, x, y)
    for b in range(blocks):
        lanes = slice(b * LANES, (b + 1) * LANES)
        for t in range(tracer_count):
            fields[b + 2, t * layers : (t + 1) * layers, :] = tracers[t, :, lanes]
        fields[b + 2, field_rows - layers : field_rows, :] = potential[:, lanes]
    at = 2 * field_rows
    for b in range(blocks + 2):
        if b == 0 or b == blocks + 1:
            x = outer[at : at + TABLE_ROWS, :]
            y = inner[at : at + TABLE_ROWS, :]
            table_rows = jnp.where(odd, y, x) if b == 0 else jnp.where(odd, x, y)
            near = table_rows[0:edges].astype(jnp.int32)
            angle = table_rows[8 : 8 + edges]
            w = table_rows[16 : 16 + edges]
        else:
            lanes = slice((b - 1) * LANES, b * LANES)
            near = neighbors[:, lanes]
            angle = normal[:, lanes]
            w = weight[:, lanes]
        target[b, 0:edges, :] = near
        scale[b, 0:edges, :] = w
        cosine[b, 0:edges, :] = w * jnp.cos(angle)
        sine[b, 0:edges, :] = w * jnp.sin(angle)

    lane1 = lane_iota(1)
    lane8 = lane_iota(8)
    per_row = LANES // capacity
    for which in range(3):
        block = jnp.clip(me + which - 1, 0, peers - 1)
        cell = slot_rows(send_rows[block])
        first = block * capacity
        pick = (first % LANES) + lane8 % capacity
        found = [jnp.zeros((8, LANES), jnp.float32) for _ in range(halves)]
        for d in range(peers):
            half = d // per_row
            found[half] = jnp.where(
                lane8 // capacity == d % per_row, lane_gather(table[d], pick), found[half]
            )
        source_half = first // LANES
        values = []
        for part in range(2):
            row = []
            for half in range(halves):
                value = found[half][part * halves : part * halves + 1]
                for h in range(1, halves):
                    at_row = part * halves + h
                    value = jnp.where(source_half == h, found[half][at_row : at_row + 1], value)
                row.append(value)
            values.append(jnp.concatenate(row, axis=1))
        values = jnp.concatenate(values, axis=0)
        names = jnp.concatenate(cell, axis=1)
        count = cells if which == 1 else LANES
        start = cells - LANES if which == 0 else 0
        number = lax.broadcasted_iota(jnp.int32, (count, halves * LANES), 0) + start
        sums = exact_dot(values, number == names)
        if which == 1:
            for b in range(blocks):
                stokes[b + 1, 0:2, :] = sums[:, b * LANES : (b + 1) * LANES]
        else:
            stokes[0 if which == 0 else blocks + 1, 0:2, :] = sums

    decay = [
        jnp.exp(-3.0 / layers * (row_iota(8) + 8 * g).astype(jnp.float32))
        for g in range(layer_groups)
    ]

    def neighbour_of(near, b, s):
        row = spread(near[s : s + 1, :], 8)
        side = row // LANES - (me * blocks + b - 1)
        return row % LANES, side

    def low_order(b, carry):
        near = target[b]
        w = scale[b]
        slope = cosine[b] * stokes[b, 0:1, :] + sine[b] * stokes[b, 1:2, :]
        own = [fields[b + 1, 8 * g : 8 * g + 8, :] for g in range(groups)]
        zero = jnp.zeros((8, LANES), jnp.float32)
        out_speed = [zero] * layer_groups
        inflow = [zero] * tracer_groups
        upper = own[:tracer_groups]
        lower = own[:tracer_groups]
        positive = [zero] * tracer_groups
        negative = [zero] * tracer_groups
        for s in range(edges):
            lane, side = neighbour_of(near, b, s)
            w8 = spread(w[s : s + 1, :], 8)
            slope8 = spread(slope[s : s + 1, :], 8)
            beside = []
            for g in range(groups):
                rows = slice(8 * g, 8 * g + 8)
                middle = lane_gather(own[g], lane)
                left = lane_gather(fields[b, rows, :], lane)
                right = lane_gather(fields[b + 2, rows, :], lane)
                beside.append(jnp.where(side == 0, middle, jnp.where(side < 0, left, right)))
            for lg in range(layer_groups):
                k = tracer_groups + lg
                speed = w8 * (beside[k] - own[k]) + decay[lg] * slope8
                up = jnp.maximum(speed, 0.0)
                down = jnp.minimum(speed, 0.0)
                half = 0.5 * (up - down)
                out_speed[lg] = out_speed[lg] + up
                for t in range(tracer_count):
                    g = t * layer_groups + lg
                    q = beside[g]
                    flux = half * (q - own[g])
                    antiflux[b, s, 8 * g : 8 * g + 8, :] = flux
                    inflow[g] = inflow[g] + down * q
                    upper[g] = jnp.maximum(upper[g], q)
                    lower[g] = jnp.minimum(lower[g], q)
                    positive[g] = positive[g] + jnp.maximum(flux, 0.0)
                    negative[g] = negative[g] - jnp.minimum(flux, 0.0)
        for g in range(tracer_groups):
            rows = slice(8 * g, 8 * g + 8)
            value = own[g] - (out_speed[g % layer_groups] * own[g] + inflow[g])
            lowered[b, rows, :] = value
            plus = jnp.maximum(upper[g] - value, 0.0) / (negative[g] + FCT_FLOOR)
            minus = jnp.maximum(value - lower[g], 0.0) / (positive[g] + FCT_FLOOR)
            ratios[b, rows, :] = jnp.minimum(1.0, plus)
            at = 8 * (tracer_groups + g)
            ratios[b, at : at + 8, :] = jnp.minimum(1.0, minus)
        return carry

    lax.fori_loop(0, blocks + 2, low_order, 0)

    def limit(i, carry):
        b = i + 1
        near = target[b]
        out = [lowered[b, 8 * g : 8 * g + 8, :] for g in range(tracer_groups)]
        own = [ratios[b, 8 * g : 8 * g + 8, :] for g in range(2 * tracer_groups)]
        for s in range(edges):
            lane, side = neighbour_of(near, b, s)
            beside = []
            for g in range(2 * tracer_groups):
                rows = slice(8 * g, 8 * g + 8)
                middle = lane_gather(own[g], lane)
                left = lane_gather(ratios[b - 1, rows, :], lane)
                right = lane_gather(ratios[b + 1, rows, :], lane)
                beside.append(jnp.where(side == 0, middle, jnp.where(side < 0, left, right)))
            for g in range(tracer_groups):
                flux = antiflux[b, s, 8 * g : 8 * g + 8, :]
                m = g + tracer_groups
                factor = jnp.where(
                    flux >= 0.0,
                    jnp.minimum(own[m], beside[g]),
                    jnp.minimum(own[g], beside[m]),
                )
                out[g] = out[g] - factor * flux
        lanes = pl.ds(pl.multiple_of(i * LANES, LANES), LANES)
        for g in range(tracer_groups):
            t, lg = g // layer_groups, g % layer_groups
            tracers_new[t, 8 * lg : 8 * lg + 8, lanes] = out[g]
        return carry

    lax.fori_loop(0, blocks, limit, 0)


def swap(message, first, peers):
    pairs = []
    for i in range(first, peers - 1, 2):
        pairs += [(i, i + 1), (i + 1, i)]
    return lax.ppermute(message, "mesh", pairs)


def whole_spec():
    return pl.BlockSpec(memory_space=pltpu.VMEM)


def local(
    tracers,
    potential,
    surface_current,
    cell_neighbors,
    cell_normal,
    cell_weight,
    spectra,
    wind_velocity,
    node_neighbors,
    node_normal,
    node_weight,
    send_rows,
    node_slot,
):
    peers = send_rows.shape[0]
    freqs, dirs, nodes = spectra.shape
    tracer_count, layers, cells = tracers.shape
    edges = cell_neighbors.shape[0]
    blocks = cells // LANES
    field_rows = (tracer_count + 1) * layers
    head_rows = 2 * field_rows + TABLE_ROWS
    message_rows = head_rows + (freqs // 2 * dirs + 7) // 8 * 8
    slots = node_slot.reshape(1, nodes)
    params = pltpu.CompilerParams(vmem_limit_bytes=VMEM_LIMIT)
    f32 = jnp.float32

    stored = pl.BlockSpec(memory_space=pltpu.HBM)
    tile, outer, inner, own_spectra = pl.pallas_call(
        pack_kernel,
        out_shape=(
            jax.ShapeDtypeStruct((8, LANES), f32),
            jax.ShapeDtypeStruct((message_rows, LANES), f32),
            jax.ShapeDtypeStruct((message_rows, LANES), f32),
            jax.ShapeDtypeStruct(spectra.shape, f32),
        ),
        in_specs=[stored] * 9,
        out_specs=(whole_spec(),) * 4,
        scratch_shapes=[
            pltpu.VMEM(tracers.shape, f32),
            pltpu.VMEM(potential.shape, f32),
            pltpu.VMEM(cell_neighbors.shape, jnp.int32),
            pltpu.VMEM(cell_normal.shape, f32),
            pltpu.VMEM(cell_weight.shape, f32),
            pltpu.VMEM(surface_current.shape, f32),
            pltpu.VMEM(send_rows.shape[1:], jnp.int32),
            pltpu.VMEM(slots.shape, jnp.int32),
            pltpu.SemaphoreType.DMA((9,)),
        ],
        compiler_params=params,
        name="pack",
    )(
        *(
            pltpu.with_memory_space_constraint(x, pltpu.HBM)
            for x in (
                spectra, tracers, potential, cell_neighbors, cell_normal, cell_weight,
                surface_current, send_rows, slots,
            )
        )
    )
    outer = swap(outer, 1, peers)
    inner = swap(inner, 0, peers)

    def everywhere(one):
        return lax.all_gather(one, "mesh")

    currents = everywhere(tile)

    spectra_new, stokes_tile = pl.pallas_call(
        wave_kernel,
        out_shape=(
            jax.ShapeDtypeStruct(spectra.shape, f32),
            jax.ShapeDtypeStruct((8, LANES), f32),
        ),
        in_specs=[whole_spec()] * 10,
        out_specs=(whole_spec(),) * 2,
        scratch_shapes=[
            pltpu.VMEM((edges, dirs, LANES), f32),
            pltpu.VMEM((8, LANES), f32),
        ],
        compiler_params=params,
        name="wave",
    )(
        own_spectra, outer, inner, currents, slots, node_neighbors, node_normal, node_weight,
        wind_velocity, send_rows,
    )

    stokes_all = everywhere(stokes_tile)

    def head_spec():
        return pl.BlockSpec((head_rows, LANES), lambda i: (0, 0))

    def full_spec(x):
        zeros = (0,) * x.ndim
        return pl.BlockSpec(x.shape, lambda i: zeros)

    rows = tracer_count * layers
    tracers_new = pl.pallas_call(
        tracer_kernel,
        grid=(1,),
        out_shape=jax.ShapeDtypeStruct(tracers.shape, f32),
        in_specs=[
            full_spec(tracers),
            full_spec(potential),
            head_spec(),
            head_spec(),
            full_spec(stokes_all),
            full_spec(cell_neighbors),
            full_spec(cell_normal),
            full_spec(cell_weight),
            full_spec(send_rows),
        ],
        out_specs=full_spec(tracers),
        scratch_shapes=[
            pltpu.VMEM((blocks + 4, field_rows, LANES), f32),
            pltpu.VMEM((blocks + 2, 8, LANES), jnp.int32),
            pltpu.VMEM((blocks + 2, 8, LANES), f32),
            pltpu.VMEM((blocks + 2, 8, LANES), f32),
            pltpu.VMEM((blocks + 2, 8, LANES), f32),
            pltpu.VMEM((blocks + 2, 8, LANES), f32),
            pltpu.VMEM((blocks + 2, edges, rows, LANES), f32),
            pltpu.VMEM((blocks + 2, rows, LANES), f32),
            pltpu.VMEM((blocks + 2, 2 * rows, LANES), f32),
        ],
        compiler_params=params,
        name="tracer",
    )(
        tracers, potential, outer, inner, stokes_all, cell_neighbors, cell_normal, cell_weight,
        send_rows,
    )
    return tracers_new, spectra_new


def solution(mesh):
    return jax.shard_map(
        local,
        mesh=mesh,
        in_specs=(
            P(None, None, ("groups", "mesh")),
            P(None, ("groups", "mesh")),
            P(None, ("groups", "mesh")),
            P(None, "mesh"),
            P(None, "mesh"),
            P(None, "mesh"),
            P(None, None, ("groups", "mesh")),
            P(None, ("groups", "mesh")),
            P(None, "mesh"),
            P(None, "mesh"),
            P(None, "mesh"),
            P(),
            P("mesh"),
        ),
        out_specs=(P(None, None, ("groups", "mesh")), P(None, None, ("groups", "mesh"))),
        check_vma=False,
    )
```

```python
import functools
import math

import jax
import jax.numpy as jnp
from jax import lax
from jax.experimental import pallas as pl
from jax.experimental.pallas import tpu as pltpu
from jax.sharding import PartitionSpec as P

LANES = 128
FCT_FLOOR = 0.001
TABLE_ROWS = 24
VMEM_LIMIT = 48 * 1024 * 1024


def lane_gather(values, index):
    return jnp.take_along_axis(values, index, axis=1, mode="promise_in_bounds")


def spread(row, count):
    return jnp.broadcast_to(row, (count, LANES))


def lane_iota(rows):
    return lax.broadcasted_iota(jnp.int32, (rows, LANES), 1)


def row_iota(rows):
    return lax.broadcasted_iota(jnp.int32, (rows, LANES), 0)


def slot_rows(entry):
    peers, capacity = entry.shape
    wide = jnp.concatenate([entry, jnp.zeros((peers, LANES - capacity), jnp.int32)], axis=1)
    wide = lane_gather(wide, lane_iota(peers) % capacity)
    owner = row_iota(peers)
    out = []
    for half in range(peers * capacity // LANES):
        wanted = (lane_iota(peers) + half * LANES) // capacity
        picked = jnp.where(owner == wanted, wide, 0).astype(jnp.float32)
        out.append(jnp.sum(picked, axis=0, keepdims=True).astype(jnp.int32))
    return out


def half_mask(rows, lower):
    half = lane_iota(rows) // (LANES // 2)
    return half == jnp.where(lower, 0, 1)


def peer_rows(values, peers, capacity):
    lane = lane_iota(peers)
    group = lane // capacity
    block = jnp.clip(row_iota(peers) - 1 + group // 2, 0, peers - 1)
    entry = block * capacity + lane % capacity
    out = jnp.zeros((peers, LANES), jnp.float32)
    for part in range(2):
        for half, row in enumerate(values[part]):
            found = lane_gather(spread(row, peers), entry % LANES)
            wanted = (group < 6) & (group % 2 == part) & (entry // LANES == half)
            out = jnp.where(wanted, found, out)
    return out


def pack_kernel(
    spectra_in, tracers_in, potential_in, neighbors_in, normal_in, weight_in, current_in,
    send_rows, slot_in, near_in, angle_in, face_in, wind_in,
    rows_out, outer, inner, spectra, node_slot, near, angle, face, wind,
    tracers, potential, neighbors, normal, weight, current, own_rows, sems,
):
    peers, _, capacity = send_rows.shape
    me = lax.axis_index("mesh")
    copies = []
    for source, target in (
        (send_rows.at[me], own_rows),
        (current_in, current),
        (slot_in, node_slot),
        (spectra_in, spectra),
        (tracers_in, tracers),
        (potential_in, potential),
        (neighbors_in, neighbors),
        (normal_in, normal),
        (weight_in, weight),
        (near_in, near),
        (angle_in, angle),
        (face_in, face),
        (wind_in, wind),
    ):
        copy = pltpu.make_async_copy(source, target, sems.at[len(copies)])
        copy.start()
        copies.append(copy)
    for copy in copies[:3]:
        copy.wait()
    freqs, dirs = spectra.shape[:2]
    layers, cells = potential.shape
    blocks = cells // LANES
    field_rows = (tracers.shape[0] + 1) * layers
    stacked = jnp.concatenate(
        [current[:, b * LANES : (b + 1) * LANES] for b in range(blocks)], axis=0
    )
    place = row_iota(2 * blocks)
    halves = slot_rows(own_rows[...])
    values = [[], []]
    for cell in halves:
        found = lane_gather(stacked, spread(cell % LANES, 2 * blocks))
        for part in range(2):
            picked = jnp.where(place == 2 * (cell // LANES) + part, found, 0.0)
            values[part].append(jnp.sum(picked, axis=0, keepdims=True))
    rows_out[...] = peer_rows(values, peers, capacity)
    for copy in copies[3:]:
        copy.wait()
    odd = me % 2 == 1
    for out, upward in ((outer, odd), (inner, jnp.logical_not(odd))):
        for b in range(2):
            high = slice((blocks - 2 + b) * LANES, (blocks - 1 + b) * LANES)
            low = slice(b * LANES, (b + 1) * LANES)
            base = b * field_rows
            for t in range(tracers.shape[0]):
                out[base + t * layers : base + (t + 1) * layers, :] = jnp.where(
                    upward, tracers[t, :, high], tracers[t, :, low]
                )
            out[base + field_rows - layers : base + field_rows, :] = jnp.where(
                upward, potential[:, high], potential[:, low]
            )
        high = slice((blocks - 1) * LANES, blocks * LANES)
        low = slice(0, LANES)
        base = 2 * field_rows
        out[base : base + TABLE_ROWS, :] = jnp.zeros((TABLE_ROWS, LANES), jnp.float32)
        edges = neighbors.shape[0]
        near = jnp.where(upward, neighbors[:, high], neighbors[:, low])
        out[base : base + edges, :] = near.astype(jnp.float32)
        out[base + edges : base + edges + 1, :] = node_slot[...].astype(jnp.float32)
        out[base + 8 : base + 8 + edges, :] = jnp.where(upward, normal[:, high], normal[:, low])
        out[base + 16 : base + 16 + edges, :] = jnp.where(upward, weight[:, high], weight[:, low])
    base = 2 * field_rows + TABLE_ROWS
    pairs = freqs // 2
    whole = dirs // 8 * 8
    rest = dirs - whole
    turns = half_mask(dirs, odd)
    for g in range(pairs):
        natural = spectra[g]
        turned = pltpu.roll(spectra[g + pairs], LANES // 2, 1)
        for out, mixed in (
            (outer, jnp.where(turns, turned, natural)),
            (inner, jnp.where(turns, natural, turned)),
        ):
            at = base + g * whole
            out[at : at + whole, :] = mixed[:whole]
            at = base + pairs * whole + g * rest
            out[at : at + rest, :] = mixed[whole:]
    at = base + pairs * dirs
    if at < outer.shape[0]:
        for out in (outer, inner):
            out[at:, :] = jnp.zeros((outer.shape[0] - at, LANES), jnp.float32)


def node_currents(table, slot, which, capacity):
    peers = table.shape[0]
    owner = row_iota(peers) == slot // capacity
    out = []
    for part in range(2):
        lane = (2 * which + part) * capacity + slot % capacity
        found = jnp.where(owner, lane_gather(table, spread(lane, peers)), 0.0)
        out.append(jnp.sum(found, axis=0, keepdims=True))
    return out


def wave_kernel(
    capacity,
    spectra, outer, inner, table, node_slot, neighbors, normal, weight, wind,
    spectra_new, rows_out, project, drift,
):
    me = lax.axis_index("mesh")
    freqs, dirs = spectra.shape[:2]
    edges = neighbors.shape[0]
    peers = table.shape[0]
    halves = peers * capacity // LANES
    pairs = freqs // 2
    whole = dirs // 8 * 8
    rest = dirs - whole
    base = outer.shape[0] - (pairs * dirs + 7) // 8 * 8
    slot = node_slot[...]
    row = base - TABLE_ROWS + edges
    halo_slot = jnp.where(
        half_mask(1, me % 2 == 1), outer[row : row + 1, :], inner[row : row + 1, :]
    ).astype(jnp.int32)
    lower = lane_iota(1) < LANES // 2
    currents = table[...]
    own_x, own_y = node_currents(currents, slot, jnp.ones((1, LANES), jnp.int32), capacity)
    halo_x, halo_y = node_currents(currents, halo_slot, jnp.where(lower, 2, 0), capacity)

    target = neighbors[...]
    lane = target % LANES
    inside = target // LANES == me
    angle = normal[...]
    w = weight[...]
    cosine = w * jnp.cos(angle)
    sine = w * jnp.sin(angle)

    def beside(own, halo):
        a = lane_gather(spread(own, edges), lane)
        b = lane_gather(spread(halo, edges), lane)
        return jnp.where(inside, a, b)

    drift[0:edges, :] = (
        0.5 * (own_x + beside(own_x, halo_x)) * cosine
        + 0.5 * (own_y + beside(own_y, halo_y)) * sine
    )
    turn = 2.0 * math.pi / dirs * lax.broadcasted_iota(jnp.int32, (dirs, LANES), 0).astype(
        jnp.float32
    )
    cos_dir = jnp.cos(turn)
    sin_dir = jnp.sin(turn)
    for s in range(edges):
        project[s] = cos_dir * cosine[s : s + 1] + sin_dir * sine[s : s + 1]

    from_outer = half_mask(dirs, me % 2 == 1)
    straight = [spread(lane[s : s + 1], dirs) for s in range(edges)]
    swapped = [spread((lane[s : s + 1] + LANES // 2) % LANES, dirs) for s in range(edges)]
    within = [spread(target[s : s + 1] // LANES, dirs) == me for s in range(edges)]
    ratio = 1.0 / 1.1
    jump = ratio**pairs

    def pair(g, carry):
        speed, total = carry
        halo_parts = []
        for message in (outer, inner):
            at = pl.multiple_of(base + g * whole, 8)
            upper = message[pl.ds(at, whole), :]
            lower = message[pl.ds(base + pairs * whole + g * rest, rest), :]
            halo_parts.append(jnp.concatenate([upper, lower], axis=0))
        x, y = halo_parts
        for f, group_speed, halo, halo_lane in (
            (g, speed, jnp.where(from_outer, x, y), straight),
            (g + pairs, speed * jump, jnp.where(from_outer, y, x), swapped),
        ):
            own = spectra[f]
            out_speed = jnp.zeros((dirs, LANES), jnp.float32)
            inflow = jnp.zeros((dirs, LANES), jnp.float32)
            for s in range(edges):
                normal_speed = group_speed * project[s] + drift[s : s + 1]
                near = jnp.where(
                    within[s], lane_gather(own, straight[s]), lane_gather(halo, halo_lane[s])
                )
                out_speed = out_speed + jnp.maximum(normal_speed, 0.0)
                inflow = inflow + jnp.minimum(normal_speed, 0.0) * near
            advected = own - (out_speed * own + inflow)
            spectra_new[f] = advected
            total = total + advected
        return speed * ratio, total

    zero = jnp.zeros((dirs, LANES), jnp.float32)
    _, total = lax.fori_loop(0, pairs, pair, (jnp.float32(1.0), zero))
    mean = jnp.sum(total, axis=0, keepdims=True) * (1.0 / (freqs * dirs))
    forcing = jnp.maximum(wind[0:1, :] * cos_dir + wind[1:2, :] * sin_dir, 0.0)
    step = jnp.exp((0.25 * forcing - 2.0 * mean) * (1.0 / freqs))

    def grow(f, carry):
        factor, weighted = carry
        factor = factor * step
        evolved = spectra_new[f] * factor
        spectra_new[f] = evolved
        kappa = (f + 1).astype(jnp.float32) * (1.0 / freqs)
        return factor, weighted + kappa * evolved

    _, weighted = lax.fori_loop(0, freqs, grow, (zero + 1.0, zero))
    stokes = jnp.concatenate(
        [
            jnp.sum(weighted * cos_dir, axis=0, keepdims=True),
            jnp.sum(weighted * sin_dir, axis=0, keepdims=True),
        ],
        axis=0,
    ) * (1.0 / dirs)
    in_order = exact_dot(
        stokes, lax.broadcasted_iota(jnp.int32, (halves * LANES, LANES), 0) == slot
    )
    values = [
        [in_order[part : part + 1, h * LANES : (h + 1) * LANES] for h in range(halves)]
        for part in range(2)
    ]
    rows_out[...] = peer_rows(values, peers, capacity)


def exact_dot(values, chosen):
    first = values.astype(jnp.bfloat16).astype(jnp.float32)
    left = values - first
    second = left.astype(jnp.bfloat16).astype(jnp.float32)
    third = left - second
    pad = jnp.zeros((10, values.shape[1]), jnp.float32)
    parts = jnp.concatenate([first, second, third, pad], axis=0).astype(jnp.bfloat16)
    picks = jnp.where(chosen, 1.0, 0.0).astype(jnp.bfloat16)
    out = lax.dot_general(
        parts, picks, (((1,), (1,)), ((), ())), preferred_element_type=jnp.float32
    )
    return out[0:2] + (out[2:4] + out[4:6])


def tracer_kernel(
    tracers, potential, outer, inner, table, neighbors, normal, weight, send_rows,
    tracers_new, fields, target, cosine, sine, scale, stokes, antiflux, lowered, ratios,
):
    me = lax.axis_index("mesh")
    peers, _, capacity = send_rows.shape
    halves = peers * capacity // LANES
    tracer_count, layers, cells = tracers.shape
    blocks = cells // LANES
    edges = neighbors.shape[0]
    field_rows = (tracer_count + 1) * layers
    groups = field_rows // 8
    layer_groups = layers // 8
    tracer_groups = tracer_count * layer_groups

    odd = me % 2 == 1
    for b in range(2):
        x = outer[b * field_rows : (b + 1) * field_rows, :]
        y = inner[b * field_rows : (b + 1) * field_rows, :]
        fields[b] = jnp.where(odd, y, x)
        fields[blocks + 2 + b] = jnp.where(odd, x, y)
    for b in range(blocks):
        lanes = slice(b * LANES, (b + 1) * LANES)
        for t in range(tracer_count):
            fields[b + 2, t * layers : (t + 1) * layers, :] = tracers[t, :, lanes]
        fields[b + 2, field_rows - layers : field_rows, :] = potential[:, lanes]
    at = 2 * field_rows
    for b in range(blocks + 2):
        if b == 0 or b == blocks + 1:
            x = outer[at : at + TABLE_ROWS, :]
            y = inner[at : at + TABLE_ROWS, :]
            table_rows = jnp.where(odd, y, x) if b == 0 else jnp.where(odd, x, y)
            near = table_rows[0:edges].astype(jnp.int32)
            angle = table_rows[8 : 8 + edges]
            w = table_rows[16 : 16 + edges]
        else:
            lanes = slice((b - 1) * LANES, b * LANES)
            near = neighbors[:, lanes]
            angle = normal[:, lanes]
            w = weight[:, lanes]
        target[b, 0:edges, :] = near
        scale[b, 0:edges, :] = w
        cosine[b, 0:edges, :] = w * jnp.cos(angle)
        sine[b, 0:edges, :] = w * jnp.sin(angle)

    received = table[...]
    lane_of = lane_iota(peers)
    for which in range(3):
        cell = slot_rows(send_rows[jnp.clip(me + which - 1, 0, peers - 1)])
        values = []
        for part in range(2):
            lane = (2 * which + part) * capacity + lane_of % capacity
            found = lane_gather(received, lane)
            row = []
            for half in range(halves):
                mine = row_iota(peers) == (lane_of + half * LANES) // capacity
                row.append(jnp.sum(jnp.where(mine, found, 0.0), axis=0, keepdims=True))
            values.append(jnp.concatenate(row, axis=1))
        values = jnp.concatenate(values, axis=0)
        names = jnp.concatenate(cell, axis=1)
        count = cells if which == 1 else LANES
        start = cells - LANES if which == 0 else 0
        number = lax.broadcasted_iota(jnp.int32, (count, halves * LANES), 0) + start
        sums = exact_dot(values, number == names)
        if which == 1:
            for b in range(blocks):
                stokes[b + 1, 0:2, :] = sums[:, b * LANES : (b + 1) * LANES]
        else:
            stokes[0 if which == 0 else blocks + 1, 0:2, :] = sums

    decay = [
        jnp.exp(-3.0 / layers * (row_iota(8) + 8 * g).astype(jnp.float32))
        for g in range(layer_groups)
    ]

    def neighbour_of(near, b, s):
        row = spread(near[s : s + 1, :], 8)
        side = row // LANES - (me * blocks + b - 1)
        return row % LANES, side

    def low_order(b, carry):
        near = target[b]
        w = scale[b]
        slope = cosine[b] * stokes[b, 0:1, :] + sine[b] * stokes[b, 1:2, :]
        own = [fields[b + 1, 8 * g : 8 * g + 8, :] for g in range(groups)]
        zero = jnp.zeros((8, LANES), jnp.float32)
        out_speed = [zero] * layer_groups
        inflow = [zero] * tracer_groups
        upper = own[:tracer_groups]
        lower = own[:tracer_groups]
        positive = [zero] * tracer_groups
        negative = [zero] * tracer_groups
        for s in range(edges):
            lane, side = neighbour_of(near, b, s)
            w8 = spread(w[s : s + 1, :], 8)
            slope8 = spread(slope[s : s + 1, :], 8)
            beside = []
            for g in range(groups):
                rows = slice(8 * g, 8 * g + 8)
                middle = lane_gather(own[g], lane)
                left = lane_gather(fields[b, rows, :], lane)
                right = lane_gather(fields[b + 2, rows, :], lane)
                beside.append(jnp.where(side == 0, middle, jnp.where(side < 0, left, right)))
            for lg in range(layer_groups):
                k = tracer_groups + lg
                speed = w8 * (beside[k] - own[k]) + decay[lg] * slope8
                up = jnp.maximum(speed, 0.0)
                down = jnp.minimum(speed, 0.0)
                half = 0.5 * (up - down)
                out_speed[lg] = out_speed[lg] + up
                for t in range(tracer_count):
                    g = t * layer_groups + lg
                    q = beside[g]
                    flux = half * (q - own[g])
                    antiflux[b, s, 8 * g : 8 * g + 8, :] = flux
                    inflow[g] = inflow[g] + down * q
                    upper[g] = jnp.maximum(upper[g], q)
                    lower[g] = jnp.minimum(lower[g], q)
                    positive[g] = positive[g] + jnp.maximum(flux, 0.0)
                    negative[g] = negative[g] - jnp.minimum(flux, 0.0)
        for g in range(tracer_groups):
            rows = slice(8 * g, 8 * g + 8)
            value = own[g] - (out_speed[g % layer_groups] * own[g] + inflow[g])
            lowered[b, rows, :] = value
            plus = jnp.maximum(upper[g] - value, 0.0) / (negative[g] + FCT_FLOOR)
            minus = jnp.maximum(value - lower[g], 0.0) / (positive[g] + FCT_FLOOR)
            ratios[b, rows, :] = jnp.minimum(1.0, plus)
            at = 8 * (tracer_groups + g)
            ratios[b, at : at + 8, :] = jnp.minimum(1.0, minus)
        return carry

    lax.fori_loop(0, blocks + 2, low_order, 0)

    def limit(i, carry):
        b = i + 1
        near = target[b]
        out = [lowered[b, 8 * g : 8 * g + 8, :] for g in range(tracer_groups)]
        own = [ratios[b, 8 * g : 8 * g + 8, :] for g in range(2 * tracer_groups)]
        for s in range(edges):
            lane, side = neighbour_of(near, b, s)
            beside = []
            for g in range(2 * tracer_groups):
                rows = slice(8 * g, 8 * g + 8)
                middle = lane_gather(own[g], lane)
                left = lane_gather(ratios[b - 1, rows, :], lane)
                right = lane_gather(ratios[b + 1, rows, :], lane)
                beside.append(jnp.where(side == 0, middle, jnp.where(side < 0, left, right)))
            for g in range(tracer_groups):
                flux = antiflux[b, s, 8 * g : 8 * g + 8, :]
                m = g + tracer_groups
                factor = jnp.where(
                    flux >= 0.0,
                    jnp.minimum(own[m], beside[g]),
                    jnp.minimum(own[g], beside[m]),
                )
                out[g] = out[g] - factor * flux
        lanes = pl.ds(pl.multiple_of(i * LANES, LANES), LANES)
        for g in range(tracer_groups):
            t, lg = g // layer_groups, g % layer_groups
            tracers_new[t, 8 * lg : 8 * lg + 8, lanes] = out[g]
        return carry

    lax.fori_loop(0, blocks, limit, 0)


def swap(message, first, peers):
    pairs = []
    for i in range(first, peers - 1, 2):
        pairs += [(i, i + 1), (i + 1, i)]
    return lax.ppermute(message, "mesh", pairs)


def whole_spec():
    return pl.BlockSpec(memory_space=pltpu.VMEM)


def local(
    tracers,
    potential,
    surface_current,
    cell_neighbors,
    cell_normal,
    cell_weight,
    spectra,
    wind_velocity,
    node_neighbors,
    node_normal,
    node_weight,
    send_rows,
    node_slot,
):
    peers, _, capacity = send_rows.shape
    freqs, dirs, nodes = spectra.shape
    tracer_count, layers, cells = tracers.shape
    edges = cell_neighbors.shape[0]
    blocks = cells // LANES
    field_rows = (tracer_count + 1) * layers
    head_rows = 2 * field_rows + TABLE_ROWS
    message_rows = head_rows + (freqs // 2 * dirs + 7) // 8 * 8
    slots = node_slot.reshape(1, nodes)
    params = pltpu.CompilerParams(vmem_limit_bytes=VMEM_LIMIT)
    f32 = jnp.float32

    stored = pl.BlockSpec(memory_space=pltpu.HBM)
    currents, outer, inner, own_spectra, *node_tables = pl.pallas_call(
        pack_kernel,
        out_shape=(
            jax.ShapeDtypeStruct((peers, LANES), f32),
            jax.ShapeDtypeStruct((message_rows, LANES), f32),
            jax.ShapeDtypeStruct((message_rows, LANES), f32),
            jax.ShapeDtypeStruct(spectra.shape, f32),
            jax.ShapeDtypeStruct(slots.shape, jnp.int32),
            jax.ShapeDtypeStruct(node_neighbors.shape, jnp.int32),
            jax.ShapeDtypeStruct(node_normal.shape, f32),
            jax.ShapeDtypeStruct(node_weight.shape, f32),
            jax.ShapeDtypeStruct(wind_velocity.shape, f32),
        ),
        in_specs=[stored] * 13,
        out_specs=(whole_spec(),) * 9,
        scratch_shapes=[
            pltpu.VMEM(tracers.shape, f32),
            pltpu.VMEM(potential.shape, f32),
            pltpu.VMEM(cell_neighbors.shape, jnp.int32),
            pltpu.VMEM(cell_normal.shape, f32),
            pltpu.VMEM(cell_weight.shape, f32),
            pltpu.VMEM(surface_current.shape, f32),
            pltpu.VMEM(send_rows.shape[1:], jnp.int32),
            pltpu.SemaphoreType.DMA((13,)),
        ],
        compiler_params=params,
        name="pack",
    )(
        *(
            pltpu.with_memory_space_constraint(x, pltpu.HBM)
            for x in (
                spectra, tracers, potential, cell_neighbors, cell_normal, cell_weight,
                surface_current, send_rows, slots, node_neighbors, node_normal, node_weight,
                wind_velocity,
            )
        )
    )
    outer = swap(outer, 1, peers)
    inner = swap(inner, 0, peers)

    currents = lax.all_to_all(currents, "mesh", 0, 0, tiled=True)

    spectra_new, stokes_rows = pl.pallas_call(
        functools.partial(wave_kernel, capacity),
        out_shape=(
            jax.ShapeDtypeStruct(spectra.shape, f32),
            jax.ShapeDtypeStruct((peers, LANES), f32),
        ),
        in_specs=[whole_spec()] * 9,
        out_specs=(whole_spec(),) * 2,
        scratch_shapes=[
            pltpu.VMEM((edges, dirs, LANES), f32),
            pltpu.VMEM((8, LANES), f32),
        ],
        compiler_params=params,
        name="wave",
    )(
        own_spectra, outer, inner, currents, *node_tables,
    )

    stokes_all = lax.all_to_all(stokes_rows, "mesh", 0, 0, tiled=True)

    def head_spec():
        return pl.BlockSpec((head_rows, LANES), lambda i: (0, 0))

    def full_spec(x):
        zeros = (0,) * x.ndim
        return pl.BlockSpec(x.shape, lambda i: zeros)

    rows = tracer_count * layers
    tracers_new = pl.pallas_call(
        tracer_kernel,
        grid=(1,),
        out_shape=jax.ShapeDtypeStruct(tracers.shape, f32),
        in_specs=[
            full_spec(tracers),
            full_spec(potential),
            head_spec(),
            head_spec(),
            full_spec(stokes_all),
            full_spec(cell_neighbors),
            full_spec(cell_normal),
            full_spec(cell_weight),
            full_spec(send_rows),
        ],
        out_specs=full_spec(tracers),
        scratch_shapes=[
            pltpu.VMEM((blocks + 4, field_rows, LANES), f32),
            pltpu.VMEM((blocks + 2, 8, LANES), jnp.int32),
            pltpu.VMEM((blocks + 2, 8, LANES), f32),
            pltpu.VMEM((blocks + 2, 8, LANES), f32),
            pltpu.VMEM((blocks + 2, 8, LANES), f32),
            pltpu.VMEM((blocks + 2, 8, LANES), f32),
            pltpu.VMEM((blocks + 2, edges, rows, LANES), f32),
            pltpu.VMEM((blocks + 2, rows, LANES), f32),
            pltpu.VMEM((blocks + 2, 2 * rows, LANES), f32),
        ],
        compiler_params=params,
        name="tracer",
    )(
        tracers, potential, outer, inner, stokes_all, cell_neighbors, cell_normal, cell_weight,
        send_rows,
    )
    return tracers_new, spectra_new


def solution(mesh):
    return jax.shard_map(
        local,
        mesh=mesh,
        in_specs=(
            P(None, None, ("groups", "mesh")),
            P(None, ("groups", "mesh")),
            P(None, ("groups", "mesh")),
            P(None, "mesh"),
            P(None, "mesh"),
            P(None, "mesh"),
            P(None, None, ("groups", "mesh")),
            P(None, ("groups", "mesh")),
            P(None, "mesh"),
            P(None, "mesh"),
            P(None, "mesh"),
            P(),
            P("mesh"),
        ),
        out_specs=(P(None, None, ("groups", "mesh")), P(None, None, ("groups", "mesh"))),
        check_vma=False,
    )
```

```python
import functools
import math

import jax
import jax.numpy as jnp
from jax import lax
from jax.experimental import pallas as pl
from jax.experimental.pallas import tpu as pltpu
from jax.sharding import PartitionSpec as P

LANES = 128
FCT_FLOOR = 0.001
TABLE_ROWS = 24
VMEM_LIMIT = 40 * 1024 * 1024


def lane_gather(values, index):
    return jnp.take_along_axis(values, index, axis=1, mode="promise_in_bounds")


def spread(row, count):
    return jnp.broadcast_to(row, (count, LANES))


def lane_iota(rows):
    return lax.broadcasted_iota(jnp.int32, (rows, LANES), 1)


def row_iota(rows):
    return lax.broadcasted_iota(jnp.int32, (rows, LANES), 0)


def slot_rows(entry):
    peers, capacity = entry.shape
    wide = jnp.concatenate([entry, jnp.zeros((peers, LANES - capacity), jnp.int32)], axis=1)
    wide = lane_gather(wide, lane_iota(peers) % capacity)
    owner = row_iota(peers)
    out = []
    for half in range(peers * capacity // LANES):
        wanted = (lane_iota(peers) + half * LANES) // capacity
        picked = jnp.where(owner == wanted, wide, 0).astype(jnp.float32)
        out.append(jnp.sum(picked, axis=0, keepdims=True).astype(jnp.int32))
    return out


def half_mask(rows, lower):
    half = lane_iota(rows) // (LANES // 2)
    return half == jnp.where(lower, 0, 1)


def peer_rows(values, peers, capacity):
    lane = lane_iota(peers)
    group = lane // capacity
    block = jnp.clip(row_iota(peers) - 1 + group // 2, 0, peers - 1)
    entry = block * capacity + lane % capacity
    out = jnp.zeros((peers, LANES), jnp.float32)
    for part in range(2):
        for half, row in enumerate(values[part]):
            found = lane_gather(spread(row, peers), entry % LANES)
            wanted = (group < 6) & (group % 2 == part) & (entry // LANES == half)
            out = jnp.where(wanted, found, out)
    return out


def direction(dirs):
    turn = row_iota(dirs).astype(jnp.float32) * (2.0 * math.pi / dirs)
    return jnp.cos(turn), jnp.sin(turn)


def node_tables(me, near, angle, face, cosine, sine, project, choice):
    edges, dirs = project.shape[:2]
    cosine[...] = face[...] * jnp.cos(angle[...])
    sine[...] = face[...] * jnp.sin(angle[...])
    cos_dir, sin_dir = direction(dirs)
    source = row_iota(LANES)
    minus = jnp.where(source == lane_iota(LANES), -1.0, 0.0)
    for s in range(edges):
        project[s] = cos_dir * cosine[s : s + 1, :] + sin_dir * sine[s : s + 1, :]
        target = near[s : s + 1, :]
        inside = target // LANES == me
        lane = target % LANES
        own = jnp.where(source == jnp.where(inside, lane, LANES), 1.0, 0.0) + minus
        halo = jnp.where(source == jnp.where(inside, LANES, lane), 1.0, 0.0)
        lanes = slice(s * LANES, (s + 1) * LANES)
        for k, part in enumerate((own, own, halo, halo)):
            choice[k * LANES : (k + 1) * LANES, lanes] = part.astype(jnp.bfloat16)


def split(x):
    first = x.astype(jnp.bfloat16)
    return first, (x - first.astype(jnp.float32)).astype(jnp.bfloat16)


def pack_kernel(
    spectra_in, tracers_in, potential_in, neighbors_in, normal_in, weight_in, current_in,
    send_rows, slot_in, near_in, angle_in, face_in, wind_in,
    rows_out, outer, inner, spectra, node_slot, near, wind, cosine, sine, project, choice,
    angle, face, tracers, potential, neighbors, normal, weight, current, own_rows, sems,
):
    peers, _, capacity = send_rows.shape
    me = lax.axis_index("mesh")
    copies = []
    for source, target in (
        (send_rows.at[me], own_rows),
        (current_in, current),
        (slot_in, node_slot),
        (spectra_in, spectra),
        (tracers_in, tracers),
        (potential_in, potential),
        (neighbors_in, neighbors),
        (normal_in, normal),
        (weight_in, weight),
        (near_in, near),
        (angle_in, angle),
        (face_in, face),
        (wind_in, wind),
    ):
        copy = pltpu.make_async_copy(source, target, sems.at[len(copies)])
        copy.start()
        copies.append(copy)
    for copy in copies[:3] + copies[9:]:
        copy.wait()
    freqs, dirs = spectra.shape[:2]
    layers, cells = potential.shape
    blocks = cells // LANES
    field_rows = (tracers.shape[0] + 1) * layers
    stacked = jnp.concatenate(
        [current[:, b * LANES : (b + 1) * LANES] for b in range(blocks)], axis=0
    )
    place = row_iota(2 * blocks)
    halves = slot_rows(own_rows[...])
    values = [[], []]
    for cell in halves:
        found = lane_gather(stacked, spread(cell % LANES, 2 * blocks))
        for part in range(2):
            picked = jnp.where(place == 2 * (cell // LANES) + part, found, 0.0)
            values[part].append(jnp.sum(picked, axis=0, keepdims=True))
    rows_out[...] = peer_rows(values, peers, capacity)
    node_tables(me, near, angle, face, cosine, sine, project, choice)
    for copy in copies[3:9]:
        copy.wait()
    odd = me % 2 == 1
    for out, upward in ((outer, odd), (inner, jnp.logical_not(odd))):
        for b in range(2):
            high = slice((blocks - 2 + b) * LANES, (blocks - 1 + b) * LANES)
            low = slice(b * LANES, (b + 1) * LANES)
            base = b * field_rows
            for t in range(tracers.shape[0]):
                out[base + t * layers : base + (t + 1) * layers, :] = jnp.where(
                    upward, tracers[t, :, high], tracers[t, :, low]
                )
            out[base + field_rows - layers : base + field_rows, :] = jnp.where(
                upward, potential[:, high], potential[:, low]
            )
        high = slice((blocks - 1) * LANES, blocks * LANES)
        low = slice(0, LANES)
        base = 2 * field_rows
        out[base : base + TABLE_ROWS, :] = jnp.zeros((TABLE_ROWS, LANES), jnp.float32)
        edges = neighbors.shape[0]
        near = jnp.where(upward, neighbors[:, high], neighbors[:, low])
        out[base : base + edges, :] = near.astype(jnp.float32)
        out[base + edges : base + edges + 1, :] = node_slot[...].astype(jnp.float32)
        out[base + 8 : base + 8 + edges, :] = jnp.where(upward, normal[:, high], normal[:, low])
        out[base + 16 : base + 16 + edges, :] = jnp.where(upward, weight[:, high], weight[:, low])
    base = 2 * field_rows + TABLE_ROWS
    pairs = freqs // 2
    whole = dirs // 8 * 8
    rest = dirs - whole
    turns = half_mask(dirs, odd)
    for g in range(pairs):
        natural = spectra[g]
        turned = pltpu.roll(spectra[g + pairs], LANES // 2, 1)
        for out, mixed in (
            (outer, jnp.where(turns, turned, natural)),
            (inner, jnp.where(turns, natural, turned)),
        ):
            at = base + g * whole
            out[at : at + whole, :] = mixed[:whole]
            at = base + pairs * whole + g * rest
            out[at : at + rest, :] = mixed[whole:]
    at = base + pairs * dirs
    if at < outer.shape[0]:
        for out in (outer, inner):
            out[at:, :] = jnp.zeros((outer.shape[0] - at, LANES), jnp.float32)


def node_currents(table, slot, which, capacity):
    peers = table.shape[0]
    owner = row_iota(peers) == slot // capacity
    out = []
    for part in range(2):
        lane = (2 * which + part) * capacity + slot % capacity
        found = jnp.where(owner, lane_gather(table, spread(lane, peers)), 0.0)
        out.append(jnp.sum(found, axis=0, keepdims=True))
    return out


def wave_kernel(
    capacity, step_pairs,
    spectra, outer, inner, table, node_slot, neighbors, wind, cosine, sine, project, choice,
    spectra_new, rows_out, drift, both, change,
):
    me = lax.axis_index("mesh")
    freqs, dirs = spectra.shape[:2]
    edges = neighbors.shape[0]
    peers = table.shape[0]
    halves = peers * capacity // LANES
    pairs = freqs // 2
    whole = dirs // 8 * 8
    rest = dirs - whole
    stride = (dirs + 7) // 8 * 8
    base = outer.shape[0] - (pairs * dirs + 7) // 8 * 8

    odd = me % 2 == 1
    slot = node_slot[...]
    row = base - TABLE_ROWS + edges
    halo_slot = jnp.where(
        half_mask(1, odd), outer[row : row + 1, :], inner[row : row + 1, :]
    ).astype(jnp.int32)
    lower = lane_iota(1) < LANES // 2
    currents = table[...]
    own_x, own_y = node_currents(currents, slot, jnp.ones((1, LANES), jnp.int32), capacity)
    halo_x, halo_y = node_currents(currents, halo_slot, jnp.where(lower, 2, 0), capacity)

    target = neighbors[...]
    lane = target % LANES
    inside = target // LANES == me

    def beside(own, halo):
        a = lane_gather(spread(own, edges), lane)
        b = lane_gather(spread(halo, edges), lane)
        return jnp.where(inside, a, b)

    drift[0:edges, :] = (
        0.5 * (own_x + beside(own_x, halo_x)) * cosine[...]
        + 0.5 * (own_y + beside(own_y, halo_y)) * sine[...]
    )
    drifts = [spread(drift[s : s + 1, :], 8) for s in range(edges)]
    drift_sum = sum(drifts[1:], drifts[0])
    from_outer = half_mask(dirs, odd)
    both[...] = jnp.zeros(both.shape, jnp.float32)
    ratio = 1.0 / 1.1
    bands = [slice(r, min(r + 8, dirs)) for r in range(0, dirs, 8)]

    def chunk(c, carry):
        first_speed, total = carry
        total = list(total)
        for i in range(step_pairs):
            g = c * step_pairs + i
            parts = []
            for message in (outer, inner):
                at = pl.multiple_of(base + g * whole, 8)
                upper = message[pl.ds(at, whole), :]
                left = message[pl.ds(base + pairs * whole + g * rest, rest), :]
                parts.append(jnp.concatenate([upper, left], axis=0))
            x, y = parts
            natural = jnp.where(from_outer, x, y)
            turned = pltpu.roll(jnp.where(from_outer, y, x), LANES // 2, 1)
            for j, f, halo in ((2 * i, g, natural), (2 * i + 1, g + pairs, turned)):
                both[j * stride : j * stride + dirs, 0:LANES] = spectra[f]
                both[j * stride : j * stride + dirs, LANES:] = halo
        own_first, own_second = split(both[:, 0:LANES])
        halo_first, halo_second = split(both[:, LANES:])
        mixed = jnp.concatenate([own_first, own_second, halo_first, halo_second], axis=1)
        change[...] = jnp.dot(mixed, choice[...], preferred_element_type=jnp.float32)
        for k, band in enumerate(bands):
            count = band.stop - band.start
            along = [project[s, band, :] for s in range(edges)]
            along_sum = sum(along[1:], along[0])
            for i in range(step_pairs):
                for j, f, speed in (
                    (2 * i, c * step_pairs + i, first_speed * ratio**i),
                    (2 * i + 1, c * step_pairs + i + pairs, first_speed * ratio ** (i + pairs)),
                ):
                    own = spectra[f, band, :]
                    at = j * stride + band.start
                    left = 1.0 - (speed * along_sum + drift_sum[:count])
                    value = left * own
                    for s in range(edges):
                        down = jnp.minimum(speed * along[s] + drifts[s][:count], 0.0)
                        lanes = slice(s * LANES, (s + 1) * LANES)
                        value = value - down * change[at : at + count, lanes]
                    spectra_new[f, band, :] = value
                    total[k] = total[k] + value
        return first_speed * ratio**step_pairs, tuple(total)

    zeros = tuple(jnp.zeros((band.stop - band.start, LANES), jnp.float32) for band in bands)
    _, total = lax.fori_loop(0, pairs // step_pairs, chunk, (jnp.float32(1.0), zeros))
    total = jnp.concatenate(total, axis=0)
    zero = jnp.zeros((dirs, LANES), jnp.float32)
    cos_dir, sin_dir = direction(dirs)
    mean = jnp.sum(total, axis=0, keepdims=True) * (1.0 / (freqs * dirs))
    forcing = jnp.maximum(wind[0:1, :] * cos_dir + wind[1:2, :] * sin_dir, 0.0)
    step = jnp.exp((0.25 * forcing - 2.0 * mean) * (1.0 / freqs))

    def grow(f, carry):
        factor, weighted = carry
        factor = factor * step
        evolved = spectra_new[f] * factor
        spectra_new[f] = evolved
        kappa = (f + 1).astype(jnp.float32) * (1.0 / freqs)
        return factor, weighted + kappa * evolved

    _, weighted = lax.fori_loop(0, freqs, grow, (zero + 1.0, zero))
    stokes = jnp.concatenate(
        [
            jnp.sum(weighted * cos_dir, axis=0, keepdims=True),
            jnp.sum(weighted * sin_dir, axis=0, keepdims=True),
        ],
        axis=0,
    ) * (1.0 / dirs)
    in_order = exact_dot(
        stokes, lax.broadcasted_iota(jnp.int32, (halves * LANES, LANES), 0) == slot
    )
    values = [
        [in_order[part : part + 1, h * LANES : (h + 1) * LANES] for h in range(halves)]
        for part in range(2)
    ]
    rows_out[...] = peer_rows(values, peers, capacity)


def exact_dot(values, chosen):
    first = values.astype(jnp.bfloat16).astype(jnp.float32)
    left = values - first
    second = left.astype(jnp.bfloat16).astype(jnp.float32)
    third = left - second
    pad = jnp.zeros((10, values.shape[1]), jnp.float32)
    parts = jnp.concatenate([first, second, third, pad], axis=0).astype(jnp.bfloat16)
    picks = jnp.where(chosen, 1.0, 0.0).astype(jnp.bfloat16)
    out = lax.dot_general(
        parts, picks, (((1,), (1,)), ((), ())), preferred_element_type=jnp.float32
    )
    return out[0:2] + (out[2:4] + out[4:6])


def tracer_kernel(
    tracers, potential, outer, inner, table, neighbors, normal, weight, send_rows, spectra,
    tracers_new, spectra_out, fields, target, cosine, sine, scale, stokes, antiflux, lowered, ratios, sem,
):
    write = pltpu.make_async_copy(spectra, spectra_out, sem)
    write.start()
    me = lax.axis_index("mesh")
    peers, _, capacity = send_rows.shape
    halves = peers * capacity // LANES
    tracer_count, layers, cells = tracers.shape
    blocks = cells // LANES
    edges = neighbors.shape[0]
    field_rows = (tracer_count + 1) * layers
    groups = field_rows // 8
    layer_groups = layers // 8
    tracer_groups = tracer_count * layer_groups

    odd = me % 2 == 1
    for b in range(2):
        x = outer[b * field_rows : (b + 1) * field_rows, :]
        y = inner[b * field_rows : (b + 1) * field_rows, :]
        fields[b] = jnp.where(odd, y, x)
        fields[blocks + 2 + b] = jnp.where(odd, x, y)
    for b in range(blocks):
        lanes = slice(b * LANES, (b + 1) * LANES)
        for t in range(tracer_count):
            fields[b + 2, t * layers : (t + 1) * layers, :] = tracers[t, :, lanes]
        fields[b + 2, field_rows - layers : field_rows, :] = potential[:, lanes]
    at = 2 * field_rows
    for b in range(blocks + 2):
        if b == 0 or b == blocks + 1:
            x = outer[at : at + TABLE_ROWS, :]
            y = inner[at : at + TABLE_ROWS, :]
            table_rows = jnp.where(odd, y, x) if b == 0 else jnp.where(odd, x, y)
            near = table_rows[0:edges].astype(jnp.int32)
            angle = table_rows[8 : 8 + edges]
            w = table_rows[16 : 16 + edges]
        else:
            lanes = slice((b - 1) * LANES, b * LANES)
            near = neighbors[:, lanes]
            angle = normal[:, lanes]
            w = weight[:, lanes]
        target[b, 0:edges, :] = near
        scale[b, 0:edges, :] = w
        cosine[b, 0:edges, :] = w * jnp.cos(angle)
        sine[b, 0:edges, :] = w * jnp.sin(angle)

    received = table[...]
    lane_of = lane_iota(peers)
    for which in range(3):
        cell = slot_rows(send_rows[jnp.clip(me + which - 1, 0, peers - 1)])
        values = []
        for part in range(2):
            lane = (2 * which + part) * capacity + lane_of % capacity
            found = lane_gather(received, lane)
            row = []
            for half in range(halves):
                mine = row_iota(peers) == (lane_of + half * LANES) // capacity
                row.append(jnp.sum(jnp.where(mine, found, 0.0), axis=0, keepdims=True))
            values.append(jnp.concatenate(row, axis=1))
        values = jnp.concatenate(values, axis=0)
        names = jnp.concatenate(cell, axis=1)
        count = cells if which == 1 else LANES
        start = cells - LANES if which == 0 else 0
        number = lax.broadcasted_iota(jnp.int32, (count, halves * LANES), 0) + start
        sums = exact_dot(values, number == names)
        if which == 1:
            for b in range(blocks):
                stokes[b + 1, 0:2, :] = sums[:, b * LANES : (b + 1) * LANES]
        else:
            stokes[0 if which == 0 else blocks + 1, 0:2, :] = sums

    decay = [
        jnp.exp(-3.0 / layers * (row_iota(8) + 8 * g).astype(jnp.float32))
        for g in range(layer_groups)
    ]

    def neighbour_of(near, b, s):
        row = spread(near[s : s + 1, :], 8)
        side = row // LANES - (me * blocks + b - 1)
        return row % LANES, side

    def low_order(b, carry):
        near = target[b]
        w = scale[b]
        slope = cosine[b] * stokes[b, 0:1, :] + sine[b] * stokes[b, 1:2, :]
        own = [fields[b + 1, 8 * g : 8 * g + 8, :] for g in range(groups)]
        zero = jnp.zeros((8, LANES), jnp.float32)
        out_speed = [zero] * layer_groups
        inflow = [zero] * tracer_groups
        upper = own[:tracer_groups]
        lower = own[:tracer_groups]
        positive = [zero] * tracer_groups
        negative = [zero] * tracer_groups
        for s in range(edges):
            lane, side = neighbour_of(near, b, s)
            w8 = spread(w[s : s + 1, :], 8)
            slope8 = spread(slope[s : s + 1, :], 8)
            beside = []
            for g in range(groups):
                rows = slice(8 * g, 8 * g + 8)
                middle = lane_gather(own[g], lane)
                left = lane_gather(fields[b, rows, :], lane)
                right = lane_gather(fields[b + 2, rows, :], lane)
                beside.append(jnp.where(side == 0, middle, jnp.where(side < 0, left, right)))
            for lg in range(layer_groups):
                k = tracer_groups + lg
                speed = w8 * (beside[k] - own[k]) + decay[lg] * slope8
                up = jnp.maximum(speed, 0.0)
                down = jnp.minimum(speed, 0.0)
                half = 0.5 * (up - down)
                out_speed[lg] = out_speed[lg] + up
                for t in range(tracer_count):
                    g = t * layer_groups + lg
                    q = beside[g]
                    flux = half * (q - own[g])
                    antiflux[b, s, 8 * g : 8 * g + 8, :] = flux
                    inflow[g] = inflow[g] + down * q
                    upper[g] = jnp.maximum(upper[g], q)
                    lower[g] = jnp.minimum(lower[g], q)
                    positive[g] = positive[g] + jnp.maximum(flux, 0.0)
                    negative[g] = negative[g] - jnp.minimum(flux, 0.0)
        for g in range(tracer_groups):
            rows = slice(8 * g, 8 * g + 8)
            value = own[g] - (out_speed[g % layer_groups] * own[g] + inflow[g])
            lowered[b, rows, :] = value
            plus = jnp.maximum(upper[g] - value, 0.0) / (negative[g] + FCT_FLOOR)
            minus = jnp.maximum(value - lower[g], 0.0) / (positive[g] + FCT_FLOOR)
            ratios[b, rows, :] = jnp.minimum(1.0, plus)
            at = 8 * (tracer_groups + g)
            ratios[b, at : at + 8, :] = jnp.minimum(1.0, minus)
        return carry

    lax.fori_loop(0, blocks + 2, low_order, 0)

    def limit(i, carry):
        b = i + 1
        near = target[b]
        out = [lowered[b, 8 * g : 8 * g + 8, :] for g in range(tracer_groups)]
        own = [ratios[b, 8 * g : 8 * g + 8, :] for g in range(2 * tracer_groups)]
        for s in range(edges):
            lane, side = neighbour_of(near, b, s)
            beside = []
            for g in range(2 * tracer_groups):
                rows = slice(8 * g, 8 * g + 8)
                middle = lane_gather(own[g], lane)
                left = lane_gather(ratios[b - 1, rows, :], lane)
                right = lane_gather(ratios[b + 1, rows, :], lane)
                beside.append(jnp.where(side == 0, middle, jnp.where(side < 0, left, right)))
            for g in range(tracer_groups):
                flux = antiflux[b, s, 8 * g : 8 * g + 8, :]
                m = g + tracer_groups
                factor = jnp.where(
                    flux >= 0.0,
                    jnp.minimum(own[m], beside[g]),
                    jnp.minimum(own[g], beside[m]),
                )
                out[g] = out[g] - factor * flux
        lanes = pl.ds(pl.multiple_of(i * LANES, LANES), LANES)
        for g in range(tracer_groups):
            t, lg = g // layer_groups, g % layer_groups
            tracers_new[t, 8 * lg : 8 * lg + 8, lanes] = out[g]
        return carry

    lax.fori_loop(0, blocks, limit, 0)
    write.wait()


def swap(message, first, peers):
    pairs = []
    for i in range(first, peers - 1, 2):
        pairs += [(i, i + 1), (i + 1, i)]
    return lax.ppermute(message, "mesh", pairs)


def whole_spec():
    return pl.BlockSpec(memory_space=pltpu.VMEM)


def local(
    tracers,
    potential,
    surface_current,
    cell_neighbors,
    cell_normal,
    cell_weight,
    spectra,
    wind_velocity,
    node_neighbors,
    node_normal,
    node_weight,
    send_rows,
    node_slot,
):
    peers, _, capacity = send_rows.shape
    freqs, dirs, nodes = spectra.shape
    tracer_count, layers, cells = tracers.shape
    edges = cell_neighbors.shape[0]
    blocks = cells // LANES
    field_rows = (tracer_count + 1) * layers
    head_rows = 2 * field_rows + TABLE_ROWS
    message_rows = head_rows + (freqs // 2 * dirs + 7) // 8 * 8
    slots = node_slot.reshape(1, nodes)
    params = pltpu.CompilerParams(vmem_limit_bytes=VMEM_LIMIT)
    f32 = jnp.float32

    stored = pl.BlockSpec(memory_space=pltpu.HBM)
    currents, outer, inner, *node_parts = pl.pallas_call(
        pack_kernel,
        out_shape=(
            jax.ShapeDtypeStruct((peers, LANES), f32),
            jax.ShapeDtypeStruct((message_rows, LANES), f32),
            jax.ShapeDtypeStruct((message_rows, LANES), f32),
            jax.ShapeDtypeStruct(spectra.shape, f32),
            jax.ShapeDtypeStruct(slots.shape, jnp.int32),
            jax.ShapeDtypeStruct(node_neighbors.shape, jnp.int32),
            jax.ShapeDtypeStruct(wind_velocity.shape, f32),
            jax.ShapeDtypeStruct(node_normal.shape, f32),
            jax.ShapeDtypeStruct(node_normal.shape, f32),
            jax.ShapeDtypeStruct((edges, dirs, LANES), f32),
            jax.ShapeDtypeStruct((4 * LANES, edges * LANES), jnp.bfloat16),
        ),
        in_specs=[stored] * 13,
        out_specs=(whole_spec(),) * 11,
        scratch_shapes=[
            pltpu.VMEM(node_normal.shape, f32),
            pltpu.VMEM(node_weight.shape, f32),
            pltpu.VMEM(tracers.shape, f32),
            pltpu.VMEM(potential.shape, f32),
            pltpu.VMEM(cell_neighbors.shape, jnp.int32),
            pltpu.VMEM(cell_normal.shape, f32),
            pltpu.VMEM(cell_weight.shape, f32),
            pltpu.VMEM(surface_current.shape, f32),
            pltpu.VMEM(send_rows.shape[1:], jnp.int32),
            pltpu.SemaphoreType.DMA((13,)),
        ],
        compiler_params=params,
        name="pack",
    )(
        *(
            pltpu.with_memory_space_constraint(x, pltpu.HBM)
            for x in (
                spectra, tracers, potential, cell_neighbors, cell_normal, cell_weight,
                surface_current, send_rows, slots, node_neighbors, node_normal, node_weight,
                wind_velocity,
            )
        )
    )
    outer = swap(outer, 1, peers)
    inner = swap(inner, 0, peers)

    currents = lax.all_to_all(currents, "mesh", 0, 0, tiled=True)

    step_pairs = 5 if freqs % 10 == 0 else 1
    stride = (dirs + 7) // 8 * 8
    spectra_new, stokes_rows = pl.pallas_call(
        functools.partial(wave_kernel, capacity, step_pairs),
        out_shape=(
            jax.ShapeDtypeStruct(spectra.shape, f32),
            jax.ShapeDtypeStruct((peers, LANES), f32),
        ),
        in_specs=[whole_spec()] * 11,
        out_specs=(whole_spec(),) * 2,
        scratch_shapes=[
            pltpu.VMEM((8, LANES), f32),
            pltpu.VMEM((2 * step_pairs * stride, 2 * LANES), f32),
            pltpu.VMEM((2 * step_pairs * stride, edges * LANES), f32),
        ],
        compiler_params=params,
        name="wave",
    )(
        node_parts[0], outer, inner, currents, *node_parts[1:],
    )

    stokes_all = lax.all_to_all(stokes_rows, "mesh", 0, 0, tiled=True)

    def head_spec():
        return pl.BlockSpec((head_rows, LANES), lambda i: (0, 0))

    def full_spec(x):
        zeros = (0,) * x.ndim
        return pl.BlockSpec(x.shape, lambda i: zeros)

    rows = tracer_count * layers
    tracers_new, spectra_new = pl.pallas_call(
        tracer_kernel,
        grid=(1,),
        out_shape=(
            jax.ShapeDtypeStruct(tracers.shape, f32),
            jax.ShapeDtypeStruct(spectra.shape, f32),
        ),
        in_specs=[
            full_spec(tracers),
            full_spec(potential),
            head_spec(),
            head_spec(),
            full_spec(stokes_all),
            full_spec(cell_neighbors),
            full_spec(cell_normal),
            full_spec(cell_weight),
            full_spec(send_rows),
            pl.BlockSpec(memory_space=pl.ANY),
        ],
        out_specs=(full_spec(tracers), stored),
        scratch_shapes=[
            pltpu.VMEM((blocks + 4, field_rows, LANES), f32),
            pltpu.VMEM((blocks + 2, 8, LANES), jnp.int32),
            pltpu.VMEM((blocks + 2, 8, LANES), f32),
            pltpu.VMEM((blocks + 2, 8, LANES), f32),
            pltpu.VMEM((blocks + 2, 8, LANES), f32),
            pltpu.VMEM((blocks + 2, 8, LANES), f32),
            pltpu.VMEM((blocks + 2, edges, rows, LANES), f32),
            pltpu.VMEM((blocks + 2, rows, LANES), f32),
            pltpu.VMEM((blocks + 2, 2 * rows, LANES), f32),
            pltpu.SemaphoreType.DMA(()),
        ],
        compiler_params=params,
        name="tracer",
    )(
        tracers, potential, outer, inner, stokes_all, cell_neighbors, cell_normal, cell_weight,
        send_rows, pltpu.with_memory_space_constraint(spectra_new, pltpu.VMEM),
    )
    return tracers_new, spectra_new


def solution(mesh):
    return jax.shard_map(
        local,
        mesh=mesh,
        in_specs=(
            P(None, None, ("groups", "mesh")),
            P(None, ("groups", "mesh")),
            P(None, ("groups", "mesh")),
            P(None, "mesh"),
            P(None, "mesh"),
            P(None, "mesh"),
            P(None, None, ("groups", "mesh")),
            P(None, ("groups", "mesh")),
            P(None, "mesh"),
            P(None, "mesh"),
            P(None, "mesh"),
            P(),
            P("mesh"),
        ),
        out_specs=(P(None, None, ("groups", "mesh")), P(None, None, ("groups", "mesh"))),
        check_vma=False,
    )
```

```python
import functools
import math

import jax
import jax.numpy as jnp
from jax import lax
from jax.experimental import pallas as pl
from jax.experimental.pallas import tpu as pltpu
from jax.sharding import PartitionSpec as P

LANES = 128
FCT_FLOOR = 0.001
TABLE_ROWS = 24
VMEM_LIMIT = 32 * 1024 * 1024


def lane_gather(values, index):
    return jnp.take_along_axis(values, index, axis=1, mode="promise_in_bounds")


def spread(row, count):
    return jnp.broadcast_to(row, (count, LANES))


def lane_iota(rows):
    return lax.broadcasted_iota(jnp.int32, (rows, LANES), 1)


def row_iota(rows):
    return lax.broadcasted_iota(jnp.int32, (rows, LANES), 0)


def slot_rows(entry):
    peers, capacity = entry.shape
    wide = jnp.concatenate([entry, jnp.zeros((peers, LANES - capacity), jnp.int32)], axis=1)
    wide = lane_gather(wide, lane_iota(peers) % capacity)
    owner = row_iota(peers)
    out = []
    for half in range(peers * capacity // LANES):
        wanted = (lane_iota(peers) + half * LANES) // capacity
        picked = jnp.where(owner == wanted, wide, 0).astype(jnp.float32)
        out.append(jnp.sum(picked, axis=0, keepdims=True).astype(jnp.int32))
    return out


def half_mask(rows, lower):
    half = lane_iota(rows) // (LANES // 2)
    return half == jnp.where(lower, 0, 1)


def peer_rows(values, peers, capacity):
    lane = lane_iota(peers)
    group = lane // capacity
    block = jnp.clip(row_iota(peers) - 1 + group // 2, 0, peers - 1)
    entry = block * capacity + lane % capacity
    out = jnp.zeros((peers, LANES), jnp.float32)
    for part in range(2):
        for half, row in enumerate(values[part]):
            found = lane_gather(spread(row, peers), entry % LANES)
            wanted = (group < 6) & (group % 2 == part) & (entry // LANES == half)
            out = jnp.where(wanted, found, out)
    return out


def direction(dirs):
    turn = row_iota(dirs).astype(jnp.float32) * (2.0 * math.pi / dirs)
    return jnp.cos(turn), jnp.sin(turn)


def node_tables(me, near, angle, face, cosine, sine, project, choice):
    edges, dirs = project.shape[:2]
    cosine[...] = face[...] * jnp.cos(angle[...])
    sine[...] = face[...] * jnp.sin(angle[...])
    cos_dir, sin_dir = direction(dirs)
    source = row_iota(LANES)
    minus = jnp.where(source == lane_iota(LANES), -1.0, 0.0)
    for s in range(edges):
        project[s] = cos_dir * cosine[s : s + 1, :] + sin_dir * sine[s : s + 1, :]
        target = near[s : s + 1, :]
        inside = target // LANES == me
        lane = target % LANES
        own = jnp.where(source == jnp.where(inside, lane, LANES), 1.0, 0.0) + minus
        halo = jnp.where(source == jnp.where(inside, LANES, lane), 1.0, 0.0)
        lanes = slice(s * LANES, (s + 1) * LANES)
        for k, part in enumerate((own, own, halo, halo)):
            choice[k * LANES : (k + 1) * LANES, lanes] = part.astype(jnp.bfloat16)


def split(x):
    first = x.astype(jnp.bfloat16)
    return first, (x - first.astype(jnp.float32)).astype(jnp.bfloat16)


def pack_kernel(
    spectra_in, tracers_in, potential_in, neighbors_in, normal_in, weight_in, current_in,
    send_rows, slot_in, near_in, angle_in, face_in, wind_in,
    rows_out, outer, inner, spectra, node_slot, near, angle, face, wind,
    tracers, potential, neighbors, normal, weight, coupled,
    current, sems,
):
    peers, _, capacity = send_rows.shape
    me = lax.axis_index("mesh")
    copies = []
    for source, target in (
        (send_rows.at[me], coupled.at[1]),
        (current_in, current),
        (slot_in, node_slot),
        (spectra_in, spectra),
        (tracers_in, tracers),
        (potential_in, potential),
        (neighbors_in, neighbors),
        (normal_in, normal),
        (weight_in, weight),
        (send_rows.at[jnp.maximum(me - 1, 0)], coupled.at[0]),
        (send_rows.at[jnp.minimum(me + 1, peers - 1)], coupled.at[2]),
        (near_in, near),
        (angle_in, angle),
        (face_in, face),
        (wind_in, wind),
    ):
        copy = pltpu.make_async_copy(source, target, sems.at[len(copies)])
        copy.start()
        copies.append(copy)
    for copy in copies[:3]:
        copy.wait()
    freqs, dirs = spectra.shape[:2]
    layers, cells = potential.shape
    blocks = cells // LANES
    field_rows = (tracers.shape[0] + 1) * layers
    stacked = jnp.concatenate(
        [current[:, b * LANES : (b + 1) * LANES] for b in range(blocks)], axis=0
    )
    place = row_iota(2 * blocks)
    halves = slot_rows(coupled[1])
    values = [[], []]
    for cell in halves:
        found = lane_gather(stacked, spread(cell % LANES, 2 * blocks))
        for part in range(2):
            picked = jnp.where(place == 2 * (cell // LANES) + part, found, 0.0)
            values[part].append(jnp.sum(picked, axis=0, keepdims=True))
    rows_out[...] = peer_rows(values, peers, capacity)
    for copy in copies[3:]:
        copy.wait()
    odd = me % 2 == 1
    for out, upward in ((outer, odd), (inner, jnp.logical_not(odd))):
        for b in range(2):
            high = slice((blocks - 2 + b) * LANES, (blocks - 1 + b) * LANES)
            low = slice(b * LANES, (b + 1) * LANES)
            base = b * field_rows
            for t in range(tracers.shape[0]):
                out[base + t * layers : base + (t + 1) * layers, :] = jnp.where(
                    upward, tracers[t, :, high], tracers[t, :, low]
                )
            out[base + field_rows - layers : base + field_rows, :] = jnp.where(
                upward, potential[:, high], potential[:, low]
            )
        high = slice((blocks - 1) * LANES, blocks * LANES)
        low = slice(0, LANES)
        base = 2 * field_rows
        out[base : base + TABLE_ROWS, :] = jnp.zeros((TABLE_ROWS, LANES), jnp.float32)
        edges = neighbors.shape[0]
        near = jnp.where(upward, neighbors[:, high], neighbors[:, low])
        out[base : base + edges, :] = near.astype(jnp.float32)
        out[base + edges : base + edges + 1, :] = node_slot[...].astype(jnp.float32)
        out[base + 8 : base + 8 + edges, :] = jnp.where(upward, normal[:, high], normal[:, low])
        out[base + 16 : base + 16 + edges, :] = jnp.where(upward, weight[:, high], weight[:, low])
    base = 2 * field_rows + TABLE_ROWS
    pairs = freqs // 2
    whole = dirs // 8 * 8
    rest = dirs - whole
    turns = half_mask(dirs, odd)
    for g in range(pairs):
        natural = spectra[g]
        turned = pltpu.roll(spectra[g + pairs], LANES // 2, 1)
        for out, mixed in (
            (outer, jnp.where(turns, turned, natural)),
            (inner, jnp.where(turns, natural, turned)),
        ):
            at = base + g * whole
            out[at : at + whole, :] = mixed[:whole]
            at = base + pairs * whole + g * rest
            out[at : at + rest, :] = mixed[whole:]
    at = base + pairs * dirs
    if at < outer.shape[0]:
        for out in (outer, inner):
            out[at:, :] = jnp.zeros((outer.shape[0] - at, LANES), jnp.float32)


def choose(cells, first, lanes, matrix):
    place = cells - first
    for k in range(3):
        source = row_iota(LANES) + k * LANES
        part = jnp.where(source == place, 1.0, 0.0)
        if k == 1:
            part = part - jnp.where(row_iota(LANES) == lane_iota(LANES), 1.0, 0.0)
        matrix[k * LANES : (k + 1) * LANES, lanes] = part.astype(jnp.bfloat16)


def stack_split(x):
    first, second = split(x)
    return jnp.concatenate([first, second], axis=0)


def differences(parts, matrix):
    mixed = jnp.concatenate(parts, axis=1)
    out = jnp.dot(mixed, matrix, preferred_element_type=jnp.float32)
    rows = out.shape[0] // 2
    return out[:rows] + out[rows:]


def prepare_kernel(
    near, angle, face, tracers, potential, neighbors, normal, weight, coupled,
    cosine, sine, project, choice,
    fields, pieces, matrices, inside, cell_cosine, cell_sine, cell_scale, sums,
):
    me = lax.axis_index("mesh")
    node_tables(me, near, angle, face, cosine, sine, project, choice)
    tracer_count, layers, cells = tracers.shape
    blocks = cells // LANES
    edges = neighbors.shape[0]
    field_rows = (tracer_count + 1) * layers
    for b in range(blocks):
        lanes = slice(b * LANES, (b + 1) * LANES)
        for t in range(tracer_count):
            fields[b, t * layers : (t + 1) * layers, :] = tracers[t, :, lanes]
        fields[b, field_rows - layers : field_rows, :] = potential[:, lanes]
        pieces[b] = stack_split(fields[b])
        w = weight[:, lanes]
        cell_scale[b, 0:edges, :] = w
        cell_cosine[b, 0:edges, :] = w * jnp.cos(normal[:, lanes])
        cell_sine[b, 0:edges, :] = w * jnp.sin(normal[:, lanes])
        for s in range(edges):
            choose(
                neighbors[s : s + 1, lanes],
                (me * blocks + b - 1) * LANES,
                slice(s * LANES, (s + 1) * LANES),
                matrices.at[b],
            )
    for b in range(1, blocks - 1):
        inside[b - 1] = differences(
            [pieces[b - 1], pieces[b], pieces[b + 1]], matrices[b]
        )
    for which in range(3):
        first = 0 if which != 0 else cells - LANES
        count = blocks if which == 1 else 1
        start = (0, 1, blocks + 1)[which]
        for half, names in enumerate(slot_rows(coupled[which])):
            named = jnp.transpose(spread(names, LANES).astype(jnp.float32))
            for b in range(count):
                cell = (lane_iota(LANES) + (first + b * LANES)).astype(jnp.float32)
                picked = jnp.where(named == cell, 1.0, 0.0).astype(jnp.bfloat16)
                lanes = slice((start + b) * LANES, (start + b + 1) * LANES)
                sums[half * LANES : (half + 1) * LANES, lanes] = picked


def node_currents(table, slot, which, capacity):
    peers = table.shape[0]
    owner = row_iota(peers) == slot // capacity
    out = []
    for part in range(2):
        lane = (2 * which + part) * capacity + slot % capacity
        found = jnp.where(owner, lane_gather(table, spread(lane, peers)), 0.0)
        out.append(jnp.sum(found, axis=0, keepdims=True))
    return out


def wave_kernel(
    capacity, step_pairs,
    spectra, outer, inner, table, node_slot, neighbors, wind, cosine, sine, project, choice,
    spectra_new, rows_out, drift, both, change,
):
    me = lax.axis_index("mesh")
    freqs, dirs = spectra.shape[:2]
    edges = neighbors.shape[0]
    peers = table.shape[0]
    halves = peers * capacity // LANES
    pairs = freqs // 2
    whole = dirs // 8 * 8
    rest = dirs - whole
    stride = (dirs + 7) // 8 * 8
    base = outer.shape[0] - (pairs * dirs + 7) // 8 * 8

    odd = me % 2 == 1
    slot = node_slot[...]
    row = base - TABLE_ROWS + edges
    halo_slot = jnp.where(
        half_mask(1, odd), outer[row : row + 1, :], inner[row : row + 1, :]
    ).astype(jnp.int32)
    lower = lane_iota(1) < LANES // 2
    currents = table[...]
    own_x, own_y = node_currents(currents, slot, jnp.ones((1, LANES), jnp.int32), capacity)
    halo_x, halo_y = node_currents(currents, halo_slot, jnp.where(lower, 2, 0), capacity)

    target = neighbors[...]
    lane = target % LANES
    inside = target // LANES == me

    def beside(own, halo):
        a = lane_gather(spread(own, edges), lane)
        b = lane_gather(spread(halo, edges), lane)
        return jnp.where(inside, a, b)

    drift[0:edges, :] = (
        0.5 * (own_x + beside(own_x, halo_x)) * cosine[...]
        + 0.5 * (own_y + beside(own_y, halo_y)) * sine[...]
    )
    drifts = [spread(drift[s : s + 1, :], 8) for s in range(edges)]
    drift_sum = sum(drifts[1:], drifts[0])
    from_outer = half_mask(dirs, odd)
    both[...] = jnp.zeros(both.shape, jnp.float32)
    ratio = 1.0 / 1.1
    bands = [slice(r, min(r + 8, dirs)) for r in range(0, dirs, 8)]

    def chunk(c, carry):
        first_speed, total = carry
        total = list(total)
        for i in range(step_pairs):
            g = c * step_pairs + i
            parts = []
            for message in (outer, inner):
                at = pl.multiple_of(base + g * whole, 8)
                upper = message[pl.ds(at, whole), :]
                left = message[pl.ds(base + pairs * whole + g * rest, rest), :]
                parts.append(jnp.concatenate([upper, left], axis=0))
            x, y = parts
            natural = jnp.where(from_outer, x, y)
            turned = pltpu.roll(jnp.where(from_outer, y, x), LANES // 2, 1)
            for j, f, halo in ((2 * i, g, natural), (2 * i + 1, g + pairs, turned)):
                both[j * stride : j * stride + dirs, 0:LANES] = spectra[f]
                both[j * stride : j * stride + dirs, LANES:] = halo
        own_first, own_second = split(both[:, 0:LANES])
        halo_first, halo_second = split(both[:, LANES:])
        mixed = jnp.concatenate([own_first, own_second, halo_first, halo_second], axis=1)
        change[...] = jnp.dot(mixed, choice[...], preferred_element_type=jnp.float32)
        for k, band in enumerate(bands):
            count = band.stop - band.start
            along = [project[s, band, :] for s in range(edges)]
            along_sum = sum(along[1:], along[0])
            for i in range(step_pairs):
                for j, f, speed in (
                    (2 * i, c * step_pairs + i, first_speed * ratio**i),
                    (2 * i + 1, c * step_pairs + i + pairs, first_speed * ratio ** (i + pairs)),
                ):
                    own = spectra[f, band, :]
                    at = j * stride + band.start
                    left = 1.0 - (speed * along_sum + drift_sum[:count])
                    value = left * own
                    for s in range(edges):
                        down = jnp.minimum(speed * along[s] + drifts[s][:count], 0.0)
                        lanes = slice(s * LANES, (s + 1) * LANES)
                        value = value - down * change[at : at + count, lanes]
                    spectra_new[f, band, :] = value
                    total[k] = total[k] + value
        return first_speed * ratio**step_pairs, tuple(total)

    zeros = tuple(jnp.zeros((band.stop - band.start, LANES), jnp.float32) for band in bands)
    _, total = lax.fori_loop(0, pairs // step_pairs, chunk, (jnp.float32(1.0), zeros))
    total = jnp.concatenate(total, axis=0)
    zero = jnp.zeros((dirs, LANES), jnp.float32)
    cos_dir, sin_dir = direction(dirs)
    mean = jnp.sum(total, axis=0, keepdims=True) * (1.0 / (freqs * dirs))
    forcing = jnp.maximum(wind[0:1, :] * cos_dir + wind[1:2, :] * sin_dir, 0.0)
    step = jnp.exp((0.25 * forcing - 2.0 * mean) * (1.0 / freqs))

    def grow(f, carry):
        factor, weighted = carry
        factor = factor * step
        evolved = spectra_new[f] * factor
        spectra_new[f] = evolved
        kappa = (f + 1).astype(jnp.float32) * (1.0 / freqs)
        return factor, weighted + kappa * evolved

    _, weighted = lax.fori_loop(0, freqs, grow, (zero + 1.0, zero))
    stokes = jnp.concatenate(
        [
            jnp.sum(weighted * cos_dir, axis=0, keepdims=True),
            jnp.sum(weighted * sin_dir, axis=0, keepdims=True),
        ],
        axis=0,
    ) * (1.0 / dirs)
    named = lax.broadcasted_iota(jnp.int32, (halves * LANES, LANES), 0) == slot
    in_order = lax.dot_general(
        three_parts(stokes),
        jnp.where(named, 1.0, 0.0).astype(jnp.bfloat16),
        (((1,), (1,)), ((), ())),
        preferred_element_type=jnp.float32,
    )
    in_order = in_order[0:2] + (in_order[2:4] + in_order[4:6])
    values = [
        [in_order[part : part + 1, h * LANES : (h + 1) * LANES] for h in range(halves)]
        for part in range(2)
    ]
    rows_out[...] = peer_rows(values, peers, capacity)


def three_parts(values):
    first = values.astype(jnp.bfloat16).astype(jnp.float32)
    left = values - first
    second = left.astype(jnp.bfloat16).astype(jnp.float32)
    third = left - second
    pad = jnp.zeros((10, values.shape[1]), jnp.float32)
    return jnp.concatenate([first, second, third, pad], axis=0).astype(jnp.bfloat16)


def tracer_kernel(
    capacity, shape,
    outer, inner, table, fields, pieces, matrices, inside, cosine, sine, scale, sums, spectra,
    tracers_new, spectra_out,
    halo, halo_pieces, halo_matrices, halo_tables, beside, stokes, antiflux, lowered, ratios,
    ratio_pieces, sem,
):
    write = pltpu.make_async_copy(spectra, spectra_out, sem)
    write.start()
    me = lax.axis_index("mesh")
    tracer_count, layers, edges = shape
    peers = table.shape[0]
    halves = peers * capacity // LANES
    blocks, field_rows, _ = fields.shape
    layer_groups = layers // 8
    tracer_groups = tracer_count * layer_groups
    odd = me % 2 == 1

    for b in range(2):
        x = outer[b * field_rows : (b + 1) * field_rows, :]
        y = inner[b * field_rows : (b + 1) * field_rows, :]
        for side, value in ((0, jnp.where(odd, y, x)), (1, jnp.where(odd, x, y))):
            halo[2 * side + b] = value
            halo_pieces[2 * side + b] = stack_split(value)
    at = 2 * field_rows
    x = outer[at : at + TABLE_ROWS, :]
    y = inner[at : at + TABLE_ROWS, :]
    for side, rows in ((0, jnp.where(odd, y, x)), (1, jnp.where(odd, x, y))):
        w = rows[16 : 16 + edges]
        halo_tables[side, 0, 0:edges, :] = w
        halo_tables[side, 1, 0:edges, :] = w * jnp.cos(rows[8 : 8 + edges])
        halo_tables[side, 2, 0:edges, :] = w * jnp.sin(rows[8 : 8 + edges])
        near = rows[0:edges].astype(jnp.int32)
        first = (me * blocks - 2 if side == 0 else me * blocks + blocks - 1) * LANES
        for s in range(edges):
            choose(
                near[s : s + 1, :],
                first,
                slice(s * LANES, (s + 1) * LANES),
                halo_matrices.at[side],
            )
    beside[0] = differences([halo_pieces[0], halo_pieces[1], pieces[0]], halo_matrices[0])
    beside[1] = differences([halo_pieces[1], pieces[0], pieces[1]], matrices[0])
    beside[2] = differences(
        [pieces[blocks - 2], pieces[blocks - 1], halo_pieces[2]], matrices[blocks - 1]
    )
    beside[3] = differences([pieces[blocks - 1], halo_pieces[2], halo_pieces[3]], halo_matrices[1])

    received = table[...]
    lane_of = lane_iota(peers)
    for which in range(3):
        values = []
        for part in range(2):
            lane = (2 * which + part) * capacity + lane_of % capacity
            found = lane_gather(received, lane)
            row = []
            for half in range(halves):
                mine = row_iota(peers) == (lane_of + half * LANES) // capacity
                row.append(jnp.sum(jnp.where(mine, found, 0.0), axis=0, keepdims=True))
            values.append(jnp.concatenate(row, axis=1))
        parts = three_parts(jnp.concatenate(values, axis=0))
        start = (0, 1, blocks + 1)[which]
        count = blocks if which == 1 else 1
        total = jnp.dot(
            parts,
            sums[:, start * LANES : (start + count) * LANES],
            preferred_element_type=jnp.float32,
        )
        total = total[0:2] + (total[2:4] + total[4:6])
        for b in range(count):
            stokes[start + b, 0:2, :] = total[:, b * LANES : (b + 1) * LANES]

    decay = [
        jnp.exp(-3.0 / layers * (row_iota(8) + 8 * g).astype(jnp.float32))
        for g in range(layer_groups)
    ]

    def low_order(b, value, change, w, wx, wy, keep):
        slope = wx * stokes[b, 0:1, :] + wy * stokes[b, 1:2, :]
        own = [value(8 * g) for g in range(tracer_groups)]
        zero = jnp.zeros((8, LANES), jnp.float32)
        speed_sum = [zero] * layer_groups
        inflow = [zero] * tracer_groups
        highest = [zero] * tracer_groups
        lowest = [zero] * tracer_groups
        positive = [zero] * tracer_groups
        negative = [zero] * tracer_groups
        for s in range(edges):
            w8 = spread(w[s : s + 1, :], 8)
            slope8 = spread(slope[s : s + 1, :], 8)
            for lg in range(layer_groups):
                speed = w8 * change(8 * (tracer_groups + lg), s) + decay[lg] * slope8
                down = jnp.minimum(speed, 0.0)
                half = 0.5 * speed - down
                speed_sum[lg] = speed_sum[lg] + speed
                for t in range(tracer_count):
                    g = t * layer_groups + lg
                    step = change(8 * g, s)
                    flux = half * step
                    if keep:
                        antiflux[b - 1, s, 8 * g : 8 * g + 8, :] = flux
                    inflow[g] = inflow[g] + down * step
                    highest[g] = jnp.maximum(highest[g], step)
                    lowest[g] = jnp.minimum(lowest[g], step)
                    positive[g] = positive[g] + jnp.maximum(flux, 0.0)
                    negative[g] = negative[g] - jnp.minimum(flux, 0.0)
        plus, minus = [], []
        for g in range(tracer_groups):
            loss = speed_sum[g % layer_groups] * own[g] + inflow[g]
            if keep:
                lowered[b - 1, 8 * g : 8 * g + 8, :] = own[g] - loss
            up = jnp.maximum(highest[g] + loss, 0.0) / (negative[g] + FCT_FLOOR)
            down = jnp.maximum(-loss - lowest[g], 0.0) / (positive[g] + FCT_FLOOR)
            plus.append(jnp.minimum(1.0, up))
            minus.append(jnp.minimum(1.0, down))
        both = jnp.concatenate(plus + minus, axis=0)
        ratios[b] = both
        ratio_pieces[b] = stack_split(both)

    def band(ref, *index):
        return lambda row: ref[(*index, slice(row, row + 8), slice(None))]

    def column(ref, index):
        return lambda row, s: ref[index, row : row + 8, s * LANES : (s + 1) * LANES]

    def own_tables(i):
        return scale[i], cosine[i], sine[i]

    def inner_block(i, carry):
        low_order(i + 2, band(fields, i + 1), column(inside, i), *own_tables(i + 1), True)
        return carry

    for side in range(2):
        b = side * (blocks + 1)
        tables = tuple(halo_tables[side, k] for k in range(3))
        near = 1 + side
        low_order(b, band(halo, near), column(beside, 3 * side), *tables, False)
        i = side * (blocks - 1)
        low_order(i + 1, band(fields, i), column(beside, 1 + side), *own_tables(i), True)
    lax.fori_loop(0, blocks - 2, inner_block, 0)

    def limit(i, carry):
        b = i + 1
        step = differences(
            [ratio_pieces[b - 1], ratio_pieces[b], ratio_pieces[b + 1]], matrices[i]
        )
        out = [lowered[i, 8 * g : 8 * g + 8, :] for g in range(tracer_groups)]
        own = [ratios[b, 8 * g : 8 * g + 8, :] for g in range(2 * tracer_groups)]
        for s in range(edges):
            lanes = slice(s * LANES, (s + 1) * LANES)
            for g in range(tracer_groups):
                m = g + tracer_groups
                flux = antiflux[i, s, 8 * g : 8 * g + 8, :]
                plus = own[g] + step[8 * g : 8 * g + 8, lanes]
                minus = own[m] + step[8 * m : 8 * m + 8, lanes]
                factor = jnp.where(
                    flux >= 0.0, jnp.minimum(own[m], plus), jnp.minimum(own[g], minus)
                )
                out[g] = out[g] - factor * flux
        lanes = pl.ds(pl.multiple_of(i * LANES, LANES), LANES)
        for g in range(tracer_groups):
            t, lg = g // layer_groups, g % layer_groups
            tracers_new[t, 8 * lg : 8 * lg + 8, lanes] = out[g]
        return carry

    lax.fori_loop(0, blocks, limit, 0)
    write.wait()


def swap(message, first, peers):
    pairs = []
    for i in range(first, peers - 1, 2):
        pairs += [(i, i + 1), (i + 1, i)]
    return lax.ppermute(message, "mesh", pairs)


def whole_spec():
    return pl.BlockSpec(memory_space=pltpu.VMEM)


def local(
    tracers,
    potential,
    surface_current,
    cell_neighbors,
    cell_normal,
    cell_weight,
    spectra,
    wind_velocity,
    node_neighbors,
    node_normal,
    node_weight,
    send_rows,
    node_slot,
):
    peers, _, capacity = send_rows.shape
    freqs, dirs, nodes = spectra.shape
    tracer_count, layers, cells = tracers.shape
    edges = cell_neighbors.shape[0]
    blocks = cells // LANES
    field_rows = (tracer_count + 1) * layers
    head_rows = 2 * field_rows + TABLE_ROWS
    message_rows = head_rows + (freqs // 2 * dirs + 7) // 8 * 8
    slots = node_slot.reshape(1, nodes)
    params = pltpu.CompilerParams(vmem_limit_bytes=VMEM_LIMIT)
    f32 = jnp.float32

    stored = pl.BlockSpec(memory_space=pltpu.HBM)
    rows = tracer_count * layers

    def like(x):
        return jax.ShapeDtypeStruct(x.shape, x.dtype)

    def shaped(*shape, dtype=f32):
        return jax.ShapeDtypeStruct(shape, dtype)

    def call(kernel, name, inputs, outputs, scratch, out_specs=None):
        return pl.pallas_call(
            kernel,
            out_shape=outputs,
            in_specs=[whole_spec()] * len(inputs),
            out_specs=out_specs or (whole_spec(),) * len(outputs),
            scratch_shapes=scratch,
            compiler_params=params,
            name=name,
        )(*inputs)

    inputs = (
        spectra, tracers, potential, cell_neighbors, cell_normal, cell_weight, surface_current,
        send_rows, slots, node_neighbors, node_normal, node_weight, wind_velocity,
    )
    (
        currents, outer, inner, own_spectra, own_slots, near, angle, face, wind,
        own_tracers, own_potential, neighbors, normal, weight, coupled,
    ) = pl.pallas_call(
        pack_kernel,
        out_shape=(
            shaped(peers, LANES),
            shaped(message_rows, LANES),
            shaped(message_rows, LANES),
            like(spectra),
            like(slots),
            like(node_neighbors),
            like(node_normal),
            like(node_weight),
            like(wind_velocity),
            like(tracers),
            like(potential),
            like(cell_neighbors),
            like(cell_normal),
            like(cell_weight),
            shaped(3, peers, capacity, dtype=jnp.int32),
        ),
        in_specs=[stored] * len(inputs),
        out_specs=(whole_spec(),) * 15,
        scratch_shapes=[
            pltpu.VMEM(surface_current.shape, f32),
            pltpu.SemaphoreType.DMA((15,)),
        ],
        compiler_params=params,
        name="pack",
    )(*(pltpu.with_memory_space_constraint(x, pltpu.HBM) for x in inputs))
    outer = swap(outer, 1, peers)
    inner = swap(inner, 0, peers)

    (
        cosine, sine, project, choice,
        fields, pieces, matrices, inside, cell_cosine, cell_sine, cell_scale, sums,
    ) = call(
        prepare_kernel,
        "prepare",
        (
            near, angle, face, own_tracers, own_potential, neighbors, normal, weight, coupled,
        ),
        (
            like(node_normal),
            like(node_normal),
            shaped(edges, dirs, LANES),
            shaped(4 * LANES, edges * LANES, dtype=jnp.bfloat16),
            shaped(blocks, field_rows, LANES),
            shaped(blocks, 2 * field_rows, LANES, dtype=jnp.bfloat16),
            shaped(blocks, 3 * LANES, edges * LANES, dtype=jnp.bfloat16),
            shaped(blocks - 2, field_rows, edges * LANES),
            shaped(blocks, 8, LANES),
            shaped(blocks, 8, LANES),
            shaped(blocks, 8, LANES),
            shaped(peers * capacity, (blocks + 2) * LANES, dtype=jnp.bfloat16),
        ),
        [],
    )
    currents, cosine = lax.optimization_barrier((currents, cosine))
    currents = lax.all_to_all(currents, "mesh", 0, 0, tiled=True)

    step_pairs = 5 if freqs % 10 == 0 else 1
    stride = (dirs + 7) // 8 * 8
    spectra_new, stokes_rows = call(
        functools.partial(wave_kernel, capacity, step_pairs),
        "wave",
        (
            own_spectra, outer, inner, currents, own_slots, near, wind,
            cosine, sine, project, choice,
        ),
        (like(spectra), shaped(peers, LANES)),
        [
            pltpu.VMEM((8, LANES), f32),
            pltpu.VMEM((2 * step_pairs * stride, 2 * LANES), f32),
            pltpu.VMEM((2 * step_pairs * stride, edges * LANES), f32),
        ],
    )
    stokes_all = lax.all_to_all(stokes_rows, "mesh", 0, 0, tiled=True)

    return call(
        functools.partial(tracer_kernel, capacity, (tracer_count, layers, edges)),
        "tracer",
        (
            outer, inner, stokes_all, fields, pieces, matrices, inside, cell_cosine, cell_sine,
            cell_scale, sums, pltpu.with_memory_space_constraint(spectra_new, pltpu.VMEM),
        ),
        (like(tracers), like(spectra)),
        [
            pltpu.VMEM((4, field_rows, LANES), f32),
            pltpu.VMEM((4, 2 * field_rows, LANES), jnp.bfloat16),
            pltpu.VMEM((2, 3 * LANES, edges * LANES), jnp.bfloat16),
            pltpu.VMEM((2, 3, 8, LANES), f32),
            pltpu.VMEM((4, field_rows, edges * LANES), f32),
            pltpu.VMEM((blocks + 2, 8, LANES), f32),
            pltpu.VMEM((blocks, edges, rows, LANES), f32),
            pltpu.VMEM((blocks, rows, LANES), f32),
            pltpu.VMEM((blocks + 2, 2 * rows, LANES), f32),
            pltpu.VMEM((blocks + 2, 4 * rows, LANES), jnp.bfloat16),
            pltpu.SemaphoreType.DMA(()),
        ],
        out_specs=(whole_spec(), stored),
    )


def solution(mesh):
    return jax.shard_map(
        local,
        mesh=mesh,
        in_specs=(
            P(None, None, ("groups", "mesh")),
            P(None, ("groups", "mesh")),
            P(None, ("groups", "mesh")),
            P(None, "mesh"),
            P(None, "mesh"),
            P(None, "mesh"),
            P(None, None, ("groups", "mesh")),
            P(None, ("groups", "mesh")),
            P(None, "mesh"),
            P(None, "mesh"),
            P(None, "mesh"),
            P(),
            P("mesh"),
        ),
        out_specs=(P(None, None, ("groups", "mesh")), P(None, None, ("groups", "mesh"))),
        check_vma=False,
    )
```

```python
import functools
import math

import jax
import jax.numpy as jnp
from jax import lax
from jax.experimental import pallas as pl
from jax.experimental.pallas import tpu as pltpu
from jax.sharding import PartitionSpec as P

LANES = 128
FCT_FLOOR = 0.001
TABLE_ROWS = 24
VMEM_LIMIT = 32 * 1024 * 1024


def lane_gather(values, index):
    return jnp.take_along_axis(values, index, axis=1, mode="promise_in_bounds")


def spread(row, count):
    return jnp.broadcast_to(row, (count, LANES))


def lane_iota(rows):
    return lax.broadcasted_iota(jnp.int32, (rows, LANES), 1)


def row_iota(rows):
    return lax.broadcasted_iota(jnp.int32, (rows, LANES), 0)


def slot_rows(entry):
    peers, capacity = entry.shape
    wide = jnp.concatenate([entry, jnp.zeros((peers, LANES - capacity), jnp.int32)], axis=1)
    wide = lane_gather(wide, lane_iota(peers) % capacity)
    owner = row_iota(peers)
    out = []
    for half in range(peers * capacity // LANES):
        wanted = (lane_iota(peers) + half * LANES) // capacity
        picked = jnp.where(owner == wanted, wide, 0).astype(jnp.float32)
        out.append(jnp.sum(picked, axis=0, keepdims=True).astype(jnp.int32))
    return out


def half_mask(rows, lower):
    half = lane_iota(rows) // (LANES // 2)
    return half == jnp.where(lower, 0, 1)


def peer_rows(values, peers, capacity):
    lane = lane_iota(peers)
    group = lane // capacity
    block = jnp.clip(row_iota(peers) - 1 + group // 2, 0, peers - 1)
    entry = block * capacity + lane % capacity
    out = jnp.zeros((peers, LANES), jnp.float32)
    for part in range(2):
        for half, row in enumerate(values[part]):
            found = lane_gather(spread(row, peers), entry % LANES)
            wanted = (group < 6) & (group % 2 == part) & (entry // LANES == half)
            out = jnp.where(wanted, found, out)
    return out


def direction(dirs, padded):
    turn = row_iota(padded).astype(jnp.float32) * (2.0 * math.pi / dirs)
    return jnp.cos(turn), jnp.sin(turn)


def node_tables(me, dirs, near, angle, face, cosine, sine, project, choice):
    edges, padded = project.shape[:2]
    cosine[...] = face[...] * jnp.cos(angle[...])
    sine[...] = face[...] * jnp.sin(angle[...])
    cos_dir, sin_dir = direction(dirs, padded)
    source = row_iota(LANES)
    minus = jnp.where(source == lane_iota(LANES), -1.0, 0.0)
    for s in range(edges):
        project[s] = cos_dir * cosine[s : s + 1, :] + sin_dir * sine[s : s + 1, :]
        target = near[s : s + 1, :]
        inside = target // LANES == me
        lane = target % LANES
        own = jnp.where(source == jnp.where(inside, lane, LANES), 1.0, 0.0) + minus
        halo = jnp.where(source == jnp.where(inside, LANES, lane), 1.0, 0.0)
        lanes = slice(s * LANES, (s + 1) * LANES)
        for k, part in enumerate((own, own, halo, halo)):
            choice[k * LANES : (k + 1) * LANES, lanes] = part.astype(jnp.bfloat16)


def split(x):
    first = x.astype(jnp.bfloat16)
    return first, (x - first.astype(jnp.float32)).astype(jnp.bfloat16)


def pack_kernel(
    spectra_in, tracers_in, potential_in, neighbors_in, normal_in, weight_in, current_in,
    send_rows, slot_in, near_in, angle_in, face_in, wind_in,
    rows_out, outer, inner, spectra, node_slot, near, angle, face, wind,
    tracers, potential, neighbors, normal, weight, coupled,
    current, sems,
):
    peers, _, capacity = send_rows.shape
    me = lax.axis_index("mesh")
    freqs, dirs = spectra_in.shape[:2]
    if dirs < spectra.shape[1]:
        for f in range(freqs):
            spectra[f, dirs // 8 * 8 :, :] = jnp.zeros((8, LANES), jnp.float32)
    copies = []
    for source, target in (
        (send_rows.at[me], coupled.at[1]),
        (current_in, current),
        (slot_in, node_slot),
        (spectra_in, spectra.at[:, 0:dirs, :]),
        (tracers_in, tracers),
        (potential_in, potential),
        (neighbors_in, neighbors),
        (normal_in, normal),
        (weight_in, weight),
        (send_rows.at[jnp.maximum(me - 1, 0)], coupled.at[0]),
        (send_rows.at[jnp.minimum(me + 1, peers - 1)], coupled.at[2]),
        (near_in, near),
        (angle_in, angle),
        (face_in, face),
        (wind_in, wind),
    ):
        copy = pltpu.make_async_copy(source, target, sems.at[len(copies)])
        copy.start()
        copies.append(copy)
    for copy in copies[:3]:
        copy.wait()
    layers, cells = potential.shape
    blocks = cells // LANES
    field_rows = (tracers.shape[0] + 1) * layers
    stacked = jnp.concatenate(
        [current[:, b * LANES : (b + 1) * LANES] for b in range(blocks)], axis=0
    )
    place = row_iota(2 * blocks)
    halves = slot_rows(coupled[1])
    values = [[], []]
    for cell in halves:
        found = lane_gather(stacked, spread(cell % LANES, 2 * blocks))
        for part in range(2):
            picked = jnp.where(place == 2 * (cell // LANES) + part, found, 0.0)
            values[part].append(jnp.sum(picked, axis=0, keepdims=True))
    rows_out[...] = peer_rows(values, peers, capacity)
    for copy in copies[3:]:
        copy.wait()
    odd = me % 2 == 1
    for out, upward in ((outer, odd), (inner, jnp.logical_not(odd))):
        for b in range(2):
            high = slice((blocks - 2 + b) * LANES, (blocks - 1 + b) * LANES)
            low = slice(b * LANES, (b + 1) * LANES)
            base = b * field_rows
            for t in range(tracers.shape[0]):
                out[base + t * layers : base + (t + 1) * layers, :] = jnp.where(
                    upward, tracers[t, :, high], tracers[t, :, low]
                )
            out[base + field_rows - layers : base + field_rows, :] = jnp.where(
                upward, potential[:, high], potential[:, low]
            )
        high = slice((blocks - 1) * LANES, blocks * LANES)
        low = slice(0, LANES)
        base = 2 * field_rows
        out[base : base + TABLE_ROWS, :] = jnp.zeros((TABLE_ROWS, LANES), jnp.float32)
        edges = neighbors.shape[0]
        near = jnp.where(upward, neighbors[:, high], neighbors[:, low])
        out[base : base + edges, :] = near.astype(jnp.float32)
        out[base + edges : base + edges + 1, :] = node_slot[...].astype(jnp.float32)
        out[base + 8 : base + 8 + edges, :] = jnp.where(upward, normal[:, high], normal[:, low])
        out[base + 16 : base + 16 + edges, :] = jnp.where(upward, weight[:, high], weight[:, low])
    base = 2 * field_rows + TABLE_ROWS
    pairs = freqs // 2
    whole = dirs // 8 * 8
    rest = dirs - whole
    turns = half_mask(dirs, odd)
    for g in range(pairs):
        natural = spectra[g, 0:dirs, :]
        turned = pltpu.roll(spectra[g + pairs, 0:dirs, :], LANES // 2, 1)
        for out, mixed in (
            (outer, jnp.where(turns, turned, natural)),
            (inner, jnp.where(turns, natural, turned)),
        ):
            at = base + g * whole
            out[at : at + whole, :] = mixed[:whole]
            at = base + pairs * whole + g * rest
            out[at : at + rest, :] = mixed[whole:]
    at = base + pairs * dirs
    if at < outer.shape[0]:
        for out in (outer, inner):
            out[at:, :] = jnp.zeros((outer.shape[0] - at, LANES), jnp.float32)


def choose(cells, first, lanes, matrix):
    place = cells - first
    for k in range(3):
        source = row_iota(LANES) + k * LANES
        part = jnp.where(source == place, 1.0, 0.0)
        if k == 1:
            part = part - jnp.where(row_iota(LANES) == lane_iota(LANES), 1.0, 0.0)
        matrix[k * LANES : (k + 1) * LANES, lanes] = part.astype(jnp.bfloat16)


def stack_split(x):
    first, second = split(x)
    return jnp.concatenate([first, second], axis=0)


def differences(parts, matrix):
    mixed = jnp.concatenate(parts, axis=1)
    out = jnp.dot(mixed, matrix, preferred_element_type=jnp.float32)
    rows = out.shape[0] // 2
    return out[:rows] + out[rows:]


def prepare_kernel(
    dirs, step_rows,
    spectra, near, angle, face, tracers, potential, neighbors, normal, weight, coupled,
    cosine, sine, project, choice, own_change,
    fields, pieces, matrices, inside, cell_cosine, cell_sine, cell_scale, sums,
):
    me = lax.axis_index("mesh")
    node_tables(me, dirs, near, angle, face, cosine, sine, project, choice)
    freqs, padded, _ = spectra.shape
    step = step_rows // padded

    def own_part(c, carry):
        own = spectra[pl.ds(c * step, step)].reshape(step_rows, LANES)
        own_change[pl.ds(pl.multiple_of(c * step_rows, 8), step_rows), :] = jnp.dot(
            jnp.concatenate(split(own), axis=1),
            choice[0 : 2 * LANES, :],
            preferred_element_type=jnp.float32,
        )
        return carry

    lax.fori_loop(0, freqs // step, own_part, 0)
    tracer_count, layers, cells = tracers.shape
    blocks = cells // LANES
    edges = neighbors.shape[0]
    field_rows = (tracer_count + 1) * layers
    for b in range(blocks):
        lanes = slice(b * LANES, (b + 1) * LANES)
        for t in range(tracer_count):
            fields[b, t * layers : (t + 1) * layers, :] = tracers[t, :, lanes]
        fields[b, field_rows - layers : field_rows, :] = potential[:, lanes]
        pieces[b] = stack_split(fields[b])
        w = weight[:, lanes]
        cell_scale[b, 0:edges, :] = w
        cell_cosine[b, 0:edges, :] = w * jnp.cos(normal[:, lanes])
        cell_sine[b, 0:edges, :] = w * jnp.sin(normal[:, lanes])
        for s in range(edges):
            choose(
                neighbors[s : s + 1, lanes],
                (me * blocks + b - 1) * LANES,
                slice(s * LANES, (s + 1) * LANES),
                matrices.at[b],
            )
    for b in range(1, blocks - 1):
        inside[b - 1] = differences(
            [pieces[b - 1], pieces[b], pieces[b + 1]], matrices[b]
        )
    for which in range(3):
        first = 0 if which != 0 else cells - LANES
        count = blocks if which == 1 else 1
        start = (0, 1, blocks + 1)[which]
        for half, names in enumerate(slot_rows(coupled[which])):
            named = jnp.transpose(spread(names, LANES).astype(jnp.float32))
            for b in range(count):
                cell = (lane_iota(LANES) + (first + b * LANES)).astype(jnp.float32)
                picked = jnp.where(named == cell, 1.0, 0.0).astype(jnp.bfloat16)
                lanes = slice((start + b) * LANES, (start + b + 1) * LANES)
                sums[half * LANES : (half + 1) * LANES, lanes] = picked


def node_currents(table, slot, which, capacity):
    peers = table.shape[0]
    owner = row_iota(peers) == slot // capacity
    out = []
    for part in range(2):
        lane = (2 * which + part) * capacity + slot % capacity
        found = jnp.where(owner, lane_gather(table, spread(lane, peers)), 0.0)
        out.append(jnp.sum(found, axis=0, keepdims=True))
    return out


def wave_kernel(
    capacity, step_pairs, dirs,
    spectra, outer, inner, table, node_slot, neighbors, wind, cosine, sine, project, choice,
    own_change,
    spectra_new, rows_out, drift, halos, change_a, change_b,
):
    me = lax.axis_index("mesh")
    freqs, stride = spectra.shape[:2]
    edges = neighbors.shape[0]
    peers = table.shape[0]
    halves = peers * capacity // LANES
    pairs = freqs // 2
    whole = dirs // 8 * 8
    rest = dirs - whole
    base = outer.shape[0] - (pairs * dirs + 7) // 8 * 8

    odd = me % 2 == 1
    slot = node_slot[...]
    row = base - TABLE_ROWS + edges
    halo_slot = jnp.where(
        half_mask(1, odd), outer[row : row + 1, :], inner[row : row + 1, :]
    ).astype(jnp.int32)
    lower = lane_iota(1) < LANES // 2
    currents = table[...]
    own_x, own_y = node_currents(currents, slot, jnp.ones((1, LANES), jnp.int32), capacity)
    halo_x, halo_y = node_currents(currents, halo_slot, jnp.where(lower, 2, 0), capacity)

    target = neighbors[...]
    lane = target % LANES
    inside = target // LANES == me

    def beside(own, halo):
        a = lane_gather(spread(own, edges), lane)
        b = lane_gather(spread(halo, edges), lane)
        return jnp.where(inside, a, b)

    drift[0:edges, :] = (
        0.5 * (own_x + beside(own_x, halo_x)) * cosine[...]
        + 0.5 * (own_y + beside(own_y, halo_y)) * sine[...]
    )
    drifts = [spread(drift[s : s + 1, :], 8) for s in range(edges)]
    drift_sum = sum(drifts[1:], drifts[0])
    from_outer = half_mask(dirs, odd)
    halos[...] = jnp.zeros(halos.shape, jnp.float32)
    ratio = 1.0 / 1.1
    bands = [slice(r, r + 8) for r in range(0, stride, 8)]

    def gather(c, change):
        for i in range(step_pairs):
            g = c * step_pairs + i
            parts = []
            for message in (outer, inner):
                at = pl.multiple_of(base + g * whole, 8)
                upper = message[pl.ds(at, whole), :]
                left = message[pl.ds(base + pairs * whole + g * rest, rest), :]
                parts.append(jnp.concatenate([upper, left], axis=0))
            x, y = parts
            at = 2 * i * stride
            halos[at : at + dirs, :] = jnp.where(from_outer, x, y)
            at += stride
            halos[at : at + dirs, :] = pltpu.roll(jnp.where(from_outer, y, x), LANES // 2, 1)
        mixed = jnp.concatenate(split(halos[...]), axis=1)
        change[...] = jnp.dot(
            mixed, choice[2 * LANES : 4 * LANES, :], preferred_element_type=jnp.float32
        )

    def advect(c, change, first_speed, total):
        total = list(total)
        for k, band in enumerate(bands):
            along = [project[s, band, :] for s in range(edges)]
            along_sum = sum(along[1:], along[0])
            for i in range(step_pairs):
                g = c * step_pairs + i
                for j, f, speed in (
                    (2 * i, g, first_speed * ratio**i),
                    (2 * i + 1, g + pairs, first_speed * ratio ** (i + pairs)),
                ):
                    own = spectra[f, band, :]
                    at = j * stride + band.start
                    own_at = pl.ds(pl.multiple_of(f * stride + band.start, 8), 8)
                    value = own - (speed * along_sum + drift_sum) * own
                    for s in range(edges):
                        down = jnp.minimum(speed * along[s] + drifts[s], 0.0)
                        lanes = slice(s * LANES, (s + 1) * LANES)
                        step = change[at : at + 8, lanes] + own_change[own_at, lanes]
                        value = value - down * step
                    spectra_new[f, band, :] = value
                    total[k] = total[k] + value
        return first_speed * ratio**step_pairs, tuple(total)

    zeros = tuple(jnp.zeros((8, LANES), jnp.float32) for _ in bands)
    chunks = pairs // step_pairs
    gather(0, change_a)

    def two_chunks(h, carry):
        gather(2 * h + 1, change_b)
        carry = advect(2 * h, change_a, *carry)
        gather(2 * h + 2, change_a)
        return advect(2 * h + 1, change_b, *carry)

    speed, total = lax.fori_loop(0, (chunks - 1) // 2, two_chunks, (jnp.float32(1.0), zeros))
    if chunks % 2 == 0:
        gather(chunks - 1, change_b)
        speed, total = advect(chunks - 2, change_a, speed, total)
        _, total = advect(chunks - 1, change_b, speed, total)
    else:
        _, total = advect(chunks - 1, change_a, speed, total)
    total = jnp.concatenate(total, axis=0)
    zero = jnp.zeros((stride, LANES), jnp.float32)
    cos_dir, sin_dir = direction(dirs, stride)
    mean = jnp.sum(total, axis=0, keepdims=True) * (1.0 / (freqs * dirs))
    forcing = jnp.maximum(wind[0:1, :] * cos_dir + wind[1:2, :] * sin_dir, 0.0)
    step = jnp.exp((0.25 * forcing - 2.0 * mean) * (1.0 / freqs))

    def grow(f, carry):
        factor, weighted = carry
        factor = factor * step
        evolved = spectra_new[f] * factor
        spectra_new[f] = evolved
        kappa = (f + 1).astype(jnp.float32) * (1.0 / freqs)
        return factor, weighted + kappa * evolved

    _, weighted = lax.fori_loop(0, freqs, grow, (zero + 1.0, zero))
    stokes = jnp.concatenate(
        [
            jnp.sum(weighted * cos_dir, axis=0, keepdims=True),
            jnp.sum(weighted * sin_dir, axis=0, keepdims=True),
        ],
        axis=0,
    ) * (1.0 / dirs)
    named = lax.broadcasted_iota(jnp.int32, (halves * LANES, LANES), 0) == slot
    in_order = lax.dot_general(
        three_parts(stokes),
        jnp.where(named, 1.0, 0.0).astype(jnp.bfloat16),
        (((1,), (1,)), ((), ())),
        preferred_element_type=jnp.float32,
    )
    in_order = in_order[0:2] + (in_order[2:4] + in_order[4:6])
    values = [
        [in_order[part : part + 1, h * LANES : (h + 1) * LANES] for h in range(halves)]
        for part in range(2)
    ]
    rows_out[...] = peer_rows(values, peers, capacity)


def three_parts(values):
    first = values.astype(jnp.bfloat16).astype(jnp.float32)
    left = values - first
    second = left.astype(jnp.bfloat16).astype(jnp.float32)
    third = left - second
    pad = jnp.zeros((10, values.shape[1]), jnp.float32)
    return jnp.concatenate([first, second, third, pad], axis=0).astype(jnp.bfloat16)


def tracer_kernel(
    capacity, shape,
    outer, inner, table, fields, pieces, matrices, inside, cosine, sine, scale, sums, spectra,
    tracers_new, spectra_out,
    halo, halo_pieces, halo_matrices, halo_tables, beside, stokes, antiflux, lowered, ratios,
    ratio_pieces, steps_a, steps_b, sem,
):
    dirs = spectra_out.shape[1]
    write = pltpu.make_async_copy(spectra.at[:, 0:dirs, :], spectra_out, sem)
    write.start()
    me = lax.axis_index("mesh")
    tracer_count, layers, edges = shape
    peers = table.shape[0]
    halves = peers * capacity // LANES
    blocks, field_rows, _ = fields.shape
    layer_groups = layers // 8
    tracer_groups = tracer_count * layer_groups
    odd = me % 2 == 1

    for b in range(2):
        x = outer[b * field_rows : (b + 1) * field_rows, :]
        y = inner[b * field_rows : (b + 1) * field_rows, :]
        for side, value in ((0, jnp.where(odd, y, x)), (1, jnp.where(odd, x, y))):
            halo[2 * side + b] = value
            halo_pieces[2 * side + b] = stack_split(value)
    at = 2 * field_rows
    x = outer[at : at + TABLE_ROWS, :]
    y = inner[at : at + TABLE_ROWS, :]
    for side, rows in ((0, jnp.where(odd, y, x)), (1, jnp.where(odd, x, y))):
        w = rows[16 : 16 + edges]
        halo_tables[side, 0, 0:edges, :] = w
        halo_tables[side, 1, 0:edges, :] = w * jnp.cos(rows[8 : 8 + edges])
        halo_tables[side, 2, 0:edges, :] = w * jnp.sin(rows[8 : 8 + edges])
        near = rows[0:edges].astype(jnp.int32)
        first = (me * blocks - 2 if side == 0 else me * blocks + blocks - 1) * LANES
        for s in range(edges):
            choose(
                near[s : s + 1, :],
                first,
                slice(s * LANES, (s + 1) * LANES),
                halo_matrices.at[side],
            )
    beside[0] = differences([halo_pieces[0], halo_pieces[1], pieces[0]], halo_matrices[0])
    beside[1] = differences([halo_pieces[1], pieces[0], pieces[1]], matrices[0])
    beside[2] = differences(
        [pieces[blocks - 2], pieces[blocks - 1], halo_pieces[2]], matrices[blocks - 1]
    )
    beside[3] = differences([pieces[blocks - 1], halo_pieces[2], halo_pieces[3]], halo_matrices[1])

    received = table[...]
    lane_of = lane_iota(peers)
    for which in range(3):
        values = []
        for part in range(2):
            lane = (2 * which + part) * capacity + lane_of % capacity
            found = lane_gather(received, lane)
            row = []
            for half in range(halves):
                mine = row_iota(peers) == (lane_of + half * LANES) // capacity
                row.append(jnp.sum(jnp.where(mine, found, 0.0), axis=0, keepdims=True))
            values.append(jnp.concatenate(row, axis=1))
        parts = three_parts(jnp.concatenate(values, axis=0))
        start = (0, 1, blocks + 1)[which]
        count = blocks if which == 1 else 1
        total = jnp.dot(
            parts,
            sums[:, start * LANES : (start + count) * LANES],
            preferred_element_type=jnp.float32,
        )
        total = total[0:2] + (total[2:4] + total[4:6])
        for b in range(count):
            stokes[start + b, 0:2, :] = total[:, b * LANES : (b + 1) * LANES]

    decay = [
        jnp.exp(-3.0 / layers * (row_iota(8) + 8 * g).astype(jnp.float32))
        for g in range(layer_groups)
    ]

    def low_order(b, value, change, w, wx, wy, keep):
        slope = wx * stokes[b, 0:1, :] + wy * stokes[b, 1:2, :]
        own = [value(8 * g) for g in range(tracer_groups)]
        zero = jnp.zeros((8, LANES), jnp.float32)
        speed_sum = [zero] * layer_groups
        inflow = [zero] * tracer_groups
        highest = [zero] * tracer_groups
        lowest = [zero] * tracer_groups
        positive = [zero] * tracer_groups
        negative = [zero] * tracer_groups
        for s in range(edges):
            w8 = spread(w[s : s + 1, :], 8)
            slope8 = spread(slope[s : s + 1, :], 8)
            for lg in range(layer_groups):
                speed = w8 * change(8 * (tracer_groups + lg), s) + decay[lg] * slope8
                down = jnp.minimum(speed, 0.0)
                half = 0.5 * speed - down
                speed_sum[lg] = speed_sum[lg] + speed
                for t in range(tracer_count):
                    g = t * layer_groups + lg
                    step = change(8 * g, s)
                    flux = half * step
                    if keep:
                        antiflux[b - 1, s, 8 * g : 8 * g + 8, :] = flux
                    inflow[g] = inflow[g] + down * step
                    highest[g] = jnp.maximum(highest[g], step)
                    lowest[g] = jnp.minimum(lowest[g], step)
                    positive[g] = positive[g] + jnp.maximum(flux, 0.0)
                    negative[g] = negative[g] - jnp.minimum(flux, 0.0)
        plus, minus = [], []
        for g in range(tracer_groups):
            loss = speed_sum[g % layer_groups] * own[g] + inflow[g]
            if keep:
                lowered[b - 1, 8 * g : 8 * g + 8, :] = own[g] - loss
            up = jnp.maximum(highest[g] + loss, 0.0) / (negative[g] + FCT_FLOOR)
            down = jnp.maximum(-loss - lowest[g], 0.0) / (positive[g] + FCT_FLOOR)
            plus.append(jnp.minimum(1.0, up))
            minus.append(jnp.minimum(1.0, down))
        both = jnp.concatenate(plus + minus, axis=0)
        ratios[b] = both
        ratio_pieces[b] = stack_split(both)

    def band(ref, *index):
        return lambda row: ref[(*index, slice(row, row + 8), slice(None))]

    def column(ref, index):
        return lambda row, s: ref[index, row : row + 8, s * LANES : (s + 1) * LANES]

    def own_tables(i):
        return scale[i], cosine[i], sine[i]

    for i in range(blocks - 2):
        low_order(i + 2, band(fields, i + 1), column(inside, i), *own_tables(i + 1), True)
    for side in range(2):
        b = side * (blocks + 1)
        tables = tuple(halo_tables[side, k] for k in range(3))
        near = 1 + side
        low_order(b, band(halo, near), column(beside, 3 * side), *tables, False)
        i = side * (blocks - 1)
        low_order(i + 1, band(fields, i), column(beside, 1 + side), *own_tables(i), True)

    def products(i, steps):
        mixed = jnp.concatenate([ratio_pieces[i], ratio_pieces[i + 1], ratio_pieces[i + 2]], axis=1)
        steps[...] = jnp.dot(mixed, matrices[i], preferred_element_type=jnp.float32)

    def limit(i, steps):
        out = [lowered[i, 8 * g : 8 * g + 8, :] for g in range(tracer_groups)]
        own = [ratios[i + 1, 8 * g : 8 * g + 8, :] for g in range(2 * tracer_groups)]
        low = 16 * tracer_groups
        for s in range(edges):
            lanes = slice(s * LANES, (s + 1) * LANES)
            beside = [
                own[g]
                + (steps[8 * g : 8 * g + 8, lanes] + steps[low + 8 * g : low + 8 * g + 8, lanes])
                for g in range(2 * tracer_groups)
            ]
            for g in range(tracer_groups):
                m = g + tracer_groups
                flux = antiflux[i, s, 8 * g : 8 * g + 8, :]
                factor = jnp.where(
                    flux >= 0.0, jnp.minimum(own[m], beside[g]), jnp.minimum(own[g], beside[m])
                )
                out[g] = out[g] - factor * flux
        lanes = slice(i * LANES, (i + 1) * LANES)
        for g in range(tracer_groups):
            t, lg = g // layer_groups, g % layer_groups
            tracers_new[t, 8 * lg : 8 * lg + 8, lanes] = out[g]

    buffers = (steps_a, steps_b)
    products(0, steps_a)
    for i in range(blocks):
        if i + 1 < blocks:
            products(i + 1, buffers[(i + 1) % 2])
        limit(i, buffers[i % 2])
    write.wait()


def swap(message, first, peers):
    pairs = []
    for i in range(first, peers - 1, 2):
        pairs += [(i, i + 1), (i + 1, i)]
    return lax.ppermute(message, "mesh", pairs)


def whole_spec():
    return pl.BlockSpec(memory_space=pltpu.VMEM)


def local(
    tracers,
    potential,
    surface_current,
    cell_neighbors,
    cell_normal,
    cell_weight,
    spectra,
    wind_velocity,
    node_neighbors,
    node_normal,
    node_weight,
    send_rows,
    node_slot,
):
    peers, _, capacity = send_rows.shape
    freqs, dirs, nodes = spectra.shape
    tracer_count, layers, cells = tracers.shape
    edges = cell_neighbors.shape[0]
    blocks = cells // LANES
    field_rows = (tracer_count + 1) * layers
    head_rows = 2 * field_rows + TABLE_ROWS
    message_rows = head_rows + (freqs // 2 * dirs + 7) // 8 * 8
    slots = node_slot.reshape(1, nodes)
    params = pltpu.CompilerParams(vmem_limit_bytes=VMEM_LIMIT)
    f32 = jnp.float32

    stored = pl.BlockSpec(memory_space=pltpu.HBM)
    rows = tracer_count * layers
    stride = (dirs + 7) // 8 * 8
    step_pairs = 5 if freqs % 10 == 0 else 1
    step_rows = 2 * step_pairs * stride

    def like(x):
        return jax.ShapeDtypeStruct(x.shape, x.dtype)

    def shaped(*shape, dtype=f32):
        return jax.ShapeDtypeStruct(shape, dtype)

    def call(kernel, name, inputs, outputs, scratch, out_specs=None):
        return pl.pallas_call(
            kernel,
            out_shape=outputs,
            in_specs=[whole_spec()] * len(inputs),
            out_specs=out_specs or (whole_spec(),) * len(outputs),
            scratch_shapes=scratch,
            compiler_params=params,
            name=name,
        )(*inputs)

    inputs = (
        spectra, tracers, potential, cell_neighbors, cell_normal, cell_weight, surface_current,
        send_rows, slots, node_neighbors, node_normal, node_weight, wind_velocity,
    )
    (
        currents, outer, inner, own_spectra, own_slots, near, angle, face, wind,
        own_tracers, own_potential, neighbors, normal, weight, coupled,
    ) = pl.pallas_call(
        pack_kernel,
        out_shape=(
            shaped(peers, LANES),
            shaped(message_rows, LANES),
            shaped(message_rows, LANES),
            shaped(freqs, stride, LANES),
            like(slots),
            like(node_neighbors),
            like(node_normal),
            like(node_weight),
            like(wind_velocity),
            like(tracers),
            like(potential),
            like(cell_neighbors),
            like(cell_normal),
            like(cell_weight),
            shaped(3, peers, capacity, dtype=jnp.int32),
        ),
        in_specs=[stored] * len(inputs),
        out_specs=(whole_spec(),) * 15,
        scratch_shapes=[
            pltpu.VMEM(surface_current.shape, f32),
            pltpu.SemaphoreType.DMA((15,)),
        ],
        compiler_params=params,
        name="pack",
    )(*(pltpu.with_memory_space_constraint(x, pltpu.HBM) for x in inputs))
    outer = swap(outer, 1, peers)
    inner = swap(inner, 0, peers)

    (
        cosine, sine, project, choice, own_change,
        fields, pieces, matrices, inside, cell_cosine, cell_sine, cell_scale, sums,
    ) = call(
        functools.partial(prepare_kernel, dirs, step_rows),
        "prepare",
        (
            own_spectra, near, angle, face, own_tracers, own_potential, neighbors, normal, weight, coupled,
        ),
        (
            like(node_normal),
            like(node_normal),
            shaped(edges, stride, LANES),
            shaped(4 * LANES, edges * LANES, dtype=jnp.bfloat16),
            shaped(freqs * stride, edges * LANES),
            shaped(blocks, field_rows, LANES),
            shaped(blocks, 2 * field_rows, LANES, dtype=jnp.bfloat16),
            shaped(blocks, 3 * LANES, edges * LANES, dtype=jnp.bfloat16),
            shaped(blocks - 2, field_rows, edges * LANES),
            shaped(blocks, 8, LANES),
            shaped(blocks, 8, LANES),
            shaped(blocks, 8, LANES),
            shaped(peers * capacity, (blocks + 2) * LANES, dtype=jnp.bfloat16),
        ),
        [],
    )
    currents, cosine = lax.optimization_barrier((currents, cosine))
    currents = lax.all_to_all(currents, "mesh", 0, 0, tiled=True)

    spectra_new, stokes_rows = call(
        functools.partial(wave_kernel, capacity, step_pairs, dirs),
        "wave",
        (
            own_spectra, outer, inner, currents, own_slots, near, wind,
            cosine, sine, project, choice, own_change,
        ),
        (shaped(freqs, stride, LANES), shaped(peers, LANES)),
        [
            pltpu.VMEM((8, LANES), f32),
            pltpu.VMEM((step_rows, LANES), f32),
            pltpu.VMEM((step_rows, edges * LANES), f32),
            pltpu.VMEM((step_rows, edges * LANES), f32),
        ],
    )
    stokes_all = lax.all_to_all(stokes_rows, "mesh", 0, 0, tiled=True)

    return call(
        functools.partial(tracer_kernel, capacity, (tracer_count, layers, edges)),
        "tracer",
        (
            outer, inner, stokes_all, fields, pieces, matrices, inside, cell_cosine, cell_sine,
            cell_scale, sums, pltpu.with_memory_space_constraint(spectra_new, pltpu.VMEM),
        ),
        (like(tracers), like(spectra)),
        [
            pltpu.VMEM((4, field_rows, LANES), f32),
            pltpu.VMEM((4, 2 * field_rows, LANES), jnp.bfloat16),
            pltpu.VMEM((2, 3 * LANES, edges * LANES), jnp.bfloat16),
            pltpu.VMEM((2, 3, 8, LANES), f32),
            pltpu.VMEM((4, field_rows, edges * LANES), f32),
            pltpu.VMEM((blocks + 2, 8, LANES), f32),
            pltpu.VMEM((blocks, edges, rows, LANES), f32),
            pltpu.VMEM((blocks, rows, LANES), f32),
            pltpu.VMEM((blocks + 2, 2 * rows, LANES), f32),
            pltpu.VMEM((blocks + 2, 4 * rows, LANES), jnp.bfloat16),
            pltpu.VMEM((4 * rows, edges * LANES), f32),
            pltpu.VMEM((4 * rows, edges * LANES), f32),
            pltpu.SemaphoreType.DMA(()),
        ],
        out_specs=(whole_spec(), stored),
    )


def solution(mesh):
    return jax.shard_map(
        local,
        mesh=mesh,
        in_specs=(
            P(None, None, ("groups", "mesh")),
            P(None, ("groups", "mesh")),
            P(None, ("groups", "mesh")),
            P(None, "mesh"),
            P(None, "mesh"),
            P(None, "mesh"),
            P(None, None, ("groups", "mesh")),
            P(None, ("groups", "mesh")),
            P(None, "mesh"),
            P(None, "mesh"),
            P(None, "mesh"),
            P(),
            P("mesh"),
        ),
        out_specs=(P(None, None, ("groups", "mesh")), P(None, None, ("groups", "mesh"))),
        check_vma=False,
    )
```

```python
import functools
import math

import jax
import jax.numpy as jnp
from jax import lax
from jax.experimental import pallas as pl
from jax.experimental.pallas import tpu as pltpu
from jax.sharding import PartitionSpec as P

LANES = 128
FCT_FLOOR = 0.001
TABLE_ROWS = 24
VMEM_LIMIT = 32 * 1024 * 1024


def lane_gather(values, index):
    return jnp.take_along_axis(values, index, axis=1, mode="promise_in_bounds")


def spread(row, count):
    return jnp.broadcast_to(row, (count, LANES))


def lane_iota(rows):
    return lax.broadcasted_iota(jnp.int32, (rows, LANES), 1)


def row_iota(rows):
    return lax.broadcasted_iota(jnp.int32, (rows, LANES), 0)


def slot_rows(entry):
    peers, capacity = entry.shape
    wide = jnp.concatenate([entry, jnp.zeros((peers, LANES - capacity), jnp.int32)], axis=1)
    wide = lane_gather(wide, lane_iota(peers) % capacity)
    owner = row_iota(peers)
    out = []
    for half in range(peers * capacity // LANES):
        wanted = (lane_iota(peers) + half * LANES) // capacity
        picked = jnp.where(owner == wanted, wide, 0).astype(jnp.float32)
        out.append(jnp.sum(picked, axis=0, keepdims=True).astype(jnp.int32))
    return out


def half_mask(rows, lower):
    half = lane_iota(rows) // (LANES // 2)
    return half == jnp.where(lower, 0, 1)


def peer_rows(values, peers, capacity):
    lane = lane_iota(peers)
    group = lane // capacity
    block = jnp.clip(row_iota(peers) - 1 + group // 2, 0, peers - 1)
    entry = block * capacity + lane % capacity
    out = jnp.zeros((peers, LANES), jnp.float32)
    for part in range(2):
        for half, row in enumerate(values[part]):
            found = lane_gather(spread(row, peers), entry % LANES)
            wanted = (group < 6) & (group % 2 == part) & (entry // LANES == half)
            out = jnp.where(wanted, found, out)
    return out


def direction(dirs, padded):
    turn = row_iota(padded).astype(jnp.float32) * (2.0 * math.pi / dirs)
    return jnp.cos(turn), jnp.sin(turn)


def node_tables(me, dirs, near, angle, face, cosine, sine, project, choice):
    edges, padded = project.shape[:2]
    cosine[...] = face[...] * jnp.cos(angle[...])
    sine[...] = face[...] * jnp.sin(angle[...])
    cos_dir, sin_dir = direction(dirs, padded)
    source = row_iota(LANES)
    minus = jnp.where(source == lane_iota(LANES), -1.0, 0.0)
    for s in range(edges):
        project[s] = cos_dir * cosine[s : s + 1, :] + sin_dir * sine[s : s + 1, :]
        target = near[s : s + 1, :]
        inside = target // LANES == me
        lane = target % LANES
        own = jnp.where(source == jnp.where(inside, lane, LANES), 1.0, 0.0) + minus
        halo = jnp.where(source == jnp.where(inside, LANES, lane), 1.0, 0.0)
        lanes = slice(s * LANES, (s + 1) * LANES)
        for k, part in enumerate((own, own, halo, halo)):
            choice[k * LANES : (k + 1) * LANES, lanes] = part.astype(jnp.bfloat16)


def split(x):
    first = x.astype(jnp.bfloat16)
    return first, (x - first.astype(jnp.float32)).astype(jnp.bfloat16)


def pack_kernel(
    spectra_in, tracers_in, potential_in, neighbors_in, normal_in, weight_in, current_in,
    send_rows, slot_in, near_in, angle_in, face_in, wind_in,
    rows_out, outer, inner, spectra, node_slot, near, angle, face, wind,
    tracers, potential, neighbors, normal, weight, coupled,
    current, sems,
):
    peers, _, capacity = send_rows.shape
    me = lax.axis_index("mesh")
    freqs, dirs = spectra_in.shape[:2]
    if dirs < spectra.shape[1]:
        for f in range(freqs):
            spectra[f, dirs // 8 * 8 :, :] = jnp.zeros((8, LANES), jnp.float32)
    copies = []
    for source, target in (
        (send_rows.at[me], coupled.at[1]),
        (current_in, current),
        (slot_in, node_slot),
        (spectra_in, spectra.at[:, 0:dirs, :]),
        (tracers_in, tracers),
        (potential_in, potential),
        (neighbors_in, neighbors),
        (normal_in, normal),
        (weight_in, weight),
        (send_rows.at[jnp.maximum(me - 1, 0)], coupled.at[0]),
        (send_rows.at[jnp.minimum(me + 1, peers - 1)], coupled.at[2]),
        (near_in, near),
        (angle_in, angle),
        (face_in, face),
        (wind_in, wind),
    ):
        copy = pltpu.make_async_copy(source, target, sems.at[len(copies)])
        copy.start()
        copies.append(copy)
    for copy in copies[:3]:
        copy.wait()
    layers, cells = potential.shape
    blocks = cells // LANES
    field_rows = (tracers.shape[0] + 1) * layers
    stacked = jnp.concatenate(
        [current[:, b * LANES : (b + 1) * LANES] for b in range(blocks)], axis=0
    )
    place = row_iota(2 * blocks)
    halves = slot_rows(coupled[1])
    values = [[], []]
    for cell in halves:
        found = lane_gather(stacked, spread(cell % LANES, 2 * blocks))
        for part in range(2):
            picked = jnp.where(place == 2 * (cell // LANES) + part, found, 0.0)
            values[part].append(jnp.sum(picked, axis=0, keepdims=True))
    rows_out[...] = peer_rows(values, peers, capacity)
    for copy in copies[3:]:
        copy.wait()
    odd = me % 2 == 1
    for out, upward in ((outer, odd), (inner, jnp.logical_not(odd))):
        for b in range(2):
            high = slice((blocks - 2 + b) * LANES, (blocks - 1 + b) * LANES)
            low = slice(b * LANES, (b + 1) * LANES)
            base = b * field_rows
            for t in range(tracers.shape[0]):
                out[base + t * layers : base + (t + 1) * layers, :] = jnp.where(
                    upward, tracers[t, :, high], tracers[t, :, low]
                )
            out[base + field_rows - layers : base + field_rows, :] = jnp.where(
                upward, potential[:, high], potential[:, low]
            )
        high = slice((blocks - 1) * LANES, blocks * LANES)
        low = slice(0, LANES)
        base = 2 * field_rows
        out[base : base + TABLE_ROWS, :] = jnp.zeros((TABLE_ROWS, LANES), jnp.float32)
        edges = neighbors.shape[0]
        near = jnp.where(upward, neighbors[:, high], neighbors[:, low])
        out[base : base + edges, :] = near.astype(jnp.float32)
        out[base + edges : base + edges + 1, :] = node_slot[...].astype(jnp.float32)
        out[base + 8 : base + 8 + edges, :] = jnp.where(upward, normal[:, high], normal[:, low])
        out[base + 16 : base + 16 + edges, :] = jnp.where(upward, weight[:, high], weight[:, low])
    base = 2 * field_rows + TABLE_ROWS
    pairs = freqs // 2
    whole = dirs // 8 * 8
    rest = dirs - whole
    turns = half_mask(dirs, odd)
    for g in range(pairs):
        natural = spectra[g, 0:dirs, :]
        turned = pltpu.roll(spectra[g + pairs, 0:dirs, :], LANES // 2, 1)
        for out, mixed in (
            (outer, jnp.where(turns, turned, natural)),
            (inner, jnp.where(turns, natural, turned)),
        ):
            at = base + g * whole
            out[at : at + whole, :] = mixed[:whole]
            at = base + pairs * whole + g * rest
            out[at : at + rest, :] = mixed[whole:]
    at = base + pairs * dirs
    if at < outer.shape[0]:
        for out in (outer, inner):
            out[at:, :] = jnp.zeros((outer.shape[0] - at, LANES), jnp.float32)


def choose(cells, first, lanes, matrix):
    place = cells - first
    for k in range(3):
        source = row_iota(LANES) + k * LANES
        part = jnp.where(source == place, 1.0, 0.0)
        if k == 1:
            part = part - jnp.where(row_iota(LANES) == lane_iota(LANES), 1.0, 0.0)
        matrix[k * LANES : (k + 1) * LANES, lanes] = part.astype(jnp.bfloat16)


def stack_split(x):
    first, second = split(x)
    return jnp.concatenate([first, second], axis=0)


def differences(parts, matrix):
    mixed = jnp.concatenate(parts, axis=1)
    out = jnp.dot(mixed, matrix, preferred_element_type=jnp.float32)
    rows = out.shape[0] // 2
    return out[:rows] + out[rows:]


def prepare_kernel(
    dirs, step_rows,
    spectra, near, angle, face, tracers, potential, neighbors, normal, weight, coupled,
    cosine, sine, project, choice, own_change,
    fields, pieces, matrices, inside, cell_cosine, cell_sine, cell_scale, sums,
):
    me = lax.axis_index("mesh")
    node_tables(me, dirs, near, angle, face, cosine, sine, project, choice)
    freqs, padded, _ = spectra.shape
    step = step_rows // padded

    def own_part(c, carry):
        own = spectra[pl.ds(c * step, step)].reshape(step_rows, LANES)
        own_change[pl.ds(pl.multiple_of(c * step_rows, 8), step_rows), :] = jnp.dot(
            jnp.concatenate(split(own), axis=1),
            choice[0 : 2 * LANES, :],
            preferred_element_type=jnp.float32,
        )
        return carry

    lax.fori_loop(0, freqs // step, own_part, 0)
    tracer_count, layers, cells = tracers.shape
    blocks = cells // LANES
    edges = neighbors.shape[0]
    field_rows = (tracer_count + 1) * layers
    for b in range(blocks):
        lanes = slice(b * LANES, (b + 1) * LANES)
        for t in range(tracer_count):
            fields[b, t * layers : (t + 1) * layers, :] = tracers[t, :, lanes]
        fields[b, field_rows - layers : field_rows, :] = potential[:, lanes]
        pieces[b] = stack_split(fields[b])
        w = weight[:, lanes]
        cell_scale[b, 0:edges, :] = w
        cell_cosine[b, 0:edges, :] = w * jnp.cos(normal[:, lanes])
        cell_sine[b, 0:edges, :] = w * jnp.sin(normal[:, lanes])
        for s in range(edges):
            choose(
                neighbors[s : s + 1, lanes],
                (me * blocks + b - 1) * LANES,
                slice(s * LANES, (s + 1) * LANES),
                matrices.at[b],
            )
    for b in range(1, blocks - 1):
        inside[b - 1] = differences(
            [pieces[b - 1], pieces[b], pieces[b + 1]], matrices[b]
        )
    for which in range(3):
        first = 0 if which != 0 else cells - LANES
        count = blocks if which == 1 else 1
        start = (0, 1, blocks + 1)[which]
        for half, names in enumerate(slot_rows(coupled[which])):
            named = jnp.transpose(spread(names, LANES).astype(jnp.float32))
            for b in range(count):
                cell = (lane_iota(LANES) + (first + b * LANES)).astype(jnp.float32)
                picked = jnp.where(named == cell, 1.0, 0.0).astype(jnp.bfloat16)
                lanes = slice((start + b) * LANES, (start + b + 1) * LANES)
                sums[half * LANES : (half + 1) * LANES, lanes] = picked


def node_currents(table, slot, which, capacity):
    peers = table.shape[0]
    owner = row_iota(peers) == slot // capacity
    out = []
    for part in range(2):
        lane = (2 * which + part) * capacity + slot % capacity
        found = jnp.where(owner, lane_gather(table, spread(lane, peers)), 0.0)
        out.append(jnp.sum(found, axis=0, keepdims=True))
    return out


def wave_kernel(
    capacity, step_pairs, dirs,
    spectra, outer, inner, table, node_slot, neighbors, wind, cosine, sine, project, choice,
    own_change,
    spectra_new, rows_out, drift, halos, change_a, change_b,
):
    me = lax.axis_index("mesh")
    freqs, stride = spectra.shape[:2]
    edges = neighbors.shape[0]
    peers = table.shape[0]
    halves = peers * capacity // LANES
    pairs = freqs // 2
    whole = dirs // 8 * 8
    rest = dirs - whole
    base = outer.shape[0] - (pairs * dirs + 7) // 8 * 8

    odd = me % 2 == 1
    slot = node_slot[...]
    row = base - TABLE_ROWS + edges
    halo_slot = jnp.where(
        half_mask(1, odd), outer[row : row + 1, :], inner[row : row + 1, :]
    ).astype(jnp.int32)
    lower = lane_iota(1) < LANES // 2
    currents = table[...]
    own_x, own_y = node_currents(currents, slot, jnp.ones((1, LANES), jnp.int32), capacity)
    halo_x, halo_y = node_currents(currents, halo_slot, jnp.where(lower, 2, 0), capacity)

    target = neighbors[...]
    lane = target % LANES
    inside = target // LANES == me

    def beside(own, halo):
        a = lane_gather(spread(own, edges), lane)
        b = lane_gather(spread(halo, edges), lane)
        return jnp.where(inside, a, b)

    drift[0:edges, :] = (
        0.5 * (own_x + beside(own_x, halo_x)) * cosine[...]
        + 0.5 * (own_y + beside(own_y, halo_y)) * sine[...]
    )
    drifts = [spread(drift[s : s + 1, :], 8) for s in range(edges)]
    drift_sum = sum(drifts[1:], drifts[0])
    from_outer = half_mask(dirs, odd)
    halos[...] = jnp.zeros(halos.shape, jnp.float32)
    ratio = 1.0 / 1.1
    bands = [slice(r, r + 8) for r in range(0, stride, 8)]

    def gather(c, change):
        for i in range(step_pairs):
            g = c * step_pairs + i
            parts = []
            for message in (outer, inner):
                at = pl.multiple_of(base + g * whole, 8)
                upper = message[pl.ds(at, whole), :]
                left = message[pl.ds(base + pairs * whole + g * rest, rest), :]
                parts.append(jnp.concatenate([upper, left], axis=0))
            x, y = parts
            at = 2 * i * stride
            halos[at : at + dirs, :] = jnp.where(from_outer, x, y)
            at += stride
            halos[at : at + dirs, :] = pltpu.roll(jnp.where(from_outer, y, x), LANES // 2, 1)
        mixed = jnp.concatenate(split(halos[...]), axis=1)
        change[...] = jnp.dot(
            mixed, choice[2 * LANES : 4 * LANES, :], preferred_element_type=jnp.float32
        )

    def advect(c, change, first_speed, total):
        total = list(total)
        for k, band in enumerate(bands):
            along = [project[s, band, :] for s in range(edges)]
            along_sum = sum(along[1:], along[0])
            for i in range(step_pairs):
                g = c * step_pairs + i
                for j, f, speed in (
                    (2 * i, g, first_speed * ratio**i),
                    (2 * i + 1, g + pairs, first_speed * ratio ** (i + pairs)),
                ):
                    own = spectra[f, band, :]
                    at = j * stride + band.start
                    own_at = pl.ds(pl.multiple_of(f * stride + band.start, 8), 8)
                    value = own - (speed * along_sum + drift_sum) * own
                    for s in range(edges):
                        down = jnp.minimum(speed * along[s] + drifts[s], 0.0)
                        lanes = slice(s * LANES, (s + 1) * LANES)
                        step = change[at : at + 8, lanes] + own_change[own_at, lanes]
                        value = value - down * step
                    spectra_new[f, band, :] = value
                    total[k] = total[k] + value
        return first_speed * ratio**step_pairs, tuple(total)

    zeros = tuple(jnp.zeros((8, LANES), jnp.float32) for _ in bands)
    chunks = pairs // step_pairs
    gather(0, change_a)

    def two_chunks(h, carry):
        gather(2 * h + 1, change_b)
        carry = advect(2 * h, change_a, *carry)
        gather(2 * h + 2, change_a)
        return advect(2 * h + 1, change_b, *carry)

    speed, total = lax.fori_loop(0, (chunks - 1) // 2, two_chunks, (jnp.float32(1.0), zeros))
    if chunks % 2 == 0:
        gather(chunks - 1, change_b)
        speed, total = advect(chunks - 2, change_a, speed, total)
        _, total = advect(chunks - 1, change_b, speed, total)
    else:
        _, total = advect(chunks - 1, change_a, speed, total)
    total = jnp.concatenate(total, axis=0)
    zero = jnp.zeros((stride, LANES), jnp.float32)
    cos_dir, sin_dir = direction(dirs, stride)
    mean = jnp.sum(total, axis=0, keepdims=True) * (1.0 / (freqs * dirs))
    forcing = jnp.maximum(wind[0:1, :] * cos_dir + wind[1:2, :] * sin_dir, 0.0)
    step = jnp.exp((0.25 * forcing - 2.0 * mean) * (1.0 / freqs))

    def grow(f, carry):
        factor, weighted = carry
        factor = factor * step
        evolved = spectra_new[f] * factor
        spectra_new[f] = evolved
        kappa = (f + 1).astype(jnp.float32) * (1.0 / freqs)
        return factor, weighted + kappa * evolved

    _, weighted = lax.fori_loop(0, freqs, grow, (zero + 1.0, zero))
    stokes = jnp.concatenate(
        [
            jnp.sum(weighted * cos_dir, axis=0, keepdims=True),
            jnp.sum(weighted * sin_dir, axis=0, keepdims=True),
        ],
        axis=0,
    ) * (1.0 / dirs)
    named = lax.broadcasted_iota(jnp.int32, (halves * LANES, LANES), 0) == slot
    in_order = lax.dot_general(
        three_parts(stokes),
        jnp.where(named, 1.0, 0.0).astype(jnp.bfloat16),
        (((1,), (1,)), ((), ())),
        preferred_element_type=jnp.float32,
    )
    in_order = in_order[0:2] + (in_order[2:4] + in_order[4:6])
    values = [
        [in_order[part : part + 1, h * LANES : (h + 1) * LANES] for h in range(halves)]
        for part in range(2)
    ]
    rows_out[...] = peer_rows(values, peers, capacity)


def three_parts(values):
    first = values.astype(jnp.bfloat16).astype(jnp.float32)
    left = values - first
    second = left.astype(jnp.bfloat16).astype(jnp.float32)
    third = left - second
    pad = jnp.zeros((10, values.shape[1]), jnp.float32)
    return jnp.concatenate([first, second, third, pad], axis=0).astype(jnp.bfloat16)


def tracer_kernel(
    capacity, shape,
    outer, inner, table, other, fields, pieces, matrices, inside, cosine, sine, scale, sums, spectra,
    tracers_new, spectra_out,
    halo, halo_pieces, halo_matrices, halo_tables, beside, stokes, antiflux, lowered, ratios,
    ratio_pieces, steps_a, steps_b, sem,
):
    dirs = spectra_out.shape[1]
    write = pltpu.make_async_copy(spectra.at[:, 0:dirs, :], spectra_out, sem)
    write.start()
    me = lax.axis_index("mesh")
    tracer_count, layers, edges = shape
    peers = table.shape[0]
    halves = peers * capacity // LANES
    blocks, field_rows, _ = fields.shape
    layer_groups = layers // 8
    tracer_groups = tracer_count * layer_groups
    odd = me % 2 == 1

    for b in range(2):
        x = outer[b * field_rows : (b + 1) * field_rows, :]
        y = inner[b * field_rows : (b + 1) * field_rows, :]
        for side, value in ((0, jnp.where(odd, y, x)), (1, jnp.where(odd, x, y))):
            halo[2 * side + b] = value
            halo_pieces[2 * side + b] = stack_split(value)
    at = 2 * field_rows
    x = outer[at : at + TABLE_ROWS, :]
    y = inner[at : at + TABLE_ROWS, :]
    for side, rows in ((0, jnp.where(odd, y, x)), (1, jnp.where(odd, x, y))):
        w = rows[16 : 16 + edges]
        halo_tables[side, 0, 0:edges, :] = w
        halo_tables[side, 1, 0:edges, :] = w * jnp.cos(rows[8 : 8 + edges])
        halo_tables[side, 2, 0:edges, :] = w * jnp.sin(rows[8 : 8 + edges])
        near = rows[0:edges].astype(jnp.int32)
        first = (me * blocks - 2 if side == 0 else me * blocks + blocks - 1) * LANES
        for s in range(edges):
            choose(
                near[s : s + 1, :],
                first,
                slice(s * LANES, (s + 1) * LANES),
                halo_matrices.at[side],
            )
    beside[0] = differences([halo_pieces[0], halo_pieces[1], pieces[0]], halo_matrices[0])
    beside[1] = differences([halo_pieces[1], pieces[0], pieces[1]], matrices[0])
    beside[2] = differences(
        [pieces[blocks - 2], pieces[blocks - 1], halo_pieces[2]], matrices[blocks - 1]
    )
    beside[3] = differences([pieces[blocks - 1], halo_pieces[2], halo_pieces[3]], halo_matrices[1])

    received = table[...]
    swapped = other[...]
    lane_of = lane_iota(peers)
    held = row_iota(peers) % 2 == me % 2
    here = jnp.where(held, row_iota(peers), -1)
    there = jnp.where(held, row_iota(peers) + 1 - 2 * (me % 2), -1)
    for which in range(3):
        values = []
        for part in range(2):
            lane = (2 * which + part) * capacity + lane_of % capacity
            near = lane_gather(received, lane)
            far = lane_gather(swapped, lane)
            row = []
            for half in range(halves):
                source = (lane_of + half * LANES) // capacity
                found = jnp.where(here == source, near, jnp.where(there == source, far, 0.0))
                row.append(jnp.sum(found, axis=0, keepdims=True))
            values.append(jnp.concatenate(row, axis=1))
        parts = three_parts(jnp.concatenate(values, axis=0))
        start = (0, 1, blocks + 1)[which]
        count = blocks if which == 1 else 1
        total = jnp.dot(
            parts,
            sums[:, start * LANES : (start + count) * LANES],
            preferred_element_type=jnp.float32,
        )
        total = total[0:2] + (total[2:4] + total[4:6])
        for b in range(count):
            stokes[start + b, 0:2, :] = total[:, b * LANES : (b + 1) * LANES]

    decay = [
        jnp.exp(-3.0 / layers * (row_iota(8) + 8 * g).astype(jnp.float32))
        for g in range(layer_groups)
    ]

    def low_order(b, value, change, w, wx, wy, keep):
        slope = wx * stokes[b, 0:1, :] + wy * stokes[b, 1:2, :]
        own = [value(8 * g) for g in range(tracer_groups)]
        zero = jnp.zeros((8, LANES), jnp.float32)
        speed_sum = [zero] * layer_groups
        inflow = [zero] * tracer_groups
        highest = [zero] * tracer_groups
        lowest = [zero] * tracer_groups
        positive = [zero] * tracer_groups
        negative = [zero] * tracer_groups
        for s in range(edges):
            w8 = spread(w[s : s + 1, :], 8)
            slope8 = spread(slope[s : s + 1, :], 8)
            for lg in range(layer_groups):
                speed = w8 * change(8 * (tracer_groups + lg), s) + decay[lg] * slope8
                down = jnp.minimum(speed, 0.0)
                half = 0.5 * speed - down
                speed_sum[lg] = speed_sum[lg] + speed
                for t in range(tracer_count):
                    g = t * layer_groups + lg
                    step = change(8 * g, s)
                    flux = half * step
                    if keep:
                        antiflux[b - 1, s, 8 * g : 8 * g + 8, :] = flux
                    inflow[g] = inflow[g] + down * step
                    highest[g] = jnp.maximum(highest[g], step)
                    lowest[g] = jnp.minimum(lowest[g], step)
                    positive[g] = positive[g] + jnp.maximum(flux, 0.0)
                    negative[g] = negative[g] - jnp.minimum(flux, 0.0)
        plus, minus = [], []
        for g in range(tracer_groups):
            loss = speed_sum[g % layer_groups] * own[g] + inflow[g]
            if keep:
                lowered[b - 1, 8 * g : 8 * g + 8, :] = own[g] - loss
            up = jnp.maximum(highest[g] + loss, 0.0) / (negative[g] + FCT_FLOOR)
            down = jnp.maximum(-loss - lowest[g], 0.0) / (positive[g] + FCT_FLOOR)
            plus.append(jnp.minimum(1.0, up))
            minus.append(jnp.minimum(1.0, down))
        both = jnp.concatenate(plus + minus, axis=0)
        ratios[b] = both
        ratio_pieces[b] = stack_split(both)

    def band(ref, *index):
        return lambda row: ref[(*index, slice(row, row + 8), slice(None))]

    def column(ref, index):
        return lambda row, s: ref[index, row : row + 8, s * LANES : (s + 1) * LANES]

    def own_tables(i):
        return scale[i], cosine[i], sine[i]

    for i in range(blocks - 2):
        low_order(i + 2, band(fields, i + 1), column(inside, i), *own_tables(i + 1), True)
    for side in range(2):
        b = side * (blocks + 1)
        tables = tuple(halo_tables[side, k] for k in range(3))
        near = 1 + side
        low_order(b, band(halo, near), column(beside, 3 * side), *tables, False)
        i = side * (blocks - 1)
        low_order(i + 1, band(fields, i), column(beside, 1 + side), *own_tables(i), True)

    def products(i, steps):
        mixed = jnp.concatenate([ratio_pieces[i], ratio_pieces[i + 1], ratio_pieces[i + 2]], axis=1)
        steps[...] = jnp.dot(mixed, matrices[i], preferred_element_type=jnp.float32)

    def limit(i, steps):
        out = [lowered[i, 8 * g : 8 * g + 8, :] for g in range(tracer_groups)]
        own = [ratios[i + 1, 8 * g : 8 * g + 8, :] for g in range(2 * tracer_groups)]
        low = 16 * tracer_groups
        for s in range(edges):
            lanes = slice(s * LANES, (s + 1) * LANES)
            beside = [
                own[g]
                + (steps[8 * g : 8 * g + 8, lanes] + steps[low + 8 * g : low + 8 * g + 8, lanes])
                for g in range(2 * tracer_groups)
            ]
            for g in range(tracer_groups):
                m = g + tracer_groups
                flux = antiflux[i, s, 8 * g : 8 * g + 8, :]
                factor = jnp.where(
                    flux >= 0.0, jnp.minimum(own[m], beside[g]), jnp.minimum(own[g], beside[m])
                )
                out[g] = out[g] - factor * flux
        lanes = slice(i * LANES, (i + 1) * LANES)
        for g in range(tracer_groups):
            t, lg = g // layer_groups, g % layer_groups
            tracers_new[t, 8 * lg : 8 * lg + 8, lanes] = out[g]

    buffers = (steps_a, steps_b)
    products(0, steps_a)
    for i in range(blocks):
        if i + 1 < blocks:
            products(i + 1, buffers[(i + 1) % 2])
        limit(i, buffers[i % 2])
    write.wait()


def swap(message, first, peers):
    pairs = []
    for i in range(first, peers - 1, 2):
        pairs += [(i, i + 1), (i + 1, i)]
    return lax.ppermute(message, "mesh", pairs)


def whole_spec():
    return pl.BlockSpec(memory_space=pltpu.VMEM)


def local(
    tracers,
    potential,
    surface_current,
    cell_neighbors,
    cell_normal,
    cell_weight,
    spectra,
    wind_velocity,
    node_neighbors,
    node_normal,
    node_weight,
    send_rows,
    node_slot,
):
    peers, _, capacity = send_rows.shape
    freqs, dirs, nodes = spectra.shape
    tracer_count, layers, cells = tracers.shape
    edges = cell_neighbors.shape[0]
    blocks = cells // LANES
    field_rows = (tracer_count + 1) * layers
    head_rows = 2 * field_rows + TABLE_ROWS
    message_rows = head_rows + (freqs // 2 * dirs + 7) // 8 * 8
    slots = node_slot.reshape(1, nodes)
    params = pltpu.CompilerParams(vmem_limit_bytes=VMEM_LIMIT)
    f32 = jnp.float32

    stored = pl.BlockSpec(memory_space=pltpu.HBM)
    rows = tracer_count * layers
    stride = (dirs + 7) // 8 * 8
    step_pairs = 5 if freqs % 10 == 0 else 1
    step_rows = 2 * step_pairs * stride

    def like(x):
        return jax.ShapeDtypeStruct(x.shape, x.dtype)

    def shaped(*shape, dtype=f32):
        return jax.ShapeDtypeStruct(shape, dtype)

    def call(kernel, name, inputs, outputs, scratch, out_specs=None):
        return pl.pallas_call(
            kernel,
            out_shape=outputs,
            in_specs=[whole_spec()] * len(inputs),
            out_specs=out_specs or (whole_spec(),) * len(outputs),
            scratch_shapes=scratch,
            compiler_params=params,
            name=name,
        )(*inputs)

    inputs = (
        spectra, tracers, potential, cell_neighbors, cell_normal, cell_weight, surface_current,
        send_rows, slots, node_neighbors, node_normal, node_weight, wind_velocity,
    )
    (
        currents, outer, inner, own_spectra, own_slots, near, angle, face, wind,
        own_tracers, own_potential, neighbors, normal, weight, coupled,
    ) = pl.pallas_call(
        pack_kernel,
        out_shape=(
            shaped(peers, LANES),
            shaped(message_rows, LANES),
            shaped(message_rows, LANES),
            shaped(freqs, stride, LANES),
            like(slots),
            like(node_neighbors),
            like(node_normal),
            like(node_weight),
            like(wind_velocity),
            like(tracers),
            like(potential),
            like(cell_neighbors),
            like(cell_normal),
            like(cell_weight),
            shaped(3, peers, capacity, dtype=jnp.int32),
        ),
        in_specs=[stored] * len(inputs),
        out_specs=(whole_spec(),) * 15,
        scratch_shapes=[
            pltpu.VMEM(surface_current.shape, f32),
            pltpu.SemaphoreType.DMA((15,)),
        ],
        compiler_params=params,
        name="pack",
    )(*(pltpu.with_memory_space_constraint(x, pltpu.HBM) for x in inputs))
    outer = swap(outer, 1, peers)
    inner = swap(inner, 0, peers)

    (
        cosine, sine, project, choice, own_change,
        fields, pieces, matrices, inside, cell_cosine, cell_sine, cell_scale, sums,
    ) = call(
        functools.partial(prepare_kernel, dirs, step_rows),
        "prepare",
        (
            own_spectra, near, angle, face, own_tracers, own_potential, neighbors, normal, weight, coupled,
        ),
        (
            like(node_normal),
            like(node_normal),
            shaped(edges, stride, LANES),
            shaped(4 * LANES, edges * LANES, dtype=jnp.bfloat16),
            shaped(freqs * stride, edges * LANES),
            shaped(blocks, field_rows, LANES),
            shaped(blocks, 2 * field_rows, LANES, dtype=jnp.bfloat16),
            shaped(blocks, 3 * LANES, edges * LANES, dtype=jnp.bfloat16),
            shaped(blocks - 2, field_rows, edges * LANES),
            shaped(blocks, 8, LANES),
            shaped(blocks, 8, LANES),
            shaped(blocks, 8, LANES),
            shaped(peers * capacity, (blocks + 2) * LANES, dtype=jnp.bfloat16),
        ),
        [],
    )
    currents, cosine = lax.optimization_barrier((currents, cosine))
    currents = lax.all_to_all(currents, "mesh", 0, 0, tiled=True)

    spectra_new, stokes_rows = call(
        functools.partial(wave_kernel, capacity, step_pairs, dirs),
        "wave",
        (
            own_spectra, outer, inner, currents, own_slots, near, wind,
            cosine, sine, project, choice, own_change,
        ),
        (shaped(freqs, stride, LANES), shaped(peers, LANES)),
        [
            pltpu.VMEM((8, LANES), f32),
            pltpu.VMEM((step_rows, LANES), f32),
            pltpu.VMEM((step_rows, edges * LANES), f32),
            pltpu.VMEM((step_rows, edges * LANES), f32),
        ],
    )
    cores = [list(range(core, peers, 2)) for core in range(2)]
    stokes_all = lax.all_to_all(
        stokes_rows, "mesh", 0, 0, axis_index_groups=cores, tiled=True
    )
    stokes_other = swap(stokes_all, 0, peers)

    return call(
        functools.partial(tracer_kernel, capacity, (tracer_count, layers, edges)),
        "tracer",
        (
            outer, inner, stokes_all, stokes_other, fields, pieces, matrices, inside, cell_cosine, cell_sine,
            cell_scale, sums, pltpu.with_memory_space_constraint(spectra_new, pltpu.VMEM),
        ),
        (like(tracers), like(spectra)),
        [
            pltpu.VMEM((4, field_rows, LANES), f32),
            pltpu.VMEM((4, 2 * field_rows, LANES), jnp.bfloat16),
            pltpu.VMEM((2, 3 * LANES, edges * LANES), jnp.bfloat16),
            pltpu.VMEM((2, 3, 8, LANES), f32),
            pltpu.VMEM((4, field_rows, edges * LANES), f32),
            pltpu.VMEM((blocks + 2, 8, LANES), f32),
            pltpu.VMEM((blocks, edges, rows, LANES), f32),
            pltpu.VMEM((blocks, rows, LANES), f32),
            pltpu.VMEM((blocks + 2, 2 * rows, LANES), f32),
            pltpu.VMEM((blocks + 2, 4 * rows, LANES), jnp.bfloat16),
            pltpu.VMEM((4 * rows, edges * LANES), f32),
            pltpu.VMEM((4 * rows, edges * LANES), f32),
            pltpu.SemaphoreType.DMA(()),
        ],
        out_specs=(whole_spec(), stored),
    )


def solution(mesh):
    return jax.shard_map(
        local,
        mesh=mesh,
        in_specs=(
            P(None, None, ("groups", "mesh")),
            P(None, ("groups", "mesh")),
            P(None, ("groups", "mesh")),
            P(None, "mesh"),
            P(None, "mesh"),
            P(None, "mesh"),
            P(None, None, ("groups", "mesh")),
            P(None, ("groups", "mesh")),
            P(None, "mesh"),
            P(None, "mesh"),
            P(None, "mesh"),
            P(),
            P("mesh"),
        ),
        out_specs=(P(None, None, ("groups", "mesh")), P(None, None, ("groups", "mesh"))),
        check_vma=False,
    )
```

```python
import functools
import math

import jax
import jax.numpy as jnp
from jax import lax
from jax.experimental import pallas as pl
from jax.experimental.pallas import tpu as pltpu
from jax.sharding import PartitionSpec as P

LANES = 128
FCT_FLOOR = 0.001
TABLE_ROWS = 24
VMEM_LIMIT = 32 * 1024 * 1024


def lane_gather(values, index):
    return jnp.take_along_axis(values, index, axis=1, mode="promise_in_bounds")


def spread(row, count):
    return jnp.broadcast_to(row, (count, LANES))


def lane_iota(rows):
    return lax.broadcasted_iota(jnp.int32, (rows, LANES), 1)


def row_iota(rows):
    return lax.broadcasted_iota(jnp.int32, (rows, LANES), 0)


def slot_rows(entry):
    peers, capacity = entry.shape
    wide = jnp.concatenate([entry, jnp.zeros((peers, LANES - capacity), jnp.int32)], axis=1)
    wide = lane_gather(wide, lane_iota(peers) % capacity)
    owner = row_iota(peers)
    out = []
    for half in range(peers * capacity // LANES):
        wanted = (lane_iota(peers) + half * LANES) // capacity
        picked = jnp.where(owner == wanted, wide, 0).astype(jnp.float32)
        out.append(jnp.sum(picked, axis=0, keepdims=True).astype(jnp.int32))
    return out


def half_mask(rows, lower):
    half = lane_iota(rows) // (LANES // 2)
    return half == jnp.where(lower, 0, 1)


def peer_rows(values, peers, capacity):
    lane = lane_iota(peers)
    group = lane // capacity
    block = jnp.clip(row_iota(peers) - 1 + group // 2, 0, peers - 1)
    entry = block * capacity + lane % capacity
    out = jnp.zeros((peers, LANES), jnp.float32)
    for part in range(2):
        for half, row in enumerate(values[part]):
            found = lane_gather(spread(row, peers), entry % LANES)
            wanted = (group < 6) & (group % 2 == part) & (entry // LANES == half)
            out = jnp.where(wanted, found, out)
    return out


def direction(dirs, padded):
    turn = row_iota(padded).astype(jnp.float32) * (2.0 * math.pi / dirs)
    return jnp.cos(turn), jnp.sin(turn)


def node_tables(
    me, dirs, near, angle, face, wind, slot, cosine, sine, project, choice, ways, slots
):
    edges, padded = project.shape[:2]
    cosine[...] = face[...] * jnp.cos(angle[...])
    sine[...] = face[...] * jnp.sin(angle[...])
    cos_dir, sin_dir = direction(dirs, padded)
    ways[0] = cos_dir
    ways[1] = sin_dir
    ways[2] = 0.25 * jnp.maximum(wind[0:1, :] * cos_dir + wind[1:2, :] * sin_dir, 0.0)
    taken = jnp.transpose(spread(slot[...].astype(jnp.float32), LANES))
    for half in range(slots.shape[1] // LANES):
        number = (lane_iota(LANES) + half * LANES).astype(jnp.float32)
        picked = jnp.where(taken == number, 1.0, 0.0).astype(jnp.bfloat16)
        slots[:, half * LANES : (half + 1) * LANES] = picked
    source = row_iota(LANES)
    minus = jnp.where(source == lane_iota(LANES), -1.0, 0.0)
    for s in range(edges):
        project[s] = cos_dir * cosine[s : s + 1, :] + sin_dir * sine[s : s + 1, :]
        target = near[s : s + 1, :]
        inside = target // LANES == me
        lane = target % LANES
        own = jnp.where(source == jnp.where(inside, lane, LANES), 1.0, 0.0) + minus
        halo = jnp.where(source == jnp.where(inside, LANES, lane), 1.0, 0.0)
        lanes = slice(s * LANES, (s + 1) * LANES)
        for k, part in enumerate((own, own, halo, halo)):
            choice[k * LANES : (k + 1) * LANES, lanes] = part.astype(jnp.bfloat16)


def split(x):
    first = x.astype(jnp.bfloat16)
    return first, (x - first.astype(jnp.float32)).astype(jnp.bfloat16)


def pack_kernel(
    spectra_in, tracers_in, potential_in, neighbors_in, normal_in, weight_in, current_in,
    send_rows, slot_in, near_in, angle_in, face_in, wind_in,
    rows_out, outer, inner, spectra, node_slot, near, angle, face, wind,
    tracers, potential, neighbors, normal, weight, coupled,
    current, sems,
):
    peers, _, capacity = send_rows.shape
    me = lax.axis_index("mesh")
    freqs, dirs = spectra_in.shape[:2]
    if dirs < spectra.shape[1]:
        for f in range(freqs):
            spectra[f, dirs // 8 * 8 :, :] = jnp.zeros((8, LANES), jnp.float32)
    pairs = freqs // 2
    piece = 5 if pairs % 5 == 0 else pairs
    pieces = [
        slice(start + first, start + first + piece)
        for first in range(0, pairs, piece)
        for start in (0, pairs)
    ]
    copies = []
    for source, target in (
        (send_rows.at[me], coupled.at[1]),
        (current_in, current),
        (slot_in, node_slot),
        (tracers_in, tracers),
        (potential_in, potential),
        (neighbors_in, neighbors),
        (normal_in, normal),
        (weight_in, weight),
        *((spectra_in.at[part], spectra.at[part, 0:dirs, :]) for part in pieces),
        (send_rows.at[jnp.maximum(me - 1, 0)], coupled.at[0]),
        (send_rows.at[jnp.minimum(me + 1, peers - 1)], coupled.at[2]),
        (near_in, near),
        (angle_in, angle),
        (face_in, face),
        (wind_in, wind),
    ):
        copy = pltpu.make_async_copy(source, target, sems.at[len(copies)])
        copy.start()
        copies.append(copy)
    for copy in copies[:3]:
        copy.wait()
    layers, cells = potential.shape
    blocks = cells // LANES
    field_rows = (tracers.shape[0] + 1) * layers
    stacked = jnp.concatenate(
        [current[:, b * LANES : (b + 1) * LANES] for b in range(blocks)], axis=0
    )
    place = row_iota(2 * blocks)
    halves = slot_rows(coupled[1])
    values = [[], []]
    for cell in halves:
        found = lane_gather(stacked, spread(cell % LANES, 2 * blocks))
        for part in range(2):
            picked = jnp.where(place == 2 * (cell // LANES) + part, found, 0.0)
            values[part].append(jnp.sum(picked, axis=0, keepdims=True))
    rows_out[...] = peer_rows(values, peers, capacity)
    for copy in copies[3:8]:
        copy.wait()
    odd = me % 2 == 1
    for out, upward in ((outer, odd), (inner, jnp.logical_not(odd))):
        for b in range(2):
            high = slice((blocks - 2 + b) * LANES, (blocks - 1 + b) * LANES)
            low = slice(b * LANES, (b + 1) * LANES)
            base = b * field_rows
            for t in range(tracers.shape[0]):
                out[base + t * layers : base + (t + 1) * layers, :] = jnp.where(
                    upward, tracers[t, :, high], tracers[t, :, low]
                )
            out[base + field_rows - layers : base + field_rows, :] = jnp.where(
                upward, potential[:, high], potential[:, low]
            )
        high = slice((blocks - 1) * LANES, blocks * LANES)
        low = slice(0, LANES)
        base = 2 * field_rows
        out[base : base + TABLE_ROWS, :] = jnp.zeros((TABLE_ROWS, LANES), jnp.float32)
        edges = neighbors.shape[0]
        near = jnp.where(upward, neighbors[:, high], neighbors[:, low])
        out[base : base + edges, :] = near.astype(jnp.float32)
        out[base + edges : base + edges + 1, :] = node_slot[...].astype(jnp.float32)
        out[base + 8 : base + 8 + edges, :] = jnp.where(upward, normal[:, high], normal[:, low])
        out[base + 16 : base + 16 + edges, :] = jnp.where(upward, weight[:, high], weight[:, low])
    base = 2 * field_rows + TABLE_ROWS
    whole = dirs // 8 * 8
    rest = dirs - whole
    turns = half_mask(dirs, odd)
    for g in range(pairs):
        if g % piece == 0:
            at = 8 + 2 * (g // piece)
            for copy in copies[at : at + 2]:
                copy.wait()
        natural = spectra[g, 0:dirs, :]
        turned = pltpu.roll(spectra[g + pairs, 0:dirs, :], LANES // 2, 1)
        for out, mixed in (
            (outer, jnp.where(turns, turned, natural)),
            (inner, jnp.where(turns, natural, turned)),
        ):
            at = base + g * whole
            out[at : at + whole, :] = mixed[:whole]
            at = base + pairs * whole + g * rest
            out[at : at + rest, :] = mixed[whole:]
    at = base + pairs * dirs
    if at < outer.shape[0]:
        for out in (outer, inner):
            out[at:, :] = jnp.zeros((outer.shape[0] - at, LANES), jnp.float32)
    for copy in copies[8 + len(pieces) :]:
        copy.wait()


def choose(cells, first, lanes, matrix):
    place = (cells - first - LANES).astype(jnp.float32).astype(jnp.bfloat16)
    place = spread(place, LANES)
    one = jnp.ones((LANES, LANES), jnp.bfloat16)
    for k in range(3):
        source = (row_iota(LANES) + (k - 1) * LANES).astype(jnp.float32).astype(jnp.bfloat16)
        part = jnp.where(source == place, one, 0 * one)
        if k == 1:
            own = jnp.where(row_iota(LANES) == lane_iota(LANES), 1.0, 0.0).astype(jnp.bfloat16)
            part = part - own
        matrix[k * LANES : (k + 1) * LANES, lanes] = part


def stack_split(x):
    first, second = split(x)
    return jnp.concatenate([first, second], axis=0)


def differences(parts, matrix):
    mixed = jnp.concatenate(parts, axis=1)
    out = jnp.dot(mixed, matrix, preferred_element_type=jnp.float32)
    rows = out.shape[0] // 2
    return out[:rows] + out[rows:]


def prepare_kernel(
    dirs, step_rows,
    spectra, near, angle, face, wind, slot, tracers, potential, neighbors, normal, weight, coupled,
    cosine, sine, project, choice, ways, slots, own_change,
    fields, pieces, matrices, inside, cell_cosine, cell_sine, cell_scale, sums,
):
    me = lax.axis_index("mesh")
    node_tables(
        me, dirs, near, angle, face, wind, slot, cosine, sine, project, choice, ways, slots
    )
    freqs, padded, _ = spectra.shape
    step = step_rows // padded

    def own_part(c, carry):
        own = spectra[pl.ds(c * step, step)].reshape(step_rows, LANES)
        own_change[pl.ds(pl.multiple_of(c * step_rows, 8), step_rows), :] = jnp.dot(
            jnp.concatenate(split(own), axis=1),
            choice[0 : 2 * LANES, :],
            preferred_element_type=jnp.float32,
        )
        return carry

    lax.fori_loop(0, freqs // step, own_part, 0)
    tracer_count, layers, cells = tracers.shape
    blocks = cells // LANES
    edges = neighbors.shape[0]
    field_rows = (tracer_count + 1) * layers
    for b in range(blocks):
        lanes = slice(b * LANES, (b + 1) * LANES)
        for t in range(tracer_count):
            fields[b, t * layers : (t + 1) * layers, :] = tracers[t, :, lanes]
        fields[b, field_rows - layers : field_rows, :] = potential[:, lanes]
        pieces[b] = stack_split(fields[b])
        w = weight[:, lanes]
        cell_scale[b, 0:edges, :] = w
        cell_cosine[b, 0:edges, :] = w * jnp.cos(normal[:, lanes])
        cell_sine[b, 0:edges, :] = w * jnp.sin(normal[:, lanes])
        for s in range(edges):
            choose(
                neighbors[s : s + 1, lanes],
                (me * blocks + b - 1) * LANES,
                slice(s * LANES, (s + 1) * LANES),
                matrices.at[b],
            )
    for b in range(1, blocks - 1):
        inside[b - 1] = differences(
            [pieces[b - 1], pieces[b], pieces[b + 1]], matrices[b]
        )
    for which in range(3):
        first = 0 if which != 0 else cells - LANES
        count = blocks if which == 1 else 1
        start = (0, 1, blocks + 1)[which]
        for half, names in enumerate(slot_rows(coupled[which])):
            named = jnp.transpose(spread(names, LANES).astype(jnp.float32))
            for b in range(count):
                cell = (lane_iota(LANES) + (first + b * LANES)).astype(jnp.float32)
                picked = jnp.where(named == cell, 1.0, 0.0).astype(jnp.bfloat16)
                lanes = slice((start + b) * LANES, (start + b + 1) * LANES)
                sums[half * LANES : (half + 1) * LANES, lanes] = picked


def node_currents(table, slot, which, capacity):
    peers = table.shape[0]
    owner = row_iota(peers) == slot // capacity
    out = []
    for part in range(2):
        lane = (2 * which + part) * capacity + slot % capacity
        found = jnp.where(owner, lane_gather(table, spread(lane, peers)), 0.0)
        out.append(jnp.sum(found, axis=0, keepdims=True))
    return out


def wave_kernel(
    capacity, step_pairs, dirs,
    spectra, outer, inner, table, node_slot, neighbors, cosine, sine, project, choice, ways, slots,
    own_change,
    spectra_new, rows_out, drift, halos, change_a, change_b,
):
    me = lax.axis_index("mesh")
    freqs, stride = spectra.shape[:2]
    edges = neighbors.shape[0]
    peers = table.shape[0]
    halves = peers * capacity // LANES
    pairs = freqs // 2
    whole = dirs // 8 * 8
    rest = dirs - whole
    base = outer.shape[0] - (pairs * dirs + 7) // 8 * 8

    odd = me % 2 == 1
    slot = node_slot[...]
    row = base - TABLE_ROWS + edges
    halo_slot = jnp.where(
        half_mask(1, odd), outer[row : row + 1, :], inner[row : row + 1, :]
    ).astype(jnp.int32)
    lower = lane_iota(1) < LANES // 2
    currents = table[...]
    own_x, own_y = node_currents(currents, slot, jnp.ones((1, LANES), jnp.int32), capacity)
    halo_x, halo_y = node_currents(currents, halo_slot, jnp.where(lower, 2, 0), capacity)

    target = neighbors[...]
    lane = target % LANES
    inside = target // LANES == me

    def beside(own, halo):
        a = lane_gather(spread(own, edges), lane)
        b = lane_gather(spread(halo, edges), lane)
        return jnp.where(inside, a, b)

    drift[0:edges, :] = (
        0.5 * (own_x + beside(own_x, halo_x)) * cosine[...]
        + 0.5 * (own_y + beside(own_y, halo_y)) * sine[...]
    )
    drifts = [spread(drift[s : s + 1, :], 8) for s in range(edges)]
    drift_sum = sum(drifts[1:], drifts[0])
    from_outer = half_mask(dirs, odd)
    halos[...] = jnp.zeros(halos.shape, jnp.float32)
    ratio = 1.0 / 1.1
    bands = [slice(r, r + 8) for r in range(0, stride, 8)]

    def gather(c, change):
        for i in range(step_pairs):
            g = c * step_pairs + i
            parts = []
            for message in (outer, inner):
                at = pl.multiple_of(base + g * whole, 8)
                upper = message[pl.ds(at, whole), :]
                left = message[pl.ds(base + pairs * whole + g * rest, rest), :]
                parts.append(jnp.concatenate([upper, left], axis=0))
            x, y = parts
            at = 2 * i * stride
            halos[at : at + dirs, :] = jnp.where(from_outer, x, y)
            at += stride
            halos[at : at + dirs, :] = pltpu.roll(jnp.where(from_outer, y, x), LANES // 2, 1)
        mixed = jnp.concatenate(split(halos[...]), axis=1)
        change[...] = jnp.dot(
            mixed, choice[2 * LANES : 4 * LANES, :], preferred_element_type=jnp.float32
        )

    def advect(c, change, first_speed, total):
        total = list(total)
        for k, band in enumerate(bands):
            along = [project[s, band, :] for s in range(edges)]
            along_sum = sum(along[1:], along[0])
            for i in range(step_pairs):
                g = c * step_pairs + i
                for j, f, speed in (
                    (2 * i, g, first_speed * ratio**i),
                    (2 * i + 1, g + pairs, first_speed * ratio ** (i + pairs)),
                ):
                    own = spectra[f, band, :]
                    at = j * stride + band.start
                    own_at = pl.ds(pl.multiple_of(f * stride + band.start, 8), 8)
                    value = own - (speed * along_sum + drift_sum) * own
                    for s in range(edges):
                        down = jnp.minimum(speed * along[s] + drifts[s], 0.0)
                        lanes = slice(s * LANES, (s + 1) * LANES)
                        step = change[at : at + 8, lanes] + own_change[own_at, lanes]
                        value = value - down * step
                    spectra_new[f, band, :] = value
                    total[k] = total[k] + value
        return first_speed * ratio**step_pairs, tuple(total)

    zeros = tuple(jnp.zeros((8, LANES), jnp.float32) for _ in bands)
    chunks = pairs // step_pairs
    gather(0, change_a)

    def two_chunks(h, carry):
        gather(2 * h + 1, change_b)
        carry = advect(2 * h, change_a, *carry)
        gather(2 * h + 2, change_a)
        return advect(2 * h + 1, change_b, *carry)

    speed, total = lax.fori_loop(0, (chunks - 1) // 2, two_chunks, (jnp.float32(1.0), zeros))
    if chunks % 2 == 0:
        gather(chunks - 1, change_b)
        speed, total = advect(chunks - 2, change_a, speed, total)
        _, total = advect(chunks - 1, change_b, speed, total)
    else:
        _, total = advect(chunks - 1, change_a, speed, total)
    total = jnp.concatenate(total, axis=0)
    zero = jnp.zeros((stride, LANES), jnp.float32)
    cos_dir, sin_dir = ways[0], ways[1]
    mean = jnp.sum(total, axis=0, keepdims=True) * (1.0 / (freqs * dirs))
    step = jnp.exp((ways[2] - 2.0 * mean) * (1.0 / freqs))
    run = 10 if freqs % 10 == 0 else 1

    def grow(c, carry):
        factor, weighted = carry
        for i in range(run):
            f = c * run + i
            factor = factor * step
            evolved = spectra_new[f] * factor
            spectra_new[f] = evolved
            kappa = (f + 1).astype(jnp.float32) * (1.0 / freqs)
            weighted = weighted + kappa * evolved
        return factor, weighted

    _, weighted = lax.fori_loop(0, freqs // run, grow, (zero + 1.0, zero))
    stokes = jnp.concatenate(
        [
            jnp.sum(weighted * cos_dir, axis=0, keepdims=True),
            jnp.sum(weighted * sin_dir, axis=0, keepdims=True),
        ],
        axis=0,
    ) * (1.0 / dirs)
    in_order = jnp.dot(
        three_parts(stokes), slots[...], preferred_element_type=jnp.float32
    )
    in_order = in_order[0:2] + (in_order[2:4] + in_order[4:6])
    values = [
        [in_order[part : part + 1, h * LANES : (h + 1) * LANES] for h in range(halves)]
        for part in range(2)
    ]
    rows_out[...] = peer_rows(values, peers, capacity)


def three_parts(values):
    first = values.astype(jnp.bfloat16).astype(jnp.float32)
    left = values - first
    second = left.astype(jnp.bfloat16).astype(jnp.float32)
    third = left - second
    pad = jnp.zeros((10, values.shape[1]), jnp.float32)
    return jnp.concatenate([first, second, third, pad], axis=0).astype(jnp.bfloat16)


def tracer_kernel(
    capacity, shape,
    outer, inner, table, fields, pieces, matrices, inside, cosine, sine, scale, sums, spectra,
    tracers_new, spectra_out,
    halo, halo_pieces, halo_matrices, halo_tables, beside, stokes, antiflux, lowered, ratios,
    ratio_pieces, steps_a, steps_b, sem,
):
    dirs = spectra_out.shape[1]
    write = pltpu.make_async_copy(spectra.at[:, 0:dirs, :], spectra_out, sem)
    write.start()
    me = lax.axis_index("mesh")
    tracer_count, layers, edges = shape
    peers = table.shape[0]
    halves = peers * capacity // LANES
    blocks, field_rows, _ = fields.shape
    layer_groups = layers // 8
    tracer_groups = tracer_count * layer_groups
    odd = me % 2 == 1

    for b in range(2):
        x = outer[b * field_rows : (b + 1) * field_rows, :]
        y = inner[b * field_rows : (b + 1) * field_rows, :]
        for side, value in ((0, jnp.where(odd, y, x)), (1, jnp.where(odd, x, y))):
            halo[2 * side + b] = value
            halo_pieces[2 * side + b] = stack_split(value)
    at = 2 * field_rows
    x = outer[at : at + TABLE_ROWS, :]
    y = inner[at : at + TABLE_ROWS, :]
    for side, rows in ((0, jnp.where(odd, y, x)), (1, jnp.where(odd, x, y))):
        w = rows[16 : 16 + edges]
        halo_tables[side, 0, 0:edges, :] = w
        halo_tables[side, 1, 0:edges, :] = w * jnp.cos(rows[8 : 8 + edges])
        halo_tables[side, 2, 0:edges, :] = w * jnp.sin(rows[8 : 8 + edges])
        near = rows[0:edges].astype(jnp.int32)
        first = (me * blocks - 2 if side == 0 else me * blocks + blocks - 1) * LANES
        for s in range(edges):
            choose(
                near[s : s + 1, :],
                first,
                slice(s * LANES, (s + 1) * LANES),
                halo_matrices.at[side],
            )
    beside[0] = differences([halo_pieces[0], halo_pieces[1], pieces[0]], halo_matrices[0])
    beside[1] = differences([halo_pieces[1], pieces[0], pieces[1]], matrices[0])
    beside[2] = differences(
        [pieces[blocks - 2], pieces[blocks - 1], halo_pieces[2]], matrices[blocks - 1]
    )
    beside[3] = differences([pieces[blocks - 1], halo_pieces[2], halo_pieces[3]], halo_matrices[1])

    received = table[...]
    lane_of = lane_iota(peers)
    for which in range(3):
        values = []
        for part in range(2):
            lane = (2 * which + part) * capacity + lane_of % capacity
            found = lane_gather(received, lane)
            row = []
            for half in range(halves):
                mine = row_iota(peers) == (lane_of + half * LANES) // capacity
                row.append(jnp.sum(jnp.where(mine, found, 0.0), axis=0, keepdims=True))
            values.append(jnp.concatenate(row, axis=1))
        parts = three_parts(jnp.concatenate(values, axis=0))
        start = (0, 1, blocks + 1)[which]
        count = blocks if which == 1 else 1
        total = jnp.dot(
            parts,
            sums[:, start * LANES : (start + count) * LANES],
            preferred_element_type=jnp.float32,
        )
        total = total[0:2] + (total[2:4] + total[4:6])
        for b in range(count):
            stokes[start + b, 0:2, :] = total[:, b * LANES : (b + 1) * LANES]

    decay = [
        jnp.exp(-3.0 / layers * (row_iota(8) + 8 * g).astype(jnp.float32))
        for g in range(layer_groups)
    ]

    def low_order(b, value, change, w, wx, wy, keep):
        slope = wx * stokes[b, 0:1, :] + wy * stokes[b, 1:2, :]
        own = [value(8 * g) for g in range(tracer_groups)]
        zero = jnp.zeros((8, LANES), jnp.float32)
        speed_sum = [zero] * layer_groups
        inflow = [zero] * tracer_groups
        highest = [zero] * tracer_groups
        lowest = [zero] * tracer_groups
        positive = [zero] * tracer_groups
        negative = [zero] * tracer_groups
        for s in range(edges):
            w8 = spread(w[s : s + 1, :], 8)
            slope8 = spread(slope[s : s + 1, :], 8)
            for lg in range(layer_groups):
                speed = w8 * change(8 * (tracer_groups + lg), s) + decay[lg] * slope8
                down = jnp.minimum(speed, 0.0)
                half = 0.5 * speed - down
                speed_sum[lg] = speed_sum[lg] + speed
                for t in range(tracer_count):
                    g = t * layer_groups + lg
                    step = change(8 * g, s)
                    flux = half * step
                    if keep:
                        antiflux[b - 1, s, 8 * g : 8 * g + 8, :] = flux
                    inflow[g] = inflow[g] + down * step
                    highest[g] = jnp.maximum(highest[g], step)
                    lowest[g] = jnp.minimum(lowest[g], step)
                    positive[g] = positive[g] + jnp.maximum(flux, 0.0)
                    negative[g] = negative[g] - jnp.minimum(flux, 0.0)
        plus, minus = [], []
        for g in range(tracer_groups):
            loss = speed_sum[g % layer_groups] * own[g] + inflow[g]
            if keep:
                lowered[b - 1, 8 * g : 8 * g + 8, :] = own[g] - loss
            up = jnp.maximum(highest[g] + loss, 0.0) / (negative[g] + FCT_FLOOR)
            down = jnp.maximum(-loss - lowest[g], 0.0) / (positive[g] + FCT_FLOOR)
            plus.append(jnp.minimum(1.0, up))
            minus.append(jnp.minimum(1.0, down))
        both = jnp.concatenate(plus + minus, axis=0)
        ratios[b] = both
        ratio_pieces[b] = stack_split(both)

    def band(ref, *index):
        return lambda row: ref[(*index, slice(row, row + 8), slice(None))]

    def column(ref, index):
        return lambda row, s: ref[index, row : row + 8, s * LANES : (s + 1) * LANES]

    def own_tables(i):
        return scale[i], cosine[i], sine[i]

    for i in range(blocks - 2):
        low_order(i + 2, band(fields, i + 1), column(inside, i), *own_tables(i + 1), True)
    for side in range(2):
        b = side * (blocks + 1)
        tables = tuple(halo_tables[side, k] for k in range(3))
        near = 1 + side
        low_order(b, band(halo, near), column(beside, 3 * side), *tables, False)
        i = side * (blocks - 1)
        low_order(i + 1, band(fields, i), column(beside, 1 + side), *own_tables(i), True)

    def products(i, steps):
        mixed = jnp.concatenate([ratio_pieces[i], ratio_pieces[i + 1], ratio_pieces[i + 2]], axis=1)
        steps[...] = jnp.dot(mixed, matrices[i], preferred_element_type=jnp.float32)

    def limit(i, steps):
        out = [lowered[i, 8 * g : 8 * g + 8, :] for g in range(tracer_groups)]
        own = [ratios[i + 1, 8 * g : 8 * g + 8, :] for g in range(2 * tracer_groups)]
        low = 16 * tracer_groups
        for s in range(edges):
            lanes = slice(s * LANES, (s + 1) * LANES)
            beside = [
                own[g]
                + (steps[8 * g : 8 * g + 8, lanes] + steps[low + 8 * g : low + 8 * g + 8, lanes])
                for g in range(2 * tracer_groups)
            ]
            for g in range(tracer_groups):
                m = g + tracer_groups
                flux = antiflux[i, s, 8 * g : 8 * g + 8, :]
                factor = jnp.where(
                    flux >= 0.0, jnp.minimum(own[m], beside[g]), jnp.minimum(own[g], beside[m])
                )
                out[g] = out[g] - factor * flux
        lanes = slice(i * LANES, (i + 1) * LANES)
        for g in range(tracer_groups):
            t, lg = g // layer_groups, g % layer_groups
            tracers_new[t, 8 * lg : 8 * lg + 8, lanes] = out[g]

    buffers = (steps_a, steps_b)
    products(0, steps_a)
    for i in range(blocks):
        if i + 1 < blocks:
            products(i + 1, buffers[(i + 1) % 2])
        limit(i, buffers[i % 2])
    write.wait()


def swap(message, first, peers):
    pairs = []
    for i in range(first, peers - 1, 2):
        pairs += [(i, i + 1), (i + 1, i)]
    return lax.ppermute(message, "mesh", pairs)


def whole_spec():
    return pl.BlockSpec(memory_space=pltpu.VMEM)


def local(
    tracers,
    potential,
    surface_current,
    cell_neighbors,
    cell_normal,
    cell_weight,
    spectra,
    wind_velocity,
    node_neighbors,
    node_normal,
    node_weight,
    send_rows,
    node_slot,
):
    peers, _, capacity = send_rows.shape
    freqs, dirs, nodes = spectra.shape
    tracer_count, layers, cells = tracers.shape
    edges = cell_neighbors.shape[0]
    blocks = cells // LANES
    field_rows = (tracer_count + 1) * layers
    head_rows = 2 * field_rows + TABLE_ROWS
    message_rows = head_rows + (freqs // 2 * dirs + 7) // 8 * 8
    slots = node_slot.reshape(1, nodes)
    params = pltpu.CompilerParams(vmem_limit_bytes=VMEM_LIMIT)
    f32 = jnp.float32

    stored = pl.BlockSpec(memory_space=pltpu.HBM)
    rows = tracer_count * layers
    stride = (dirs + 7) // 8 * 8
    step_pairs = 5 if freqs % 10 == 0 else 1
    step_rows = 2 * step_pairs * stride

    def like(x):
        return jax.ShapeDtypeStruct(x.shape, x.dtype)

    def shaped(*shape, dtype=f32):
        return jax.ShapeDtypeStruct(shape, dtype)

    def call(kernel, name, inputs, outputs, scratch, out_specs=None):
        return pl.pallas_call(
            kernel,
            out_shape=outputs,
            in_specs=[whole_spec()] * len(inputs),
            out_specs=out_specs or (whole_spec(),) * len(outputs),
            scratch_shapes=scratch,
            compiler_params=params,
            name=name,
        )(*inputs)

    inputs = (
        spectra, tracers, potential, cell_neighbors, cell_normal, cell_weight, surface_current,
        send_rows, slots, node_neighbors, node_normal, node_weight, wind_velocity,
    )
    (
        currents, outer, inner, own_spectra, own_slots, near, angle, face, wind,
        own_tracers, own_potential, neighbors, normal, weight, coupled,
    ) = pl.pallas_call(
        pack_kernel,
        out_shape=(
            shaped(peers, LANES),
            shaped(message_rows, LANES),
            shaped(message_rows, LANES),
            shaped(freqs, stride, LANES),
            like(slots),
            like(node_neighbors),
            like(node_normal),
            like(node_weight),
            like(wind_velocity),
            like(tracers),
            like(potential),
            like(cell_neighbors),
            like(cell_normal),
            like(cell_weight),
            shaped(3, peers, capacity, dtype=jnp.int32),
        ),
        in_specs=[stored] * len(inputs),
        out_specs=(whole_spec(),) * 15,
        scratch_shapes=[
            pltpu.VMEM(surface_current.shape, f32),
            pltpu.SemaphoreType.DMA((64,)),
        ],
        compiler_params=params,
        name="pack",
    )(*(pltpu.with_memory_space_constraint(x, pltpu.HBM) for x in inputs))
    outer = swap(outer, 1, peers)
    inner = swap(inner, 0, peers)

    (
        cosine, sine, project, choice, ways, slot_choice, own_change,
        fields, pieces, matrices, inside, cell_cosine, cell_sine, cell_scale, sums,
    ) = call(
        functools.partial(prepare_kernel, dirs, step_rows),
        "prepare",
        (
            own_spectra, near, angle, face, wind, own_slots, own_tracers, own_potential,
            neighbors, normal, weight, coupled,
        ),
        (
            like(node_normal),
            like(node_normal),
            shaped(edges, stride, LANES),
            shaped(4 * LANES, edges * LANES, dtype=jnp.bfloat16),
            shaped(3, stride, LANES),
            shaped(nodes, peers * capacity, dtype=jnp.bfloat16),
            shaped(freqs * stride, edges * LANES),
            shaped(blocks, field_rows, LANES),
            shaped(blocks, 2 * field_rows, LANES, dtype=jnp.bfloat16),
            shaped(blocks, 3 * LANES, edges * LANES, dtype=jnp.bfloat16),
            shaped(blocks - 2, field_rows, edges * LANES),
            shaped(blocks, 8, LANES),
            shaped(blocks, 8, LANES),
            shaped(blocks, 8, LANES),
            shaped(peers * capacity, (blocks + 2) * LANES, dtype=jnp.bfloat16),
        ),
        [],
    )
    currents, cosine = lax.optimization_barrier((currents, cosine))
    currents = lax.all_to_all(currents, "mesh", 0, 0, tiled=True)

    spectra_new, stokes_rows = call(
        functools.partial(wave_kernel, capacity, step_pairs, dirs),
        "wave",
        (
            own_spectra, outer, inner, currents, own_slots, near,
            cosine, sine, project, choice, ways, slot_choice, own_change,
        ),
        (shaped(freqs, stride, LANES), shaped(peers, LANES)),
        [
            pltpu.VMEM((8, LANES), f32),
            pltpu.VMEM((step_rows, LANES), f32),
            pltpu.VMEM((step_rows, edges * LANES), f32),
            pltpu.VMEM((step_rows, edges * LANES), f32),
        ],
    )
    stokes_all = lax.all_to_all(stokes_rows, "mesh", 0, 0, tiled=True)

    return call(
        functools.partial(tracer_kernel, capacity, (tracer_count, layers, edges)),
        "tracer",
        (
            outer, inner, stokes_all, fields, pieces, matrices, inside, cell_cosine, cell_sine,
            cell_scale, sums, pltpu.with_memory_space_constraint(spectra_new, pltpu.VMEM),
        ),
        (like(tracers), like(spectra)),
        [
            pltpu.VMEM((4, field_rows, LANES), f32),
            pltpu.VMEM((4, 2 * field_rows, LANES), jnp.bfloat16),
            pltpu.VMEM((2, 3 * LANES, edges * LANES), jnp.bfloat16),
            pltpu.VMEM((2, 3, 8, LANES), f32),
            pltpu.VMEM((4, field_rows, edges * LANES), f32),
            pltpu.VMEM((blocks + 2, 8, LANES), f32),
            pltpu.VMEM((blocks, edges, rows, LANES), f32),
            pltpu.VMEM((blocks, rows, LANES), f32),
            pltpu.VMEM((blocks + 2, 2 * rows, LANES), f32),
            pltpu.VMEM((blocks + 2, 4 * rows, LANES), jnp.bfloat16),
            pltpu.VMEM((4 * rows, edges * LANES), f32),
            pltpu.VMEM((4 * rows, edges * LANES), f32),
            pltpu.SemaphoreType.DMA(()),
        ],
        out_specs=(whole_spec(), stored),
    )


def solution(mesh):
    return jax.shard_map(
        local,
        mesh=mesh,
        in_specs=(
            P(None, None, ("groups", "mesh")),
            P(None, ("groups", "mesh")),
            P(None, ("groups", "mesh")),
            P(None, "mesh"),
            P(None, "mesh"),
            P(None, "mesh"),
            P(None, None, ("groups", "mesh")),
            P(None, ("groups", "mesh")),
            P(None, "mesh"),
            P(None, "mesh"),
            P(None, "mesh"),
            P(),
            P("mesh"),
        ),
        out_specs=(P(None, None, ("groups", "mesh")), P(None, None, ("groups", "mesh"))),
        check_vma=False,
    )
```

```python
import functools
import math

import jax
import jax.numpy as jnp
from jax import lax
from jax.experimental import pallas as pl
from jax.experimental.pallas import tpu as pltpu
from jax.sharding import PartitionSpec as P

LANES = 128
FCT_FLOOR = 0.001
TABLE_ROWS = 24
VMEM_LIMIT = 32 * 1024 * 1024


def lane_gather(values, index):
    return jnp.take_along_axis(values, index, axis=1, mode="promise_in_bounds")


def spread(row, count):
    return jnp.broadcast_to(row, (count, LANES))


def lane_iota(rows):
    return lax.broadcasted_iota(jnp.int32, (rows, LANES), 1)


def row_iota(rows):
    return lax.broadcasted_iota(jnp.int32, (rows, LANES), 0)


def slot_rows(entry):
    peers, capacity = entry.shape
    wide = jnp.concatenate([entry, jnp.zeros((peers, LANES - capacity), jnp.int32)], axis=1)
    wide = lane_gather(wide, lane_iota(peers) % capacity)
    owner = row_iota(peers)
    out = []
    for half in range(peers * capacity // LANES):
        wanted = (lane_iota(peers) + half * LANES) // capacity
        picked = jnp.where(owner == wanted, wide, 0).astype(jnp.float32)
        out.append(jnp.sum(picked, axis=0, keepdims=True).astype(jnp.int32))
    return out


def half_mask(rows, lower):
    half = lane_iota(rows) // (LANES // 2)
    return half == jnp.where(lower, 0, 1)


def peer_rows(values, peers, capacity):
    lane = lane_iota(peers)
    group = lane // capacity
    block = jnp.clip(row_iota(peers) - 1 + group // 2, 0, peers - 1)
    entry = block * capacity + lane % capacity
    out = jnp.zeros((peers, LANES), jnp.float32)
    for part in range(2):
        for half, row in enumerate(values[part]):
            found = lane_gather(spread(row, peers), entry % LANES)
            wanted = (group < 6) & (group % 2 == part) & (entry // LANES == half)
            out = jnp.where(wanted, found, out)
    return out


def direction(dirs, padded):
    turn = row_iota(padded).astype(jnp.float32) * (2.0 * math.pi / dirs)
    return jnp.cos(turn), jnp.sin(turn)


def node_tables(
    me, dirs, near, angle, face, wind, slot, cosine, sine, project, choice, ways, slots
):
    edges, padded = project.shape[:2]
    cosine[...] = face[...] * jnp.cos(angle[...])
    sine[...] = face[...] * jnp.sin(angle[...])
    cos_dir, sin_dir = direction(dirs, padded)
    ways[0] = cos_dir
    ways[1] = sin_dir
    ways[2] = 0.25 * jnp.maximum(wind[0:1, :] * cos_dir + wind[1:2, :] * sin_dir, 0.0)
    taken = jnp.transpose(spread(slot[...].astype(jnp.float32), LANES))
    for half in range(slots.shape[1] // LANES):
        number = (lane_iota(LANES) + half * LANES).astype(jnp.float32)
        picked = jnp.where(taken == number, 1.0, 0.0).astype(jnp.bfloat16)
        slots[:, half * LANES : (half + 1) * LANES] = picked
    source = row_iota(LANES)
    minus = jnp.where(source == lane_iota(LANES), -1.0, 0.0)
    for s in range(edges):
        project[s] = cos_dir * cosine[s : s + 1, :] + sin_dir * sine[s : s + 1, :]
        target = near[s : s + 1, :]
        inside = target // LANES == me
        lane = target % LANES
        own = jnp.where(source == jnp.where(inside, lane, LANES), 1.0, 0.0) + minus
        halo = jnp.where(source == jnp.where(inside, LANES, lane), 1.0, 0.0)
        lanes = slice(s * LANES, (s + 1) * LANES)
        for k, part in enumerate((own, own, halo, halo)):
            choice[k * LANES : (k + 1) * LANES, lanes] = part.astype(jnp.bfloat16)


def split(x):
    first = x.astype(jnp.bfloat16)
    return first, (x - first.astype(jnp.float32)).astype(jnp.bfloat16)


def pack_kernel(
    spectra_in, tracers_in, potential_in, neighbors_in, normal_in, weight_in, slot_in,
    outer, inner, spectra, tracers, potential, neighbors, normal, weight, node_slot,
    sems,
):
    me = lax.axis_index("mesh")
    freqs, dirs = spectra_in.shape[:2]
    if dirs < spectra.shape[1]:
        for f in range(freqs):
            spectra[f, dirs // 8 * 8 :, :] = jnp.zeros((8, LANES), jnp.float32)
    copies = []
    for source, target in (
        (spectra_in, spectra.at[:, 0:dirs, :]),
        (tracers_in, tracers),
        (potential_in, potential),
        (neighbors_in, neighbors),
        (normal_in, normal),
        (weight_in, weight),
        (slot_in, node_slot),
    ):
        copy = pltpu.make_async_copy(source, target, sems.at[len(copies)])
        copy.start()
        copies.append(copy)
    pairs = freqs // 2
    layers, cells = potential.shape
    blocks = cells // LANES
    field_rows = (tracers.shape[0] + 1) * layers
    for copy in copies[1:]:
        copy.wait()
    odd = me % 2 == 1
    for out, upward in ((outer, odd), (inner, jnp.logical_not(odd))):
        for b in range(2):
            high = slice((blocks - 2 + b) * LANES, (blocks - 1 + b) * LANES)
            low = slice(b * LANES, (b + 1) * LANES)
            base = b * field_rows
            for t in range(tracers.shape[0]):
                out[base + t * layers : base + (t + 1) * layers, :] = jnp.where(
                    upward, tracers[t, :, high], tracers[t, :, low]
                )
            out[base + field_rows - layers : base + field_rows, :] = jnp.where(
                upward, potential[:, high], potential[:, low]
            )
        high = slice((blocks - 1) * LANES, blocks * LANES)
        low = slice(0, LANES)
        base = 2 * field_rows
        out[base : base + TABLE_ROWS, :] = jnp.zeros((TABLE_ROWS, LANES), jnp.float32)
        edges = neighbors.shape[0]
        near = jnp.where(upward, neighbors[:, high], neighbors[:, low])
        out[base : base + edges, :] = near.astype(jnp.float32)
        out[base + edges : base + edges + 1, :] = node_slot[...].astype(jnp.float32)
        out[base + 8 : base + 8 + edges, :] = jnp.where(upward, normal[:, high], normal[:, low])
        out[base + 16 : base + 16 + edges, :] = jnp.where(upward, weight[:, high], weight[:, low])
    base = 2 * field_rows + TABLE_ROWS
    whole = dirs // 8 * 8
    rest = dirs - whole
    turns = half_mask(dirs, odd)
    copies[0].wait()
    for g in range(pairs):
        natural = spectra[g, 0:dirs, :]
        turned = pltpu.roll(spectra[g + pairs, 0:dirs, :], LANES // 2, 1)
        for out, mixed in (
            (outer, jnp.where(turns, turned, natural)),
            (inner, jnp.where(turns, natural, turned)),
        ):
            at = base + g * whole
            out[at : at + whole, :] = mixed[:whole]
            at = base + pairs * whole + g * rest
            out[at : at + rest, :] = mixed[whole:]
    at = base + pairs * dirs
    if at < outer.shape[0]:
        for out in (outer, inner):
            out[at:, :] = jnp.zeros((outer.shape[0] - at, LANES), jnp.float32)


def current_rows(current, coupled, rows_out):
    peers, capacity = coupled.shape[1:]
    blocks = current.shape[1] // LANES
    stacked = jnp.concatenate(
        [current[:, b * LANES : (b + 1) * LANES] for b in range(blocks)], axis=0
    )
    place = row_iota(2 * blocks)
    values = [[], []]
    for cell in slot_rows(coupled[1]):
        found = lane_gather(stacked, spread(cell % LANES, 2 * blocks))
        for part in range(2):
            picked = jnp.where(place == 2 * (cell // LANES) + part, found, 0.0)
            values[part].append(jnp.sum(picked, axis=0, keepdims=True))
    rows_out[...] = peer_rows(values, peers, capacity)


def choose(cells, first, lanes, matrix):
    place = (cells - first - LANES).astype(jnp.float32).astype(jnp.bfloat16)
    place = spread(place, LANES)
    one = jnp.ones((LANES, LANES), jnp.bfloat16)
    for k in range(3):
        source = (row_iota(LANES) + (k - 1) * LANES).astype(jnp.float32).astype(jnp.bfloat16)
        part = jnp.where(source == place, one, 0 * one)
        if k == 1:
            own = jnp.where(row_iota(LANES) == lane_iota(LANES), 1.0, 0.0).astype(jnp.bfloat16)
            part = part - own
        matrix[k * LANES : (k + 1) * LANES, lanes] = part


def stack_split(x):
    first, second = split(x)
    return jnp.concatenate([first, second], axis=0)


def differences(parts, matrix):
    mixed = jnp.concatenate(parts, axis=1)
    out = jnp.dot(mixed, matrix, preferred_element_type=jnp.float32)
    rows = out.shape[0] // 2
    return out[:rows] + out[rows:]


def prepare_kernel(
    dirs, step_rows,
    spectra, slot, tracers, potential, neighbors, normal, weight,
    near_in, angle_in, face_in, wind_in, send_rows, current_in,
    near, rows_out, cosine, sine, project, choice, ways, slots, own_change,
    fields, pieces, matrices, inside, cell_cosine, cell_sine, cell_scale, sums,
    angle, face, wind, coupled, current, sems,
):
    me = lax.axis_index("mesh")
    peers = send_rows.shape[0]
    copies = []
    for source, target in (
        (near_in, near),
        (angle_in, angle),
        (face_in, face),
        (wind_in, wind),
        (current_in, current),
        (send_rows.at[jnp.maximum(me - 1, 0)], coupled.at[0]),
        (send_rows.at[me], coupled.at[1]),
        (send_rows.at[jnp.minimum(me + 1, peers - 1)], coupled.at[2]),
    ):
        copy = pltpu.make_async_copy(source, target, sems.at[len(copies)])
        copy.start()
        copies.append(copy)
    tracer_count, layers, cells = tracers.shape
    blocks = cells // LANES
    edges = neighbors.shape[0]
    field_rows = (tracer_count + 1) * layers
    for b in range(blocks):
        lanes = slice(b * LANES, (b + 1) * LANES)
        for t in range(tracer_count):
            fields[b, t * layers : (t + 1) * layers, :] = tracers[t, :, lanes]
        fields[b, field_rows - layers : field_rows, :] = potential[:, lanes]
        pieces[b] = stack_split(fields[b])
        w = weight[:, lanes]
        cell_scale[b, 0:edges, :] = w
        cell_cosine[b, 0:edges, :] = w * jnp.cos(normal[:, lanes])
        cell_sine[b, 0:edges, :] = w * jnp.sin(normal[:, lanes])
        for s in range(edges):
            choose(
                neighbors[s : s + 1, lanes],
                (me * blocks + b - 1) * LANES,
                slice(s * LANES, (s + 1) * LANES),
                matrices.at[b],
            )
    for b in range(1, blocks - 1):
        inside[b - 1] = differences(
            [pieces[b - 1], pieces[b], pieces[b + 1]], matrices[b]
        )
    for copy in copies:
        copy.wait()
    current_rows(current, coupled, rows_out)
    node_tables(
        me, dirs, near, angle, face, wind, slot, cosine, sine, project, choice, ways, slots
    )
    freqs, padded, _ = spectra.shape
    step = step_rows // padded

    def own_part(c, carry):
        own = spectra[pl.ds(c * step, step)].reshape(step_rows, LANES)
        own_change[pl.ds(pl.multiple_of(c * step_rows, 8), step_rows), :] = jnp.dot(
            jnp.concatenate(split(own), axis=1),
            choice[0 : 2 * LANES, :],
            preferred_element_type=jnp.float32,
        )
        return carry

    lax.fori_loop(0, freqs // step, own_part, 0)
    for which in range(3):
        first = 0 if which != 0 else cells - LANES
        count = blocks if which == 1 else 1
        start = (0, 1, blocks + 1)[which]
        for half, names in enumerate(slot_rows(coupled[which])):
            named = jnp.transpose(spread(names, LANES).astype(jnp.float32))
            for b in range(count):
                cell = (lane_iota(LANES) + (first + b * LANES)).astype(jnp.float32)
                picked = jnp.where(named == cell, 1.0, 0.0).astype(jnp.bfloat16)
                lanes = slice((start + b) * LANES, (start + b + 1) * LANES)
                sums[half * LANES : (half + 1) * LANES, lanes] = picked


def node_currents(table, slot, which, capacity):
    peers = table.shape[0]
    owner = row_iota(peers) == slot // capacity
    out = []
    for part in range(2):
        lane = (2 * which + part) * capacity + slot % capacity
        found = jnp.where(owner, lane_gather(table, spread(lane, peers)), 0.0)
        out.append(jnp.sum(found, axis=0, keepdims=True))
    return out


def wave_kernel(
    capacity, step_pairs, dirs,
    spectra, outer, inner, table, node_slot, neighbors, cosine, sine, project, choice, ways, slots,
    own_change,
    spectra_new, rows_out, drift, halos, change_a, change_b,
):
    me = lax.axis_index("mesh")
    freqs, stride = spectra.shape[:2]
    edges = neighbors.shape[0]
    peers = table.shape[0]
    halves = peers * capacity // LANES
    pairs = freqs // 2
    whole = dirs // 8 * 8
    rest = dirs - whole
    base = outer.shape[0] - (pairs * dirs + 7) // 8 * 8

    odd = me % 2 == 1
    slot = node_slot[...]
    row = base - TABLE_ROWS + edges
    halo_slot = jnp.where(
        half_mask(1, odd), outer[row : row + 1, :], inner[row : row + 1, :]
    ).astype(jnp.int32)
    lower = lane_iota(1) < LANES // 2
    currents = table[...]
    own_x, own_y = node_currents(currents, slot, jnp.ones((1, LANES), jnp.int32), capacity)
    halo_x, halo_y = node_currents(currents, halo_slot, jnp.where(lower, 2, 0), capacity)

    target = neighbors[...]
    lane = target % LANES
    inside = target // LANES == me

    def beside(own, halo):
        a = lane_gather(spread(own, edges), lane)
        b = lane_gather(spread(halo, edges), lane)
        return jnp.where(inside, a, b)

    drift[0:edges, :] = (
        0.5 * (own_x + beside(own_x, halo_x)) * cosine[...]
        + 0.5 * (own_y + beside(own_y, halo_y)) * sine[...]
    )
    drifts = [spread(drift[s : s + 1, :], 8) for s in range(edges)]
    drift_sum = sum(drifts[1:], drifts[0])
    from_outer = half_mask(dirs, odd)
    halos[...] = jnp.zeros(halos.shape, jnp.float32)
    ratio = 1.0 / 1.1
    bands = [slice(r, r + 8) for r in range(0, stride, 8)]

    def gather(c, change):
        for i in range(step_pairs):
            g = c * step_pairs + i
            parts = []
            for message in (outer, inner):
                at = pl.multiple_of(base + g * whole, 8)
                upper = message[pl.ds(at, whole), :]
                left = message[pl.ds(base + pairs * whole + g * rest, rest), :]
                parts.append(jnp.concatenate([upper, left], axis=0))
            x, y = parts
            at = 2 * i * stride
            halos[at : at + dirs, :] = jnp.where(from_outer, x, y)
            at += stride
            halos[at : at + dirs, :] = pltpu.roll(jnp.where(from_outer, y, x), LANES // 2, 1)
        mixed = jnp.concatenate(split(halos[...]), axis=1)
        change[...] = jnp.dot(
            mixed, choice[2 * LANES : 4 * LANES, :], preferred_element_type=jnp.float32
        )

    def advect(c, change, first_speed, total):
        total = list(total)
        for k, band in enumerate(bands):
            along = [project[s, band, :] for s in range(edges)]
            along_sum = sum(along[1:], along[0])
            for i in range(step_pairs):
                g = c * step_pairs + i
                for j, f, speed in (
                    (2 * i, g, first_speed * ratio**i),
                    (2 * i + 1, g + pairs, first_speed * ratio ** (i + pairs)),
                ):
                    own = spectra[f, band, :]
                    at = j * stride + band.start
                    own_at = pl.ds(pl.multiple_of(f * stride + band.start, 8), 8)
                    value = own - (speed * along_sum + drift_sum) * own
                    for s in range(edges):
                        down = jnp.minimum(speed * along[s] + drifts[s], 0.0)
                        lanes = slice(s * LANES, (s + 1) * LANES)
                        step = change[at : at + 8, lanes] + own_change[own_at, lanes]
                        value = value - down * step
                    spectra_new[f, band, :] = value
                    total[k] = total[k] + value
        return first_speed * ratio**step_pairs, tuple(total)

    zeros = tuple(jnp.zeros((8, LANES), jnp.float32) for _ in bands)
    chunks = pairs // step_pairs
    gather(0, change_a)

    def two_chunks(h, carry):
        gather(2 * h + 1, change_b)
        carry = advect(2 * h, change_a, *carry)
        gather(2 * h + 2, change_a)
        return advect(2 * h + 1, change_b, *carry)

    speed, total = lax.fori_loop(0, (chunks - 1) // 2, two_chunks, (jnp.float32(1.0), zeros))
    if chunks % 2 == 0:
        gather(chunks - 1, change_b)
        speed, total = advect(chunks - 2, change_a, speed, total)
        _, total = advect(chunks - 1, change_b, speed, total)
    else:
        _, total = advect(chunks - 1, change_a, speed, total)
    total = jnp.concatenate(total, axis=0)
    zero = jnp.zeros((stride, LANES), jnp.float32)
    cos_dir, sin_dir = ways[0], ways[1]
    mean = jnp.sum(total, axis=0, keepdims=True) * (1.0 / (freqs * dirs))
    step = jnp.exp((ways[2] - 2.0 * mean) * (1.0 / freqs))
    run = 10 if freqs % 10 == 0 else 1

    def grow(c, carry):
        factor, weighted = carry
        for i in range(run):
            f = c * run + i
            factor = factor * step
            evolved = spectra_new[f] * factor
            spectra_new[f] = evolved
            kappa = (f + 1).astype(jnp.float32) * (1.0 / freqs)
            weighted = weighted + kappa * evolved
        return factor, weighted

    _, weighted = lax.fori_loop(0, freqs // run, grow, (zero + 1.0, zero))
    stokes = jnp.concatenate(
        [
            jnp.sum(weighted * cos_dir, axis=0, keepdims=True),
            jnp.sum(weighted * sin_dir, axis=0, keepdims=True),
        ],
        axis=0,
    ) * (1.0 / dirs)
    in_order = jnp.dot(
        three_parts(stokes), slots[...], preferred_element_type=jnp.float32
    )
    in_order = in_order[0:2] + (in_order[2:4] + in_order[4:6])
    values = [
        [in_order[part : part + 1, h * LANES : (h + 1) * LANES] for h in range(halves)]
        for part in range(2)
    ]
    rows_out[...] = peer_rows(values, peers, capacity)


def three_parts(values):
    first = values.astype(jnp.bfloat16).astype(jnp.float32)
    left = values - first
    second = left.astype(jnp.bfloat16).astype(jnp.float32)
    third = left - second
    pad = jnp.zeros((10, values.shape[1]), jnp.float32)
    return jnp.concatenate([first, second, third, pad], axis=0).astype(jnp.bfloat16)


def tracer_kernel(
    capacity, shape,
    outer, inner, table, fields, pieces, matrices, inside, cosine, sine, scale, sums, spectra,
    tracers_new, spectra_out,
    halo, halo_pieces, halo_matrices, halo_tables, beside, stokes, antiflux, lowered, ratios,
    ratio_pieces, steps_a, steps_b, sem,
):
    dirs = spectra_out.shape[1]
    write = pltpu.make_async_copy(spectra.at[:, 0:dirs, :], spectra_out, sem)
    write.start()
    me = lax.axis_index("mesh")
    tracer_count, layers, edges = shape
    peers = table.shape[0]
    halves = peers * capacity // LANES
    blocks, field_rows, _ = fields.shape
    layer_groups = layers // 8
    tracer_groups = tracer_count * layer_groups
    odd = me % 2 == 1

    for b in range(2):
        x = outer[b * field_rows : (b + 1) * field_rows, :]
        y = inner[b * field_rows : (b + 1) * field_rows, :]
        for side, value in ((0, jnp.where(odd, y, x)), (1, jnp.where(odd, x, y))):
            halo[2 * side + b] = value
            halo_pieces[2 * side + b] = stack_split(value)
    at = 2 * field_rows
    x = outer[at : at + TABLE_ROWS, :]
    y = inner[at : at + TABLE_ROWS, :]
    for side, rows in ((0, jnp.where(odd, y, x)), (1, jnp.where(odd, x, y))):
        w = rows[16 : 16 + edges]
        halo_tables[side, 0, 0:edges, :] = w
        halo_tables[side, 1, 0:edges, :] = w * jnp.cos(rows[8 : 8 + edges])
        halo_tables[side, 2, 0:edges, :] = w * jnp.sin(rows[8 : 8 + edges])
        near = rows[0:edges].astype(jnp.int32)
        first = (me * blocks - 2 if side == 0 else me * blocks + blocks - 1) * LANES
        for s in range(edges):
            choose(
                near[s : s + 1, :],
                first,
                slice(s * LANES, (s + 1) * LANES),
                halo_matrices.at[side],
            )
    beside[0] = differences([halo_pieces[0], halo_pieces[1], pieces[0]], halo_matrices[0])
    beside[1] = differences([halo_pieces[1], pieces[0], pieces[1]], matrices[0])
    beside[2] = differences(
        [pieces[blocks - 2], pieces[blocks - 1], halo_pieces[2]], matrices[blocks - 1]
    )
    beside[3] = differences([pieces[blocks - 1], halo_pieces[2], halo_pieces[3]], halo_matrices[1])

    received = table[...]
    lane_of = lane_iota(peers)
    for which in range(3):
        values = []
        for part in range(2):
            lane = (2 * which + part) * capacity + lane_of % capacity
            found = lane_gather(received, lane)
            row = []
            for half in range(halves):
                mine = row_iota(peers) == (lane_of + half * LANES) // capacity
                row.append(jnp.sum(jnp.where(mine, found, 0.0), axis=0, keepdims=True))
            values.append(jnp.concatenate(row, axis=1))
        parts = three_parts(jnp.concatenate(values, axis=0))
        start = (0, 1, blocks + 1)[which]
        count = blocks if which == 1 else 1
        total = jnp.dot(
            parts,
            sums[:, start * LANES : (start + count) * LANES],
            preferred_element_type=jnp.float32,
        )
        total = total[0:2] + (total[2:4] + total[4:6])
        for b in range(count):
            stokes[start + b, 0:2, :] = total[:, b * LANES : (b + 1) * LANES]

    decay = [
        jnp.exp(-3.0 / layers * (row_iota(8) + 8 * g).astype(jnp.float32))
        for g in range(layer_groups)
    ]

    def low_order(b, value, change, w, wx, wy, keep):
        slope = wx * stokes[b, 0:1, :] + wy * stokes[b, 1:2, :]
        own = [value(8 * g) for g in range(tracer_groups)]
        zero = jnp.zeros((8, LANES), jnp.float32)
        speed_sum = [zero] * layer_groups
        inflow = [zero] * tracer_groups
        highest = [zero] * tracer_groups
        lowest = [zero] * tracer_groups
        positive = [zero] * tracer_groups
        negative = [zero] * tracer_groups
        for s in range(edges):
            w8 = spread(w[s : s + 1, :], 8)
            slope8 = spread(slope[s : s + 1, :], 8)
            for lg in range(layer_groups):
                speed = w8 * change(8 * (tracer_groups + lg), s) + decay[lg] * slope8
                down = jnp.minimum(speed, 0.0)
                half = 0.5 * speed - down
                speed_sum[lg] = speed_sum[lg] + speed
                for t in range(tracer_count):
                    g = t * layer_groups + lg
                    step = change(8 * g, s)
                    flux = half * step
                    if keep:
                        antiflux[b - 1, s, 8 * g : 8 * g + 8, :] = flux
                    inflow[g] = inflow[g] + down * step
                    highest[g] = jnp.maximum(highest[g], step)
                    lowest[g] = jnp.minimum(lowest[g], step)
                    positive[g] = positive[g] + jnp.maximum(flux, 0.0)
                    negative[g] = negative[g] - jnp.minimum(flux, 0.0)
        plus, minus = [], []
        for g in range(tracer_groups):
            loss = speed_sum[g % layer_groups] * own[g] + inflow[g]
            if keep:
                lowered[b - 1, 8 * g : 8 * g + 8, :] = own[g] - loss
            up = jnp.maximum(highest[g] + loss, 0.0) / (negative[g] + FCT_FLOOR)
            down = jnp.maximum(-loss - lowest[g], 0.0) / (positive[g] + FCT_FLOOR)
            plus.append(jnp.minimum(1.0, up))
            minus.append(jnp.minimum(1.0, down))
        both = jnp.concatenate(plus + minus, axis=0)
        ratios[b] = both
        ratio_pieces[b] = stack_split(both)

    def band(ref, *index):
        return lambda row: ref[(*index, slice(row, row + 8), slice(None))]

    def column(ref, index):
        return lambda row, s: ref[index, row : row + 8, s * LANES : (s + 1) * LANES]

    def own_tables(i):
        return scale[i], cosine[i], sine[i]

    for i in range(blocks - 2):
        low_order(i + 2, band(fields, i + 1), column(inside, i), *own_tables(i + 1), True)
    for side in range(2):
        b = side * (blocks + 1)
        tables = tuple(halo_tables[side, k] for k in range(3))
        near = 1 + side
        low_order(b, band(halo, near), column(beside, 3 * side), *tables, False)
        i = side * (blocks - 1)
        low_order(i + 1, band(fields, i), column(beside, 1 + side), *own_tables(i), True)

    def products(i, steps):
        mixed = jnp.concatenate([ratio_pieces[i], ratio_pieces[i + 1], ratio_pieces[i + 2]], axis=1)
        steps[...] = jnp.dot(mixed, matrices[i], preferred_element_type=jnp.float32)

    def limit(i, steps):
        out = [lowered[i, 8 * g : 8 * g + 8, :] for g in range(tracer_groups)]
        own = [ratios[i + 1, 8 * g : 8 * g + 8, :] for g in range(2 * tracer_groups)]
        low = 16 * tracer_groups
        for s in range(edges):
            lanes = slice(s * LANES, (s + 1) * LANES)
            beside = [
                own[g]
                + (steps[8 * g : 8 * g + 8, lanes] + steps[low + 8 * g : low + 8 * g + 8, lanes])
                for g in range(2 * tracer_groups)
            ]
            for g in range(tracer_groups):
                m = g + tracer_groups
                flux = antiflux[i, s, 8 * g : 8 * g + 8, :]
                factor = jnp.where(
                    flux >= 0.0, jnp.minimum(own[m], beside[g]), jnp.minimum(own[g], beside[m])
                )
                out[g] = out[g] - factor * flux
        lanes = slice(i * LANES, (i + 1) * LANES)
        for g in range(tracer_groups):
            t, lg = g // layer_groups, g % layer_groups
            tracers_new[t, 8 * lg : 8 * lg + 8, lanes] = out[g]

    buffers = (steps_a, steps_b)
    products(0, steps_a)
    for i in range(blocks):
        if i + 1 < blocks:
            products(i + 1, buffers[(i + 1) % 2])
        limit(i, buffers[i % 2])
    write.wait()


def swap(message, first, peers):
    pairs = []
    for i in range(first, peers - 1, 2):
        pairs += [(i, i + 1), (i + 1, i)]
    return lax.ppermute(message, "mesh", pairs)


def whole_spec():
    return pl.BlockSpec(memory_space=pltpu.VMEM)


def local(
    tracers,
    potential,
    surface_current,
    cell_neighbors,
    cell_normal,
    cell_weight,
    spectra,
    wind_velocity,
    node_neighbors,
    node_normal,
    node_weight,
    send_rows,
    node_slot,
):
    peers, _, capacity = send_rows.shape
    freqs, dirs, nodes = spectra.shape
    tracer_count, layers, cells = tracers.shape
    edges = cell_neighbors.shape[0]
    blocks = cells // LANES
    field_rows = (tracer_count + 1) * layers
    head_rows = 2 * field_rows + TABLE_ROWS
    message_rows = head_rows + (freqs // 2 * dirs + 7) // 8 * 8
    slots = node_slot.reshape(1, nodes)
    params = pltpu.CompilerParams(vmem_limit_bytes=VMEM_LIMIT)
    f32 = jnp.float32

    stored = pl.BlockSpec(memory_space=pltpu.HBM)
    rows = tracer_count * layers
    stride = (dirs + 7) // 8 * 8
    step_pairs = 5 if freqs % 10 == 0 else 1
    step_rows = 2 * step_pairs * stride

    def like(x):
        return jax.ShapeDtypeStruct(x.shape, x.dtype)

    def shaped(*shape, dtype=f32):
        return jax.ShapeDtypeStruct(shape, dtype)

    def call(kernel, name, inputs, outputs, scratch, in_specs=None, out_specs=None):
        return pl.pallas_call(
            kernel,
            out_shape=outputs,
            in_specs=in_specs or [whole_spec()] * len(inputs),
            out_specs=out_specs or (whole_spec(),) * len(outputs),
            scratch_shapes=scratch,
            compiler_params=params,
            name=name,
        )(*inputs)

    inputs = (
        spectra, tracers, potential, cell_neighbors, cell_normal, cell_weight, slots,
    )
    (
        outer, inner, own_spectra, own_tracers, own_potential, neighbors, normal, weight, own_slots,
    ) = pl.pallas_call(
        pack_kernel,
        out_shape=(
            shaped(message_rows, LANES),
            shaped(message_rows, LANES),
            shaped(freqs, stride, LANES),
            *(like(x) for x in inputs[1:]),
        ),
        in_specs=[stored] * len(inputs),
        out_specs=(whole_spec(),) * 9,
        scratch_shapes=[pltpu.SemaphoreType.DMA((7,))],
        compiler_params=params,
        name="pack",
    )(*(pltpu.with_memory_space_constraint(x, pltpu.HBM) for x in inputs))
    outer = swap(outer, 1, peers)
    inner = swap(inner, 0, peers)

    (
        near, currents, cosine, sine, project, choice, ways, slot_choice, own_change,
        fields, pieces, matrices, inside, cell_cosine, cell_sine, cell_scale, sums,
    ) = call(
        functools.partial(prepare_kernel, dirs, step_rows),
        "prepare",
        (
            own_spectra, own_slots, own_tracers, own_potential, neighbors, normal, weight,
            *(
                pltpu.with_memory_space_constraint(x, pltpu.HBM)
                for x in (
                    node_neighbors, node_normal, node_weight, wind_velocity, send_rows,
                    surface_current,
                )
            ),
        ),
        (
            like(node_neighbors),
            shaped(peers, LANES),
            like(node_normal),
            like(node_normal),
            shaped(edges, stride, LANES),
            shaped(4 * LANES, edges * LANES, dtype=jnp.bfloat16),
            shaped(3, stride, LANES),
            shaped(nodes, peers * capacity, dtype=jnp.bfloat16),
            shaped(freqs * stride, edges * LANES),
            shaped(blocks, field_rows, LANES),
            shaped(blocks, 2 * field_rows, LANES, dtype=jnp.bfloat16),
            shaped(blocks, 3 * LANES, edges * LANES, dtype=jnp.bfloat16),
            shaped(blocks - 2, field_rows, edges * LANES),
            shaped(blocks, 8, LANES),
            shaped(blocks, 8, LANES),
            shaped(blocks, 8, LANES),
            shaped(peers * capacity, (blocks + 2) * LANES, dtype=jnp.bfloat16),
        ),
        [
            pltpu.VMEM(node_normal.shape, f32),
            pltpu.VMEM(node_weight.shape, f32),
            pltpu.VMEM(wind_velocity.shape, f32),
            pltpu.VMEM((3, peers, capacity), jnp.int32),
            pltpu.VMEM(surface_current.shape, f32),
            pltpu.SemaphoreType.DMA((8,)),
        ],
        in_specs=[whole_spec()] * 7 + [stored] * 6,
    )
    currents = lax.all_to_all(currents, "mesh", 0, 0, tiled=True)

    spectra_new, stokes_rows = call(
        functools.partial(wave_kernel, capacity, step_pairs, dirs),
        "wave",
        (
            own_spectra, outer, inner, currents, own_slots, near,
            cosine, sine, project, choice, ways, slot_choice, own_change,
        ),
        (shaped(freqs, stride, LANES), shaped(peers, LANES)),
        [
            pltpu.VMEM((8, LANES), f32),
            pltpu.VMEM((step_rows, LANES), f32),
            pltpu.VMEM((step_rows, edges * LANES), f32),
            pltpu.VMEM((step_rows, edges * LANES), f32),
        ],
    )
    stokes_all = lax.all_to_all(stokes_rows, "mesh", 0, 0, tiled=True)

    return call(
        functools.partial(tracer_kernel, capacity, (tracer_count, layers, edges)),
        "tracer",
        (
            outer, inner, stokes_all, fields, pieces, matrices, inside, cell_cosine, cell_sine,
            cell_scale, sums, pltpu.with_memory_space_constraint(spectra_new, pltpu.VMEM),
        ),
        (like(tracers), like(spectra)),
        [
            pltpu.VMEM((4, field_rows, LANES), f32),
            pltpu.VMEM((4, 2 * field_rows, LANES), jnp.bfloat16),
            pltpu.VMEM((2, 3 * LANES, edges * LANES), jnp.bfloat16),
            pltpu.VMEM((2, 3, 8, LANES), f32),
            pltpu.VMEM((4, field_rows, edges * LANES), f32),
            pltpu.VMEM((blocks + 2, 8, LANES), f32),
            pltpu.VMEM((blocks, edges, rows, LANES), f32),
            pltpu.VMEM((blocks, rows, LANES), f32),
            pltpu.VMEM((blocks + 2, 2 * rows, LANES), f32),
            pltpu.VMEM((blocks + 2, 4 * rows, LANES), jnp.bfloat16),
            pltpu.VMEM((4 * rows, edges * LANES), f32),
            pltpu.VMEM((4 * rows, edges * LANES), f32),
            pltpu.SemaphoreType.DMA(()),
        ],
        out_specs=(whole_spec(), stored),
    )


def solution(mesh):
    return jax.shard_map(
        local,
        mesh=mesh,
        in_specs=(
            P(None, None, ("groups", "mesh")),
            P(None, ("groups", "mesh")),
            P(None, ("groups", "mesh")),
            P(None, "mesh"),
            P(None, "mesh"),
            P(None, "mesh"),
            P(None, None, ("groups", "mesh")),
            P(None, ("groups", "mesh")),
            P(None, "mesh"),
            P(None, "mesh"),
            P(None, "mesh"),
            P(),
            P("mesh"),
        ),
        out_specs=(P(None, None, ("groups", "mesh")), P(None, None, ("groups", "mesh"))),
        check_vma=False,
    )
```

```python
import functools
import math

import jax
import jax.numpy as jnp
from jax import lax
from jax.experimental import pallas as pl
from jax.experimental.pallas import tpu as pltpu
from jax.sharding import PartitionSpec as P

LANES = 128
FCT_FLOOR = 0.001
TABLE_ROWS = 24
VMEM_LIMIT = 32 * 1024 * 1024


def lane_gather(values, index):
    return jnp.take_along_axis(values, index, axis=1, mode="promise_in_bounds")


def spread(row, count):
    return jnp.broadcast_to(row, (count, LANES))


def lane_iota(rows):
    return lax.broadcasted_iota(jnp.int32, (rows, LANES), 1)


def row_iota(rows):
    return lax.broadcasted_iota(jnp.int32, (rows, LANES), 0)


def slot_rows(entry):
    peers, capacity = entry.shape
    wide = jnp.concatenate([entry, jnp.zeros((peers, LANES - capacity), jnp.int32)], axis=1)
    wide = lane_gather(wide, lane_iota(peers) % capacity)
    owner = row_iota(peers)
    out = []
    for half in range(peers * capacity // LANES):
        wanted = (lane_iota(peers) + half * LANES) // capacity
        picked = jnp.where(owner == wanted, wide, 0).astype(jnp.float32)
        out.append(jnp.sum(picked, axis=0, keepdims=True).astype(jnp.int32))
    return out


def half_mask(rows, lower):
    half = lane_iota(rows) // (LANES // 2)
    return half == jnp.where(lower, 0, 1)


def peer_rows(values, peers, capacity):
    lane = lane_iota(peers)
    group = lane // capacity
    block = jnp.clip(row_iota(peers) - 1 + group // 2, 0, peers - 1)
    entry = block * capacity + lane % capacity
    out = jnp.zeros((peers, LANES), jnp.float32)
    for part in range(2):
        for half, row in enumerate(values[part]):
            found = lane_gather(spread(row, peers), entry % LANES)
            wanted = (group < 6) & (group % 2 == part) & (entry // LANES == half)
            out = jnp.where(wanted, found, out)
    return out


def direction(dirs, padded):
    turn = row_iota(padded).astype(jnp.float32) * (2.0 * math.pi / dirs)
    return jnp.cos(turn), jnp.sin(turn)


def node_tables(
    me, dirs, near, angle, face, wind, slot, cosine, sine, project, choice, ways, slots
):
    edges, padded = project.shape[:2]
    cosine[...] = face[...] * jnp.cos(angle[...])
    sine[...] = face[...] * jnp.sin(angle[...])
    cos_dir, sin_dir = direction(dirs, padded)
    ways[0] = cos_dir
    ways[1] = sin_dir
    ways[2] = 0.25 * jnp.maximum(wind[0:1, :] * cos_dir + wind[1:2, :] * sin_dir, 0.0)
    taken = jnp.transpose(spread(slot[...].astype(jnp.float32), LANES))
    for half in range(slots.shape[1] // LANES):
        number = (lane_iota(LANES) + half * LANES).astype(jnp.float32)
        picked = jnp.where(taken == number, 1.0, 0.0).astype(jnp.bfloat16)
        slots[:, half * LANES : (half + 1) * LANES] = picked
    source = row_iota(LANES)
    minus = jnp.where(source == lane_iota(LANES), -1.0, 0.0)
    for s in range(edges):
        project[s] = cos_dir * cosine[s : s + 1, :] + sin_dir * sine[s : s + 1, :]
        target = near[s : s + 1, :]
        inside = target // LANES == me
        lane = target % LANES
        own = jnp.where(source == jnp.where(inside, lane, LANES), 1.0, 0.0) + minus
        halo = jnp.where(source == jnp.where(inside, LANES, lane), 1.0, 0.0)
        lanes = slice(s * LANES, (s + 1) * LANES)
        for k, part in enumerate((own, own, halo, halo)):
            choice[k * LANES : (k + 1) * LANES, lanes] = part.astype(jnp.bfloat16)


def split(x):
    first = x.astype(jnp.bfloat16)
    return first, (x - first.astype(jnp.float32)).astype(jnp.bfloat16)


def pack_kernel(
    spectra_in, tracers_in, potential_in, neighbors_in, normal_in, weight_in, current_in,
    send_rows, slot_in, near_in, angle_in, face_in, wind_in,
    rows_out, outer, inner, spectra, node_slot, near, angle, face, wind,
    tracers, potential, neighbors, normal, weight, coupled,
    current, sems,
):
    peers, _, capacity = send_rows.shape
    me = lax.axis_index("mesh")
    freqs, dirs = spectra_in.shape[:2]
    if dirs < spectra.shape[1]:
        for f in range(freqs):
            spectra[f, dirs // 8 * 8 :, :] = jnp.zeros((8, LANES), jnp.float32)
    pairs = freqs // 2
    copies = []
    for source, target in (
        (send_rows.at[me], coupled.at[1]),
        (current_in, current),
        (slot_in, node_slot),
        (spectra_in, spectra.at[:, 0:dirs, :]),
        (tracers_in, tracers),
        (potential_in, potential),
        (neighbors_in, neighbors),
        (normal_in, normal),
        (weight_in, weight),
        (send_rows.at[jnp.maximum(me - 1, 0)], coupled.at[0]),
        (send_rows.at[jnp.minimum(me + 1, peers - 1)], coupled.at[2]),
        (near_in, near),
        (angle_in, angle),
        (face_in, face),
        (wind_in, wind),
    ):
        copy = pltpu.make_async_copy(source, target, sems.at[len(copies)])
        copy.start()
        copies.append(copy)
    for copy in copies[:3]:
        copy.wait()
    layers, cells = potential.shape
    blocks = cells // LANES
    field_rows = (tracers.shape[0] + 1) * layers
    stacked = jnp.concatenate(
        [current[:, b * LANES : (b + 1) * LANES] for b in range(blocks)], axis=0
    )
    place = row_iota(2 * blocks)
    halves = slot_rows(coupled[1])
    values = [[], []]
    for cell in halves:
        found = lane_gather(stacked, spread(cell % LANES, 2 * blocks))
        for part in range(2):
            picked = jnp.where(place == 2 * (cell // LANES) + part, found, 0.0)
            values[part].append(jnp.sum(picked, axis=0, keepdims=True))
    rows_out[...] = peer_rows(values, peers, capacity)
    for copy in copies[4:9]:
        copy.wait()
    odd = me % 2 == 1
    for out, upward in ((outer, odd), (inner, jnp.logical_not(odd))):
        for b in range(2):
            high = slice((blocks - 2 + b) * LANES, (blocks - 1 + b) * LANES)
            low = slice(b * LANES, (b + 1) * LANES)
            base = b * field_rows
            for t in range(tracers.shape[0]):
                out[base + t * layers : base + (t + 1) * layers, :] = jnp.where(
                    upward, tracers[t, :, high], tracers[t, :, low]
                )
            out[base + field_rows - layers : base + field_rows, :] = jnp.where(
                upward, potential[:, high], potential[:, low]
            )
        high = slice((blocks - 1) * LANES, blocks * LANES)
        low = slice(0, LANES)
        base = 2 * field_rows
        out[base : base + TABLE_ROWS, :] = jnp.zeros((TABLE_ROWS, LANES), jnp.float32)
        edges = neighbors.shape[0]
        near = jnp.where(upward, neighbors[:, high], neighbors[:, low])
        out[base : base + edges, :] = near.astype(jnp.float32)
        out[base + edges : base + edges + 1, :] = node_slot[...].astype(jnp.float32)
        out[base + 8 : base + 8 + edges, :] = jnp.where(upward, normal[:, high], normal[:, low])
        out[base + 16 : base + 16 + edges, :] = jnp.where(upward, weight[:, high], weight[:, low])
    base = 2 * field_rows + TABLE_ROWS
    whole = dirs // 8 * 8
    rest = dirs - whole
    turns = half_mask(dirs, odd)
    copies[3].wait()
    for g in range(pairs):
        natural = spectra[g, 0:dirs, :]
        turned = pltpu.roll(spectra[g + pairs, 0:dirs, :], LANES // 2, 1)
        for out, mixed in (
            (outer, jnp.where(turns, turned, natural)),
            (inner, jnp.where(turns, natural, turned)),
        ):
            at = base + g * whole
            out[at : at + whole, :] = mixed[:whole]
            at = base + pairs * whole + g * rest
            out[at : at + rest, :] = mixed[whole:]
    at = base + pairs * dirs
    if at < outer.shape[0]:
        for out in (outer, inner):
            out[at:, :] = jnp.zeros((outer.shape[0] - at, LANES), jnp.float32)
    for copy in copies[9:]:
        copy.wait()


def choose(cells, first, lanes, matrix):
    place = (cells - first - LANES).astype(jnp.float32).astype(jnp.bfloat16)
    place = spread(place, LANES)
    one = jnp.ones((LANES, LANES), jnp.bfloat16)
    for k in range(3):
        source = (row_iota(LANES) + (k - 1) * LANES).astype(jnp.float32).astype(jnp.bfloat16)
        part = jnp.where(source == place, one, 0 * one)
        if k == 1:
            own = jnp.where(row_iota(LANES) == lane_iota(LANES), 1.0, 0.0).astype(jnp.bfloat16)
            part = part - own
        matrix[k * LANES : (k + 1) * LANES, lanes] = part


def stack_split(x):
    first, second = split(x)
    return jnp.concatenate([first, second], axis=0)


def differences(parts, matrix):
    mixed = jnp.concatenate(parts, axis=1)
    out = jnp.dot(mixed, matrix, preferred_element_type=jnp.float32)
    rows = out.shape[0] // 2
    return out[:rows] + out[rows:]


def prepare_kernel(
    dirs, step_rows,
    spectra, near, angle, face, wind, slot, tracers, potential, neighbors, normal, weight, coupled,
    cosine, sine, project, choice, ways, slots, own_change,
    fields, matrices, inside, cell_cosine, cell_sine, cell_scale, sums,
    pieces,
):
    me = lax.axis_index("mesh")
    node_tables(
        me, dirs, near, angle, face, wind, slot, cosine, sine, project, choice, ways, slots
    )
    freqs, padded, _ = spectra.shape
    step = step_rows // padded

    def own_part(c, carry):
        own = spectra[pl.ds(c * step, step)].reshape(step_rows, LANES)
        own_change[pl.ds(pl.multiple_of(c * step_rows, 8), step_rows), :] = jnp.dot(
            jnp.concatenate(split(own), axis=1),
            choice[0 : 2 * LANES, :],
            preferred_element_type=jnp.float32,
        )
        return carry

    lax.fori_loop(0, freqs // step, own_part, 0)
    tracer_count, layers, cells = tracers.shape
    blocks = cells // LANES
    edges = neighbors.shape[0]
    field_rows = (tracer_count + 1) * layers
    for b in range(blocks):
        lanes = slice(b * LANES, (b + 1) * LANES)
        for t in range(tracer_count):
            fields[b, t * layers : (t + 1) * layers, :] = tracers[t, :, lanes]
        fields[b, field_rows - layers : field_rows, :] = potential[:, lanes]
        pieces[b] = stack_split(fields[b])
        w = weight[:, lanes]
        cell_scale[b, 0:edges, :] = w
        cell_cosine[b, 0:edges, :] = w * jnp.cos(normal[:, lanes])
        cell_sine[b, 0:edges, :] = w * jnp.sin(normal[:, lanes])
        for s in range(edges):
            choose(
                neighbors[s : s + 1, lanes],
                (me * blocks + b - 1) * LANES,
                slice(s * LANES, (s + 1) * LANES),
                matrices.at[b],
            )
    for b in range(blocks):
        first, last = max(b - 1, 0), min(b + 1, blocks - 1)
        rows = slice((first - b + 1) * LANES, (last - b + 2) * LANES)
        parts = [pieces[k] for k in range(first, last + 1)]
        inside[b] = differences(parts, matrices[b, rows, :])
    for which in range(3):
        first = 0 if which != 0 else cells - LANES
        count = blocks if which == 1 else 1
        start = (0, 1, blocks + 1)[which]
        for half, names in enumerate(slot_rows(coupled[which])):
            named = jnp.transpose(spread(names, LANES).astype(jnp.float32))
            for b in range(count):
                cell = (lane_iota(LANES) + (first + b * LANES)).astype(jnp.float32)
                picked = jnp.where(named == cell, 1.0, 0.0).astype(jnp.bfloat16)
                lanes = slice((start + b) * LANES, (start + b + 1) * LANES)
                sums[half * LANES : (half + 1) * LANES, lanes] = picked


def node_currents(table, slot, which, capacity):
    peers = table.shape[0]
    owner = row_iota(peers) == slot // capacity
    out = []
    for part in range(2):
        lane = (2 * which + part) * capacity + slot % capacity
        found = jnp.where(owner, lane_gather(table, spread(lane, peers)), 0.0)
        out.append(jnp.sum(found, axis=0, keepdims=True))
    return out


def wave_kernel(
    capacity, step_pairs, dirs,
    spectra, outer, inner, table, node_slot, neighbors, cosine, sine, project, choice, ways, slots,
    own_change,
    spectra_new, rows_out, drift, halos, change_a, change_b,
):
    me = lax.axis_index("mesh")
    freqs, stride = spectra.shape[:2]
    edges = neighbors.shape[0]
    peers = table.shape[0]
    halves = peers * capacity // LANES
    pairs = freqs // 2
    whole = dirs // 8 * 8
    rest = dirs - whole
    base = outer.shape[0] - (pairs * dirs + 7) // 8 * 8

    odd = me % 2 == 1
    slot = node_slot[...]
    row = base - TABLE_ROWS + edges
    halo_slot = jnp.where(
        half_mask(1, odd), outer[row : row + 1, :], inner[row : row + 1, :]
    ).astype(jnp.int32)
    lower = lane_iota(1) < LANES // 2
    currents = table[...]
    own_x, own_y = node_currents(currents, slot, jnp.ones((1, LANES), jnp.int32), capacity)
    halo_x, halo_y = node_currents(currents, halo_slot, jnp.where(lower, 2, 0), capacity)

    target = neighbors[...]
    lane = target % LANES
    inside = target // LANES == me

    def beside(own, halo):
        a = lane_gather(spread(own, edges), lane)
        b = lane_gather(spread(halo, edges), lane)
        return jnp.where(inside, a, b)

    drift[0:edges, :] = (
        0.5 * (own_x + beside(own_x, halo_x)) * cosine[...]
        + 0.5 * (own_y + beside(own_y, halo_y)) * sine[...]
    )
    drifts = [spread(drift[s : s + 1, :], 8) for s in range(edges)]
    from_outer = half_mask(dirs, odd)
    halos[...] = jnp.zeros(halos.shape, jnp.float32)
    ratio = 1.0 / 1.1
    bands = [slice(r, r + 8) for r in range(0, stride, 8)]

    def gather(c, change):
        for i in range(step_pairs):
            g = c * step_pairs + i
            parts = []
            for message in (outer, inner):
                at = pl.multiple_of(base + g * whole, 8)
                upper = message[pl.ds(at, whole), :]
                left = message[pl.ds(base + pairs * whole + g * rest, rest), :]
                parts.append(jnp.concatenate([upper, left], axis=0))
            x, y = parts
            at = 2 * i * stride
            halos[at : at + dirs, :] = jnp.where(from_outer, x, y)
            at += stride
            halos[at : at + dirs, :] = pltpu.roll(jnp.where(from_outer, y, x), LANES // 2, 1)
        mixed = jnp.concatenate(split(halos[...]), axis=1)
        change[...] = jnp.dot(
            mixed, choice[2 * LANES : 4 * LANES, :], preferred_element_type=jnp.float32
        )

    def advect(c, change, first_speed, first_slow, total):
        total = list(total)
        speeds = []
        for i in range(step_pairs):
            speeds += [first_speed * ratio**i, first_speed * ratio ** (i + pairs)]
        slowness = []
        for i in range(step_pairs):
            slowness += [first_slow * ratio**-i, first_slow * ratio ** -(i + pairs)]
        relative = [[drift * slow for drift in drifts] for slow in slowness]
        relative_sum = [sum(each[1:], each[0]) for each in relative]
        for k, band in enumerate(bands):
            along = [project[s, band, :] for s in range(edges)]
            along_sum = sum(along[1:], along[0])
            for i in range(step_pairs):
                g = c * step_pairs + i
                for j, f in ((2 * i, g), (2 * i + 1, g + pairs)):
                    own = spectra[f, band, :]
                    at = j * stride + band.start
                    own_at = pl.ds(pl.multiple_of(f * stride + band.start, 8), 8)
                    flux = (along_sum + relative_sum[j]) * own
                    for s in range(edges):
                        down = jnp.minimum(along[s] + relative[j][s], 0.0)
                        lanes = slice(s * LANES, (s + 1) * LANES)
                        step = change[at : at + 8, lanes] + own_change[own_at, lanes]
                        flux = flux + down * step
                    value = own - speeds[j] * flux
                    spectra_new[f, band, :] = value
                    total[k] = total[k] + value
        return first_speed * ratio**step_pairs, first_slow * ratio**-step_pairs, tuple(total)

    zeros = tuple(jnp.zeros((8, LANES), jnp.float32) for _ in bands)
    chunks = pairs // step_pairs
    gather(0, change_a)

    def two_chunks(h, carry):
        gather(2 * h + 1, change_b)
        carry = advect(2 * h, change_a, *carry)
        gather(2 * h + 2, change_a)
        return advect(2 * h + 1, change_b, *carry)

    carry = (jnp.float32(1.0), jnp.float32(1.0), zeros)
    carry = lax.fori_loop(0, (chunks - 1) // 2, two_chunks, carry)
    if chunks % 2 == 0:
        gather(chunks - 1, change_b)
        carry = advect(chunks - 2, change_a, *carry)
        carry = advect(chunks - 1, change_b, *carry)
    else:
        carry = advect(chunks - 1, change_a, *carry)
    total = carry[2]
    total = jnp.concatenate(total, axis=0)
    zero = jnp.zeros((stride, LANES), jnp.float32)
    cos_dir, sin_dir = ways[0], ways[1]
    mean = jnp.sum(total, axis=0, keepdims=True) * (1.0 / (freqs * dirs))
    step = jnp.exp((ways[2] - 2.0 * mean) * (1.0 / freqs))
    run = 10 if freqs % 10 == 0 else 1

    def grow(c, carry):
        factor, weighted = carry
        for i in range(run):
            f = c * run + i
            factor = factor * step
            evolved = spectra_new[f] * factor
            spectra_new[f] = evolved
            kappa = (f + 1).astype(jnp.float32) * (1.0 / freqs)
            weighted = weighted + kappa * evolved
        return factor, weighted

    _, weighted = lax.fori_loop(0, freqs // run, grow, (zero + 1.0, zero))
    stokes = jnp.concatenate(
        [
            jnp.sum(weighted * cos_dir, axis=0, keepdims=True),
            jnp.sum(weighted * sin_dir, axis=0, keepdims=True),
        ],
        axis=0,
    ) * (1.0 / dirs)
    in_order = jnp.dot(
        three_parts(stokes), slots[...], preferred_element_type=jnp.float32
    )
    in_order = in_order[0:2] + (in_order[2:4] + in_order[4:6])
    values = [
        [in_order[part : part + 1, h * LANES : (h + 1) * LANES] for h in range(halves)]
        for part in range(2)
    ]
    rows_out[...] = peer_rows(values, peers, capacity)


def three_parts(values):
    first = values.astype(jnp.bfloat16).astype(jnp.float32)
    left = values - first
    second = left.astype(jnp.bfloat16).astype(jnp.float32)
    third = left - second
    pad = jnp.zeros((10, values.shape[1]), jnp.float32)
    return jnp.concatenate([first, second, third, pad], axis=0).astype(jnp.bfloat16)


def tracer_kernel(
    capacity, shape,
    outer, inner, table, fields, neighbors, matrices, inside, cosine, sine, scale, sums, spectra,
    tracers_new, spectra_out,
    halo, halo_near, halo_tables, stokes, antiflux, lowered, ratios,
    ratio_pieces, steps_a, steps_b, sem,
):
    dirs = spectra_out.shape[1]
    write = pltpu.make_async_copy(spectra.at[:, 0:dirs, :], spectra_out, sem)
    write.start()
    me = lax.axis_index("mesh")
    tracer_count, layers, edges = shape
    peers = table.shape[0]
    halves = peers * capacity // LANES
    blocks, field_rows, _ = fields.shape
    layer_groups = layers // 8
    tracer_groups = tracer_count * layer_groups
    odd = me % 2 == 1

    for b in range(2):
        x = outer[b * field_rows : (b + 1) * field_rows, :]
        y = inner[b * field_rows : (b + 1) * field_rows, :]
        for side, value in ((0, jnp.where(odd, y, x)), (1, jnp.where(odd, x, y))):
            halo[2 * side + b] = value
    at = 2 * field_rows
    x = outer[at : at + TABLE_ROWS, :]
    y = inner[at : at + TABLE_ROWS, :]
    for side, rows in ((0, jnp.where(odd, y, x)), (1, jnp.where(odd, x, y))):
        w = rows[16 : 16 + edges]
        halo_tables[side, 0, 0:edges, :] = w
        halo_tables[side, 1, 0:edges, :] = w * jnp.cos(rows[8 : 8 + edges])
        halo_tables[side, 2, 0:edges, :] = w * jnp.sin(rows[8 : 8 + edges])
        halo_near[side, 0:edges, :] = rows[0:edges].astype(jnp.int32)

    received = table[...]
    lane_of = lane_iota(peers)
    for which in range(3):
        values = []
        for part in range(2):
            lane = (2 * which + part) * capacity + lane_of % capacity
            found = lane_gather(received, lane)
            row = []
            for half in range(halves):
                mine = row_iota(peers) == (lane_of + half * LANES) // capacity
                row.append(jnp.sum(jnp.where(mine, found, 0.0), axis=0, keepdims=True))
            values.append(jnp.concatenate(row, axis=1))
        parts = three_parts(jnp.concatenate(values, axis=0))
        start = (0, 1, blocks + 1)[which]
        count = blocks if which == 1 else 1
        total = jnp.dot(
            parts,
            sums[:, start * LANES : (start + count) * LANES],
            preferred_element_type=jnp.float32,
        )
        total = total[0:2] + (total[2:4] + total[4:6])
        for b in range(count):
            stokes[start + b, 0:2, :] = total[:, b * LANES : (b + 1) * LANES]

    decay = [
        jnp.exp(-3.0 / layers * (row_iota(8) + 8 * g).astype(jnp.float32))
        for g in range(layer_groups)
    ]

    def low_order(b, value, change, w, wx, wy, keep):
        slope = wx * stokes[b, 0:1, :] + wy * stokes[b, 1:2, :]
        own = [value(8 * g) for g in range(tracer_groups)]
        zero = jnp.zeros((8, LANES), jnp.float32)
        speed_sum = [zero] * layer_groups
        inflow = [zero] * tracer_groups
        highest = [zero] * tracer_groups
        lowest = [zero] * tracer_groups
        positive = [zero] * tracer_groups
        negative = [zero] * tracer_groups
        for s in range(edges):
            w8 = spread(w[s : s + 1, :], 8)
            slope8 = spread(slope[s : s + 1, :], 8)
            for lg in range(layer_groups):
                speed = w8 * change(8 * (tracer_groups + lg), s) + decay[lg] * slope8
                down = jnp.minimum(speed, 0.0)
                half = 0.5 * speed - down
                speed_sum[lg] = speed_sum[lg] + speed
                for t in range(tracer_count):
                    g = t * layer_groups + lg
                    step = change(8 * g, s)
                    flux = half * step
                    if keep:
                        antiflux[b - 1, s, 8 * g : 8 * g + 8, :] = flux
                    inflow[g] = inflow[g] + down * step
                    highest[g] = jnp.maximum(highest[g], step)
                    lowest[g] = jnp.minimum(lowest[g], step)
                    positive[g] = positive[g] + jnp.maximum(flux, 0.0)
                    negative[g] = negative[g] - jnp.minimum(flux, 0.0)
        plus, minus = [], []
        for g in range(tracer_groups):
            loss = speed_sum[g % layer_groups] * own[g] + inflow[g]
            if keep:
                lowered[b - 1, 8 * g : 8 * g + 8, :] = own[g] - loss
            up = jnp.maximum(highest[g] + loss, 0.0) / (negative[g] + FCT_FLOOR)
            down = jnp.maximum(-loss - lowest[g], 0.0) / (positive[g] + FCT_FLOOR)
            plus.append(jnp.minimum(1.0, up))
            minus.append(jnp.minimum(1.0, down))
        both = jnp.concatenate(plus + minus, axis=0)
        ratios[b] = both
        ratio_pieces[b] = stack_split(both)

    def band(ref, *index):
        return lambda row: ref[(*index, slice(row, row + 8), slice(None))]

    def own_tables(i):
        return scale[i], cosine[i], sine[i]

    def within(i):
        return lambda row, s: inside[i, row : row + 8, s * LANES : (s + 1) * LANES]

    def edge(i, side):
        beside = halo.at[1 + side]
        sign = 2 * side - 1

        def change(row, s):
            near = spread(neighbors[s : s + 1, i * LANES : (i + 1) * LANES], 8)
            from_halo = near // LANES - (me * blocks + i) == sign
            picked = lane_gather(beside[row : row + 8, :], near % LANES)
            return within(i)(row, s) + jnp.where(from_halo, picked, 0.0)

        return change

    def outside(side):
        i = side * (blocks - 1)
        low, own, high = (
            (halo.at[0], halo.at[1], fields.at[i]),
            (fields.at[i], halo.at[2], halo.at[3]),
        )[side]

        def change(row, s):
            rows = slice(row, row + 8)
            near = spread(halo_near[side, s : s + 1, :], 8)
            place = near // LANES - (me * blocks + i + 2 * side - 1)
            lane = near % LANES
            mine = own[rows, :]
            middle = lane_gather(mine, lane)
            left = lane_gather(low[rows, :], lane)
            right = lane_gather(high[rows, :], lane)
            return jnp.where(place == 0, middle, jnp.where(place < 0, left, right)) - mine

        return change

    for i in range(1, blocks - 1):
        low_order(i + 1, band(fields, i), within(i), *own_tables(i), True)
    for side in range(2):
        b = side * (blocks + 1)
        tables = tuple(halo_tables[side, k] for k in range(3))
        low_order(b, band(halo, 1 + side), outside(side), *tables, False)
        i = side * (blocks - 1)
        low_order(i + 1, band(fields, i), edge(i, side), *own_tables(i), True)

    def products(i, steps):
        mixed = jnp.concatenate([ratio_pieces[i], ratio_pieces[i + 1], ratio_pieces[i + 2]], axis=1)
        steps[...] = jnp.dot(mixed, matrices[i], preferred_element_type=jnp.float32)

    def limit(i, steps):
        out = [lowered[i, 8 * g : 8 * g + 8, :] for g in range(tracer_groups)]
        own = [ratios[i + 1, 8 * g : 8 * g + 8, :] for g in range(2 * tracer_groups)]
        low = 16 * tracer_groups
        for s in range(edges):
            lanes = slice(s * LANES, (s + 1) * LANES)
            beside = [
                own[g]
                + (steps[8 * g : 8 * g + 8, lanes] + steps[low + 8 * g : low + 8 * g + 8, lanes])
                for g in range(2 * tracer_groups)
            ]
            for g in range(tracer_groups):
                m = g + tracer_groups
                flux = antiflux[i, s, 8 * g : 8 * g + 8, :]
                factor = jnp.where(
                    flux >= 0.0, jnp.minimum(own[m], beside[g]), jnp.minimum(own[g], beside[m])
                )
                out[g] = out[g] - factor * flux
        lanes = slice(i * LANES, (i + 1) * LANES)
        for g in range(tracer_groups):
            t, lg = g // layer_groups, g % layer_groups
            tracers_new[t, 8 * lg : 8 * lg + 8, lanes] = out[g]

    buffers = (steps_a, steps_b)
    products(0, steps_a)
    for i in range(blocks):
        if i + 1 < blocks:
            products(i + 1, buffers[(i + 1) % 2])
        limit(i, buffers[i % 2])
    write.wait()


def swap(message, first, peers):
    pairs = []
    for i in range(first, peers - 1, 2):
        pairs += [(i, i + 1), (i + 1, i)]
    return lax.ppermute(message, "mesh", pairs)


def whole_spec():
    return pl.BlockSpec(memory_space=pltpu.VMEM)


def local(
    tracers,
    potential,
    surface_current,
    cell_neighbors,
    cell_normal,
    cell_weight,
    spectra,
    wind_velocity,
    node_neighbors,
    node_normal,
    node_weight,
    send_rows,
    node_slot,
):
    peers, _, capacity = send_rows.shape
    freqs, dirs, nodes = spectra.shape
    tracer_count, layers, cells = tracers.shape
    edges = cell_neighbors.shape[0]
    blocks = cells // LANES
    field_rows = (tracer_count + 1) * layers
    head_rows = 2 * field_rows + TABLE_ROWS
    message_rows = head_rows + (freqs // 2 * dirs + 7) // 8 * 8
    slots = node_slot.reshape(1, nodes)
    params = pltpu.CompilerParams(vmem_limit_bytes=VMEM_LIMIT)
    f32 = jnp.float32

    stored = pl.BlockSpec(memory_space=pltpu.HBM)
    rows = tracer_count * layers
    stride = (dirs + 7) // 8 * 8
    step_pairs = 5 if freqs % 10 == 0 else 1
    step_rows = 2 * step_pairs * stride

    def like(x):
        return jax.ShapeDtypeStruct(x.shape, x.dtype)

    def shaped(*shape, dtype=f32):
        return jax.ShapeDtypeStruct(shape, dtype)

    def call(kernel, name, inputs, outputs, scratch, out_specs=None):
        return pl.pallas_call(
            kernel,
            out_shape=outputs,
            in_specs=[whole_spec()] * len(inputs),
            out_specs=out_specs or (whole_spec(),) * len(outputs),
            scratch_shapes=scratch,
            compiler_params=params,
            name=name,
        )(*inputs)

    inputs = (
        spectra, tracers, potential, cell_neighbors, cell_normal, cell_weight, surface_current,
        send_rows, slots, node_neighbors, node_normal, node_weight, wind_velocity,
    )
    (
        currents, outer, inner, own_spectra, own_slots, near, angle, face, wind,
        own_tracers, own_potential, neighbors, normal, weight, coupled,
    ) = pl.pallas_call(
        pack_kernel,
        out_shape=(
            shaped(peers, LANES),
            shaped(message_rows, LANES),
            shaped(message_rows, LANES),
            shaped(freqs, stride, LANES),
            like(slots),
            like(node_neighbors),
            like(node_normal),
            like(node_weight),
            like(wind_velocity),
            like(tracers),
            like(potential),
            like(cell_neighbors),
            like(cell_normal),
            like(cell_weight),
            shaped(3, peers, capacity, dtype=jnp.int32),
        ),
        in_specs=[stored] * len(inputs),
        out_specs=(whole_spec(),) * 15,
        scratch_shapes=[
            pltpu.VMEM(surface_current.shape, f32),
            pltpu.SemaphoreType.DMA((15,)),
        ],
        compiler_params=params,
        name="pack",
    )(*(pltpu.with_memory_space_constraint(x, pltpu.HBM) for x in inputs))
    outer = swap(outer, 1, peers)
    inner = swap(inner, 0, peers)

    (
        cosine, sine, project, choice, ways, slot_choice, own_change,
        fields, matrices, inside, cell_cosine, cell_sine, cell_scale, sums,
    ) = call(
        functools.partial(prepare_kernel, dirs, step_rows),
        "prepare",
        (
            own_spectra, near, angle, face, wind, own_slots, own_tracers, own_potential,
            neighbors, normal, weight, coupled,
        ),
        (
            like(node_normal),
            like(node_normal),
            shaped(edges, stride, LANES),
            shaped(4 * LANES, edges * LANES, dtype=jnp.bfloat16),
            shaped(3, stride, LANES),
            shaped(nodes, peers * capacity, dtype=jnp.bfloat16),
            shaped(freqs * stride, edges * LANES),
            shaped(blocks, field_rows, LANES),
            shaped(blocks, 3 * LANES, edges * LANES, dtype=jnp.bfloat16),
            shaped(blocks, field_rows, edges * LANES),
            shaped(blocks, 8, LANES),
            shaped(blocks, 8, LANES),
            shaped(blocks, 8, LANES),
            shaped(peers * capacity, (blocks + 2) * LANES, dtype=jnp.bfloat16),
        ),
        [pltpu.VMEM((blocks, 2 * field_rows, LANES), jnp.bfloat16)],
    )
    currents, cosine = lax.optimization_barrier((currents, cosine))
    currents = lax.all_to_all(currents, "mesh", 0, 0, tiled=True)

    spectra_new, stokes_rows = call(
        functools.partial(wave_kernel, capacity, step_pairs, dirs),
        "wave",
        (
            own_spectra, outer, inner, currents, own_slots, near,
            cosine, sine, project, choice, ways, slot_choice, own_change,
        ),
        (shaped(freqs, stride, LANES), shaped(peers, LANES)),
        [
            pltpu.VMEM((8, LANES), f32),
            pltpu.VMEM((step_rows, LANES), f32),
            pltpu.VMEM((step_rows, edges * LANES), f32),
            pltpu.VMEM((step_rows, edges * LANES), f32),
        ],
    )
    stokes_all = lax.all_to_all(stokes_rows, "mesh", 0, 0, tiled=True)

    return call(
        functools.partial(tracer_kernel, capacity, (tracer_count, layers, edges)),
        "tracer",
        (
            outer, inner, stokes_all, fields, neighbors, matrices, inside, cell_cosine, cell_sine,
            cell_scale, sums, pltpu.with_memory_space_constraint(spectra_new, pltpu.VMEM),
        ),
        (like(tracers), like(spectra)),
        [
            pltpu.VMEM((4, field_rows, LANES), f32),
            pltpu.VMEM((2, 8, LANES), jnp.int32),
            pltpu.VMEM((2, 3, 8, LANES), f32),
            pltpu.VMEM((blocks + 2, 8, LANES), f32),
            pltpu.VMEM((blocks, edges, rows, LANES), f32),
            pltpu.VMEM((blocks, rows, LANES), f32),
            pltpu.VMEM((blocks + 2, 2 * rows, LANES), f32),
            pltpu.VMEM((blocks + 2, 4 * rows, LANES), jnp.bfloat16),
            pltpu.VMEM((4 * rows, edges * LANES), f32),
            pltpu.VMEM((4 * rows, edges * LANES), f32),
            pltpu.SemaphoreType.DMA(()),
        ],
        out_specs=(whole_spec(), stored),
    )


def solution(mesh):
    return jax.shard_map(
        local,
        mesh=mesh,
        in_specs=(
            P(None, None, ("groups", "mesh")),
            P(None, ("groups", "mesh")),
            P(None, ("groups", "mesh")),
            P(None, "mesh"),
            P(None, "mesh"),
            P(None, "mesh"),
            P(None, None, ("groups", "mesh")),
            P(None, ("groups", "mesh")),
            P(None, "mesh"),
            P(None, "mesh"),
            P(None, "mesh"),
            P(),
            P("mesh"),
        ),
        out_specs=(P(None, None, ("groups", "mesh")), P(None, None, ("groups", "mesh"))),
        check_vma=False,
    )
```

```python
import functools
import math

import jax
import jax.numpy as jnp
from jax import lax
from jax.experimental import pallas as pl
from jax.experimental.pallas import tpu as pltpu
from jax.sharding import PartitionSpec as P

LANES = 128
FCT_FLOOR = 0.001
TABLE_ROWS = 24
VMEM_LIMIT = 32 * 1024 * 1024


def lane_gather(values, index):
    return jnp.take_along_axis(values, index, axis=1, mode="promise_in_bounds")


def spread(row, count):
    return jnp.broadcast_to(row, (count, LANES))


def lane_iota(rows):
    return lax.broadcasted_iota(jnp.int32, (rows, LANES), 1)


def row_iota(rows):
    return lax.broadcasted_iota(jnp.int32, (rows, LANES), 0)


def slot_rows(entry):
    peers, capacity = entry.shape
    wide = jnp.concatenate([entry, jnp.zeros((peers, LANES - capacity), jnp.int32)], axis=1)
    wide = lane_gather(wide, lane_iota(peers) % capacity)
    owner = row_iota(peers)
    out = []
    for half in range(peers * capacity // LANES):
        wanted = (lane_iota(peers) + half * LANES) // capacity
        picked = jnp.where(owner == wanted, wide, 0).astype(jnp.float32)
        out.append(jnp.sum(picked, axis=0, keepdims=True).astype(jnp.int32))
    return out


def half_mask(rows, lower):
    half = lane_iota(rows) // (LANES // 2)
    return half == jnp.where(lower, 0, 1)


def peer_rows(values, peers, capacity):
    lane = lane_iota(peers)
    group = lane // capacity
    block = jnp.clip(row_iota(peers) - 1 + group // 2, 0, peers - 1)
    entry = block * capacity + lane % capacity
    out = jnp.zeros((peers, LANES), jnp.float32)
    for part in range(2):
        for half, row in enumerate(values[part]):
            found = lane_gather(spread(row, peers), entry % LANES)
            wanted = (group < 6) & (group % 2 == part) & (entry // LANES == half)
            out = jnp.where(wanted, found, out)
    return out


def direction(dirs, padded):
    turn = row_iota(padded).astype(jnp.float32) * (2.0 * math.pi / dirs)
    return jnp.cos(turn), jnp.sin(turn)


def node_tables(
    me, dirs, near, angle, face, wind, slot, cosine, sine, project, choice, ways, slots
):
    edges, padded = project.shape[:2]
    cosine[...] = face[...] * jnp.cos(angle[...])
    sine[...] = face[...] * jnp.sin(angle[...])
    cos_dir, sin_dir = direction(dirs, padded)
    ways[0] = cos_dir
    ways[1] = sin_dir
    ways[2] = 0.25 * jnp.maximum(wind[0:1, :] * cos_dir + wind[1:2, :] * sin_dir, 0.0)
    taken = jnp.transpose(spread(slot[...].astype(jnp.float32), LANES))
    for half in range(slots.shape[1] // LANES):
        number = (lane_iota(LANES) + half * LANES).astype(jnp.float32)
        picked = jnp.where(taken == number, 1.0, 0.0).astype(jnp.bfloat16)
        slots[:, half * LANES : (half + 1) * LANES] = picked
    source = row_iota(LANES)
    minus = jnp.where(source == lane_iota(LANES), -1.0, 0.0)
    for s in range(edges):
        project[s] = cos_dir * cosine[s : s + 1, :] + sin_dir * sine[s : s + 1, :]
        target = near[s : s + 1, :]
        inside = target // LANES == me
        lane = target % LANES
        own = jnp.where(source == jnp.where(inside, lane, LANES), 1.0, 0.0) + minus
        halo = jnp.where(source == jnp.where(inside, LANES, lane), 1.0, 0.0)
        lanes = slice(s * LANES, (s + 1) * LANES)
        for k, part in enumerate((own, own, halo, halo)):
            choice[k * LANES : (k + 1) * LANES, lanes] = part.astype(jnp.bfloat16)


def split(x):
    first = x.astype(jnp.bfloat16)
    return first, (x - first.astype(jnp.float32)).astype(jnp.bfloat16)


def pack_kernel(
    spectra_in, tracers_in, potential_in, neighbors_in, normal_in, weight_in, current_in,
    send_rows, slot_in, near_in, angle_in, face_in, wind_in,
    rows_out, outer, inner, spectra, node_slot, near, angle, face, wind,
    tracers, potential, neighbors, normal, weight, coupled,
    current, sems,
):
    peers, _, capacity = send_rows.shape
    me = lax.axis_index("mesh")
    freqs, dirs = spectra_in.shape[:2]
    if dirs < spectra.shape[1]:
        for f in range(freqs):
            spectra[f, dirs // 8 * 8 :, :] = jnp.zeros((8, LANES), jnp.float32)
    pairs = freqs // 2
    copies = []
    for source, target in (
        (send_rows.at[me], coupled.at[1]),
        (current_in, current),
        (slot_in, node_slot),
        (spectra_in, spectra.at[:, 0:dirs, :]),
        (tracers_in, tracers),
        (potential_in, potential),
        (neighbors_in, neighbors),
        (normal_in, normal),
        (weight_in, weight),
        (send_rows.at[jnp.maximum(me - 1, 0)], coupled.at[0]),
        (send_rows.at[jnp.minimum(me + 1, peers - 1)], coupled.at[2]),
        (near_in, near),
        (angle_in, angle),
        (face_in, face),
        (wind_in, wind),
    ):
        copy = pltpu.make_async_copy(source, target, sems.at[len(copies)])
        copy.start()
        copies.append(copy)
    for copy in copies[:3]:
        copy.wait()
    layers, cells = potential.shape
    blocks = cells // LANES
    field_rows = (tracers.shape[0] + 1) * layers
    stacked = jnp.concatenate(
        [current[:, b * LANES : (b + 1) * LANES] for b in range(blocks)], axis=0
    )
    place = row_iota(2 * blocks)
    halves = slot_rows(coupled[1])
    values = [[], []]
    for cell in halves:
        found = lane_gather(stacked, spread(cell % LANES, 2 * blocks))
        for part in range(2):
            picked = jnp.where(place == 2 * (cell // LANES) + part, found, 0.0)
            values[part].append(jnp.sum(picked, axis=0, keepdims=True))
    rows_out[...] = peer_rows(values, peers, capacity)
    for copy in copies[4:9]:
        copy.wait()
    odd = me % 2 == 1
    for out, upward in ((outer, odd), (inner, jnp.logical_not(odd))):
        for b in range(2):
            high = slice((blocks - 2 + b) * LANES, (blocks - 1 + b) * LANES)
            low = slice(b * LANES, (b + 1) * LANES)
            base = b * field_rows
            for t in range(tracers.shape[0]):
                out[base + t * layers : base + (t + 1) * layers, :] = jnp.where(
                    upward, tracers[t, :, high], tracers[t, :, low]
                )
            out[base + field_rows - layers : base + field_rows, :] = jnp.where(
                upward, potential[:, high], potential[:, low]
            )
        high = slice((blocks - 1) * LANES, blocks * LANES)
        low = slice(0, LANES)
        base = 2 * field_rows
        out[base : base + TABLE_ROWS, :] = jnp.zeros((TABLE_ROWS, LANES), jnp.float32)
        edges = neighbors.shape[0]
        near = jnp.where(upward, neighbors[:, high], neighbors[:, low])
        out[base : base + edges, :] = near.astype(jnp.float32)
        out[base + edges : base + edges + 1, :] = node_slot[...].astype(jnp.float32)
        out[base + 8 : base + 8 + edges, :] = jnp.where(upward, normal[:, high], normal[:, low])
        out[base + 16 : base + 16 + edges, :] = jnp.where(upward, weight[:, high], weight[:, low])
    base = 2 * field_rows + TABLE_ROWS
    whole = dirs // 8 * 8
    rest = dirs - whole
    turns = half_mask(dirs, odd)
    copies[3].wait()
    for g in range(pairs):
        natural = spectra[g, 0:dirs, :]
        turned = pltpu.roll(spectra[g + pairs, 0:dirs, :], LANES // 2, 1)
        for out, mixed in (
            (outer, jnp.where(turns, turned, natural)),
            (inner, jnp.where(turns, natural, turned)),
        ):
            at = base + g * whole
            out[at : at + whole, :] = mixed[:whole]
            at = base + pairs * whole + g * rest
            out[at : at + rest, :] = mixed[whole:]
    at = base + pairs * dirs
    if at < outer.shape[0]:
        for out in (outer, inner):
            out[at:, :] = jnp.zeros((outer.shape[0] - at, LANES), jnp.float32)
    for copy in copies[9:]:
        copy.wait()


def choose(cells, first, lanes, matrix):
    place = (cells - first - LANES).astype(jnp.float32).astype(jnp.bfloat16)
    place = spread(place, LANES)
    one = jnp.ones((LANES, LANES), jnp.bfloat16)
    for k in range(3):
        source = (row_iota(LANES) + (k - 1) * LANES).astype(jnp.float32).astype(jnp.bfloat16)
        part = jnp.where(source == place, one, 0 * one)
        if k == 1:
            own = jnp.where(row_iota(LANES) == lane_iota(LANES), 1.0, 0.0).astype(jnp.bfloat16)
            part = part - own
        matrix[k * LANES : (k + 1) * LANES, lanes] = part


def stack_split(x):
    first, second = split(x)
    return jnp.concatenate([first, second], axis=0)


def differences(parts, matrix):
    mixed = jnp.concatenate(parts, axis=1)
    out = jnp.dot(mixed, matrix, preferred_element_type=jnp.float32)
    rows = out.shape[0] // 2
    return out[:rows] + out[rows:]


def prepare_kernel(
    dirs, step_rows,
    spectra, near, angle, face, wind, slot, tracers, potential, neighbors, normal, weight, coupled,
    cosine, sine, project, choice, ways, slots, own_change,
    fields, matrices, inside, cell_cosine, cell_sine, cell_scale, sums,
    pieces,
):
    me = lax.axis_index("mesh")
    node_tables(
        me, dirs, near, angle, face, wind, slot, cosine, sine, project, choice, ways, slots
    )
    freqs, padded, _ = spectra.shape
    step = step_rows // padded

    def own_part(c, carry):
        own = spectra[pl.ds(c * step, step)].reshape(step_rows, LANES)
        own_change[pl.ds(pl.multiple_of(c * step_rows, 8), step_rows), :] = jnp.dot(
            jnp.concatenate(split(own), axis=1),
            choice[0 : 2 * LANES, :],
            preferred_element_type=jnp.float32,
        )
        return carry

    lax.fori_loop(0, freqs // step, own_part, 0)
    tracer_count, layers, cells = tracers.shape
    blocks = cells // LANES
    edges = neighbors.shape[0]
    field_rows = (tracer_count + 1) * layers
    for b in range(blocks):
        lanes = slice(b * LANES, (b + 1) * LANES)
        for t in range(tracer_count):
            fields[b, t * layers : (t + 1) * layers, :] = tracers[t, :, lanes]
        fields[b, field_rows - layers : field_rows, :] = potential[:, lanes]
        pieces[b] = stack_split(fields[b])
        w = weight[:, lanes]
        cell_scale[b, 0:edges, :] = w
        cell_cosine[b, 0:edges, :] = w * jnp.cos(normal[:, lanes])
        cell_sine[b, 0:edges, :] = w * jnp.sin(normal[:, lanes])
        for s in range(edges):
            choose(
                neighbors[s : s + 1, lanes],
                (me * blocks + b - 1) * LANES,
                slice(s * LANES, (s + 1) * LANES),
                matrices.at[b],
            )
    for b in range(blocks):
        first, last = max(b - 1, 0), min(b + 1, blocks - 1)
        rows = slice((first - b + 1) * LANES, (last - b + 2) * LANES)
        parts = [pieces[k] for k in range(first, last + 1)]
        change = differences(parts, matrices[b, rows, :])
        last_field = field_rows - layers
        inside[b, 0:last_field, :] = change[:last_field]
        for s in range(edges):
            at = slice(s * LANES, (s + 1) * LANES)
            inside[b, last_field:, at] = change[last_field:, at] * cell_scale[b, s : s + 1, :]
    for which in range(3):
        first = 0 if which != 0 else cells - LANES
        count = blocks if which == 1 else 1
        start = (0, 1, blocks + 1)[which]
        for half, names in enumerate(slot_rows(coupled[which])):
            named = jnp.transpose(spread(names, LANES).astype(jnp.float32))
            for b in range(count):
                cell = (lane_iota(LANES) + (first + b * LANES)).astype(jnp.float32)
                picked = jnp.where(named == cell, 1.0, 0.0).astype(jnp.bfloat16)
                lanes = slice((start + b) * LANES, (start + b + 1) * LANES)
                sums[half * LANES : (half + 1) * LANES, lanes] = picked


def node_currents(table, slot, which, capacity):
    peers = table.shape[0]
    owner = row_iota(peers) == slot // capacity
    out = []
    for part in range(2):
        lane = (2 * which + part) * capacity + slot % capacity
        found = jnp.where(owner, lane_gather(table, spread(lane, peers)), 0.0)
        out.append(jnp.sum(found, axis=0, keepdims=True))
    return out


def wave_kernel(
    capacity, step_pairs, dirs,
    spectra, outer, inner, table, node_slot, neighbors, cosine, sine, project, choice, ways, slots,
    own_change,
    spectra_new, rows_out, drift, halos, change_a, change_b,
):
    me = lax.axis_index("mesh")
    freqs, stride = spectra.shape[:2]
    edges = neighbors.shape[0]
    peers = table.shape[0]
    halves = peers * capacity // LANES
    pairs = freqs // 2
    whole = dirs // 8 * 8
    rest = dirs - whole
    base = outer.shape[0] - (pairs * dirs + 7) // 8 * 8

    odd = me % 2 == 1
    slot = node_slot[...]
    row = base - TABLE_ROWS + edges
    halo_slot = jnp.where(
        half_mask(1, odd), outer[row : row + 1, :], inner[row : row + 1, :]
    ).astype(jnp.int32)
    lower = lane_iota(1) < LANES // 2
    currents = table[...]
    own_x, own_y = node_currents(currents, slot, jnp.ones((1, LANES), jnp.int32), capacity)
    halo_x, halo_y = node_currents(currents, halo_slot, jnp.where(lower, 2, 0), capacity)

    target = neighbors[...]
    lane = target % LANES
    inside = target // LANES == me

    def beside(own, halo):
        a = lane_gather(spread(own, edges), lane)
        b = lane_gather(spread(halo, edges), lane)
        return jnp.where(inside, a, b)

    drift[0:edges, :] = (
        0.5 * (own_x + beside(own_x, halo_x)) * cosine[...]
        + 0.5 * (own_y + beside(own_y, halo_y)) * sine[...]
    )
    drifts = [spread(drift[s : s + 1, :], 8) for s in range(edges)]
    from_outer = half_mask(dirs, odd)
    halos[...] = jnp.zeros(halos.shape, jnp.float32)
    ratio = 1.0 / 1.1
    bands = [slice(r, r + 8) for r in range(0, stride, 8)]

    def gather(c, change):
        for i in range(step_pairs):
            g = c * step_pairs + i
            parts = []
            for message in (outer, inner):
                at = base + g * whole
                upper = message[at : at + whole, :]
                at = base + pairs * whole + g * rest
                left = message[at : at + rest, :]
                parts.append(jnp.concatenate([upper, left], axis=0))
            x, y = parts
            at = 2 * i * stride
            halos[at : at + dirs, :] = jnp.where(from_outer, x, y)
            at += stride
            halos[at : at + dirs, :] = pltpu.roll(jnp.where(from_outer, y, x), LANES // 2, 1)
        mixed = jnp.concatenate(split(halos[...]), axis=1)
        change[...] = jnp.dot(
            mixed, choice[2 * LANES : 4 * LANES, :], preferred_element_type=jnp.float32
        )

    def advect(c, change, first_speed, first_slow, total):
        total = list(total)
        speeds = []
        for i in range(step_pairs):
            speeds += [first_speed * ratio**i, first_speed * ratio ** (i + pairs)]
        slowness = []
        for i in range(step_pairs):
            slowness += [first_slow * ratio**-i, first_slow * ratio ** -(i + pairs)]
        relative = [[drift * slow for drift in drifts] for slow in slowness]
        relative_sum = [sum(each[1:], each[0]) for each in relative]
        for k, band in enumerate(bands):
            along = [project[s, band, :] for s in range(edges)]
            along_sum = sum(along[1:], along[0])
            for i in range(step_pairs):
                g = c * step_pairs + i
                for j, f in ((2 * i, g), (2 * i + 1, g + pairs)):
                    own = spectra[f, band, :]
                    at = j * stride + band.start
                    own_at = slice(f * stride + band.start, f * stride + band.stop)
                    flux = (along_sum + relative_sum[j]) * own
                    for s in range(edges):
                        down = jnp.minimum(along[s] + relative[j][s], 0.0)
                        lanes = slice(s * LANES, (s + 1) * LANES)
                        step = change[at : at + 8, lanes] + own_change[own_at, lanes]
                        flux = flux + down * step
                    value = own - speeds[j] * flux
                    spectra_new[f, band, :] = value
                    total[k] = total[k] + value
        return first_speed * ratio**step_pairs, first_slow * ratio**-step_pairs, tuple(total)

    zeros = tuple(jnp.zeros((8, LANES), jnp.float32) for _ in bands)
    chunks = pairs // step_pairs
    buffers = (change_a, change_b)
    carry = (1.0, 1.0, zeros)
    gather(0, change_a)
    for c in range(chunks):
        if c + 1 < chunks:
            gather(c + 1, buffers[(c + 1) % 2])
        carry = advect(c, buffers[c % 2], *carry)
    total = carry[2]
    total = jnp.concatenate(total, axis=0)
    zero = jnp.zeros((stride, LANES), jnp.float32)
    cos_dir, sin_dir = ways[0], ways[1]
    mean = jnp.sum(total, axis=0, keepdims=True) * (1.0 / (freqs * dirs))
    step = jnp.exp((ways[2] - 2.0 * mean) * (1.0 / freqs))
    run = 10 if freqs % 10 == 0 else 1

    def grow(c, carry):
        factor, weighted = carry
        for i in range(run):
            f = c * run + i
            factor = factor * step
            evolved = spectra_new[f] * factor
            spectra_new[f] = evolved
            kappa = (f + 1).astype(jnp.float32) * (1.0 / freqs)
            weighted = weighted + kappa * evolved
        return factor, weighted

    _, weighted = lax.fori_loop(0, freqs // run, grow, (zero + 1.0, zero))
    stokes = jnp.concatenate(
        [
            jnp.sum(weighted * cos_dir, axis=0, keepdims=True),
            jnp.sum(weighted * sin_dir, axis=0, keepdims=True),
        ],
        axis=0,
    ) * (1.0 / dirs)
    in_order = jnp.dot(
        three_parts(stokes), slots[...], preferred_element_type=jnp.float32
    )
    in_order = in_order[0:2] + (in_order[2:4] + in_order[4:6])
    values = [
        [in_order[part : part + 1, h * LANES : (h + 1) * LANES] for h in range(halves)]
        for part in range(2)
    ]
    rows_out[...] = peer_rows(values, peers, capacity)


def three_parts(values):
    first = values.astype(jnp.bfloat16).astype(jnp.float32)
    left = values - first
    second = left.astype(jnp.bfloat16).astype(jnp.float32)
    third = left - second
    pad = jnp.zeros((10, values.shape[1]), jnp.float32)
    return jnp.concatenate([first, second, third, pad], axis=0).astype(jnp.bfloat16)


def tracer_kernel(
    capacity, shape,
    outer, inner, table, fields, neighbors, matrices, inside, cosine, sine, scale, sums, spectra,
    tracers_new, spectra_out,
    halo, halo_near, halo_tables, stokes, antiflux, lowered, ratios,
    ratio_pieces, steps_a, steps_b, sem,
):
    dirs = spectra_out.shape[1]
    write = pltpu.make_async_copy(spectra.at[:, 0:dirs, :], spectra_out, sem)
    write.start()
    me = lax.axis_index("mesh")
    tracer_count, layers, edges = shape
    peers = table.shape[0]
    halves = peers * capacity // LANES
    blocks, field_rows, _ = fields.shape
    layer_groups = layers // 8
    tracer_groups = tracer_count * layer_groups
    odd = me % 2 == 1

    for b in range(2):
        x = outer[b * field_rows : (b + 1) * field_rows, :]
        y = inner[b * field_rows : (b + 1) * field_rows, :]
        for side, value in ((0, jnp.where(odd, y, x)), (1, jnp.where(odd, x, y))):
            halo[2 * side + b] = value
    at = 2 * field_rows
    x = outer[at : at + TABLE_ROWS, :]
    y = inner[at : at + TABLE_ROWS, :]
    for side, rows in ((0, jnp.where(odd, y, x)), (1, jnp.where(odd, x, y))):
        w = rows[16 : 16 + edges]
        halo_tables[side, 0, 0:edges, :] = w
        halo_tables[side, 1, 0:edges, :] = w * jnp.cos(rows[8 : 8 + edges])
        halo_tables[side, 2, 0:edges, :] = w * jnp.sin(rows[8 : 8 + edges])
        halo_near[side, 0:edges, :] = rows[0:edges].astype(jnp.int32)

    received = table[...]
    lane_of = lane_iota(peers)
    sections = []
    for which in range(3):
        values = []
        for part in range(2):
            lane = (2 * which + part) * capacity + lane_of % capacity
            found = lane_gather(received, lane)
            row = []
            for half in range(halves):
                mine = row_iota(peers) == (lane_of + half * LANES) // capacity
                row.append(jnp.sum(jnp.where(mine, found, 0.0), axis=0, keepdims=True))
            values.append(jnp.concatenate(row, axis=1))
        sections.append(three_parts(jnp.concatenate(values, axis=0)))
    total = jnp.dot(
        jnp.concatenate(sections, axis=0), sums[...], preferred_element_type=jnp.float32
    )
    for b in range(blocks + 2):
        which = 0 if b == 0 else 2 if b == blocks + 1 else 1
        at = 16 * which
        lanes = slice(b * LANES, (b + 1) * LANES)
        first, second, third = (total[at + k : at + k + 2, lanes] for k in (0, 2, 4))
        stokes[b, 0:2, :] = first + (second + third)

    decay = [
        jnp.exp(-3.0 / layers * (row_iota(8) + 8 * g).astype(jnp.float32))
        for g in range(layer_groups)
    ]

    def low_order(b, value, change, wx, wy, keep):
        slope = wx * stokes[b, 0:1, :] + wy * stokes[b, 1:2, :]
        own = [value(8 * g) for g in range(tracer_groups)]
        zero = jnp.zeros((8, LANES), jnp.float32)
        speed_sum = [zero] * layer_groups
        inflow = [zero] * tracer_groups
        highest = [zero] * tracer_groups
        lowest = [zero] * tracer_groups
        positive = [zero] * tracer_groups
        negative = [zero] * tracer_groups
        for s in range(edges):
            slope8 = spread(slope[s : s + 1, :], 8)
            for lg in range(layer_groups):
                speed = change(8 * (tracer_groups + lg), s) + decay[lg] * slope8
                down = jnp.minimum(speed, 0.0)
                half = 0.5 * speed - down
                speed_sum[lg] = speed_sum[lg] + speed
                for t in range(tracer_count):
                    g = t * layer_groups + lg
                    step = change(8 * g, s)
                    flux = half * step
                    if keep:
                        antiflux[b - 1, s, 8 * g : 8 * g + 8, :] = flux
                    inflow[g] = inflow[g] + down * step
                    highest[g] = jnp.maximum(highest[g], step)
                    lowest[g] = jnp.minimum(lowest[g], step)
                    positive[g] = positive[g] + jnp.maximum(flux, 0.0)
                    negative[g] = negative[g] - jnp.minimum(flux, 0.0)
        plus, minus = [], []
        for g in range(tracer_groups):
            loss = speed_sum[g % layer_groups] * own[g] + inflow[g]
            if keep:
                lowered[b - 1, 8 * g : 8 * g + 8, :] = own[g] - loss
            up = jnp.maximum(highest[g] + loss, 0.0) / (negative[g] + FCT_FLOOR)
            down = jnp.maximum(-loss - lowest[g], 0.0) / (positive[g] + FCT_FLOOR)
            plus.append(jnp.minimum(1.0, up))
            minus.append(jnp.minimum(1.0, down))
        both = jnp.concatenate(plus + minus, axis=0)
        ratios[b] = both
        ratio_pieces[b] = stack_split(both)

    def band(ref, *index):
        return lambda row: ref[(*index, slice(row, row + 8), slice(None))]

    potential_row = tracer_groups * 8

    def within(i):
        return lambda row, s: inside[i, row : row + 8, s * LANES : (s + 1) * LANES]

    def edge(i, side):
        beside = halo.at[1 + side]
        sign = 2 * side - 1

        def change(row, s):
            near = spread(neighbors[s : s + 1, i * LANES : (i + 1) * LANES], 8)
            from_halo = near // LANES - (me * blocks + i) == sign
            picked = lane_gather(beside[row : row + 8, :], near % LANES)
            if row >= potential_row:
                picked = picked * spread(scale[i, s : s + 1, :], 8)
            return within(i)(row, s) + jnp.where(from_halo, picked, 0.0)

        return change

    def outside(side):
        i = side * (blocks - 1)
        low, own, high = (
            (halo.at[0], halo.at[1], fields.at[i]),
            (fields.at[i], halo.at[2], halo.at[3]),
        )[side]

        def change(row, s):
            rows = slice(row, row + 8)
            near = spread(halo_near[side, s : s + 1, :], 8)
            place = near // LANES - (me * blocks + i + 2 * side - 1)
            lane = near % LANES
            mine = own[rows, :]
            middle = lane_gather(mine, lane)
            left = lane_gather(low[rows, :], lane)
            right = lane_gather(high[rows, :], lane)
            out = jnp.where(place == 0, middle, jnp.where(place < 0, left, right)) - mine
            if row >= potential_row:
                out = out * spread(halo_tables[side, 0, s : s + 1, :], 8)
            return out

        return change

    for i in range(1, blocks - 1):
        low_order(i + 1, band(fields, i), within(i), cosine[i], sine[i], True)
    for side in range(2):
        b = side * (blocks + 1)
        tables = (halo_tables[side, 1], halo_tables[side, 2])
        low_order(b, band(halo, 1 + side), outside(side), *tables, False)
        i = side * (blocks - 1)
        low_order(i + 1, band(fields, i), edge(i, side), cosine[i], sine[i], True)

    def products(i, steps):
        mixed = jnp.concatenate([ratio_pieces[i], ratio_pieces[i + 1], ratio_pieces[i + 2]], axis=1)
        steps[...] = jnp.dot(mixed, matrices[i], preferred_element_type=jnp.float32)

    def limit(i, steps):
        out = [lowered[i, 8 * g : 8 * g + 8, :] for g in range(tracer_groups)]
        own = [ratios[i + 1, 8 * g : 8 * g + 8, :] for g in range(2 * tracer_groups)]
        low = 16 * tracer_groups
        for s in range(edges):
            lanes = slice(s * LANES, (s + 1) * LANES)
            beside = [
                own[g]
                + (steps[8 * g : 8 * g + 8, lanes] + steps[low + 8 * g : low + 8 * g + 8, lanes])
                for g in range(2 * tracer_groups)
            ]
            for g in range(tracer_groups):
                m = g + tracer_groups
                flux = antiflux[i, s, 8 * g : 8 * g + 8, :]
                factor = jnp.where(
                    flux >= 0.0, jnp.minimum(own[m], beside[g]), jnp.minimum(own[g], beside[m])
                )
                out[g] = out[g] - factor * flux
        lanes = slice(i * LANES, (i + 1) * LANES)
        for g in range(tracer_groups):
            t, lg = g // layer_groups, g % layer_groups
            tracers_new[t, 8 * lg : 8 * lg + 8, lanes] = out[g]

    buffers = (steps_a, steps_b)
    products(0, steps_a)
    for i in range(blocks):
        if i + 1 < blocks:
            products(i + 1, buffers[(i + 1) % 2])
        limit(i, buffers[i % 2])
    write.wait()


def swap(message, first, peers):
    pairs = []
    for i in range(first, peers - 1, 2):
        pairs += [(i, i + 1), (i + 1, i)]
    return lax.ppermute(message, "mesh", pairs)


def whole_spec():
    return pl.BlockSpec(memory_space=pltpu.VMEM)


def local(
    tracers,
    potential,
    surface_current,
    cell_neighbors,
    cell_normal,
    cell_weight,
    spectra,
    wind_velocity,
    node_neighbors,
    node_normal,
    node_weight,
    send_rows,
    node_slot,
):
    peers, _, capacity = send_rows.shape
    freqs, dirs, nodes = spectra.shape
    tracer_count, layers, cells = tracers.shape
    edges = cell_neighbors.shape[0]
    blocks = cells // LANES
    field_rows = (tracer_count + 1) * layers
    head_rows = 2 * field_rows + TABLE_ROWS
    message_rows = head_rows + (freqs // 2 * dirs + 7) // 8 * 8
    slots = node_slot.reshape(1, nodes)
    params = pltpu.CompilerParams(vmem_limit_bytes=VMEM_LIMIT)
    f32 = jnp.float32

    stored = pl.BlockSpec(memory_space=pltpu.HBM)
    rows = tracer_count * layers
    stride = (dirs + 7) // 8 * 8
    step_pairs = 5 if freqs % 10 == 0 else 1
    step_rows = 2 * step_pairs * stride

    def like(x):
        return jax.ShapeDtypeStruct(x.shape, x.dtype)

    def shaped(*shape, dtype=f32):
        return jax.ShapeDtypeStruct(shape, dtype)

    def call(kernel, name, inputs, outputs, scratch, out_specs=None):
        return pl.pallas_call(
            kernel,
            out_shape=outputs,
            in_specs=[whole_spec()] * len(inputs),
            out_specs=out_specs or (whole_spec(),) * len(outputs),
            scratch_shapes=scratch,
            compiler_params=params,
            name=name,
        )(*inputs)

    inputs = (
        spectra, tracers, potential, cell_neighbors, cell_normal, cell_weight, surface_current,
        send_rows, slots, node_neighbors, node_normal, node_weight, wind_velocity,
    )
    (
        currents, outer, inner, own_spectra, own_slots, near, angle, face, wind,
        own_tracers, own_potential, neighbors, normal, weight, coupled,
    ) = pl.pallas_call(
        pack_kernel,
        out_shape=(
            shaped(peers, LANES),
            shaped(message_rows, LANES),
            shaped(message_rows, LANES),
            shaped(freqs, stride, LANES),
            like(slots),
            like(node_neighbors),
            like(node_normal),
            like(node_weight),
            like(wind_velocity),
            like(tracers),
            like(potential),
            like(cell_neighbors),
            like(cell_normal),
            like(cell_weight),
            shaped(3, peers, capacity, dtype=jnp.int32),
        ),
        in_specs=[stored] * len(inputs),
        out_specs=(whole_spec(),) * 15,
        scratch_shapes=[
            pltpu.VMEM(surface_current.shape, f32),
            pltpu.SemaphoreType.DMA((15,)),
        ],
        compiler_params=params,
        name="pack",
    )(*(pltpu.with_memory_space_constraint(x, pltpu.HBM) for x in inputs))
    outer = swap(outer, 1, peers)
    inner = swap(inner, 0, peers)

    (
        cosine, sine, project, choice, ways, slot_choice, own_change,
        fields, matrices, inside, cell_cosine, cell_sine, cell_scale, sums,
    ) = call(
        functools.partial(prepare_kernel, dirs, step_rows),
        "prepare",
        (
            own_spectra, near, angle, face, wind, own_slots, own_tracers, own_potential,
            neighbors, normal, weight, coupled,
        ),
        (
            like(node_normal),
            like(node_normal),
            shaped(edges, stride, LANES),
            shaped(4 * LANES, edges * LANES, dtype=jnp.bfloat16),
            shaped(3, stride, LANES),
            shaped(nodes, peers * capacity, dtype=jnp.bfloat16),
            shaped(freqs * stride, edges * LANES),
            shaped(blocks, field_rows, LANES),
            shaped(blocks, 3 * LANES, edges * LANES, dtype=jnp.bfloat16),
            shaped(blocks, field_rows, edges * LANES),
            shaped(blocks, 8, LANES),
            shaped(blocks, 8, LANES),
            shaped(blocks, 8, LANES),
            shaped(peers * capacity, (blocks + 2) * LANES, dtype=jnp.bfloat16),
        ),
        [pltpu.VMEM((blocks, 2 * field_rows, LANES), jnp.bfloat16)],
    )
    currents, cosine = lax.optimization_barrier((currents, cosine))
    currents = lax.all_to_all(currents, "mesh", 0, 0, tiled=True)

    spectra_new, stokes_rows = call(
        functools.partial(wave_kernel, capacity, step_pairs, dirs),
        "wave",
        (
            own_spectra, outer, inner, currents, own_slots, near,
            cosine, sine, project, choice, ways, slot_choice, own_change,
        ),
        (shaped(freqs, stride, LANES), shaped(peers, LANES)),
        [
            pltpu.VMEM((8, LANES), f32),
            pltpu.VMEM((step_rows, LANES), f32),
            pltpu.VMEM((step_rows, edges * LANES), f32),
            pltpu.VMEM((step_rows, edges * LANES), f32),
        ],
    )
    stokes_all = lax.all_to_all(stokes_rows, "mesh", 0, 0, tiled=True)

    return call(
        functools.partial(tracer_kernel, capacity, (tracer_count, layers, edges)),
        "tracer",
        (
            outer, inner, stokes_all, fields, neighbors, matrices, inside, cell_cosine, cell_sine,
            cell_scale, sums, pltpu.with_memory_space_constraint(spectra_new, pltpu.VMEM),
        ),
        (like(tracers), like(spectra)),
        [
            pltpu.VMEM((4, field_rows, LANES), f32),
            pltpu.VMEM((2, 8, LANES), jnp.int32),
            pltpu.VMEM((2, 3, 8, LANES), f32),
            pltpu.VMEM((blocks + 2, 8, LANES), f32),
            pltpu.VMEM((blocks, edges, rows, LANES), f32),
            pltpu.VMEM((blocks, rows, LANES), f32),
            pltpu.VMEM((blocks + 2, 2 * rows, LANES), f32),
            pltpu.VMEM((blocks + 2, 4 * rows, LANES), jnp.bfloat16),
            pltpu.VMEM((4 * rows, edges * LANES), f32),
            pltpu.VMEM((4 * rows, edges * LANES), f32),
            pltpu.SemaphoreType.DMA(()),
        ],
        out_specs=(whole_spec(), stored),
    )


def solution(mesh):
    return jax.shard_map(
        local,
        mesh=mesh,
        in_specs=(
            P(None, None, ("groups", "mesh")),
            P(None, ("groups", "mesh")),
            P(None, ("groups", "mesh")),
            P(None, "mesh"),
            P(None, "mesh"),
            P(None, "mesh"),
            P(None, None, ("groups", "mesh")),
            P(None, ("groups", "mesh")),
            P(None, "mesh"),
            P(None, "mesh"),
            P(None, "mesh"),
            P(),
            P("mesh"),
        ),
        out_specs=(P(None, None, ("groups", "mesh")), P(None, None, ("groups", "mesh"))),
        check_vma=False,
    )
```

```python
import functools
import math

import jax
import jax.numpy as jnp
from jax import lax
from jax.experimental import pallas as pl
from jax.experimental.pallas import tpu as pltpu
from jax.sharding import PartitionSpec as P

LANES = 128
FCT_FLOOR = 0.001
TABLE_ROWS = 24
VMEM_LIMIT = 32 * 1024 * 1024


def lane_gather(values, index):
    return jnp.take_along_axis(values, index, axis=1, mode="promise_in_bounds")


def spread(row, count):
    return jnp.broadcast_to(row, (count, LANES))


def lane_iota(rows):
    return lax.broadcasted_iota(jnp.int32, (rows, LANES), 1)


def row_iota(rows):
    return lax.broadcasted_iota(jnp.int32, (rows, LANES), 0)


def slot_rows(entry):
    peers, capacity = entry.shape
    wide = jnp.concatenate([entry, jnp.zeros((peers, LANES - capacity), jnp.int32)], axis=1)
    wide = lane_gather(wide, lane_iota(peers) % capacity)
    owner = row_iota(peers)
    out = []
    for half in range(peers * capacity // LANES):
        wanted = (lane_iota(peers) + half * LANES) // capacity
        picked = jnp.where(owner == wanted, wide, 0).astype(jnp.float32)
        out.append(jnp.sum(picked, axis=0, keepdims=True).astype(jnp.int32))
    return out


def half_mask(rows, lower):
    half = lane_iota(rows) // (LANES // 2)
    return half == jnp.where(lower, 0, 1)


def peer_rows(values, peers, capacity):
    lane = lane_iota(peers)
    group = lane // capacity
    block = jnp.clip(row_iota(peers) - 1 + group // 2, 0, peers - 1)
    entry = block * capacity + lane % capacity
    out = jnp.zeros((peers, LANES), jnp.float32)
    for part in range(2):
        for half, row in enumerate(values[part]):
            found = lane_gather(spread(row, peers), entry % LANES)
            wanted = (group < 6) & (group % 2 == part) & (entry // LANES == half)
            out = jnp.where(wanted, found, out)
    return out


def direction(dirs, padded):
    turn = row_iota(padded).astype(jnp.float32) * (2.0 * math.pi / dirs)
    return jnp.cos(turn), jnp.sin(turn)


def node_tables(
    me, dirs, near, angle, face, wind, slot, cosine, sine, project, choice, ways, slots
):
    edges, padded = project.shape[:2]
    cosine[...] = face[...] * jnp.cos(angle[...])
    sine[...] = face[...] * jnp.sin(angle[...])
    cos_dir, sin_dir = direction(dirs, padded)
    ways[0] = cos_dir
    ways[1] = sin_dir
    ways[2] = 0.25 * jnp.maximum(wind[0:1, :] * cos_dir + wind[1:2, :] * sin_dir, 0.0)
    taken = jnp.transpose(spread(slot[...].astype(jnp.float32), LANES))
    for half in range(slots.shape[1] // LANES):
        number = (lane_iota(LANES) + half * LANES).astype(jnp.float32)
        picked = jnp.where(taken == number, 1.0, 0.0).astype(jnp.bfloat16)
        slots[:, half * LANES : (half + 1) * LANES] = picked
    source = row_iota(LANES)
    minus = jnp.where(source == lane_iota(LANES), -1.0, 0.0)
    for s in range(edges):
        project[s] = cos_dir * cosine[s : s + 1, :] + sin_dir * sine[s : s + 1, :]
        target = near[s : s + 1, :]
        inside = target // LANES == me
        lane = target % LANES
        own = jnp.where(source == jnp.where(inside, lane, LANES), 1.0, 0.0) + minus
        halo = jnp.where(source == jnp.where(inside, LANES, lane), 1.0, 0.0)
        lanes = slice(s * LANES, (s + 1) * LANES)
        for k, part in enumerate((own, own, halo, halo)):
            choice[k * LANES : (k + 1) * LANES, lanes] = part.astype(jnp.bfloat16)


def split(x):
    first = x.astype(jnp.bfloat16)
    return first, (x - first.astype(jnp.float32)).astype(jnp.bfloat16)


def pack_kernel(
    spectra_in, tracers_in, potential_in, neighbors_in, normal_in, weight_in, current_in,
    send_rows, slot_in, near_in, angle_in, face_in, wind_in,
    rows_out, outer, inner, spectra, node_slot, near, angle, face, wind,
    tracers, potential, neighbors, normal, weight, coupled,
    current, sems,
):
    peers, _, capacity = send_rows.shape
    me = lax.axis_index("mesh")
    freqs, dirs = spectra_in.shape[:2]
    if dirs < spectra.shape[1]:
        for f in range(freqs):
            spectra[f, dirs // 8 * 8 :, :] = jnp.zeros((8, LANES), jnp.float32)
    pairs = freqs // 2
    copies = []
    for source, target in (
        (send_rows.at[me], coupled.at[1]),
        (current_in, current),
        (slot_in, node_slot),
        (spectra_in, spectra.at[:, 0:dirs, :]),
        (tracers_in, tracers),
        (potential_in, potential),
        (neighbors_in, neighbors),
        (normal_in, normal),
        (weight_in, weight),
        (send_rows.at[jnp.maximum(me - 1, 0)], coupled.at[0]),
        (send_rows.at[jnp.minimum(me + 1, peers - 1)], coupled.at[2]),
        (near_in, near),
        (angle_in, angle),
        (face_in, face),
        (wind_in, wind),
    ):
        copy = pltpu.make_async_copy(source, target, sems.at[len(copies)])
        copy.start()
        copies.append(copy)
    for copy in copies[:3]:
        copy.wait()
    layers, cells = potential.shape
    blocks = cells // LANES
    field_rows = (tracers.shape[0] + 1) * layers
    stacked = jnp.concatenate(
        [current[:, b * LANES : (b + 1) * LANES] for b in range(blocks)], axis=0
    )
    place = row_iota(2 * blocks)
    halves = slot_rows(coupled[1])
    values = [[], []]
    for cell in halves:
        found = lane_gather(stacked, spread(cell % LANES, 2 * blocks))
        for part in range(2):
            picked = jnp.where(place == 2 * (cell // LANES) + part, found, 0.0)
            values[part].append(jnp.sum(picked, axis=0, keepdims=True))
    rows_out[...] = peer_rows(values, peers, capacity)
    for copy in copies[4:9]:
        copy.wait()
    odd = me % 2 == 1
    for out, upward in ((outer, odd), (inner, jnp.logical_not(odd))):
        for b in range(2):
            high = slice((blocks - 2 + b) * LANES, (blocks - 1 + b) * LANES)
            low = slice(b * LANES, (b + 1) * LANES)
            base = b * field_rows
            for t in range(tracers.shape[0]):
                out[base + t * layers : base + (t + 1) * layers, :] = jnp.where(
                    upward, tracers[t, :, high], tracers[t, :, low]
                )
            out[base + field_rows - layers : base + field_rows, :] = jnp.where(
                upward, potential[:, high], potential[:, low]
            )
        high = slice((blocks - 1) * LANES, blocks * LANES)
        low = slice(0, LANES)
        base = 2 * field_rows
        out[base : base + TABLE_ROWS, :] = jnp.zeros((TABLE_ROWS, LANES), jnp.float32)
        edges = neighbors.shape[0]
        near = jnp.where(upward, neighbors[:, high], neighbors[:, low])
        out[base : base + edges, :] = near.astype(jnp.float32)
        out[base + edges : base + edges + 1, :] = node_slot[...].astype(jnp.float32)
        out[base + 8 : base + 8 + edges, :] = jnp.where(upward, normal[:, high], normal[:, low])
        out[base + 16 : base + 16 + edges, :] = jnp.where(upward, weight[:, high], weight[:, low])
    base = 2 * field_rows + TABLE_ROWS
    whole = dirs // 8 * 8
    rest = dirs - whole
    turns = half_mask(dirs, odd)
    copies[3].wait()
    for g in range(pairs):
        natural = spectra[g, 0:dirs, :]
        turned = pltpu.roll(spectra[g + pairs, 0:dirs, :], LANES // 2, 1)
        for out, mixed in (
            (outer, jnp.where(turns, turned, natural)),
            (inner, jnp.where(turns, natural, turned)),
        ):
            at = base + g * whole
            out[at : at + whole, :] = mixed[:whole]
            at = base + pairs * whole + g * rest
            out[at : at + rest, :] = mixed[whole:]
    at = base + pairs * dirs
    if at < outer.shape[0]:
        for out in (outer, inner):
            out[at:, :] = jnp.zeros((outer.shape[0] - at, LANES), jnp.float32)
    for copy in copies[9:]:
        copy.wait()


def choose(cells, first, lanes, matrix):
    place = (cells - first - LANES).astype(jnp.float32).astype(jnp.bfloat16)
    place = spread(place, LANES)
    one = jnp.ones((LANES, LANES), jnp.bfloat16)
    for k in range(2):
        source = (row_iota(LANES) + (2 * k - 1) * LANES).astype(jnp.float32)
        part = jnp.where(source.astype(jnp.bfloat16) == place, one, 0 * one)
        matrix[k * LANES : (k + 1) * LANES, lanes] = part


def stack_split(x):
    first, second = split(x)
    return jnp.concatenate([first, second], axis=0)


def prepare_kernel(
    dirs, step_rows,
    spectra, near, angle, face, wind, slot, tracers, potential, neighbors, normal, weight, coupled,
    cosine, sine, project, choice, ways, slots, own_change,
    fields, matrices, inside, cell_cosine, cell_sine, cell_scale, sums,
    pieces, beside,
):
    me = lax.axis_index("mesh")
    node_tables(
        me, dirs, near, angle, face, wind, slot, cosine, sine, project, choice, ways, slots
    )
    freqs, padded, _ = spectra.shape
    step = step_rows // padded

    def own_part(c, carry):
        own = spectra[pl.ds(c * step, step)].reshape(step_rows, LANES)
        own_change[pl.ds(pl.multiple_of(c * step_rows, 8), step_rows), :] = jnp.dot(
            jnp.concatenate(split(own), axis=1),
            choice[0 : 2 * LANES, :],
            preferred_element_type=jnp.float32,
        )
        return carry

    lax.fori_loop(0, freqs // step, own_part, 0)
    tracer_count, layers, cells = tracers.shape
    blocks = cells // LANES
    edges = neighbors.shape[0]
    field_rows = (tracer_count + 1) * layers
    for b in range(blocks):
        lanes = slice(b * LANES, (b + 1) * LANES)
        for t in range(tracer_count):
            fields[b, t * layers : (t + 1) * layers, :] = tracers[t, :, lanes]
        fields[b, field_rows - layers : field_rows, :] = potential[:, lanes]
        pieces[b] = stack_split(fields[b])
        w = weight[:, lanes]
        cell_scale[b, 0:edges, :] = w
        cell_cosine[b, 0:edges, :] = w * jnp.cos(normal[:, lanes])
        cell_sine[b, 0:edges, :] = w * jnp.sin(normal[:, lanes])
        for s in range(edges):
            choose(
                neighbors[s : s + 1, lanes],
                (me * blocks + b - 1) * LANES,
                slice(s * LANES, (s + 1) * LANES),
                matrices.at[b],
            )
    for b in range(blocks):
        parts = [pieces[k] for k in (b - 1, b + 1) if 0 <= k < blocks]
        rows = slice(LANES if b == 0 else 0, LANES if b == blocks - 1 else 2 * LANES)
        beside[...] = jnp.dot(
            jnp.concatenate(parts, axis=1), matrices[b, rows, :], preferred_element_type=jnp.float32
        )
        for s in range(edges):
            at = slice(s * LANES, (s + 1) * LANES)
            near = spread(neighbors[s : s + 1, b * LANES : (b + 1) * LANES], 8)
            same = near // LANES == me * blocks + b
            lane = near % LANES
            for row in range(0, field_rows, 8):
                own = fields[b, row : row + 8, :]
                other = (
                    beside[row : row + 8, at]
                    + beside[field_rows + row : field_rows + row + 8, at]
                )
                change = jnp.where(same, lane_gather(own, lane), other) - own
                if row >= field_rows - layers:
                    change = change * cell_scale[b, s : s + 1, :]
                inside[b, row : row + 8, at] = change
    for which in range(3):
        first = 0 if which != 0 else cells - LANES
        count = blocks if which == 1 else 1
        start = (0, 1, blocks + 1)[which]
        for half, names in enumerate(slot_rows(coupled[which])):
            named = jnp.transpose(spread(names, LANES).astype(jnp.float32))
            for b in range(count):
                cell = (lane_iota(LANES) + (first + b * LANES)).astype(jnp.float32)
                picked = jnp.where(named == cell, 1.0, 0.0).astype(jnp.bfloat16)
                lanes = slice((start + b) * LANES, (start + b + 1) * LANES)
                sums[half * LANES : (half + 1) * LANES, lanes] = picked


def node_currents(table, slot, which, capacity):
    peers = table.shape[0]
    owner = row_iota(peers) == slot // capacity
    out = []
    for part in range(2):
        lane = (2 * which + part) * capacity + slot % capacity
        found = jnp.where(owner, lane_gather(table, spread(lane, peers)), 0.0)
        out.append(jnp.sum(found, axis=0, keepdims=True))
    return out


def wave_kernel(
    capacity, step_pairs, dirs,
    spectra, outer, inner, table, node_slot, neighbors, cosine, sine, project, choice, ways, slots,
    own_change,
    spectra_new, rows_out, drift, halos, change_a, change_b,
):
    me = lax.axis_index("mesh")
    freqs, stride = spectra.shape[:2]
    edges = neighbors.shape[0]
    peers = table.shape[0]
    halves = peers * capacity // LANES
    pairs = freqs // 2
    whole = dirs // 8 * 8
    rest = dirs - whole
    base = outer.shape[0] - (pairs * dirs + 7) // 8 * 8

    odd = me % 2 == 1
    slot = node_slot[...]
    row = base - TABLE_ROWS + edges
    halo_slot = jnp.where(
        half_mask(1, odd), outer[row : row + 1, :], inner[row : row + 1, :]
    ).astype(jnp.int32)
    lower = lane_iota(1) < LANES // 2
    currents = table[...]
    own_x, own_y = node_currents(currents, slot, jnp.ones((1, LANES), jnp.int32), capacity)
    halo_x, halo_y = node_currents(currents, halo_slot, jnp.where(lower, 2, 0), capacity)

    target = neighbors[...]
    lane = target % LANES
    inside = target // LANES == me

    def beside(own, halo):
        a = lane_gather(spread(own, edges), lane)
        b = lane_gather(spread(halo, edges), lane)
        return jnp.where(inside, a, b)

    drift[0:edges, :] = (
        0.5 * (own_x + beside(own_x, halo_x)) * cosine[...]
        + 0.5 * (own_y + beside(own_y, halo_y)) * sine[...]
    )
    drifts = [spread(drift[s : s + 1, :], 8) for s in range(edges)]
    from_outer = half_mask(dirs, odd)
    halos[...] = jnp.zeros(halos.shape, jnp.float32)
    ratio = 1.0 / 1.1
    bands = [slice(r, r + 8) for r in range(0, stride, 8)]

    def gather(c, change):
        for i in range(step_pairs):
            g = c * step_pairs + i
            parts = []
            for message in (outer, inner):
                at = base + g * whole
                upper = message[at : at + whole, :]
                at = base + pairs * whole + g * rest
                left = message[at : at + rest, :]
                parts.append(jnp.concatenate([upper, left], axis=0))
            x, y = parts
            at = 2 * i * stride
            halos[at : at + dirs, :] = jnp.where(from_outer, x, y)
            at += stride
            halos[at : at + dirs, :] = pltpu.roll(jnp.where(from_outer, y, x), LANES // 2, 1)
        mixed = jnp.concatenate(split(halos[...]), axis=1)
        change[...] = jnp.dot(
            mixed, choice[2 * LANES : 4 * LANES, :], preferred_element_type=jnp.float32
        )

    def advect(c, change, first_speed, first_slow, total):
        total = list(total)
        speeds = []
        for i in range(step_pairs):
            speeds += [first_speed * ratio**i, first_speed * ratio ** (i + pairs)]
        slowness = []
        for i in range(step_pairs):
            slowness += [first_slow * ratio**-i, first_slow * ratio ** -(i + pairs)]
        relative = [[drift * slow for drift in drifts] for slow in slowness]
        relative_sum = [sum(each[1:], each[0]) for each in relative]
        for k, band in enumerate(bands):
            along = [project[s, band, :] for s in range(edges)]
            along_sum = sum(along[1:], along[0])
            for i in range(step_pairs):
                g = c * step_pairs + i
                for j, f in ((2 * i, g), (2 * i + 1, g + pairs)):
                    own = spectra[f, band, :]
                    at = j * stride + band.start
                    own_at = slice(f * stride + band.start, f * stride + band.stop)
                    flux = (along_sum + relative_sum[j]) * own
                    for s in range(edges):
                        down = jnp.minimum(along[s] + relative[j][s], 0.0)
                        lanes = slice(s * LANES, (s + 1) * LANES)
                        step = change[at : at + 8, lanes] + own_change[own_at, lanes]
                        flux = flux + down * step
                    value = own - speeds[j] * flux
                    spectra_new[f, band, :] = value
                    total[k] = total[k] + value
        return first_speed * ratio**step_pairs, first_slow * ratio**-step_pairs, tuple(total)

    zeros = tuple(jnp.zeros((8, LANES), jnp.float32) for _ in bands)
    chunks = pairs // step_pairs
    buffers = (change_a, change_b)
    carry = (1.0, 1.0, zeros)
    gather(0, change_a)
    for c in range(chunks):
        if c + 1 < chunks:
            gather(c + 1, buffers[(c + 1) % 2])
        carry = advect(c, buffers[c % 2], *carry)
    total = carry[2]
    total = jnp.concatenate(total, axis=0)
    zero = jnp.zeros((stride, LANES), jnp.float32)
    cos_dir, sin_dir = ways[0], ways[1]
    mean = jnp.sum(total, axis=0, keepdims=True) * (1.0 / (freqs * dirs))
    step = jnp.exp((ways[2] - 2.0 * mean) * (1.0 / freqs))
    run = 10 if freqs % 10 == 0 else 1

    def grow(c, carry):
        factor, weighted = carry
        for i in range(run):
            f = c * run + i
            factor = factor * step
            evolved = spectra_new[f] * factor
            spectra_new[f] = evolved
            kappa = (f + 1).astype(jnp.float32) * (1.0 / freqs)
            weighted = weighted + kappa * evolved
        return factor, weighted

    _, weighted = lax.fori_loop(0, freqs // run, grow, (zero + 1.0, zero))
    stokes = jnp.concatenate(
        [
            jnp.sum(weighted * cos_dir, axis=0, keepdims=True),
            jnp.sum(weighted * sin_dir, axis=0, keepdims=True),
        ],
        axis=0,
    ) * (1.0 / dirs)
    in_order = jnp.dot(
        three_parts(stokes), slots[...], preferred_element_type=jnp.float32
    )
    in_order = in_order[0:2] + (in_order[2:4] + in_order[4:6])
    values = [
        [in_order[part : part + 1, h * LANES : (h + 1) * LANES] for h in range(halves)]
        for part in range(2)
    ]
    rows_out[...] = peer_rows(values, peers, capacity)


def three_parts(values):
    first = values.astype(jnp.bfloat16).astype(jnp.float32)
    left = values - first
    second = left.astype(jnp.bfloat16).astype(jnp.float32)
    third = left - second
    pad = jnp.zeros((10, values.shape[1]), jnp.float32)
    return jnp.concatenate([first, second, third, pad], axis=0).astype(jnp.bfloat16)


def tracer_kernel(
    capacity, shape,
    outer, inner, table, fields, neighbors, matrices, inside, cosine, sine, scale, sums, spectra,
    tracers_new, spectra_out,
    halo, halo_near, halo_tables, stokes, antiflux, lowered, ratios,
    ratio_pieces, steps_a, steps_b, sem,
):
    dirs = spectra_out.shape[1]
    write = pltpu.make_async_copy(spectra.at[:, 0:dirs, :], spectra_out, sem)
    write.start()
    me = lax.axis_index("mesh")
    tracer_count, layers, edges = shape
    peers = table.shape[0]
    halves = peers * capacity // LANES
    blocks, field_rows, _ = fields.shape
    layer_groups = layers // 8
    tracer_groups = tracer_count * layer_groups
    odd = me % 2 == 1

    for b in range(2):
        x = outer[b * field_rows : (b + 1) * field_rows, :]
        y = inner[b * field_rows : (b + 1) * field_rows, :]
        for side, value in ((0, jnp.where(odd, y, x)), (1, jnp.where(odd, x, y))):
            halo[2 * side + b] = value
    at = 2 * field_rows
    x = outer[at : at + TABLE_ROWS, :]
    y = inner[at : at + TABLE_ROWS, :]
    for side, rows in ((0, jnp.where(odd, y, x)), (1, jnp.where(odd, x, y))):
        w = rows[16 : 16 + edges]
        halo_tables[side, 0, 0:edges, :] = w
        halo_tables[side, 1, 0:edges, :] = w * jnp.cos(rows[8 : 8 + edges])
        halo_tables[side, 2, 0:edges, :] = w * jnp.sin(rows[8 : 8 + edges])
        halo_near[side, 0:edges, :] = rows[0:edges].astype(jnp.int32)

    received = table[...]
    lane_of = lane_iota(peers)
    sections = []
    for which in range(3):
        values = []
        for part in range(2):
            lane = (2 * which + part) * capacity + lane_of % capacity
            found = lane_gather(received, lane)
            row = []
            for half in range(halves):
                mine = row_iota(peers) == (lane_of + half * LANES) // capacity
                row.append(jnp.sum(jnp.where(mine, found, 0.0), axis=0, keepdims=True))
            values.append(jnp.concatenate(row, axis=1))
        sections.append(three_parts(jnp.concatenate(values, axis=0)))
    total = jnp.dot(
        jnp.concatenate(sections, axis=0), sums[...], preferred_element_type=jnp.float32
    )
    for b in range(blocks + 2):
        which = 0 if b == 0 else 2 if b == blocks + 1 else 1
        at = 16 * which
        lanes = slice(b * LANES, (b + 1) * LANES)
        first, second, third = (total[at + k : at + k + 2, lanes] for k in (0, 2, 4))
        stokes[b, 0:2, :] = first + (second + third)

    decay = [
        jnp.exp(-3.0 / layers * (row_iota(8) + 8 * g).astype(jnp.float32))
        for g in range(layer_groups)
    ]

    def low_order(b, value, change, wx, wy, keep):
        slope = wx * stokes[b, 0:1, :] + wy * stokes[b, 1:2, :]
        own = [value(8 * g) for g in range(tracer_groups)]
        zero = jnp.zeros((8, LANES), jnp.float32)
        speed_sum = [zero] * layer_groups
        inflow = [zero] * tracer_groups
        highest = [zero] * tracer_groups
        lowest = [zero] * tracer_groups
        positive = [zero] * tracer_groups
        negative = [zero] * tracer_groups
        for s in range(edges):
            slope8 = spread(slope[s : s + 1, :], 8)
            for lg in range(layer_groups):
                speed = change(8 * (tracer_groups + lg), s) + decay[lg] * slope8
                down = jnp.minimum(speed, 0.0)
                half = 0.5 * speed - down
                speed_sum[lg] = speed_sum[lg] + speed
                for t in range(tracer_count):
                    g = t * layer_groups + lg
                    step = change(8 * g, s)
                    flux = half * step
                    if keep:
                        antiflux[b - 1, s, 8 * g : 8 * g + 8, :] = flux
                    inflow[g] = inflow[g] + down * step
                    highest[g] = jnp.maximum(highest[g], step)
                    lowest[g] = jnp.minimum(lowest[g], step)
                    positive[g] = positive[g] + jnp.maximum(flux, 0.0)
                    negative[g] = negative[g] - jnp.minimum(flux, 0.0)
        plus, minus = [], []
        for g in range(tracer_groups):
            loss = speed_sum[g % layer_groups] * own[g] + inflow[g]
            if keep:
                lowered[b - 1, 8 * g : 8 * g + 8, :] = own[g] - loss
            up = jnp.maximum(highest[g] + loss, 0.0) / (negative[g] + FCT_FLOOR)
            down = jnp.maximum(-loss - lowest[g], 0.0) / (positive[g] + FCT_FLOOR)
            plus.append(jnp.minimum(1.0, up))
            minus.append(jnp.minimum(1.0, down))
        both = jnp.concatenate(plus + minus, axis=0)
        ratios[b] = both
        ratio_pieces[b] = stack_split(both)

    def band(ref, *index):
        return lambda row: ref[(*index, slice(row, row + 8), slice(None))]

    potential_row = tracer_groups * 8

    def within(i):
        return lambda row, s: inside[i, row : row + 8, s * LANES : (s + 1) * LANES]

    def edge(i, side):
        beside = halo.at[1 + side]
        sign = 2 * side - 1

        def change(row, s):
            near = spread(neighbors[s : s + 1, i * LANES : (i + 1) * LANES], 8)
            from_halo = near // LANES - (me * blocks + i) == sign
            picked = lane_gather(beside[row : row + 8, :], near % LANES)
            if row >= potential_row:
                picked = picked * spread(scale[i, s : s + 1, :], 8)
            return within(i)(row, s) + jnp.where(from_halo, picked, 0.0)

        return change

    def outside(side):
        i = side * (blocks - 1)
        low, own, high = (
            (halo.at[0], halo.at[1], fields.at[i]),
            (fields.at[i], halo.at[2], halo.at[3]),
        )[side]

        def change(row, s):
            rows = slice(row, row + 8)
            near = spread(halo_near[side, s : s + 1, :], 8)
            place = near // LANES - (me * blocks + i + 2 * side - 1)
            lane = near % LANES
            mine = own[rows, :]
            middle = lane_gather(mine, lane)
            left = lane_gather(low[rows, :], lane)
            right = lane_gather(high[rows, :], lane)
            out = jnp.where(place == 0, middle, jnp.where(place < 0, left, right)) - mine
            if row >= potential_row:
                out = out * spread(halo_tables[side, 0, s : s + 1, :], 8)
            return out

        return change

    for i in range(1, blocks - 1):
        low_order(i + 1, band(fields, i), within(i), cosine[i], sine[i], True)
    for side in range(2):
        b = side * (blocks + 1)
        tables = (halo_tables[side, 1], halo_tables[side, 2])
        low_order(b, band(halo, 1 + side), outside(side), *tables, False)
        i = side * (blocks - 1)
        low_order(i + 1, band(fields, i), edge(i, side), cosine[i], sine[i], True)

    def products(i, steps):
        mixed = jnp.concatenate([ratio_pieces[i], ratio_pieces[i + 2]], axis=1)
        steps[...] = jnp.dot(mixed, matrices[i], preferred_element_type=jnp.float32)

    def limit(i, steps):
        out = [lowered[i, 8 * g : 8 * g + 8, :] for g in range(tracer_groups)]
        own = [ratios[i + 1, 8 * g : 8 * g + 8, :] for g in range(2 * tracer_groups)]
        low = 16 * tracer_groups
        for s in range(edges):
            lanes = slice(s * LANES, (s + 1) * LANES)
            near = spread(neighbors[s : s + 1, i * LANES : (i + 1) * LANES], 8)
            same = near // LANES == me * blocks + i
            lane = near % LANES
            beside = [
                jnp.where(
                    same,
                    lane_gather(own[g], lane),
                    steps[8 * g : 8 * g + 8, lanes] + steps[low + 8 * g : low + 8 * g + 8, lanes],
                )
                for g in range(2 * tracer_groups)
            ]
            for g in range(tracer_groups):
                m = g + tracer_groups
                flux = antiflux[i, s, 8 * g : 8 * g + 8, :]
                factor = jnp.where(
                    flux >= 0.0, jnp.minimum(own[m], beside[g]), jnp.minimum(own[g], beside[m])
                )
                out[g] = out[g] - factor * flux
        lanes = slice(i * LANES, (i + 1) * LANES)
        for g in range(tracer_groups):
            t, lg = g // layer_groups, g % layer_groups
            tracers_new[t, 8 * lg : 8 * lg + 8, lanes] = out[g]

    buffers = (steps_a, steps_b)
    products(0, steps_a)
    for i in range(blocks):
        if i + 1 < blocks:
            products(i + 1, buffers[(i + 1) % 2])
        limit(i, buffers[i % 2])
    write.wait()


def swap(message, first, peers):
    pairs = []
    for i in range(first, peers - 1, 2):
        pairs += [(i, i + 1), (i + 1, i)]
    return lax.ppermute(message, "mesh", pairs)


def whole_spec():
    return pl.BlockSpec(memory_space=pltpu.VMEM)


def local(
    tracers,
    potential,
    surface_current,
    cell_neighbors,
    cell_normal,
    cell_weight,
    spectra,
    wind_velocity,
    node_neighbors,
    node_normal,
    node_weight,
    send_rows,
    node_slot,
):
    peers, _, capacity = send_rows.shape
    freqs, dirs, nodes = spectra.shape
    tracer_count, layers, cells = tracers.shape
    edges = cell_neighbors.shape[0]
    blocks = cells // LANES
    field_rows = (tracer_count + 1) * layers
    head_rows = 2 * field_rows + TABLE_ROWS
    message_rows = head_rows + (freqs // 2 * dirs + 7) // 8 * 8
    slots = node_slot.reshape(1, nodes)
    params = pltpu.CompilerParams(vmem_limit_bytes=VMEM_LIMIT)
    f32 = jnp.float32

    stored = pl.BlockSpec(memory_space=pltpu.HBM)
    rows = tracer_count * layers
    stride = (dirs + 7) // 8 * 8
    step_pairs = 5 if freqs % 10 == 0 else 1
    step_rows = 2 * step_pairs * stride

    def like(x):
        return jax.ShapeDtypeStruct(x.shape, x.dtype)

    def shaped(*shape, dtype=f32):
        return jax.ShapeDtypeStruct(shape, dtype)

    def call(kernel, name, inputs, outputs, scratch, out_specs=None):
        return pl.pallas_call(
            kernel,
            out_shape=outputs,
            in_specs=[whole_spec()] * len(inputs),
            out_specs=out_specs or (whole_spec(),) * len(outputs),
            scratch_shapes=scratch,
            compiler_params=params,
            name=name,
        )(*inputs)

    inputs = (
        spectra, tracers, potential, cell_neighbors, cell_normal, cell_weight, surface_current,
        send_rows, slots, node_neighbors, node_normal, node_weight, wind_velocity,
    )
    (
        currents, outer, inner, own_spectra, own_slots, near, angle, face, wind,
        own_tracers, own_potential, neighbors, normal, weight, coupled,
    ) = pl.pallas_call(
        pack_kernel,
        out_shape=(
            shaped(peers, LANES),
            shaped(message_rows, LANES),
            shaped(message_rows, LANES),
            shaped(freqs, stride, LANES),
            like(slots),
            like(node_neighbors),
            like(node_normal),
            like(node_weight),
            like(wind_velocity),
            like(tracers),
            like(potential),
            like(cell_neighbors),
            like(cell_normal),
            like(cell_weight),
            shaped(3, peers, capacity, dtype=jnp.int32),
        ),
        in_specs=[stored] * len(inputs),
        out_specs=(whole_spec(),) * 15,
        scratch_shapes=[
            pltpu.VMEM(surface_current.shape, f32),
            pltpu.SemaphoreType.DMA((15,)),
        ],
        compiler_params=params,
        name="pack",
    )(*(pltpu.with_memory_space_constraint(x, pltpu.HBM) for x in inputs))
    outer = swap(outer, 1, peers)
    inner = swap(inner, 0, peers)

    (
        cosine, sine, project, choice, ways, slot_choice, own_change,
        fields, matrices, inside, cell_cosine, cell_sine, cell_scale, sums,
    ) = call(
        functools.partial(prepare_kernel, dirs, step_rows),
        "prepare",
        (
            own_spectra, near, angle, face, wind, own_slots, own_tracers, own_potential,
            neighbors, normal, weight, coupled,
        ),
        (
            like(node_normal),
            like(node_normal),
            shaped(edges, stride, LANES),
            shaped(4 * LANES, edges * LANES, dtype=jnp.bfloat16),
            shaped(3, stride, LANES),
            shaped(nodes, peers * capacity, dtype=jnp.bfloat16),
            shaped(freqs * stride, edges * LANES),
            shaped(blocks, field_rows, LANES),
            shaped(blocks, 2 * LANES, edges * LANES, dtype=jnp.bfloat16),
            shaped(blocks, field_rows, edges * LANES),
            shaped(blocks, 8, LANES),
            shaped(blocks, 8, LANES),
            shaped(blocks, 8, LANES),
            shaped(peers * capacity, (blocks + 2) * LANES, dtype=jnp.bfloat16),
        ),
        [
            pltpu.VMEM((blocks, 2 * field_rows, LANES), jnp.bfloat16),
            pltpu.VMEM((2 * field_rows, edges * LANES), f32),
        ],
    )
    currents, cosine = lax.optimization_barrier((currents, cosine))
    currents = lax.all_to_all(currents, "mesh", 0, 0, tiled=True)

    spectra_new, stokes_rows = call(
        functools.partial(wave_kernel, capacity, step_pairs, dirs),
        "wave",
        (
            own_spectra, outer, inner, currents, own_slots, near,
            cosine, sine, project, choice, ways, slot_choice, own_change,
        ),
        (shaped(freqs, stride, LANES), shaped(peers, LANES)),
        [
            pltpu.VMEM((8, LANES), f32),
            pltpu.VMEM((step_rows, LANES), f32),
            pltpu.VMEM((step_rows, edges * LANES), f32),
            pltpu.VMEM((step_rows, edges * LANES), f32),
        ],
    )
    stokes_all = lax.all_to_all(stokes_rows, "mesh", 0, 0, tiled=True)

    return call(
        functools.partial(tracer_kernel, capacity, (tracer_count, layers, edges)),
        "tracer",
        (
            outer, inner, stokes_all, fields, neighbors, matrices, inside, cell_cosine, cell_sine,
            cell_scale, sums, pltpu.with_memory_space_constraint(spectra_new, pltpu.VMEM),
        ),
        (like(tracers), like(spectra)),
        [
            pltpu.VMEM((4, field_rows, LANES), f32),
            pltpu.VMEM((2, 8, LANES), jnp.int32),
            pltpu.VMEM((2, 3, 8, LANES), f32),
            pltpu.VMEM((blocks + 2, 8, LANES), f32),
            pltpu.VMEM((blocks, edges, rows, LANES), f32),
            pltpu.VMEM((blocks, rows, LANES), f32),
            pltpu.VMEM((blocks + 2, 2 * rows, LANES), f32),
            pltpu.VMEM((blocks + 2, 4 * rows, LANES), jnp.bfloat16),
            pltpu.VMEM((4 * rows, edges * LANES), f32),
            pltpu.VMEM((4 * rows, edges * LANES), f32),
            pltpu.SemaphoreType.DMA(()),
        ],
        out_specs=(whole_spec(), stored),
    )


def solution(mesh):
    return jax.shard_map(
        local,
        mesh=mesh,
        in_specs=(
            P(None, None, ("groups", "mesh")),
            P(None, ("groups", "mesh")),
            P(None, ("groups", "mesh")),
            P(None, "mesh"),
            P(None, "mesh"),
            P(None, "mesh"),
            P(None, None, ("groups", "mesh")),
            P(None, ("groups", "mesh")),
            P(None, "mesh"),
            P(None, "mesh"),
            P(None, "mesh"),
            P(),
            P("mesh"),
        ),
        out_specs=(P(None, None, ("groups", "mesh")), P(None, None, ("groups", "mesh"))),
        check_vma=False,
    )
```

```python
import functools
import math

import jax
import jax.numpy as jnp
from jax import lax
from jax.experimental import pallas as pl
from jax.experimental.pallas import tpu as pltpu
from jax.sharding import PartitionSpec as P

LANES = 128
FCT_FLOOR = 0.001
TABLE_ROWS = 24
VMEM_LIMIT = 32 * 1024 * 1024


def lane_gather(values, index):
    return jnp.take_along_axis(values, index, axis=1, mode="promise_in_bounds")


def spread(row, count):
    return jnp.broadcast_to(row, (count, LANES))


def lane_iota(rows):
    return lax.broadcasted_iota(jnp.int32, (rows, LANES), 1)


def row_iota(rows):
    return lax.broadcasted_iota(jnp.int32, (rows, LANES), 0)


def slot_rows(entry):
    peers, capacity = entry.shape
    wide = jnp.concatenate([entry, jnp.zeros((peers, LANES - capacity), jnp.int32)], axis=1)
    wide = lane_gather(wide, lane_iota(peers) % capacity)
    owner = row_iota(peers)
    out = []
    for half in range(peers * capacity // LANES):
        wanted = (lane_iota(peers) + half * LANES) // capacity
        picked = jnp.where(owner == wanted, wide, 0).astype(jnp.float32)
        out.append(jnp.sum(picked, axis=0, keepdims=True).astype(jnp.int32))
    return out


def half_mask(rows, lower):
    half = lane_iota(rows) // (LANES // 2)
    return half == jnp.where(lower, 0, 1)


def peer_rows(values, peers, capacity):
    lane = lane_iota(peers)
    group = lane // capacity
    block = jnp.clip(row_iota(peers) - 1 + group // 2, 0, peers - 1)
    entry = block * capacity + lane % capacity
    out = jnp.zeros((peers, LANES), jnp.float32)
    for part in range(2):
        for half, row in enumerate(values[part]):
            found = lane_gather(spread(row, peers), entry % LANES)
            wanted = (group < 6) & (group % 2 == part) & (entry // LANES == half)
            out = jnp.where(wanted, found, out)
    return out


def direction(dirs, padded):
    turn = row_iota(padded).astype(jnp.float32) * (2.0 * math.pi / dirs)
    return jnp.cos(turn), jnp.sin(turn)


def node_tables(
    me, dirs, near, angle, face, wind, slot, cosine, sine, project, choice, ways, slots
):
    edges, padded = project.shape[:2]
    cosine[...] = face[...] * jnp.cos(angle[...])
    sine[...] = face[...] * jnp.sin(angle[...])
    cos_dir, sin_dir = direction(dirs, padded)
    ways[0] = cos_dir
    ways[1] = sin_dir
    ways[2] = 0.25 * jnp.maximum(wind[0:1, :] * cos_dir + wind[1:2, :] * sin_dir, 0.0)
    taken = jnp.transpose(spread(slot[...].astype(jnp.float32), LANES))
    for half in range(slots.shape[1] // LANES):
        number = (lane_iota(LANES) + half * LANES).astype(jnp.float32)
        picked = jnp.where(taken == number, 1.0, 0.0).astype(jnp.bfloat16)
        slots[:, half * LANES : (half + 1) * LANES] = picked
    source = row_iota(LANES)
    minus = jnp.where(source == lane_iota(LANES), -1.0, 0.0)
    for s in range(edges):
        project[s] = cos_dir * cosine[s : s + 1, :] + sin_dir * sine[s : s + 1, :]
        target = near[s : s + 1, :]
        inside = target // LANES == me
        lane = target % LANES
        own = jnp.where(source == jnp.where(inside, lane, LANES), 1.0, 0.0) + minus
        halo = jnp.where(source == jnp.where(inside, LANES, lane), 1.0, 0.0)
        lanes = slice(s * LANES, (s + 1) * LANES)
        for k, part in enumerate((own, own, halo, halo)):
            choice[k * LANES : (k + 1) * LANES, lanes] = part.astype(jnp.bfloat16)


def split(x):
    first = x.astype(jnp.bfloat16)
    return first, (x - first.astype(jnp.float32)).astype(jnp.bfloat16)


def pack_kernel(
    spectra_in, tracers_in, potential_in, neighbors_in, normal_in, weight_in, current_in,
    send_rows, slot_in, near_in, angle_in, face_in, wind_in,
    rows_out, outer, inner, spectra, node_slot, near, angle, face, wind,
    tracers, potential, neighbors, normal, weight, coupled,
    current, sems,
):
    peers, _, capacity = send_rows.shape
    me = lax.axis_index("mesh")
    freqs, dirs = spectra_in.shape[:2]
    if dirs < spectra.shape[1]:
        for f in range(freqs):
            spectra[f, dirs // 8 * 8 :, :] = jnp.zeros((8, LANES), jnp.float32)
    pairs = freqs // 2
    copies = []
    for source, target in (
        (send_rows.at[me], coupled.at[1]),
        (current_in, current),
        (slot_in, node_slot),
        (spectra_in, spectra.at[:, 0:dirs, :]),
        (tracers_in, tracers),
        (potential_in, potential),
        (neighbors_in, neighbors),
        (normal_in, normal),
        (weight_in, weight),
        (send_rows.at[jnp.maximum(me - 1, 0)], coupled.at[0]),
        (send_rows.at[jnp.minimum(me + 1, peers - 1)], coupled.at[2]),
        (near_in, near),
        (angle_in, angle),
        (face_in, face),
        (wind_in, wind),
    ):
        copy = pltpu.make_async_copy(source, target, sems.at[len(copies)])
        copy.start()
        copies.append(copy)
    for copy in copies[:3]:
        copy.wait()
    layers, cells = potential.shape
    blocks = cells // LANES
    field_rows = (tracers.shape[0] + 1) * layers
    stacked = jnp.concatenate(
        [current[:, b * LANES : (b + 1) * LANES] for b in range(blocks)], axis=0
    )
    place = row_iota(2 * blocks)
    halves = slot_rows(coupled[1])
    values = [[], []]
    for cell in halves:
        found = lane_gather(stacked, spread(cell % LANES, 2 * blocks))
        for part in range(2):
            picked = jnp.where(place == 2 * (cell // LANES) + part, found, 0.0)
            values[part].append(jnp.sum(picked, axis=0, keepdims=True))
    rows_out[...] = peer_rows(values, peers, capacity)
    for copy in copies[4:9]:
        copy.wait()
    odd = me % 2 == 1
    for out, upward in ((outer, odd), (inner, jnp.logical_not(odd))):
        for b in range(2):
            high = slice((blocks - 2 + b) * LANES, (blocks - 1 + b) * LANES)
            low = slice(b * LANES, (b + 1) * LANES)
            base = b * field_rows
            for t in range(tracers.shape[0]):
                out[base + t * layers : base + (t + 1) * layers, :] = jnp.where(
                    upward, tracers[t, :, high], tracers[t, :, low]
                )
            out[base + field_rows - layers : base + field_rows, :] = jnp.where(
                upward, potential[:, high], potential[:, low]
            )
        high = slice((blocks - 1) * LANES, blocks * LANES)
        low = slice(0, LANES)
        base = 2 * field_rows
        out[base : base + TABLE_ROWS, :] = jnp.zeros((TABLE_ROWS, LANES), jnp.float32)
        edges = neighbors.shape[0]
        near = jnp.where(upward, neighbors[:, high], neighbors[:, low])
        out[base : base + edges, :] = near.astype(jnp.float32)
        out[base + edges : base + edges + 1, :] = node_slot[...].astype(jnp.float32)
        out[base + 8 : base + 8 + edges, :] = jnp.where(upward, normal[:, high], normal[:, low])
        out[base + 16 : base + 16 + edges, :] = jnp.where(upward, weight[:, high], weight[:, low])
    base = 2 * field_rows + TABLE_ROWS
    whole = dirs // 8 * 8
    rest = dirs - whole
    turns = half_mask(dirs, odd)
    copies[3].wait()
    for g in range(pairs):
        natural = spectra[g, 0:dirs, :]
        turned = pltpu.roll(spectra[g + pairs, 0:dirs, :], LANES // 2, 1)
        for out, mixed in (
            (outer, jnp.where(turns, turned, natural)),
            (inner, jnp.where(turns, natural, turned)),
        ):
            at = base + g * whole
            out[at : at + whole, :] = mixed[:whole]
            at = base + pairs * whole + g * rest
            out[at : at + rest, :] = mixed[whole:]
    at = base + pairs * dirs
    if at < outer.shape[0]:
        for out in (outer, inner):
            out[at:, :] = jnp.zeros((outer.shape[0] - at, LANES), jnp.float32)
    for copy in copies[9:]:
        copy.wait()


def choose(cells, first, lanes, matrix):
    place = (cells - first - LANES).astype(jnp.float32).astype(jnp.bfloat16)
    place = spread(place, LANES)
    one = jnp.ones((LANES, LANES), jnp.bfloat16)
    for k in range(3):
        source = (row_iota(LANES) + (k - 1) * LANES).astype(jnp.float32).astype(jnp.bfloat16)
        part = jnp.where(source == place, one, 0 * one)
        if k == 1:
            own = jnp.where(row_iota(LANES) == lane_iota(LANES), 1.0, 0.0).astype(jnp.bfloat16)
            part = part - own
        matrix[k * LANES : (k + 1) * LANES, lanes] = part


def stack_split(x):
    first, second = split(x)
    return jnp.concatenate([first, second], axis=0)


def differences(parts, matrix):
    mixed = jnp.concatenate(parts, axis=1)
    out = jnp.dot(mixed, matrix, preferred_element_type=jnp.float32)
    rows = out.shape[0] // 2
    return out[:rows] + out[rows:]


def prepare_kernel(
    dirs, step_rows,
    spectra, near, angle, face, wind, slot, tracers, potential, neighbors, normal, weight, coupled,
    cosine, sine, project, choice, ways, slots, own_change,
    fields, matrices, inside, cell_cosine, cell_sine, cell_scale, sums,
    pieces,
):
    me = lax.axis_index("mesh")
    node_tables(
        me, dirs, near, angle, face, wind, slot, cosine, sine, project, choice, ways, slots
    )
    freqs, padded, _ = spectra.shape
    step = step_rows // padded

    def own_part(c, carry):
        own = spectra[pl.ds(c * step, step)].reshape(step_rows, LANES)
        own_change[pl.ds(pl.multiple_of(c * step_rows, 8), step_rows), :] = jnp.dot(
            jnp.concatenate(split(own), axis=1),
            choice[0 : 2 * LANES, :],
            preferred_element_type=jnp.float32,
        )
        return carry

    lax.fori_loop(0, freqs // step, own_part, 0)
    tracer_count, layers, cells = tracers.shape
    blocks = cells // LANES
    edges = neighbors.shape[0]
    field_rows = (tracer_count + 1) * layers
    for b in range(blocks):
        lanes = slice(b * LANES, (b + 1) * LANES)
        for t in range(tracer_count):
            fields[b, t * layers : (t + 1) * layers, :] = tracers[t, :, lanes]
        fields[b, field_rows - layers : field_rows, :] = potential[:, lanes]
        pieces[b] = stack_split(fields[b])
        w = weight[:, lanes]
        cell_scale[b, 0:edges, :] = w
        cell_cosine[b, 0:edges, :] = w * jnp.cos(normal[:, lanes])
        cell_sine[b, 0:edges, :] = w * jnp.sin(normal[:, lanes])
        for s in range(edges):
            choose(
                neighbors[s : s + 1, lanes],
                (me * blocks + b - 1) * LANES,
                slice(s * LANES, (s + 1) * LANES),
                matrices.at[b],
            )
    for b in range(blocks):
        first, last = max(b - 1, 0), min(b + 1, blocks - 1)
        rows = slice((first - b + 1) * LANES, (last - b + 2) * LANES)
        parts = [pieces[k] for k in range(first, last + 1)]
        change = differences(parts, matrices[b, rows, :])
        last_field = field_rows - layers
        inside[b, 0:last_field, :] = change[:last_field]
        for s in range(edges):
            at = slice(s * LANES, (s + 1) * LANES)
            inside[b, last_field:, at] = change[last_field:, at] * cell_scale[b, s : s + 1, :]
    for which in range(3):
        first = 0 if which != 0 else cells - LANES
        count = blocks if which == 1 else 1
        start = (0, 1, blocks + 1)[which]
        for half, names in enumerate(slot_rows(coupled[which])):
            named = jnp.transpose(spread(names, LANES).astype(jnp.float32))
            for b in range(count):
                cell = (lane_iota(LANES) + (first + b * LANES)).astype(jnp.float32)
                picked = jnp.where(named == cell, 1.0, 0.0).astype(jnp.bfloat16)
                lanes = slice((start + b) * LANES, (start + b + 1) * LANES)
                sums[half * LANES : (half + 1) * LANES, lanes] = picked


def node_currents(table, slot, which, capacity):
    peers = table.shape[0]
    owner = row_iota(peers) == slot // capacity
    out = []
    for part in range(2):
        lane = (2 * which + part) * capacity + slot % capacity
        found = jnp.where(owner, lane_gather(table, spread(lane, peers)), 0.0)
        out.append(jnp.sum(found, axis=0, keepdims=True))
    return out


def halo_tasks(
    layers, outer, inner, fields, neighbors, inside, scale,
    halo, tables, edge_change, halo_change, near_cells,
):
    me = lax.axis_index("mesh")
    odd = me % 2 == 1
    blocks, field_rows, _ = fields.shape
    edges = neighbors.shape[0]
    for b in range(2):
        x = outer[b * field_rows : (b + 1) * field_rows, :]
        y = inner[b * field_rows : (b + 1) * field_rows, :]
        halo[b] = jnp.where(odd, y, x)
        halo[2 + b] = jnp.where(odd, x, y)
    at = 2 * field_rows
    x = outer[at : at + TABLE_ROWS, :]
    y = inner[at : at + TABLE_ROWS, :]
    for side, rows in ((0, jnp.where(odd, y, x)), (1, jnp.where(odd, x, y))):
        w = rows[16 : 16 + edges]
        tables[side, 0, 0:edges, :] = w
        tables[side, 1, 0:edges, :] = w * jnp.cos(rows[8 : 8 + edges])
        tables[side, 2, 0:edges, :] = w * jnp.sin(rows[8 : 8 + edges])
        near_cells[side, 0:edges, :] = rows[0:edges].astype(jnp.int32)

    def task(side, s):
        i = side * (blocks - 1)
        lanes = slice(s * LANES, (s + 1) * LANES)
        low, own, high = (
            (halo.at[0], halo.at[1], fields.at[i]),
            (fields.at[i], halo.at[2], halo.at[3]),
        )[side]
        near = spread(neighbors[s : s + 1, i * LANES : (i + 1) * LANES], 8)
        from_halo = near // LANES - (me * blocks + i) == 2 * side - 1
        lane = near % LANES
        far = spread(near_cells[side, s : s + 1, :], 8)
        place = far // LANES - (me * blocks + i + 2 * side - 1)
        far_lane = far % LANES
        for row in range(0, field_rows, 8):
            rows = slice(row, row + 8)
            mine = own[rows, :]
            picked = lane_gather(mine, lane)
            middle = lane_gather(mine, far_lane)
            left = lane_gather(low[rows, :], far_lane)
            right = lane_gather(high[rows, :], far_lane)
            out = jnp.where(place == 0, middle, jnp.where(place < 0, left, right)) - mine
            if row >= field_rows - layers:
                picked = picked * spread(scale[i, s : s + 1, :], 8)
                out = out * spread(tables[side, 0, s : s + 1, :], 8)
            halo_change[side, rows, lanes] = out
            edge_change[side, rows, lanes] = inside[i, rows, lanes] + jnp.where(
                from_halo, picked, 0.0
            )

    return [functools.partial(task, side, s) for s in range(edges) for side in range(2)]


def wave_kernel(
    capacity, step_pairs, dirs, layers,
    spectra, outer, inner, table, node_slot, neighbors, cosine, sine, project, choice, ways, slots,
    own_change, fields, cell_neighbors, cell_inside, scale,
    spectra_new, rows_out, halo, tables, edge_change, halo_change,
    drift, halos, change_a, change_b, near_cells,
):
    me = lax.axis_index("mesh")
    freqs, stride = spectra.shape[:2]
    edges = neighbors.shape[0]
    peers = table.shape[0]
    halves = peers * capacity // LANES
    pairs = freqs // 2
    whole = dirs // 8 * 8
    rest = dirs - whole
    base = outer.shape[0] - (pairs * dirs + 7) // 8 * 8

    odd = me % 2 == 1
    slot = node_slot[...]
    row = base - TABLE_ROWS + edges
    halo_slot = jnp.where(
        half_mask(1, odd), outer[row : row + 1, :], inner[row : row + 1, :]
    ).astype(jnp.int32)
    lower = lane_iota(1) < LANES // 2
    currents = table[...]
    own_x, own_y = node_currents(currents, slot, jnp.ones((1, LANES), jnp.int32), capacity)
    halo_x, halo_y = node_currents(currents, halo_slot, jnp.where(lower, 2, 0), capacity)

    target = neighbors[...]
    lane = target % LANES
    inside = target // LANES == me

    def beside(own, halo):
        a = lane_gather(spread(own, edges), lane)
        b = lane_gather(spread(halo, edges), lane)
        return jnp.where(inside, a, b)

    drift[0:edges, :] = (
        0.5 * (own_x + beside(own_x, halo_x)) * cosine[...]
        + 0.5 * (own_y + beside(own_y, halo_y)) * sine[...]
    )
    drifts = [spread(drift[s : s + 1, :], 8) for s in range(edges)]
    from_outer = half_mask(dirs, odd)
    halos[...] = jnp.zeros(halos.shape, jnp.float32)
    ratio = 1.0 / 1.1
    bands = [slice(r, r + 8) for r in range(0, stride, 8)]

    def gather(c, change):
        for i in range(step_pairs):
            g = c * step_pairs + i
            parts = []
            for message in (outer, inner):
                at = base + g * whole
                upper = message[at : at + whole, :]
                at = base + pairs * whole + g * rest
                left = message[at : at + rest, :]
                parts.append(jnp.concatenate([upper, left], axis=0))
            x, y = parts
            at = 2 * i * stride
            halos[at : at + dirs, :] = jnp.where(from_outer, x, y)
            at += stride
            halos[at : at + dirs, :] = pltpu.roll(jnp.where(from_outer, y, x), LANES // 2, 1)
        mixed = jnp.concatenate(split(halos[...]), axis=1)
        change[...] = jnp.dot(
            mixed, choice[2 * LANES : 4 * LANES, :], preferred_element_type=jnp.float32
        )

    def advect(c, change, first_speed, first_slow, total):
        total = list(total)
        speeds = []
        for i in range(step_pairs):
            speeds += [first_speed * ratio**i, first_speed * ratio ** (i + pairs)]
        slowness = []
        for i in range(step_pairs):
            slowness += [first_slow * ratio**-i, first_slow * ratio ** -(i + pairs)]
        relative = [[drift * slow for drift in drifts] for slow in slowness]
        relative_sum = [sum(each[1:], each[0]) for each in relative]
        for k, band in enumerate(bands):
            along = [project[s, band, :] for s in range(edges)]
            along_sum = sum(along[1:], along[0])
            for i in range(step_pairs):
                g = c * step_pairs + i
                for j, f in ((2 * i, g), (2 * i + 1, g + pairs)):
                    own = spectra[f, band, :]
                    at = j * stride + band.start
                    own_at = slice(f * stride + band.start, f * stride + band.stop)
                    flux = (along_sum + relative_sum[j]) * own
                    for s in range(edges):
                        down = jnp.minimum(along[s] + relative[j][s], 0.0)
                        lanes = slice(s * LANES, (s + 1) * LANES)
                        step = change[at : at + 8, lanes] + own_change[own_at, lanes]
                        flux = flux + down * step
                    value = own - speeds[j] * flux
                    spectra_new[f, band, :] = value
                    total[k] = total[k] + value
        return first_speed * ratio**step_pairs, first_slow * ratio**-step_pairs, tuple(total)

    zeros = tuple(jnp.zeros((8, LANES), jnp.float32) for _ in bands)
    chunks = pairs // step_pairs
    buffers = (change_a, change_b)
    carry = (1.0, 1.0, zeros)
    gather(0, change_a)
    tasks = halo_tasks(
        layers, outer, inner, fields, cell_neighbors, cell_inside, scale,
        halo, tables, edge_change, halo_change, near_cells,
    )
    for c in range(chunks):
        if c + 1 < chunks:
            gather(c + 1, buffers[(c + 1) % 2])
        for task in tasks[c * len(tasks) // chunks : (c + 1) * len(tasks) // chunks]:
            task()
        carry = advect(c, buffers[c % 2], *carry)
    total = carry[2]
    total = jnp.concatenate(total, axis=0)
    zero = jnp.zeros((stride, LANES), jnp.float32)
    cos_dir, sin_dir = ways[0], ways[1]
    mean = jnp.sum(total, axis=0, keepdims=True) * (1.0 / (freqs * dirs))
    step = jnp.exp((ways[2] - 2.0 * mean) * (1.0 / freqs))
    run = 10 if freqs % 10 == 0 else 1

    def grow(c, carry):
        factor, weighted = carry
        for i in range(run):
            f = c * run + i
            factor = factor * step
            evolved = spectra_new[f] * factor
            spectra_new[f] = evolved
            kappa = (f + 1).astype(jnp.float32) * (1.0 / freqs)
            weighted = weighted + kappa * evolved
        return factor, weighted

    _, weighted = lax.fori_loop(0, freqs // run, grow, (zero + 1.0, zero))
    stokes = jnp.concatenate(
        [
            jnp.sum(weighted * cos_dir, axis=0, keepdims=True),
            jnp.sum(weighted * sin_dir, axis=0, keepdims=True),
        ],
        axis=0,
    ) * (1.0 / dirs)
    in_order = jnp.dot(
        three_parts(stokes), slots[...], preferred_element_type=jnp.float32
    )
    in_order = in_order[0:2] + (in_order[2:4] + in_order[4:6])
    values = [
        [in_order[part : part + 1, h * LANES : (h + 1) * LANES] for h in range(halves)]
        for part in range(2)
    ]
    rows_out[...] = peer_rows(values, peers, capacity)


def three_parts(values):
    first = values.astype(jnp.bfloat16).astype(jnp.float32)
    left = values - first
    second = left.astype(jnp.bfloat16).astype(jnp.float32)
    third = left - second
    pad = jnp.zeros((10, values.shape[1]), jnp.float32)
    return jnp.concatenate([first, second, third, pad], axis=0).astype(jnp.bfloat16)


def tracer_kernel(
    capacity, shape,
    halo, halo_tables, edge_change, halo_change, table, fields, matrices, inside, cosine, sine,
    sums, spectra,
    tracers_new, spectra_out,
    stokes, antiflux, lowered, ratios,
    ratio_pieces, steps_a, steps_b, sem,
):
    dirs = spectra_out.shape[1]
    write = pltpu.make_async_copy(spectra.at[:, 0:dirs, :], spectra_out, sem)
    write.start()
    tracer_count, layers, edges = shape
    peers = table.shape[0]
    halves = peers * capacity // LANES
    blocks, field_rows, _ = fields.shape
    layer_groups = layers // 8
    tracer_groups = tracer_count * layer_groups

    received = table[...]
    lane_of = lane_iota(peers)
    sections = []
    for which in range(3):
        values = []
        for part in range(2):
            lane = (2 * which + part) * capacity + lane_of % capacity
            found = lane_gather(received, lane)
            row = []
            for half in range(halves):
                mine = row_iota(peers) == (lane_of + half * LANES) // capacity
                row.append(jnp.sum(jnp.where(mine, found, 0.0), axis=0, keepdims=True))
            values.append(jnp.concatenate(row, axis=1))
        sections.append(three_parts(jnp.concatenate(values, axis=0)))
    total = jnp.dot(
        jnp.concatenate(sections, axis=0), sums[...], preferred_element_type=jnp.float32
    )
    for b in range(blocks + 2):
        which = 0 if b == 0 else 2 if b == blocks + 1 else 1
        at = 16 * which
        lanes = slice(b * LANES, (b + 1) * LANES)
        first, second, third = (total[at + k : at + k + 2, lanes] for k in (0, 2, 4))
        stokes[b, 0:2, :] = first + (second + third)

    decay = [
        jnp.exp(-3.0 / layers * (row_iota(8) + 8 * g).astype(jnp.float32))
        for g in range(layer_groups)
    ]

    def low_order(b, value, change, wx, wy, keep):
        slope = wx * stokes[b, 0:1, :] + wy * stokes[b, 1:2, :]
        own = [value(8 * g) for g in range(tracer_groups)]
        zero = jnp.zeros((8, LANES), jnp.float32)
        speed_sum = [zero] * layer_groups
        inflow = [zero] * tracer_groups
        highest = [zero] * tracer_groups
        lowest = [zero] * tracer_groups
        positive = [zero] * tracer_groups
        negative = [zero] * tracer_groups
        for s in range(edges):
            slope8 = spread(slope[s : s + 1, :], 8)
            for lg in range(layer_groups):
                speed = change(8 * (tracer_groups + lg), s) + decay[lg] * slope8
                down = jnp.minimum(speed, 0.0)
                half = 0.5 * speed - down
                speed_sum[lg] = speed_sum[lg] + speed
                for t in range(tracer_count):
                    g = t * layer_groups + lg
                    step = change(8 * g, s)
                    flux = half * step
                    if keep:
                        antiflux[b - 1, s, 8 * g : 8 * g + 8, :] = flux
                    inflow[g] = inflow[g] + down * step
                    highest[g] = jnp.maximum(highest[g], step)
                    lowest[g] = jnp.minimum(lowest[g], step)
                    positive[g] = positive[g] + jnp.maximum(flux, 0.0)
                    negative[g] = negative[g] - jnp.minimum(flux, 0.0)
        plus, minus = [], []
        for g in range(tracer_groups):
            loss = speed_sum[g % layer_groups] * own[g] + inflow[g]
            if keep:
                lowered[b - 1, 8 * g : 8 * g + 8, :] = own[g] - loss
            up = jnp.maximum(highest[g] + loss, 0.0) / (negative[g] + FCT_FLOOR)
            down = jnp.maximum(-loss - lowest[g], 0.0) / (positive[g] + FCT_FLOOR)
            plus.append(jnp.minimum(1.0, up))
            minus.append(jnp.minimum(1.0, down))
        both = jnp.concatenate(plus + minus, axis=0)
        ratios[b] = both
        ratio_pieces[b] = stack_split(both)

    def band(ref, *index):
        return lambda row: ref[(*index, slice(row, row + 8), slice(None))]

    def column(ref, index):
        return lambda row, s: ref[index, row : row + 8, s * LANES : (s + 1) * LANES]

    for side in range(2):
        b = side * (blocks + 1)
        normals = (halo_tables[side, 1], halo_tables[side, 2])
        low_order(b, band(halo, 1 + side), column(halo_change, side), *normals, False)
    for i in range(blocks):
        change = column(inside, i)
        if i in (0, blocks - 1):
            change = column(edge_change, min(i, 1))
        low_order(i + 1, band(fields, i), change, cosine[i], sine[i], True)

    def products(i, steps):
        mixed = jnp.concatenate([ratio_pieces[i], ratio_pieces[i + 1], ratio_pieces[i + 2]], axis=1)
        steps[...] = jnp.dot(mixed, matrices[i], preferred_element_type=jnp.float32)

    def limit(i, steps):
        out = [lowered[i, 8 * g : 8 * g + 8, :] for g in range(tracer_groups)]
        own = [ratios[i + 1, 8 * g : 8 * g + 8, :] for g in range(2 * tracer_groups)]
        low = 16 * tracer_groups
        for s in range(edges):
            lanes = slice(s * LANES, (s + 1) * LANES)
            beside = [
                own[g]
                + (steps[8 * g : 8 * g + 8, lanes] + steps[low + 8 * g : low + 8 * g + 8, lanes])
                for g in range(2 * tracer_groups)
            ]
            for g in range(tracer_groups):
                m = g + tracer_groups
                flux = antiflux[i, s, 8 * g : 8 * g + 8, :]
                factor = jnp.where(
                    flux >= 0.0, jnp.minimum(own[m], beside[g]), jnp.minimum(own[g], beside[m])
                )
                out[g] = out[g] - factor * flux
        lanes = slice(i * LANES, (i + 1) * LANES)
        for g in range(tracer_groups):
            t, lg = g // layer_groups, g % layer_groups
            tracers_new[t, 8 * lg : 8 * lg + 8, lanes] = out[g]

    buffers = (steps_a, steps_b)
    products(0, steps_a)
    for i in range(blocks):
        if i + 1 < blocks:
            products(i + 1, buffers[(i + 1) % 2])
        limit(i, buffers[i % 2])
    write.wait()


def swap(message, first, peers):
    pairs = []
    for i in range(first, peers - 1, 2):
        pairs += [(i, i + 1), (i + 1, i)]
    return lax.ppermute(message, "mesh", pairs)


def whole_spec():
    return pl.BlockSpec(memory_space=pltpu.VMEM)


def local(
    tracers,
    potential,
    surface_current,
    cell_neighbors,
    cell_normal,
    cell_weight,
    spectra,
    wind_velocity,
    node_neighbors,
    node_normal,
    node_weight,
    send_rows,
    node_slot,
):
    peers, _, capacity = send_rows.shape
    freqs, dirs, nodes = spectra.shape
    tracer_count, layers, cells = tracers.shape
    edges = cell_neighbors.shape[0]
    blocks = cells // LANES
    field_rows = (tracer_count + 1) * layers
    head_rows = 2 * field_rows + TABLE_ROWS
    message_rows = head_rows + (freqs // 2 * dirs + 7) // 8 * 8
    slots = node_slot.reshape(1, nodes)
    params = pltpu.CompilerParams(vmem_limit_bytes=VMEM_LIMIT)
    f32 = jnp.float32

    stored = pl.BlockSpec(memory_space=pltpu.HBM)
    rows = tracer_count * layers
    stride = (dirs + 7) // 8 * 8
    step_pairs = 5 if freqs % 10 == 0 else 1
    step_rows = 2 * step_pairs * stride

    def like(x):
        return jax.ShapeDtypeStruct(x.shape, x.dtype)

    def shaped(*shape, dtype=f32):
        return jax.ShapeDtypeStruct(shape, dtype)

    def call(kernel, name, inputs, outputs, scratch, out_specs=None):
        return pl.pallas_call(
            kernel,
            out_shape=outputs,
            in_specs=[whole_spec()] * len(inputs),
            out_specs=out_specs or (whole_spec(),) * len(outputs),
            scratch_shapes=scratch,
            compiler_params=params,
            name=name,
        )(*inputs)

    inputs = (
        spectra, tracers, potential, cell_neighbors, cell_normal, cell_weight, surface_current,
        send_rows, slots, node_neighbors, node_normal, node_weight, wind_velocity,
    )
    (
        currents, outer, inner, own_spectra, own_slots, near, angle, face, wind,
        own_tracers, own_potential, neighbors, normal, weight, coupled,
    ) = pl.pallas_call(
        pack_kernel,
        out_shape=(
            shaped(peers, LANES),
            shaped(message_rows, LANES),
            shaped(message_rows, LANES),
            shaped(freqs, stride, LANES),
            like(slots),
            like(node_neighbors),
            like(node_normal),
            like(node_weight),
            like(wind_velocity),
            like(tracers),
            like(potential),
            like(cell_neighbors),
            like(cell_normal),
            like(cell_weight),
            shaped(3, peers, capacity, dtype=jnp.int32),
        ),
        in_specs=[stored] * len(inputs),
        out_specs=(whole_spec(),) * 15,
        scratch_shapes=[
            pltpu.VMEM(surface_current.shape, f32),
            pltpu.SemaphoreType.DMA((15,)),
        ],
        compiler_params=params,
        name="pack",
    )(*(pltpu.with_memory_space_constraint(x, pltpu.HBM) for x in inputs))
    outer = swap(outer, 1, peers)
    inner = swap(inner, 0, peers)

    (
        cosine, sine, project, choice, ways, slot_choice, own_change,
        fields, matrices, inside, cell_cosine, cell_sine, cell_scale, sums,
    ) = call(
        functools.partial(prepare_kernel, dirs, step_rows),
        "prepare",
        (
            own_spectra, near, angle, face, wind, own_slots, own_tracers, own_potential,
            neighbors, normal, weight, coupled,
        ),
        (
            like(node_normal),
            like(node_normal),
            shaped(edges, stride, LANES),
            shaped(4 * LANES, edges * LANES, dtype=jnp.bfloat16),
            shaped(3, stride, LANES),
            shaped(nodes, peers * capacity, dtype=jnp.bfloat16),
            shaped(freqs * stride, edges * LANES),
            shaped(blocks, field_rows, LANES),
            shaped(blocks, 3 * LANES, edges * LANES, dtype=jnp.bfloat16),
            shaped(blocks, field_rows, edges * LANES),
            shaped(blocks, 8, LANES),
            shaped(blocks, 8, LANES),
            shaped(blocks, 8, LANES),
            shaped(peers * capacity, (blocks + 2) * LANES, dtype=jnp.bfloat16),
        ),
        [pltpu.VMEM((blocks, 2 * field_rows, LANES), jnp.bfloat16)],
    )
    currents, cosine = lax.optimization_barrier((currents, cosine))
    currents = lax.all_to_all(currents, "mesh", 0, 0, tiled=True)

    spectra_new, stokes_rows, halo, halo_tables, edge_change, halo_change = call(
        functools.partial(wave_kernel, capacity, step_pairs, dirs, layers),
        "wave",
        (
            own_spectra, outer, inner, currents, own_slots, near,
            cosine, sine, project, choice, ways, slot_choice, own_change,
            fields, neighbors, inside, cell_scale,
        ),
        (
            shaped(freqs, stride, LANES),
            shaped(peers, LANES),
            shaped(4, field_rows, LANES),
            shaped(2, 3, 8, LANES),
            shaped(2, field_rows, edges * LANES),
            shaped(2, field_rows, edges * LANES),
        ),
        [
            pltpu.VMEM((8, LANES), f32),
            pltpu.VMEM((step_rows, LANES), f32),
            pltpu.VMEM((step_rows, edges * LANES), f32),
            pltpu.VMEM((step_rows, edges * LANES), f32),
            pltpu.VMEM((2, 8, LANES), jnp.int32),
        ],
    )
    stokes_all = lax.all_to_all(stokes_rows, "mesh", 0, 0, tiled=True)

    return call(
        functools.partial(tracer_kernel, capacity, (tracer_count, layers, edges)),
        "tracer",
        (
            halo, halo_tables, edge_change, halo_change, stokes_all, fields, matrices, inside,
            cell_cosine, cell_sine, sums, pltpu.with_memory_space_constraint(spectra_new, pltpu.VMEM),
        ),
        (like(tracers), like(spectra)),
        [
            pltpu.VMEM((blocks + 2, 8, LANES), f32),
            pltpu.VMEM((blocks, edges, rows, LANES), f32),
            pltpu.VMEM((blocks, rows, LANES), f32),
            pltpu.VMEM((blocks + 2, 2 * rows, LANES), f32),
            pltpu.VMEM((blocks + 2, 4 * rows, LANES), jnp.bfloat16),
            pltpu.VMEM((4 * rows, edges * LANES), f32),
            pltpu.VMEM((4 * rows, edges * LANES), f32),
            pltpu.SemaphoreType.DMA(()),
        ],
        out_specs=(whole_spec(), stored),
    )


def solution(mesh):
    return jax.shard_map(
        local,
        mesh=mesh,
        in_specs=(
            P(None, None, ("groups", "mesh")),
            P(None, ("groups", "mesh")),
            P(None, ("groups", "mesh")),
            P(None, "mesh"),
            P(None, "mesh"),
            P(None, "mesh"),
            P(None, None, ("groups", "mesh")),
            P(None, ("groups", "mesh")),
            P(None, "mesh"),
            P(None, "mesh"),
            P(None, "mesh"),
            P(),
            P("mesh"),
        ),
        out_specs=(P(None, None, ("groups", "mesh")), P(None, None, ("groups", "mesh"))),
        check_vma=False,
    )
```

```python
import functools
import math

import jax
import jax.numpy as jnp
from jax import lax
from jax.experimental import pallas as pl
from jax.experimental.pallas import tpu as pltpu
from jax.sharding import PartitionSpec as P

LANES = 128
FCT_FLOOR = 0.001
TABLE_ROWS = 24
VMEM_LIMIT = 32 * 1024 * 1024


def lane_gather(values, index):
    return jnp.take_along_axis(values, index, axis=1, mode="promise_in_bounds")


def spread(row, count):
    return jnp.broadcast_to(row, (count, LANES))


def lane_iota(rows):
    return lax.broadcasted_iota(jnp.int32, (rows, LANES), 1)


def row_iota(rows):
    return lax.broadcasted_iota(jnp.int32, (rows, LANES), 0)


def slot_rows(entry):
    peers, capacity = entry.shape
    wide = jnp.concatenate([entry, jnp.zeros((peers, LANES - capacity), jnp.int32)], axis=1)
    wide = lane_gather(wide, lane_iota(peers) % capacity)
    owner = row_iota(peers)
    out = []
    for half in range(peers * capacity // LANES):
        wanted = (lane_iota(peers) + half * LANES) // capacity
        picked = jnp.where(owner == wanted, wide, 0).astype(jnp.float32)
        out.append(jnp.sum(picked, axis=0, keepdims=True).astype(jnp.int32))
    return out


def half_mask(rows, lower):
    half = lane_iota(rows) // (LANES // 2)
    return half == jnp.where(lower, 0, 1)


def peer_rows(values, peers, capacity):
    lane = lane_iota(peers)
    group = lane // capacity
    block = jnp.clip(row_iota(peers) - 1 + group // 2, 0, peers - 1)
    entry = block * capacity + lane % capacity
    out = jnp.zeros((peers, LANES), jnp.float32)
    for part in range(2):
        for half, row in enumerate(values[part]):
            found = lane_gather(spread(row, peers), entry % LANES)
            wanted = (group < 6) & (group % 2 == part) & (entry // LANES == half)
            out = jnp.where(wanted, found, out)
    return out


def direction(dirs, padded):
    turn = row_iota(padded).astype(jnp.float32) * (2.0 * math.pi / dirs)
    return jnp.cos(turn), jnp.sin(turn)


def node_tables(
    me, dirs, near, angle, face, wind, slot, cosine, sine, project, choice, ways, slots
):
    edges, padded = project.shape[:2]
    cosine[...] = face[...] * jnp.cos(angle[...])
    sine[...] = face[...] * jnp.sin(angle[...])
    cos_dir, sin_dir = direction(dirs, padded)
    ways[0] = cos_dir
    ways[1] = sin_dir
    ways[2] = 0.25 * jnp.maximum(wind[0:1, :] * cos_dir + wind[1:2, :] * sin_dir, 0.0)
    taken = jnp.transpose(spread(slot[...].astype(jnp.float32), LANES))
    for half in range(slots.shape[1] // LANES):
        number = (lane_iota(LANES) + half * LANES).astype(jnp.float32)
        picked = jnp.where(taken == number, 1.0, 0.0).astype(jnp.bfloat16)
        slots[:, half * LANES : (half + 1) * LANES] = picked
    source = row_iota(LANES)
    minus = jnp.where(source == lane_iota(LANES), -1.0, 0.0)
    for s in range(edges):
        project[s] = cos_dir * cosine[s : s + 1, :] + sin_dir * sine[s : s + 1, :]
        target = near[s : s + 1, :]
        inside = target // LANES == me
        lane = target % LANES
        own = jnp.where(source == jnp.where(inside, lane, LANES), 1.0, 0.0) + minus
        halo = jnp.where(source == jnp.where(inside, LANES, lane), 1.0, 0.0)
        lanes = slice(s * LANES, (s + 1) * LANES)
        for k, part in enumerate((own, own, halo, halo)):
            choice[k * LANES : (k + 1) * LANES, lanes] = part.astype(jnp.bfloat16)


def split(x):
    first = x.astype(jnp.bfloat16)
    return first, (x - first.astype(jnp.float32)).astype(jnp.bfloat16)


def pack_kernel(
    spectra_in, tracers_in, potential_in, neighbors_in, normal_in, weight_in, current_in,
    send_rows, slot_in, near_in, angle_in, face_in, wind_in,
    rows_out, outer, inner, spectra, node_slot, near, angle, face, wind,
    tracers, potential, neighbors, normal, weight, coupled,
    current, sems,
):
    peers, _, capacity = send_rows.shape
    me = lax.axis_index("mesh")
    freqs, dirs = spectra_in.shape[:2]
    if dirs < spectra.shape[1]:
        for f in range(freqs):
            spectra[f, dirs // 8 * 8 :, :] = jnp.zeros((8, LANES), jnp.float32)
    pairs = freqs // 2
    copies = []
    for source, target in (
        (send_rows.at[me], coupled.at[1]),
        (current_in, current),
        (slot_in, node_slot),
        (spectra_in, spectra.at[:, 0:dirs, :]),
        (tracers_in, tracers),
        (potential_in, potential),
        (neighbors_in, neighbors),
        (normal_in, normal),
        (weight_in, weight),
        (send_rows.at[jnp.maximum(me - 1, 0)], coupled.at[0]),
        (send_rows.at[jnp.minimum(me + 1, peers - 1)], coupled.at[2]),
        (near_in, near),
        (angle_in, angle),
        (face_in, face),
        (wind_in, wind),
    ):
        copy = pltpu.make_async_copy(source, target, sems.at[len(copies)])
        copy.start()
        copies.append(copy)
    for copy in copies[:3]:
        copy.wait()
    layers, cells = potential.shape
    blocks = cells // LANES
    field_rows = (tracers.shape[0] + 1) * layers
    stacked = jnp.concatenate(
        [current[:, b * LANES : (b + 1) * LANES] for b in range(blocks)], axis=0
    )
    place = row_iota(2 * blocks)
    halves = slot_rows(coupled[1])
    values = [[], []]
    for cell in halves:
        found = lane_gather(stacked, spread(cell % LANES, 2 * blocks))
        for part in range(2):
            picked = jnp.where(place == 2 * (cell // LANES) + part, found, 0.0)
            values[part].append(jnp.sum(picked, axis=0, keepdims=True))
    rows_out[...] = peer_rows(values, peers, capacity)
    for copy in copies[4:9]:
        copy.wait()
    odd = me % 2 == 1
    for out, upward in ((outer, odd), (inner, jnp.logical_not(odd))):
        for b in range(2):
            high = slice((blocks - 2 + b) * LANES, (blocks - 1 + b) * LANES)
            low = slice(b * LANES, (b + 1) * LANES)
            base = b * field_rows
            for t in range(tracers.shape[0]):
                out[base + t * layers : base + (t + 1) * layers, :] = jnp.where(
                    upward, tracers[t, :, high], tracers[t, :, low]
                )
            out[base + field_rows - layers : base + field_rows, :] = jnp.where(
                upward, potential[:, high], potential[:, low]
            )
        high = slice((blocks - 1) * LANES, blocks * LANES)
        low = slice(0, LANES)
        base = 2 * field_rows
        out[base : base + TABLE_ROWS, :] = jnp.zeros((TABLE_ROWS, LANES), jnp.float32)
        edges = neighbors.shape[0]
        near = jnp.where(upward, neighbors[:, high], neighbors[:, low])
        out[base : base + edges, :] = near.astype(jnp.float32)
        out[base + edges : base + edges + 1, :] = node_slot[...].astype(jnp.float32)
        out[base + 8 : base + 8 + edges, :] = jnp.where(upward, normal[:, high], normal[:, low])
        out[base + 16 : base + 16 + edges, :] = jnp.where(upward, weight[:, high], weight[:, low])
    base = 2 * field_rows + TABLE_ROWS
    whole = dirs // 8 * 8
    rest = dirs - whole
    turns = half_mask(dirs, odd)
    copies[3].wait()
    for g in range(pairs):
        natural = spectra[g, 0:dirs, :]
        turned = pltpu.roll(spectra[g + pairs, 0:dirs, :], LANES // 2, 1)
        for out, mixed in (
            (outer, jnp.where(turns, turned, natural)),
            (inner, jnp.where(turns, natural, turned)),
        ):
            at = base + g * whole
            out[at : at + whole, :] = mixed[:whole]
            at = base + pairs * whole + g * rest
            out[at : at + rest, :] = mixed[whole:]
    at = base + pairs * dirs
    if at < outer.shape[0]:
        for out in (outer, inner):
            out[at:, :] = jnp.zeros((outer.shape[0] - at, LANES), jnp.float32)
    for copy in copies[9:]:
        copy.wait()


def choose(cells, first, lanes, matrix):
    place = (cells - first - LANES).astype(jnp.float32).astype(jnp.bfloat16)
    place = spread(place, LANES)
    one = jnp.ones((LANES, LANES), jnp.bfloat16)
    for k in range(3):
        source = (row_iota(LANES) + (k - 1) * LANES).astype(jnp.float32).astype(jnp.bfloat16)
        part = jnp.where(source == place, one, 0 * one)
        if k == 1:
            own = jnp.where(row_iota(LANES) == lane_iota(LANES), 1.0, 0.0).astype(jnp.bfloat16)
            part = part - own
        matrix[k * LANES : (k + 1) * LANES, lanes] = part


def stack_split(x):
    first, second = split(x)
    return jnp.concatenate([first, second], axis=0)


def differences(parts, matrix):
    mixed = jnp.concatenate(parts, axis=1)
    out = jnp.dot(mixed, matrix, preferred_element_type=jnp.float32)
    rows = out.shape[0] // 2
    return out[:rows] + out[rows:]


def prepare_kernel(
    dirs, step_rows,
    spectra, near, angle, face, wind, slot, tracers, potential, neighbors, normal, weight, coupled,
    cosine, sine, project, choice, ways, slots, own_change,
    fields, matrices, inside, cell_cosine, cell_sine, cell_scale, sums,
    pieces,
):
    me = lax.axis_index("mesh")
    node_tables(
        me, dirs, near, angle, face, wind, slot, cosine, sine, project, choice, ways, slots
    )
    freqs, padded, _ = spectra.shape
    step = step_rows // padded

    def own_part(c, carry):
        own = spectra[pl.ds(c * step, step)].reshape(step_rows, LANES)
        own_change[pl.ds(pl.multiple_of(c * step_rows, 8), step_rows), :] = jnp.dot(
            jnp.concatenate(split(own), axis=1),
            choice[0 : 2 * LANES, :],
            preferred_element_type=jnp.float32,
        )
        return carry

    lax.fori_loop(0, freqs // step, own_part, 0)
    tracer_count, layers, cells = tracers.shape
    blocks = cells // LANES
    edges = neighbors.shape[0]
    field_rows = (tracer_count + 1) * layers
    for b in range(blocks):
        lanes = slice(b * LANES, (b + 1) * LANES)
        for t in range(tracer_count):
            fields[b, t * layers : (t + 1) * layers, :] = tracers[t, :, lanes]
        fields[b, field_rows - layers : field_rows, :] = potential[:, lanes]
        pieces[b] = stack_split(fields[b])
        w = weight[:, lanes]
        cell_scale[b, 0:edges, :] = w
        cell_cosine[b, 0:edges, :] = w * jnp.cos(normal[:, lanes])
        cell_sine[b, 0:edges, :] = w * jnp.sin(normal[:, lanes])
        for s in range(edges):
            choose(
                neighbors[s : s + 1, lanes],
                (me * blocks + b - 1) * LANES,
                slice(s * LANES, (s + 1) * LANES),
                matrices.at[b],
            )
    for b in range(blocks):
        first, last = max(b - 1, 0), min(b + 1, blocks - 1)
        rows = slice((first - b + 1) * LANES, (last - b + 2) * LANES)
        parts = [pieces[k] for k in range(first, last + 1)]
        change = differences(parts, matrices[b, rows, :])
        last_field = field_rows - layers
        inside[b, 0:last_field, :] = change[:last_field]
        for s in range(edges):
            at = slice(s * LANES, (s + 1) * LANES)
            inside[b, last_field:, at] = change[last_field:, at] * cell_scale[b, s : s + 1, :]
    for which in range(3):
        first = 0 if which != 0 else cells - LANES
        count = blocks if which == 1 else 1
        start = (0, 1, blocks + 1)[which]
        for half, names in enumerate(slot_rows(coupled[which])):
            named = jnp.transpose(spread(names, LANES).astype(jnp.float32))
            for b in range(count):
                cell = (lane_iota(LANES) + (first + b * LANES)).astype(jnp.float32)
                picked = jnp.where(named == cell, 1.0, 0.0).astype(jnp.bfloat16)
                lanes = slice((start + b) * LANES, (start + b + 1) * LANES)
                sums[half * LANES : (half + 1) * LANES, lanes] = picked


def node_currents(table, slot, which, capacity):
    peers = table.shape[0]
    owner = row_iota(peers) == slot // capacity
    out = []
    for part in range(2):
        lane = (2 * which + part) * capacity + slot % capacity
        found = jnp.where(owner, lane_gather(table, spread(lane, peers)), 0.0)
        out.append(jnp.sum(found, axis=0, keepdims=True))
    return out


def halo_tasks(
    layers, outer, inner, fields, neighbors, inside, scale,
    halo, tables, edge_change, halo_change, near_cells,
):
    me = lax.axis_index("mesh")
    odd = me % 2 == 1
    blocks, field_rows, _ = fields.shape
    edges = neighbors.shape[0]
    for b in range(2):
        x = outer[b * field_rows : (b + 1) * field_rows, :]
        y = inner[b * field_rows : (b + 1) * field_rows, :]
        halo[b] = jnp.where(odd, y, x)
        halo[2 + b] = jnp.where(odd, x, y)
    at = 2 * field_rows
    x = outer[at : at + TABLE_ROWS, :]
    y = inner[at : at + TABLE_ROWS, :]
    for side, rows in ((0, jnp.where(odd, y, x)), (1, jnp.where(odd, x, y))):
        w = rows[16 : 16 + edges]
        tables[side, 0, 0:edges, :] = w
        tables[side, 1, 0:edges, :] = w * jnp.cos(rows[8 : 8 + edges])
        tables[side, 2, 0:edges, :] = w * jnp.sin(rows[8 : 8 + edges])
        near_cells[side, 0:edges, :] = rows[0:edges].astype(jnp.int32)

    def task(side, s):
        i = side * (blocks - 1)
        lanes = slice(s * LANES, (s + 1) * LANES)
        low, own, high = (
            (halo.at[0], halo.at[1], fields.at[i]),
            (fields.at[i], halo.at[2], halo.at[3]),
        )[side]
        near = spread(neighbors[s : s + 1, i * LANES : (i + 1) * LANES], 8)
        from_halo = near // LANES - (me * blocks + i) == 2 * side - 1
        lane = near % LANES
        far = spread(near_cells[side, s : s + 1, :], 8)
        place = far // LANES - (me * blocks + i + 2 * side - 1)
        far_lane = far % LANES
        for row in range(0, field_rows, 8):
            rows = slice(row, row + 8)
            mine = own[rows, :]
            picked = lane_gather(mine, lane)
            middle = lane_gather(mine, far_lane)
            left = lane_gather(low[rows, :], far_lane)
            right = lane_gather(high[rows, :], far_lane)
            out = jnp.where(place == 0, middle, jnp.where(place < 0, left, right)) - mine
            if row >= field_rows - layers:
                picked = picked * spread(scale[i, s : s + 1, :], 8)
                out = out * spread(tables[side, 0, s : s + 1, :], 8)
            halo_change[side, rows, lanes] = out
            edge_change[side, rows, lanes] = inside[i, rows, lanes] + jnp.where(
                from_halo, picked, 0.0
            )

    return [functools.partial(task, side, s) for s in range(edges) for side in range(2)]


def wave_kernel(
    capacity, step_pairs, dirs, layers,
    spectra, outer, inner, table, node_slot, neighbors, cosine, sine, project, choice, ways, slots,
    own_change, fields, cell_neighbors, cell_inside, scale,
    spectra_new, rows_out, halo, tables, edge_change, halo_change,
    drift, halos, change_a, change_b, near_cells,
):
    me = lax.axis_index("mesh")
    freqs, stride = spectra.shape[:2]
    edges = neighbors.shape[0]
    peers = table.shape[0]
    halves = peers * capacity // LANES
    pairs = freqs // 2
    whole = dirs // 8 * 8
    rest = dirs - whole
    base = outer.shape[0] - (pairs * dirs + 7) // 8 * 8

    odd = me % 2 == 1
    slot = node_slot[...]
    row = base - TABLE_ROWS + edges
    halo_slot = jnp.where(
        half_mask(1, odd), outer[row : row + 1, :], inner[row : row + 1, :]
    ).astype(jnp.int32)
    lower = lane_iota(1) < LANES // 2
    currents = table[...]
    own_x, own_y = node_currents(currents, slot, jnp.ones((1, LANES), jnp.int32), capacity)
    halo_x, halo_y = node_currents(currents, halo_slot, jnp.where(lower, 2, 0), capacity)

    target = neighbors[...]
    lane = target % LANES
    inside = target // LANES == me

    def beside(own, halo):
        a = lane_gather(spread(own, edges), lane)
        b = lane_gather(spread(halo, edges), lane)
        return jnp.where(inside, a, b)

    drift[0:edges, :] = (
        0.5 * (own_x + beside(own_x, halo_x)) * cosine[...]
        + 0.5 * (own_y + beside(own_y, halo_y)) * sine[...]
    )
    drifts = [spread(drift[s : s + 1, :], 8) for s in range(edges)]
    from_outer = half_mask(dirs, odd)
    halos[...] = jnp.zeros(halos.shape, jnp.float32)
    ratio = 1.0 / 1.1
    bands = [slice(r, r + 8) for r in range(0, stride, 8)]

    def gather(c, change):
        for i in range(step_pairs):
            g = c * step_pairs + i
            parts = []
            for message in (outer, inner):
                at = base + g * whole
                upper = message[at : at + whole, :]
                at = base + pairs * whole + g * rest
                left = message[at : at + rest, :]
                parts.append(jnp.concatenate([upper, left], axis=0))
            x, y = parts
            at = 2 * i * stride
            halos[at : at + dirs, :] = jnp.where(from_outer, x, y)
            at += stride
            halos[at : at + dirs, :] = pltpu.roll(jnp.where(from_outer, y, x), LANES // 2, 1)
        mixed = jnp.concatenate(split(halos[...]), axis=1)
        change[...] = jnp.dot(
            mixed, choice[2 * LANES : 4 * LANES, :], preferred_element_type=jnp.float32
        )

    def advect(c, change, first_speed, first_slow, total):
        total = list(total)
        speeds = []
        for i in range(step_pairs):
            speeds += [first_speed * ratio**i, first_speed * ratio ** (i + pairs)]
        slowness = []
        for i in range(step_pairs):
            slowness += [first_slow * ratio**-i, first_slow * ratio ** -(i + pairs)]
        relative = [[drift * slow for drift in drifts] for slow in slowness]
        relative_sum = [sum(each[1:], each[0]) for each in relative]
        for k, band in enumerate(bands):
            along = [project[s, band, :] for s in range(edges)]
            along_sum = sum(along[1:], along[0])
            for i in range(step_pairs):
                g = c * step_pairs + i
                for j, f in ((2 * i, g), (2 * i + 1, g + pairs)):
                    own = spectra[f, band, :]
                    at = j * stride + band.start
                    own_at = slice(f * stride + band.start, f * stride + band.stop)
                    flux = (along_sum + relative_sum[j]) * own
                    for s in range(edges):
                        down = jnp.minimum(along[s] + relative[j][s], 0.0)
                        lanes = slice(s * LANES, (s + 1) * LANES)
                        step = change[at : at + 8, lanes] + own_change[own_at, lanes]
                        flux = flux + down * step
                    value = own - speeds[j] * flux
                    spectra_new[f, band, :] = value
                    total[k] = total[k] + value
        return first_speed * ratio**step_pairs, first_slow * ratio**-step_pairs, tuple(total)

    zeros = tuple(jnp.zeros((8, LANES), jnp.float32) for _ in bands)
    chunks = pairs // step_pairs
    buffers = (change_a, change_b)
    carry = (1.0, 1.0, zeros)
    gather(0, change_a)
    tasks = halo_tasks(
        layers, outer, inner, fields, cell_neighbors, cell_inside, scale,
        halo, tables, edge_change, halo_change, near_cells,
    )
    for c in range(chunks):
        if c + 1 < chunks:
            gather(c + 1, buffers[(c + 1) % 2])
        for task in tasks[c * len(tasks) // chunks : (c + 1) * len(tasks) // chunks]:
            task()
        carry = advect(c, buffers[c % 2], *carry)
    total = carry[2]
    total = jnp.concatenate(total, axis=0)
    zero = jnp.zeros((stride, LANES), jnp.float32)
    cos_dir, sin_dir = ways[0], ways[1]
    mean = jnp.sum(total, axis=0, keepdims=True) * (1.0 / (freqs * dirs))
    step = jnp.exp((ways[2] - 2.0 * mean) * (1.0 / freqs))
    run = 10 if freqs % 10 == 0 else 1

    def grow(c, carry):
        factor, weighted = carry
        for i in range(run):
            f = c * run + i
            factor = factor * step
            evolved = spectra_new[f] * factor
            spectra_new[f] = evolved
            kappa = (f + 1).astype(jnp.float32) * (1.0 / freqs)
            weighted = weighted + kappa * evolved
        return factor, weighted

    _, weighted = lax.fori_loop(0, freqs // run, grow, (zero + 1.0, zero))
    stokes = jnp.concatenate(
        [
            jnp.sum(weighted * cos_dir, axis=0, keepdims=True),
            jnp.sum(weighted * sin_dir, axis=0, keepdims=True),
        ],
        axis=0,
    ) * (1.0 / dirs)
    in_order = jnp.dot(
        three_parts(stokes), slots[...], preferred_element_type=jnp.float32
    )
    in_order = in_order[0:2] + (in_order[2:4] + in_order[4:6])
    values = [
        [in_order[part : part + 1, h * LANES : (h + 1) * LANES] for h in range(halves)]
        for part in range(2)
    ]
    rows_out[...] = peer_rows(values, peers, capacity)


def three_parts(values):
    first = values.astype(jnp.bfloat16).astype(jnp.float32)
    left = values - first
    second = left.astype(jnp.bfloat16).astype(jnp.float32)
    third = left - second
    pad = jnp.zeros((10, values.shape[1]), jnp.float32)
    return jnp.concatenate([first, second, third, pad], axis=0).astype(jnp.bfloat16)


def tracer_kernel(
    capacity, shape,
    halo, halo_tables, edge_change, halo_change, table, fields, matrices, inside, cosine, sine,
    sums, spectra,
    tracers_new, spectra_out,
    stokes, antiflux, lowered, ratios,
    ratio_pieces, steps_a, steps_b, sem,
):
    dirs = spectra_out.shape[1]
    write = pltpu.make_async_copy(spectra.at[:, 0:dirs, :], spectra_out, sem)
    write.start()
    tracer_count, layers, edges = shape
    peers = table.shape[0]
    halves = peers * capacity // LANES
    blocks, field_rows, _ = fields.shape
    layer_groups = layers // 8
    tracer_groups = tracer_count * layer_groups

    received = table[...]
    lane_of = lane_iota(peers)
    sections = []
    for which in range(3):
        values = []
        for part in range(2):
            lane = (2 * which + part) * capacity + lane_of % capacity
            found = lane_gather(received, lane)
            row = []
            for half in range(halves):
                mine = row_iota(peers) == (lane_of + half * LANES) // capacity
                row.append(jnp.sum(jnp.where(mine, found, 0.0), axis=0, keepdims=True))
            values.append(jnp.concatenate(row, axis=1))
        sections.append(three_parts(jnp.concatenate(values, axis=0)))
    total = jnp.dot(
        jnp.concatenate(sections, axis=0), sums[...], preferred_element_type=jnp.float32
    )
    for b in range(blocks + 2):
        which = 0 if b == 0 else 2 if b == blocks + 1 else 1
        at = 16 * which
        lanes = slice(b * LANES, (b + 1) * LANES)
        first, second, third = (total[at + k : at + k + 2, lanes] for k in (0, 2, 4))
        stokes[b, 0:2, :] = first + (second + third)

    decay = [
        jnp.exp(-3.0 / layers * (row_iota(8) + 8 * g).astype(jnp.float32))
        for g in range(layer_groups)
    ]

    def low_order(b, value, change, wx, wy, keep):
        slope = wx * stokes[b, 0:1, :] + wy * stokes[b, 1:2, :]
        own = [value(8 * g) for g in range(tracer_groups)]
        zero = jnp.zeros((8, LANES), jnp.float32)
        speed_sum = [zero] * layer_groups
        inflow = [zero] * tracer_groups
        highest = [zero] * tracer_groups
        lowest = [zero] * tracer_groups
        positive = [zero] * tracer_groups
        negative = [zero] * tracer_groups
        for s in range(edges):
            slope8 = spread(slope[s : s + 1, :], 8)
            for lg in range(layer_groups):
                speed = change(8 * (tracer_groups + lg), s) + decay[lg] * slope8
                down = jnp.minimum(speed, 0.0)
                half = 0.5 * speed - down
                speed_sum[lg] = speed_sum[lg] + speed
                for t in range(tracer_count):
                    g = t * layer_groups + lg
                    step = change(8 * g, s)
                    flux = half * step
                    if keep:
                        antiflux[b - 1, s, 8 * g : 8 * g + 8, :] = flux
                    inflow[g] = inflow[g] + down * step
                    highest[g] = jnp.maximum(highest[g], step)
                    lowest[g] = jnp.minimum(lowest[g], step)
                    positive[g] = positive[g] + jnp.maximum(flux, 0.0)
                    negative[g] = negative[g] - jnp.minimum(flux, 0.0)
        plus, minus = [], []
        for g in range(tracer_groups):
            loss = speed_sum[g % layer_groups] * own[g] + inflow[g]
            if keep:
                lowered[b - 1, 8 * g : 8 * g + 8, :] = own[g] - loss
            up = jnp.maximum(highest[g] + loss, 0.0) / (negative[g] + FCT_FLOOR)
            down = jnp.maximum(-loss - lowest[g], 0.0) / (positive[g] + FCT_FLOOR)
            plus.append(jnp.minimum(1.0, up))
            minus.append(jnp.minimum(1.0, down))
        both = jnp.concatenate(plus + minus, axis=0)
        ratios[b] = both
        ratio_pieces[b] = stack_split(both)

    def band(ref, *index):
        return lambda row: ref[(*index, slice(row, row + 8), slice(None))]

    def column(ref, index):
        return lambda row, s: ref[index, row : row + 8, s * LANES : (s + 1) * LANES]

    def ratios_of(b):
        if b in (0, blocks + 1):
            side = min(b, 1)
            normals = (halo_tables[side, 1], halo_tables[side, 2])
            low_order(b, band(halo, 1 + side), column(halo_change, side), *normals, False)
        else:
            i = b - 1
            change = column(inside, i)
            if i in (0, blocks - 1):
                change = column(edge_change, min(i, 1))
            low_order(b, band(fields, i), change, cosine[i], sine[i], True)

    def products(i, steps):
        mixed = jnp.concatenate([ratio_pieces[i], ratio_pieces[i + 1], ratio_pieces[i + 2]], axis=1)
        steps[...] = jnp.dot(mixed, matrices[i], preferred_element_type=jnp.float32)

    def limit(i, steps):
        out = [lowered[i, 8 * g : 8 * g + 8, :] for g in range(tracer_groups)]
        own = [ratios[i + 1, 8 * g : 8 * g + 8, :] for g in range(2 * tracer_groups)]
        low = 16 * tracer_groups
        for s in range(edges):
            lanes = slice(s * LANES, (s + 1) * LANES)
            beside = [
                own[g]
                + (steps[8 * g : 8 * g + 8, lanes] + steps[low + 8 * g : low + 8 * g + 8, lanes])
                for g in range(2 * tracer_groups)
            ]
            for g in range(tracer_groups):
                m = g + tracer_groups
                flux = antiflux[i, s, 8 * g : 8 * g + 8, :]
                factor = jnp.where(
                    flux >= 0.0, jnp.minimum(own[m], beside[g]), jnp.minimum(own[g], beside[m])
                )
                out[g] = out[g] - factor * flux
        lanes = slice(i * LANES, (i + 1) * LANES)
        for g in range(tracer_groups):
            t, lg = g // layer_groups, g % layer_groups
            tracers_new[t, 8 * lg : 8 * lg + 8, lanes] = out[g]

    buffers = (steps_a, steps_b)
    for b in range(3):
        ratios_of(b)
    for i in range(blocks):
        products(i, buffers[i % 2])
        if i + 3 < blocks + 2:
            ratios_of(i + 3)
        if i > 0:
            limit(i - 1, buffers[(i - 1) % 2])
    limit(blocks - 1, buffers[(blocks - 1) % 2])
    write.wait()


def swap(message, first, peers):
    pairs = []
    for i in range(first, peers - 1, 2):
        pairs += [(i, i + 1), (i + 1, i)]
    return lax.ppermute(message, "mesh", pairs)


def whole_spec():
    return pl.BlockSpec(memory_space=pltpu.VMEM)


def local(
    tracers,
    potential,
    surface_current,
    cell_neighbors,
    cell_normal,
    cell_weight,
    spectra,
    wind_velocity,
    node_neighbors,
    node_normal,
    node_weight,
    send_rows,
    node_slot,
):
    peers, _, capacity = send_rows.shape
    freqs, dirs, nodes = spectra.shape
    tracer_count, layers, cells = tracers.shape
    edges = cell_neighbors.shape[0]
    blocks = cells // LANES
    field_rows = (tracer_count + 1) * layers
    head_rows = 2 * field_rows + TABLE_ROWS
    message_rows = head_rows + (freqs // 2 * dirs + 7) // 8 * 8
    slots = node_slot.reshape(1, nodes)
    params = pltpu.CompilerParams(vmem_limit_bytes=VMEM_LIMIT)
    f32 = jnp.float32

    stored = pl.BlockSpec(memory_space=pltpu.HBM)
    rows = tracer_count * layers
    stride = (dirs + 7) // 8 * 8
    step_pairs = 5 if freqs % 10 == 0 else 1
    step_rows = 2 * step_pairs * stride

    def like(x):
        return jax.ShapeDtypeStruct(x.shape, x.dtype)

    def shaped(*shape, dtype=f32):
        return jax.ShapeDtypeStruct(shape, dtype)

    def call(kernel, name, inputs, outputs, scratch, out_specs=None):
        return pl.pallas_call(
            kernel,
            out_shape=outputs,
            in_specs=[whole_spec()] * len(inputs),
            out_specs=out_specs or (whole_spec(),) * len(outputs),
            scratch_shapes=scratch,
            compiler_params=params,
            name=name,
        )(*inputs)

    inputs = (
        spectra, tracers, potential, cell_neighbors, cell_normal, cell_weight, surface_current,
        send_rows, slots, node_neighbors, node_normal, node_weight, wind_velocity,
    )
    (
        currents, outer, inner, own_spectra, own_slots, near, angle, face, wind,
        own_tracers, own_potential, neighbors, normal, weight, coupled,
    ) = pl.pallas_call(
        pack_kernel,
        out_shape=(
            shaped(peers, LANES),
            shaped(message_rows, LANES),
            shaped(message_rows, LANES),
            shaped(freqs, stride, LANES),
            like(slots),
            like(node_neighbors),
            like(node_normal),
            like(node_weight),
            like(wind_velocity),
            like(tracers),
            like(potential),
            like(cell_neighbors),
            like(cell_normal),
            like(cell_weight),
            shaped(3, peers, capacity, dtype=jnp.int32),
        ),
        in_specs=[stored] * len(inputs),
        out_specs=(whole_spec(),) * 15,
        scratch_shapes=[
            pltpu.VMEM(surface_current.shape, f32),
            pltpu.SemaphoreType.DMA((15,)),
        ],
        compiler_params=params,
        name="pack",
    )(*(pltpu.with_memory_space_constraint(x, pltpu.HBM) for x in inputs))
    outer = swap(outer, 1, peers)
    inner = swap(inner, 0, peers)

    (
        cosine, sine, project, choice, ways, slot_choice, own_change,
        fields, matrices, inside, cell_cosine, cell_sine, cell_scale, sums,
    ) = call(
        functools.partial(prepare_kernel, dirs, step_rows),
        "prepare",
        (
            own_spectra, near, angle, face, wind, own_slots, own_tracers, own_potential,
            neighbors, normal, weight, coupled,
        ),
        (
            like(node_normal),
            like(node_normal),
            shaped(edges, stride, LANES),
            shaped(4 * LANES, edges * LANES, dtype=jnp.bfloat16),
            shaped(3, stride, LANES),
            shaped(nodes, peers * capacity, dtype=jnp.bfloat16),
            shaped(freqs * stride, edges * LANES),
            shaped(blocks, field_rows, LANES),
            shaped(blocks, 3 * LANES, edges * LANES, dtype=jnp.bfloat16),
            shaped(blocks, field_rows, edges * LANES),
            shaped(blocks, 8, LANES),
            shaped(blocks, 8, LANES),
            shaped(blocks, 8, LANES),
            shaped(peers * capacity, (blocks + 2) * LANES, dtype=jnp.bfloat16),
        ),
        [pltpu.VMEM((blocks, 2 * field_rows, LANES), jnp.bfloat16)],
    )
    currents, cosine = lax.optimization_barrier((currents, cosine))
    currents = lax.all_to_all(currents, "mesh", 0, 0, tiled=True)

    spectra_new, stokes_rows, halo, halo_tables, edge_change, halo_change = call(
        functools.partial(wave_kernel, capacity, step_pairs, dirs, layers),
        "wave",
        (
            own_spectra, outer, inner, currents, own_slots, near,
            cosine, sine, project, choice, ways, slot_choice, own_change,
            fields, neighbors, inside, cell_scale,
        ),
        (
            shaped(freqs, stride, LANES),
            shaped(peers, LANES),
            shaped(4, field_rows, LANES),
            shaped(2, 3, 8, LANES),
            shaped(2, field_rows, edges * LANES),
            shaped(2, field_rows, edges * LANES),
        ),
        [
            pltpu.VMEM((8, LANES), f32),
            pltpu.VMEM((step_rows, LANES), f32),
            pltpu.VMEM((step_rows, edges * LANES), f32),
            pltpu.VMEM((step_rows, edges * LANES), f32),
            pltpu.VMEM((2, 8, LANES), jnp.int32),
        ],
    )
    stokes_all = lax.all_to_all(stokes_rows, "mesh", 0, 0, tiled=True)

    return call(
        functools.partial(tracer_kernel, capacity, (tracer_count, layers, edges)),
        "tracer",
        (
            halo, halo_tables, edge_change, halo_change, stokes_all, fields, matrices, inside,
            cell_cosine, cell_sine, sums, pltpu.with_memory_space_constraint(spectra_new, pltpu.VMEM),
        ),
        (like(tracers), like(spectra)),
        [
            pltpu.VMEM((blocks + 2, 8, LANES), f32),
            pltpu.VMEM((blocks, edges, rows, LANES), f32),
            pltpu.VMEM((blocks, rows, LANES), f32),
            pltpu.VMEM((blocks + 2, 2 * rows, LANES), f32),
            pltpu.VMEM((blocks + 2, 4 * rows, LANES), jnp.bfloat16),
            pltpu.VMEM((4 * rows, edges * LANES), f32),
            pltpu.VMEM((4 * rows, edges * LANES), f32),
            pltpu.SemaphoreType.DMA(()),
        ],
        out_specs=(whole_spec(), stored),
    )


def solution(mesh):
    return jax.shard_map(
        local,
        mesh=mesh,
        in_specs=(
            P(None, None, ("groups", "mesh")),
            P(None, ("groups", "mesh")),
            P(None, ("groups", "mesh")),
            P(None, "mesh"),
            P(None, "mesh"),
            P(None, "mesh"),
            P(None, None, ("groups", "mesh")),
            P(None, ("groups", "mesh")),
            P(None, "mesh"),
            P(None, "mesh"),
            P(None, "mesh"),
            P(),
            P("mesh"),
        ),
        out_specs=(P(None, None, ("groups", "mesh")), P(None, None, ("groups", "mesh"))),
        check_vma=False,
    )
```

```python
import functools
import math

import jax
import jax.numpy as jnp
from jax import lax
from jax.experimental import pallas as pl
from jax.experimental.pallas import tpu as pltpu
from jax.sharding import PartitionSpec as P

LANES = 128
FCT_FLOOR = 0.001
TABLE_ROWS = 24
VMEM_LIMIT = 32 * 1024 * 1024


def lane_gather(values, index):
    return jnp.take_along_axis(values, index, axis=1, mode="promise_in_bounds")


def spread(row, count):
    return jnp.broadcast_to(row, (count, LANES))


def lane_iota(rows):
    return lax.broadcasted_iota(jnp.int32, (rows, LANES), 1)


def row_iota(rows):
    return lax.broadcasted_iota(jnp.int32, (rows, LANES), 0)


def slot_rows(entry):
    peers, capacity = entry.shape
    wide = jnp.concatenate([entry, jnp.zeros((peers, LANES - capacity), jnp.int32)], axis=1)
    wide = lane_gather(wide, lane_iota(peers) % capacity)
    owner = row_iota(peers)
    out = []
    for half in range(peers * capacity // LANES):
        wanted = (lane_iota(peers) + half * LANES) // capacity
        picked = jnp.where(owner == wanted, wide, 0).astype(jnp.float32)
        out.append(jnp.sum(picked, axis=0, keepdims=True).astype(jnp.int32))
    return out


def half_mask(rows, lower):
    half = lane_iota(rows) // (LANES // 2)
    return half == jnp.where(lower, 0, 1)


def peer_rows(values, peers, capacity):
    lane = lane_iota(peers)
    group = lane // capacity
    block = jnp.clip(row_iota(peers) - 1 + group // 2, 0, peers - 1)
    entry = block * capacity + lane % capacity
    out = jnp.zeros((peers, LANES), jnp.float32)
    for part in range(2):
        for half, row in enumerate(values[part]):
            found = lane_gather(spread(row, peers), entry % LANES)
            wanted = (group < 6) & (group % 2 == part) & (entry // LANES == half)
            out = jnp.where(wanted, found, out)
    return out


def direction(dirs, padded):
    turn = row_iota(padded).astype(jnp.float32) * (2.0 * math.pi / dirs)
    return jnp.cos(turn), jnp.sin(turn)


def node_tables(
    me, dirs, near, angle, face, wind, slot, cosine, sine, project, choice, ways, slots
):
    edges, padded = project.shape[:2]
    cosine[...] = face[...] * jnp.cos(angle[...])
    sine[...] = face[...] * jnp.sin(angle[...])
    cos_dir, sin_dir = direction(dirs, padded)
    ways[0] = cos_dir
    ways[1] = sin_dir
    ways[2] = 0.25 * jnp.maximum(wind[0:1, :] * cos_dir + wind[1:2, :] * sin_dir, 0.0)
    taken = jnp.transpose(spread(slot[...].astype(jnp.float32), LANES))
    for half in range(slots.shape[1] // LANES):
        number = (lane_iota(LANES) + half * LANES).astype(jnp.float32)
        picked = jnp.where(taken == number, 1.0, 0.0).astype(jnp.bfloat16)
        slots[:, half * LANES : (half + 1) * LANES] = picked
    source = row_iota(LANES)
    minus = jnp.where(source == lane_iota(LANES), -1.0, 0.0)
    for s in range(edges):
        project[s] = cos_dir * cosine[s : s + 1, :] + sin_dir * sine[s : s + 1, :]
        target = near[s : s + 1, :]
        inside = target // LANES == me
        lane = target % LANES
        own = jnp.where(source == jnp.where(inside, lane, LANES), 1.0, 0.0) + minus
        halo = jnp.where(source == jnp.where(inside, LANES, lane), 1.0, 0.0)
        lanes = slice(s * LANES, (s + 1) * LANES)
        for k, part in enumerate((own, own, halo, halo)):
            choice[k * LANES : (k + 1) * LANES, lanes] = part.astype(jnp.bfloat16)


def split(x):
    first = x.astype(jnp.bfloat16)
    return first, (x - first.astype(jnp.float32)).astype(jnp.bfloat16)


def pack_kernel(
    spectra_in, tracers_in, potential_in, neighbors_in, normal_in, weight_in, current_in,
    send_rows, slot_in, near_in, angle_in, face_in, wind_in,
    rows_out, outer, inner, spectra, node_slot, near, angle, face, wind,
    tracers, potential, neighbors, normal, weight, coupled,
    current, sems,
):
    peers, _, capacity = send_rows.shape
    me = lax.axis_index("mesh")
    freqs, dirs = spectra_in.shape[:2]
    if dirs < spectra.shape[1]:
        for f in range(freqs):
            spectra[f, dirs // 8 * 8 :, :] = jnp.zeros((8, LANES), jnp.float32)
    pairs = freqs // 2
    copies = []
    for source, target in (
        (send_rows.at[me], coupled.at[1]),
        (current_in, current),
        (slot_in, node_slot),
        (spectra_in, spectra.at[:, 0:dirs, :]),
        (tracers_in, tracers),
        (potential_in, potential),
        (neighbors_in, neighbors),
        (normal_in, normal),
        (weight_in, weight),
        (send_rows.at[jnp.maximum(me - 1, 0)], coupled.at[0]),
        (send_rows.at[jnp.minimum(me + 1, peers - 1)], coupled.at[2]),
        (near_in, near),
        (angle_in, angle),
        (face_in, face),
        (wind_in, wind),
    ):
        copy = pltpu.make_async_copy(source, target, sems.at[len(copies)])
        copy.start()
        copies.append(copy)
    for copy in copies[:3]:
        copy.wait()
    layers, cells = potential.shape
    blocks = cells // LANES
    field_rows = (tracers.shape[0] + 1) * layers
    stacked = jnp.concatenate(
        [current[:, b * LANES : (b + 1) * LANES] for b in range(blocks)], axis=0
    )
    place = row_iota(2 * blocks)
    halves = slot_rows(coupled[1])
    values = [[], []]
    for cell in halves:
        found = lane_gather(stacked, spread(cell % LANES, 2 * blocks))
        for part in range(2):
            picked = jnp.where(place == 2 * (cell // LANES) + part, found, 0.0)
            values[part].append(jnp.sum(picked, axis=0, keepdims=True))
    rows_out[...] = peer_rows(values, peers, capacity)
    for copy in copies[4:9]:
        copy.wait()
    odd = me % 2 == 1
    for out, upward in ((outer, odd), (inner, jnp.logical_not(odd))):
        for b in range(2):
            high = slice((blocks - 2 + b) * LANES, (blocks - 1 + b) * LANES)
            low = slice(b * LANES, (b + 1) * LANES)
            base = b * field_rows
            for t in range(tracers.shape[0]):
                out[base + t * layers : base + (t + 1) * layers, :] = jnp.where(
                    upward, tracers[t, :, high], tracers[t, :, low]
                )
            out[base + field_rows - layers : base + field_rows, :] = jnp.where(
                upward, potential[:, high], potential[:, low]
            )
        high = slice((blocks - 1) * LANES, blocks * LANES)
        low = slice(0, LANES)
        base = 2 * field_rows
        out[base : base + TABLE_ROWS, :] = jnp.zeros((TABLE_ROWS, LANES), jnp.float32)
        edges = neighbors.shape[0]
        near = jnp.where(upward, neighbors[:, high], neighbors[:, low])
        out[base : base + edges, :] = near.astype(jnp.float32)
        out[base + edges : base + edges + 1, :] = node_slot[...].astype(jnp.float32)
        out[base + 8 : base + 8 + edges, :] = jnp.where(upward, normal[:, high], normal[:, low])
        out[base + 16 : base + 16 + edges, :] = jnp.where(upward, weight[:, high], weight[:, low])
    base = 2 * field_rows + TABLE_ROWS
    whole = dirs // 8 * 8
    rest = dirs - whole
    turns = half_mask(dirs, odd)
    copies[3].wait()
    for g in range(pairs):
        natural = spectra[g, 0:dirs, :]
        turned = pltpu.roll(spectra[g + pairs, 0:dirs, :], LANES // 2, 1)
        for out, mixed in (
            (outer, jnp.where(turns, turned, natural)),
            (inner, jnp.where(turns, natural, turned)),
        ):
            at = base + g * whole
            out[at : at + whole, :] = mixed[:whole]
            at = base + pairs * whole + g * rest
            out[at : at + rest, :] = mixed[whole:]
    at = base + pairs * dirs
    if at < outer.shape[0]:
        for out in (outer, inner):
            out[at:, :] = jnp.zeros((outer.shape[0] - at, LANES), jnp.float32)
    for copy in copies[9:]:
        copy.wait()


def choose(cells, first, lanes, matrix):
    place = (cells - first - LANES).astype(jnp.float32).astype(jnp.bfloat16)
    place = spread(place, LANES)
    one = jnp.ones((LANES, LANES), jnp.bfloat16)
    for k in range(3):
        source = (row_iota(LANES) + (k - 1) * LANES).astype(jnp.float32).astype(jnp.bfloat16)
        part = jnp.where(source == place, one, 0 * one)
        if k == 1:
            own = jnp.where(row_iota(LANES) == lane_iota(LANES), 1.0, 0.0).astype(jnp.bfloat16)
            part = part - own
        matrix[k * LANES : (k + 1) * LANES, lanes] = part


def stack_split(x):
    first, second = split(x)
    return jnp.concatenate([first, second], axis=0)


def differences(parts, matrix):
    mixed = jnp.concatenate(parts, axis=1)
    out = jnp.dot(mixed, matrix, preferred_element_type=jnp.float32)
    rows = out.shape[0] // 2
    return out[:rows] + out[rows:]


def prepare_kernel(
    dirs, step_rows,
    spectra, near, angle, face, wind, slot, tracers, potential, neighbors, normal, weight, coupled,
    cosine, sine, project, choice, ways, slots, own_change,
    fields, matrices, inside, cell_cosine, cell_sine, cell_scale, sums,
    pieces,
):
    me = lax.axis_index("mesh")
    node_tables(
        me, dirs, near, angle, face, wind, slot, cosine, sine, project, choice, ways, slots
    )
    freqs, padded, _ = spectra.shape
    step = step_rows // padded

    def own_part(c, carry):
        own = spectra[pl.ds(c * step, step)].reshape(step_rows, LANES)
        own_change[pl.ds(pl.multiple_of(c * step_rows, 8), step_rows), :] = jnp.dot(
            jnp.concatenate(split(own), axis=1),
            choice[0 : 2 * LANES, :],
            preferred_element_type=jnp.float32,
        )
        return carry

    lax.fori_loop(0, freqs // step, own_part, 0)
    tracer_count, layers, cells = tracers.shape
    blocks = cells // LANES
    edges = neighbors.shape[0]
    field_rows = (tracer_count + 1) * layers
    for b in range(blocks):
        lanes = slice(b * LANES, (b + 1) * LANES)
        for t in range(tracer_count):
            fields[b, t * layers : (t + 1) * layers, :] = tracers[t, :, lanes]
        fields[b, field_rows - layers : field_rows, :] = potential[:, lanes]
        pieces[b] = stack_split(fields[b])
        w = weight[:, lanes]
        cell_scale[b, 0:edges, :] = w
        cell_cosine[b, 0:edges, :] = w * jnp.cos(normal[:, lanes])
        cell_sine[b, 0:edges, :] = w * jnp.sin(normal[:, lanes])
        for s in range(edges):
            choose(
                neighbors[s : s + 1, lanes],
                (me * blocks + b - 1) * LANES,
                slice(s * LANES, (s + 1) * LANES),
                matrices.at[b],
            )
    for b in range(blocks):
        first, last = max(b - 1, 0), min(b + 1, blocks - 1)
        rows = slice((first - b + 1) * LANES, (last - b + 2) * LANES)
        parts = [pieces[k] for k in range(first, last + 1)]
        change = differences(parts, matrices[b, rows, :])
        last_field = field_rows - layers
        inside[b, 0:last_field, :] = change[:last_field]
        for s in range(edges):
            at = slice(s * LANES, (s + 1) * LANES)
            inside[b, last_field:, at] = change[last_field:, at] * cell_scale[b, s : s + 1, :]
    for which in range(3):
        first = 0 if which != 0 else cells - LANES
        count = blocks if which == 1 else 1
        start = (0, 1, blocks + 1)[which]
        for half, names in enumerate(slot_rows(coupled[which])):
            named = jnp.transpose(spread(names, LANES).astype(jnp.float32))
            for b in range(count):
                cell = (lane_iota(LANES) + (first + b * LANES)).astype(jnp.float32)
                picked = jnp.where(named == cell, 1.0, 0.0).astype(jnp.bfloat16)
                lanes = slice((start + b) * LANES, (start + b + 1) * LANES)
                sums[half * LANES : (half + 1) * LANES, lanes] = picked


def node_currents(table, slot, which, capacity):
    peers = table.shape[0]
    owner = row_iota(peers) == slot // capacity
    out = []
    for part in range(2):
        lane = (2 * which + part) * capacity + slot % capacity
        found = jnp.where(owner, lane_gather(table, spread(lane, peers)), 0.0)
        out.append(jnp.sum(found, axis=0, keepdims=True))
    return out


def halo_tasks(
    layers, outer, inner, fields, neighbors, inside, scale,
    halo, tables, edge_change, halo_change, near_cells,
):
    me = lax.axis_index("mesh")
    odd = me % 2 == 1
    blocks, field_rows, _ = fields.shape
    edges = neighbors.shape[0]
    for b in range(2):
        x = outer[b * field_rows : (b + 1) * field_rows, :]
        y = inner[b * field_rows : (b + 1) * field_rows, :]
        halo[b] = jnp.where(odd, y, x)
        halo[2 + b] = jnp.where(odd, x, y)
    at = 2 * field_rows
    x = outer[at : at + TABLE_ROWS, :]
    y = inner[at : at + TABLE_ROWS, :]
    for side, rows in ((0, jnp.where(odd, y, x)), (1, jnp.where(odd, x, y))):
        w = rows[16 : 16 + edges]
        tables[side, 0, 0:edges, :] = w
        tables[side, 1, 0:edges, :] = w * jnp.cos(rows[8 : 8 + edges])
        tables[side, 2, 0:edges, :] = w * jnp.sin(rows[8 : 8 + edges])
        near_cells[side, 0:edges, :] = rows[0:edges].astype(jnp.int32)

    def task(side, s):
        i = side * (blocks - 1)
        lanes = slice(s * LANES, (s + 1) * LANES)
        low, own, high = (
            (halo.at[0], halo.at[1], fields.at[i]),
            (fields.at[i], halo.at[2], halo.at[3]),
        )[side]
        near = spread(neighbors[s : s + 1, i * LANES : (i + 1) * LANES], 8)
        from_halo = near // LANES - (me * blocks + i) == 2 * side - 1
        lane = near % LANES
        far = spread(near_cells[side, s : s + 1, :], 8)
        place = far // LANES - (me * blocks + i + 2 * side - 1)
        far_lane = far % LANES
        for row in range(0, field_rows, 8):
            rows = slice(row, row + 8)
            mine = own[rows, :]
            picked = lane_gather(mine, lane)
            middle = lane_gather(mine, far_lane)
            left = lane_gather(low[rows, :], far_lane)
            right = lane_gather(high[rows, :], far_lane)
            out = jnp.where(place == 0, middle, jnp.where(place < 0, left, right)) - mine
            if row >= field_rows - layers:
                picked = picked * spread(scale[i, s : s + 1, :], 8)
                out = out * spread(tables[side, 0, s : s + 1, :], 8)
            halo_change[side, rows, lanes] = out
            edge_change[side, rows, lanes] = inside[i, rows, lanes] + jnp.where(
                from_halo, picked, 0.0
            )

    return [functools.partial(task, side, s) for s in range(edges) for side in range(2)]


def wave_kernel(
    capacity, step_pairs, dirs, layers,
    spectra, outer, inner, table, node_slot, neighbors, cosine, sine, project, choice, ways, slots,
    own_change, fields, cell_neighbors, cell_inside, scale,
    spectra_new, rows_out, halo, tables, edge_change, halo_change,
    drift, halos, change_a, change_b, near_cells,
):
    me = lax.axis_index("mesh")
    freqs, stride = spectra.shape[:2]
    edges = neighbors.shape[0]
    peers = table.shape[0]
    halves = peers * capacity // LANES
    pairs = freqs // 2
    whole = dirs // 8 * 8
    rest = dirs - whole
    base = outer.shape[0] - (pairs * dirs + 7) // 8 * 8

    odd = me % 2 == 1
    slot = node_slot[...]
    row = base - TABLE_ROWS + edges
    halo_slot = jnp.where(
        half_mask(1, odd), outer[row : row + 1, :], inner[row : row + 1, :]
    ).astype(jnp.int32)
    lower = lane_iota(1) < LANES // 2
    currents = table[...]
    own_x, own_y = node_currents(currents, slot, jnp.ones((1, LANES), jnp.int32), capacity)
    halo_x, halo_y = node_currents(currents, halo_slot, jnp.where(lower, 2, 0), capacity)

    target = neighbors[...]
    lane = target % LANES
    inside = target // LANES == me

    def beside(own, halo):
        a = lane_gather(spread(own, edges), lane)
        b = lane_gather(spread(halo, edges), lane)
        return jnp.where(inside, a, b)

    drift[0:edges, :] = (
        0.5 * (own_x + beside(own_x, halo_x)) * cosine[...]
        + 0.5 * (own_y + beside(own_y, halo_y)) * sine[...]
    )
    drifts = [spread(drift[s : s + 1, :], 8) for s in range(edges)]
    from_outer = half_mask(dirs, odd)
    halos[...] = jnp.zeros(halos.shape, jnp.float32)
    ratio = 1.0 / 1.1
    bands = [slice(r, r + 8) for r in range(0, stride, 8)]

    def gather(c, change):
        for i in range(step_pairs):
            g = c * step_pairs + i
            parts = []
            for message in (outer, inner):
                at = base + g * whole
                upper = message[at : at + whole, :]
                at = base + pairs * whole + g * rest
                left = message[at : at + rest, :]
                parts.append(jnp.concatenate([upper, left], axis=0))
            x, y = parts
            at = 2 * i * stride
            halos[at : at + dirs, :] = jnp.where(from_outer, x, y)
            at += stride
            halos[at : at + dirs, :] = pltpu.roll(jnp.where(from_outer, y, x), LANES // 2, 1)
        mixed = jnp.concatenate(split(halos[...]), axis=1)
        change[...] = jnp.dot(
            mixed, choice[2 * LANES : 4 * LANES, :], preferred_element_type=jnp.float32
        )

    def advect(c, change, first_speed, first_slow, total):
        total = list(total)
        speeds = []
        for i in range(step_pairs):
            speeds += [first_speed * ratio**i, first_speed * ratio ** (i + pairs)]
        slowness = []
        for i in range(step_pairs):
            slowness += [first_slow * ratio**-i, first_slow * ratio ** -(i + pairs)]
        relative = [[drift * slow for drift in drifts] for slow in slowness]
        relative_sum = [sum(each[1:], each[0]) for each in relative]
        for k, band in enumerate(bands):
            along = [project[s, band, :] for s in range(edges)]
            along_sum = sum(along[1:], along[0])
            for i in range(step_pairs):
                g = c * step_pairs + i
                for j, f in ((2 * i, g), (2 * i + 1, g + pairs)):
                    own = spectra[f, band, :]
                    at = j * stride + band.start
                    own_at = slice(f * stride + band.start, f * stride + band.stop)
                    flux = (along_sum + relative_sum[j]) * own
                    for s in range(edges):
                        down = jnp.minimum(along[s] + relative[j][s], 0.0)
                        lanes = slice(s * LANES, (s + 1) * LANES)
                        step = change[at : at + 8, lanes] + own_change[own_at, lanes]
                        flux = flux + down * step
                    value = own - speeds[j] * flux
                    spectra_new[f, band, :] = value
                    total[k] = total[k] + value
        return first_speed * ratio**step_pairs, first_slow * ratio**-step_pairs, tuple(total)

    zeros = tuple(jnp.zeros((8, LANES), jnp.float32) for _ in bands)
    chunks = pairs // step_pairs
    buffers = (change_a, change_b)
    carry = (1.0, 1.0, zeros)
    gather(0, change_a)
    tasks = halo_tasks(
        layers, outer, inner, fields, cell_neighbors, cell_inside, scale,
        halo, tables, edge_change, halo_change, near_cells,
    )
    for c in range(chunks):
        if c + 1 < chunks:
            gather(c + 1, buffers[(c + 1) % 2])
        for task in tasks[c * len(tasks) // chunks : (c + 1) * len(tasks) // chunks]:
            task()
        carry = advect(c, buffers[c % 2], *carry)
    total = carry[2]
    total = jnp.concatenate(total, axis=0)
    zero = jnp.zeros((stride, LANES), jnp.float32)
    cos_dir, sin_dir = ways[0], ways[1]
    mean = jnp.sum(total, axis=0, keepdims=True) * (1.0 / (freqs * dirs))
    step = jnp.exp((ways[2] - 2.0 * mean) * (1.0 / freqs))
    run = 10 if freqs % 10 == 0 else 1

    def grow(c, carry):
        factor, weighted = carry
        for i in range(run):
            f = c * run + i
            factor = factor * step
            evolved = spectra_new[f] * factor
            spectra_new[f] = evolved
            kappa = (f + 1).astype(jnp.float32) * (1.0 / freqs)
            weighted = weighted + kappa * evolved
        return factor, weighted

    _, weighted = lax.fori_loop(0, freqs // run, grow, (zero + 1.0, zero))
    stokes = jnp.concatenate(
        [
            jnp.sum(weighted * cos_dir, axis=0, keepdims=True),
            jnp.sum(weighted * sin_dir, axis=0, keepdims=True),
        ],
        axis=0,
    ) * (1.0 / dirs)
    in_order = jnp.dot(
        three_parts(stokes), slots[...], preferred_element_type=jnp.float32
    )
    in_order = in_order[0:2] + (in_order[2:4] + in_order[4:6])
    values = [
        [in_order[part : part + 1, h * LANES : (h + 1) * LANES] for h in range(halves)]
        for part in range(2)
    ]
    rows_out[...] = peer_rows(values, peers, capacity)


def three_parts(values):
    first = values.astype(jnp.bfloat16).astype(jnp.float32)
    left = values - first
    second = left.astype(jnp.bfloat16).astype(jnp.float32)
    third = left - second
    pad = jnp.zeros((10, values.shape[1]), jnp.float32)
    return jnp.concatenate([first, second, third, pad], axis=0).astype(jnp.bfloat16)


def tracer_kernel(
    capacity, shape,
    halo, halo_tables, edge_change, halo_change, table, fields, matrices, inside, cosine, sine,
    sums, spectra,
    tracers_new, spectra_out,
    stokes, antiflux, lowered, ratios,
    ratio_pieces, changes, sem,
):
    dirs = spectra_out.shape[1]
    write = pltpu.make_async_copy(spectra.at[:, 0:dirs, :], spectra_out, sem)
    write.start()
    tracer_count, layers, edges = shape
    peers = table.shape[0]
    halves = peers * capacity // LANES
    blocks, field_rows, _ = fields.shape
    layer_groups = layers // 8
    tracer_groups = tracer_count * layer_groups

    received = table[...]
    lane_of = lane_iota(peers)
    sections = []
    for which in range(3):
        values = []
        for part in range(2):
            lane = (2 * which + part) * capacity + lane_of % capacity
            found = lane_gather(received, lane)
            row = []
            for half in range(halves):
                mine = row_iota(peers) == (lane_of + half * LANES) // capacity
                row.append(jnp.sum(jnp.where(mine, found, 0.0), axis=0, keepdims=True))
            values.append(jnp.concatenate(row, axis=1))
        sections.append(three_parts(jnp.concatenate(values, axis=0)))
    total = jnp.dot(
        jnp.concatenate(sections, axis=0), sums[...], preferred_element_type=jnp.float32
    )
    for b in range(blocks + 2):
        which = 0 if b == 0 else 2 if b == blocks + 1 else 1
        at = 16 * which
        lanes = slice(b * LANES, (b + 1) * LANES)
        first, second, third = (total[at + k : at + k + 2, lanes] for k in (0, 2, 4))
        stokes[b, 0:2, :] = first + (second + third)

    decay = [
        jnp.exp(-3.0 / layers * (row_iota(8) + 8 * g).astype(jnp.float32))
        for g in range(layer_groups)
    ]

    def low_order(b, value, change, wx, wy, keep):
        slope = wx * stokes[b, 0:1, :] + wy * stokes[b, 1:2, :]
        own = [value(8 * g) for g in range(tracer_groups)]
        zero = jnp.zeros((8, LANES), jnp.float32)
        speed_sum = [zero] * layer_groups
        inflow = [zero] * tracer_groups
        highest = [zero] * tracer_groups
        lowest = [zero] * tracer_groups
        positive = [zero] * tracer_groups
        negative = [zero] * tracer_groups
        for s in range(edges):
            slope8 = spread(slope[s : s + 1, :], 8)
            for lg in range(layer_groups):
                speed = change(8 * (tracer_groups + lg), s) + decay[lg] * slope8
                down = jnp.minimum(speed, 0.0)
                half = 0.5 * speed - down
                speed_sum[lg] = speed_sum[lg] + speed
                for t in range(tracer_count):
                    g = t * layer_groups + lg
                    step = change(8 * g, s)
                    flux = half * step
                    if keep:
                        antiflux[b - 1, s, 8 * g : 8 * g + 8, :] = flux
                    inflow[g] = inflow[g] + down * step
                    highest[g] = jnp.maximum(highest[g], step)
                    lowest[g] = jnp.minimum(lowest[g], step)
                    positive[g] = positive[g] + jnp.maximum(flux, 0.0)
                    negative[g] = negative[g] - jnp.minimum(flux, 0.0)
        plus, minus = [], []
        for g in range(tracer_groups):
            loss = speed_sum[g % layer_groups] * own[g] + inflow[g]
            if keep:
                lowered[b - 1, 8 * g : 8 * g + 8, :] = own[g] - loss
            up = jnp.maximum(highest[g] + loss, 0.0) / (negative[g] + FCT_FLOOR)
            down = jnp.maximum(-loss - lowest[g], 0.0) / (positive[g] + FCT_FLOOR)
            plus.append(jnp.minimum(1.0, up))
            minus.append(jnp.minimum(1.0, down))
        both = jnp.concatenate(plus + minus, axis=0)
        ratios[b] = both
        ratio_pieces[b] = stack_split(both)

    def band(ref, *index):
        return lambda row: ref[(*index, slice(row, row + 8), slice(None))]

    def column(ref, index):
        return lambda row, s: ref[index, row : row + 8, s * LANES : (s + 1) * LANES]

    def ratios_of(b):
        if b in (0, blocks + 1):
            side = min(b, 1)
            normals = (halo_tables[side, 1], halo_tables[side, 2])
            low_order(b, band(halo, 1 + side), column(halo_change, side), *normals, False)
        else:
            i = b - 1
            change = column(inside, i)
            if i in (0, blocks - 1):
                change = column(edge_change, min(i, 1))
            low_order(b, band(fields, i), change, cosine[i], sine[i], True)

    def products(i):
        mixed = jnp.concatenate([ratio_pieces[i], ratio_pieces[i + 1], ratio_pieces[i + 2]], axis=1)
        changes[i % 2] = jnp.dot(mixed, matrices[i], preferred_element_type=jnp.float32)

    def limit(i):
        steps = changes.at[i % 2]
        out = [lowered[i, 8 * g : 8 * g + 8, :] for g in range(tracer_groups)]
        own = [ratios[i + 1, 8 * g : 8 * g + 8, :] for g in range(2 * tracer_groups)]
        low = 16 * tracer_groups
        for s in range(edges):
            lanes = slice(s * LANES, (s + 1) * LANES)
            beside = [
                own[g]
                + (steps[8 * g : 8 * g + 8, lanes] + steps[low + 8 * g : low + 8 * g + 8, lanes])
                for g in range(2 * tracer_groups)
            ]
            for g in range(tracer_groups):
                m = g + tracer_groups
                flux = antiflux[i, s, 8 * g : 8 * g + 8, :]
                factor = jnp.where(
                    flux >= 0.0, jnp.minimum(own[m], beside[g]), jnp.minimum(own[g], beside[m])
                )
                out[g] = out[g] - factor * flux
        lanes = pl.ds(pl.multiple_of(i * LANES, LANES), LANES)
        for g in range(tracer_groups):
            t, lg = g // layer_groups, g % layer_groups
            tracers_new[t, 8 * lg : 8 * lg + 8, lanes] = out[g]

    for b in range(blocks + 2):
        ratios_of(b)
    products(0)

    def next_block(i, carry):
        products(i + 1)
        limit(i)
        return carry

    lax.fori_loop(0, blocks - 1, next_block, 0)
    limit(jnp.int32(blocks - 1))
    write.wait()


def swap(message, first, peers):
    pairs = []
    for i in range(first, peers - 1, 2):
        pairs += [(i, i + 1), (i + 1, i)]
    return lax.ppermute(message, "mesh", pairs)


def whole_spec():
    return pl.BlockSpec(memory_space=pltpu.VMEM)


def local(
    tracers,
    potential,
    surface_current,
    cell_neighbors,
    cell_normal,
    cell_weight,
    spectra,
    wind_velocity,
    node_neighbors,
    node_normal,
    node_weight,
    send_rows,
    node_slot,
):
    peers, _, capacity = send_rows.shape
    freqs, dirs, nodes = spectra.shape
    tracer_count, layers, cells = tracers.shape
    edges = cell_neighbors.shape[0]
    blocks = cells // LANES
    field_rows = (tracer_count + 1) * layers
    head_rows = 2 * field_rows + TABLE_ROWS
    message_rows = head_rows + (freqs // 2 * dirs + 7) // 8 * 8
    slots = node_slot.reshape(1, nodes)
    params = pltpu.CompilerParams(vmem_limit_bytes=VMEM_LIMIT)
    f32 = jnp.float32

    stored = pl.BlockSpec(memory_space=pltpu.HBM)
    rows = tracer_count * layers
    stride = (dirs + 7) // 8 * 8
    step_pairs = 5 if freqs % 10 == 0 else 1
    step_rows = 2 * step_pairs * stride

    def like(x):
        return jax.ShapeDtypeStruct(x.shape, x.dtype)

    def shaped(*shape, dtype=f32):
        return jax.ShapeDtypeStruct(shape, dtype)

    def call(kernel, name, inputs, outputs, scratch, out_specs=None):
        return pl.pallas_call(
            kernel,
            out_shape=outputs,
            in_specs=[whole_spec()] * len(inputs),
            out_specs=out_specs or (whole_spec(),) * len(outputs),
            scratch_shapes=scratch,
            compiler_params=params,
            name=name,
        )(*inputs)

    inputs = (
        spectra, tracers, potential, cell_neighbors, cell_normal, cell_weight, surface_current,
        send_rows, slots, node_neighbors, node_normal, node_weight, wind_velocity,
    )
    (
        currents, outer, inner, own_spectra, own_slots, near, angle, face, wind,
        own_tracers, own_potential, neighbors, normal, weight, coupled,
    ) = pl.pallas_call(
        pack_kernel,
        out_shape=(
            shaped(peers, LANES),
            shaped(message_rows, LANES),
            shaped(message_rows, LANES),
            shaped(freqs, stride, LANES),
            like(slots),
            like(node_neighbors),
            like(node_normal),
            like(node_weight),
            like(wind_velocity),
            like(tracers),
            like(potential),
            like(cell_neighbors),
            like(cell_normal),
            like(cell_weight),
            shaped(3, peers, capacity, dtype=jnp.int32),
        ),
        in_specs=[stored] * len(inputs),
        out_specs=(whole_spec(),) * 15,
        scratch_shapes=[
            pltpu.VMEM(surface_current.shape, f32),
            pltpu.SemaphoreType.DMA((15,)),
        ],
        compiler_params=params,
        name="pack",
    )(*(pltpu.with_memory_space_constraint(x, pltpu.HBM) for x in inputs))
    outer = swap(outer, 1, peers)
    inner = swap(inner, 0, peers)

    (
        cosine, sine, project, choice, ways, slot_choice, own_change,
        fields, matrices, inside, cell_cosine, cell_sine, cell_scale, sums,
    ) = call(
        functools.partial(prepare_kernel, dirs, step_rows),
        "prepare",
        (
            own_spectra, near, angle, face, wind, own_slots, own_tracers, own_potential,
            neighbors, normal, weight, coupled,
        ),
        (
            like(node_normal),
            like(node_normal),
            shaped(edges, stride, LANES),
            shaped(4 * LANES, edges * LANES, dtype=jnp.bfloat16),
            shaped(3, stride, LANES),
            shaped(nodes, peers * capacity, dtype=jnp.bfloat16),
            shaped(freqs * stride, edges * LANES),
            shaped(blocks, field_rows, LANES),
            shaped(blocks, 3 * LANES, edges * LANES, dtype=jnp.bfloat16),
            shaped(blocks, field_rows, edges * LANES),
            shaped(blocks, 8, LANES),
            shaped(blocks, 8, LANES),
            shaped(blocks, 8, LANES),
            shaped(peers * capacity, (blocks + 2) * LANES, dtype=jnp.bfloat16),
        ),
        [pltpu.VMEM((blocks, 2 * field_rows, LANES), jnp.bfloat16)],
    )
    currents, cosine = lax.optimization_barrier((currents, cosine))
    currents = lax.all_to_all(currents, "mesh", 0, 0, tiled=True)

    spectra_new, stokes_rows, halo, halo_tables, edge_change, halo_change = call(
        functools.partial(wave_kernel, capacity, step_pairs, dirs, layers),
        "wave",
        (
            own_spectra, outer, inner, currents, own_slots, near,
            cosine, sine, project, choice, ways, slot_choice, own_change,
            fields, neighbors, inside, cell_scale,
        ),
        (
            shaped(freqs, stride, LANES),
            shaped(peers, LANES),
            shaped(4, field_rows, LANES),
            shaped(2, 3, 8, LANES),
            shaped(2, field_rows, edges * LANES),
            shaped(2, field_rows, edges * LANES),
        ),
        [
            pltpu.VMEM((8, LANES), f32),
            pltpu.VMEM((step_rows, LANES), f32),
            pltpu.VMEM((step_rows, edges * LANES), f32),
            pltpu.VMEM((step_rows, edges * LANES), f32),
            pltpu.VMEM((2, 8, LANES), jnp.int32),
        ],
    )
    stokes_all = lax.all_to_all(stokes_rows, "mesh", 0, 0, tiled=True)

    return call(
        functools.partial(tracer_kernel, capacity, (tracer_count, layers, edges)),
        "tracer",
        (
            halo, halo_tables, edge_change, halo_change, stokes_all, fields, matrices, inside,
            cell_cosine, cell_sine, sums, pltpu.with_memory_space_constraint(spectra_new, pltpu.VMEM),
        ),
        (like(tracers), like(spectra)),
        [
            pltpu.VMEM((blocks + 2, 8, LANES), f32),
            pltpu.VMEM((blocks, edges, rows, LANES), f32),
            pltpu.VMEM((blocks, rows, LANES), f32),
            pltpu.VMEM((blocks + 2, 2 * rows, LANES), f32),
            pltpu.VMEM((blocks + 2, 4 * rows, LANES), jnp.bfloat16),
            pltpu.VMEM((2, 4 * rows, edges * LANES), f32),
            pltpu.SemaphoreType.DMA(()),
        ],
        out_specs=(whole_spec(), stored),
    )


def solution(mesh):
    return jax.shard_map(
        local,
        mesh=mesh,
        in_specs=(
            P(None, None, ("groups", "mesh")),
            P(None, ("groups", "mesh")),
            P(None, ("groups", "mesh")),
            P(None, "mesh"),
            P(None, "mesh"),
            P(None, "mesh"),
            P(None, None, ("groups", "mesh")),
            P(None, ("groups", "mesh")),
            P(None, "mesh"),
            P(None, "mesh"),
            P(None, "mesh"),
            P(),
            P("mesh"),
        ),
        out_specs=(P(None, None, ("groups", "mesh")), P(None, None, ("groups", "mesh"))),
        check_vma=False,
    )
```

```python
import functools
import math

import jax
import jax.numpy as jnp
from jax import lax
from jax.experimental import pallas as pl
from jax.experimental.pallas import tpu as pltpu
from jax.sharding import PartitionSpec as P

LANES = 128
FCT_FLOOR = 0.001
TABLE_ROWS = 24
VMEM_LIMIT = 32 * 1024 * 1024


def lane_gather(values, index):
    return jnp.take_along_axis(values, index, axis=1, mode="promise_in_bounds")


def spread(row, count):
    return jnp.broadcast_to(row, (count, LANES))


def lane_iota(rows):
    return lax.broadcasted_iota(jnp.int32, (rows, LANES), 1)


def row_iota(rows):
    return lax.broadcasted_iota(jnp.int32, (rows, LANES), 0)


def slot_rows(entry):
    peers, capacity = entry.shape
    wide = jnp.concatenate([entry, jnp.zeros((peers, LANES - capacity), jnp.int32)], axis=1)
    wide = lane_gather(wide, lane_iota(peers) % capacity)
    owner = row_iota(peers)
    out = []
    for half in range(peers * capacity // LANES):
        wanted = (lane_iota(peers) + half * LANES) // capacity
        picked = jnp.where(owner == wanted, wide, 0).astype(jnp.float32)
        out.append(jnp.sum(picked, axis=0, keepdims=True).astype(jnp.int32))
    return out


def half_mask(rows, lower):
    half = lane_iota(rows) // (LANES // 2)
    return half == jnp.where(lower, 0, 1)


def peer_rows(values, peers, capacity):
    lane = lane_iota(peers)
    group = lane // capacity
    block = jnp.clip(row_iota(peers) - 1 + group // 2, 0, peers - 1)
    entry = block * capacity + lane % capacity
    out = jnp.zeros((peers, LANES), jnp.float32)
    for part in range(2):
        for half, row in enumerate(values[part]):
            found = lane_gather(spread(row, peers), entry % LANES)
            wanted = (group < 6) & (group % 2 == part) & (entry // LANES == half)
            out = jnp.where(wanted, found, out)
    return out


def direction(dirs, padded):
    turn = row_iota(padded).astype(jnp.float32) * (2.0 * math.pi / dirs)
    return jnp.cos(turn), jnp.sin(turn)


def node_tables(
    me, dirs, capacity, near, angle, face, wind, slot, cosine, sine, project, choice, ways, slots
):
    edges, padded = project.shape[:2]
    peers = slots.shape[0]
    cosine[...] = face[...] * jnp.cos(angle[...])
    sine[...] = face[...] * jnp.sin(angle[...])
    cos_dir, sin_dir = direction(dirs, padded)
    ways[0] = cos_dir
    ways[1] = sin_dir
    ways[2] = 0.25 * jnp.maximum(wind[0:1, :] * cos_dir + wind[1:2, :] * sin_dir, 0.0)
    taken = jnp.transpose(spread(slot[...].astype(jnp.float32), LANES))
    node = (row_iota(LANES) + 1).astype(jnp.float32)
    holders = []
    for half in range(peers * capacity // LANES):
        number = (lane_iota(LANES) + half * LANES).astype(jnp.float32)
        holders.append(jnp.sum(jnp.where(taken == number, node, 0.0), axis=0, keepdims=True))
    slots[...] = peer_rows([holders, holders], peers, capacity).astype(jnp.int32)
    source = row_iota(LANES)
    minus = jnp.where(source == lane_iota(LANES), -1.0, 0.0)
    for s in range(edges):
        project[s] = cos_dir * cosine[s : s + 1, :] + sin_dir * sine[s : s + 1, :]
        target = near[s : s + 1, :]
        inside = target // LANES == me
        lane = target % LANES
        own = jnp.where(source == jnp.where(inside, lane, LANES), 1.0, 0.0) + minus
        halo = jnp.where(source == jnp.where(inside, LANES, lane), 1.0, 0.0)
        lanes = slice(s * LANES, (s + 1) * LANES)
        for k, part in enumerate((own, own, halo, halo)):
            choice[k * LANES : (k + 1) * LANES, lanes] = part.astype(jnp.bfloat16)


def split(x):
    first = x.astype(jnp.bfloat16)
    return first, (x - first.astype(jnp.float32)).astype(jnp.bfloat16)


def pack_kernel(
    spectra_in, tracers_in, potential_in, neighbors_in, normal_in, weight_in, current_in,
    send_rows, slot_in, near_in, angle_in, face_in, wind_in,
    rows_out, outer, inner, spectra, node_slot, near, angle, face, wind,
    tracers, potential, neighbors, normal, weight, coupled,
    current, sems,
):
    peers, _, capacity = send_rows.shape
    me = lax.axis_index("mesh")
    freqs, dirs = spectra_in.shape[:2]
    if dirs < spectra.shape[1]:
        for f in range(freqs):
            spectra[f, dirs // 8 * 8 :, :] = jnp.zeros((8, LANES), jnp.float32)
    pairs = freqs // 2
    copies = []
    for source, target in (
        (send_rows.at[me], coupled.at[1]),
        (current_in, current),
        (slot_in, node_slot),
        (spectra_in, spectra.at[:, 0:dirs, :]),
        (tracers_in, tracers),
        (potential_in, potential),
        (neighbors_in, neighbors),
        (normal_in, normal),
        (weight_in, weight),
        (send_rows.at[jnp.maximum(me - 1, 0)], coupled.at[0]),
        (send_rows.at[jnp.minimum(me + 1, peers - 1)], coupled.at[2]),
        (near_in, near),
        (angle_in, angle),
        (face_in, face),
        (wind_in, wind),
    ):
        copy = pltpu.make_async_copy(source, target, sems.at[len(copies)])
        copy.start()
        copies.append(copy)
    for copy in copies[:3]:
        copy.wait()
    layers, cells = potential.shape
    blocks = cells // LANES
    field_rows = (tracers.shape[0] + 1) * layers
    stacked = jnp.concatenate(
        [current[:, b * LANES : (b + 1) * LANES] for b in range(blocks)], axis=0
    )
    place = row_iota(2 * blocks)
    halves = slot_rows(coupled[1])
    values = [[], []]
    for cell in halves:
        found = lane_gather(stacked, spread(cell % LANES, 2 * blocks))
        for part in range(2):
            picked = jnp.where(place == 2 * (cell // LANES) + part, found, 0.0)
            values[part].append(jnp.sum(picked, axis=0, keepdims=True))
    rows_out[...] = peer_rows(values, peers, capacity)
    for copy in copies[4:9]:
        copy.wait()
    odd = me % 2 == 1
    for out, upward in ((outer, odd), (inner, jnp.logical_not(odd))):
        for b in range(2):
            high = slice((blocks - 2 + b) * LANES, (blocks - 1 + b) * LANES)
            low = slice(b * LANES, (b + 1) * LANES)
            base = b * field_rows
            for t in range(tracers.shape[0]):
                out[base + t * layers : base + (t + 1) * layers, :] = jnp.where(
                    upward, tracers[t, :, high], tracers[t, :, low]
                )
            out[base + field_rows - layers : base + field_rows, :] = jnp.where(
                upward, potential[:, high], potential[:, low]
            )
        high = slice((blocks - 1) * LANES, blocks * LANES)
        low = slice(0, LANES)
        base = 2 * field_rows
        out[base : base + TABLE_ROWS, :] = jnp.zeros((TABLE_ROWS, LANES), jnp.float32)
        edges = neighbors.shape[0]
        near = jnp.where(upward, neighbors[:, high], neighbors[:, low])
        out[base : base + edges, :] = near.astype(jnp.float32)
        out[base + edges : base + edges + 1, :] = node_slot[...].astype(jnp.float32)
        out[base + 8 : base + 8 + edges, :] = jnp.where(upward, normal[:, high], normal[:, low])
        out[base + 16 : base + 16 + edges, :] = jnp.where(upward, weight[:, high], weight[:, low])
    base = 2 * field_rows + TABLE_ROWS
    whole = dirs // 8 * 8
    rest = dirs - whole
    turns = half_mask(dirs, odd)
    copies[3].wait()
    for g in range(pairs):
        natural = spectra[g, 0:dirs, :]
        turned = pltpu.roll(spectra[g + pairs, 0:dirs, :], LANES // 2, 1)
        for out, mixed in (
            (outer, jnp.where(turns, turned, natural)),
            (inner, jnp.where(turns, natural, turned)),
        ):
            at = base + g * whole
            out[at : at + whole, :] = mixed[:whole]
            at = base + pairs * whole + g * rest
            out[at : at + rest, :] = mixed[whole:]
    at = base + pairs * dirs
    if at < outer.shape[0]:
        for out in (outer, inner):
            out[at:, :] = jnp.zeros((outer.shape[0] - at, LANES), jnp.float32)
    for copy in copies[9:]:
        copy.wait()


def choose(cells, first, lanes, matrix):
    place = (cells - first - LANES).astype(jnp.float32).astype(jnp.bfloat16)
    place = spread(place, LANES)
    one = jnp.ones((LANES, LANES), jnp.bfloat16)
    for k in range(3):
        source = (row_iota(LANES) + (k - 1) * LANES).astype(jnp.float32).astype(jnp.bfloat16)
        part = jnp.where(source == place, one, 0 * one)
        if k == 1:
            own = jnp.where(row_iota(LANES) == lane_iota(LANES), 1.0, 0.0).astype(jnp.bfloat16)
            part = part - own
        matrix[k * LANES : (k + 1) * LANES, lanes] = part


def stack_split(x):
    first, second = split(x)
    return jnp.concatenate([first, second], axis=0)


def differences(parts, matrix):
    mixed = jnp.concatenate(parts, axis=1)
    out = jnp.dot(mixed, matrix, preferred_element_type=jnp.float32)
    rows = out.shape[0] // 2
    return out[:rows] + out[rows:]


def prepare_kernel(
    dirs, step_rows,
    spectra, near, angle, face, wind, slot, tracers, potential, neighbors, normal, weight, coupled,
    cosine, sine, project, choice, ways, slots, own_change,
    fields, matrices, inside, cell_cosine, cell_sine, cell_scale, sums,
    pieces,
):
    me = lax.axis_index("mesh")
    node_tables(
        me, dirs, coupled.shape[2], near, angle, face, wind, slot, cosine, sine, project, choice,
        ways, slots,
    )
    freqs, padded, _ = spectra.shape
    step = step_rows // padded

    def own_part(c, carry):
        own = spectra[pl.ds(c * step, step)].reshape(step_rows, LANES)
        own_change[pl.ds(pl.multiple_of(c * step_rows, 8), step_rows), :] = jnp.dot(
            jnp.concatenate(split(own), axis=1),
            choice[0 : 2 * LANES, :],
            preferred_element_type=jnp.float32,
        )
        return carry

    lax.fori_loop(0, freqs // step, own_part, 0)
    tracer_count, layers, cells = tracers.shape
    blocks = cells // LANES
    edges = neighbors.shape[0]
    field_rows = (tracer_count + 1) * layers
    for b in range(blocks):
        lanes = slice(b * LANES, (b + 1) * LANES)
        for t in range(tracer_count):
            fields[b, t * layers : (t + 1) * layers, :] = tracers[t, :, lanes]
        fields[b, field_rows - layers : field_rows, :] = potential[:, lanes]
        pieces[b] = stack_split(fields[b])
        w = weight[:, lanes]
        cell_scale[b, 0:edges, :] = w
        cell_cosine[b, 0:edges, :] = w * jnp.cos(normal[:, lanes])
        cell_sine[b, 0:edges, :] = w * jnp.sin(normal[:, lanes])
        for s in range(edges):
            choose(
                neighbors[s : s + 1, lanes],
                (me * blocks + b - 1) * LANES,
                slice(s * LANES, (s + 1) * LANES),
                matrices.at[b],
            )
    for b in range(blocks):
        first, last = max(b - 1, 0), min(b + 1, blocks - 1)
        rows = slice((first - b + 1) * LANES, (last - b + 2) * LANES)
        parts = [pieces[k] for k in range(first, last + 1)]
        change = differences(parts, matrices[b, rows, :])
        last_field = field_rows - layers
        inside[b, 0:last_field, :] = change[:last_field]
        for s in range(edges):
            at = slice(s * LANES, (s + 1) * LANES)
            inside[b, last_field:, at] = change[last_field:, at] * cell_scale[b, s : s + 1, :]
    for which in range(3):
        first = 0 if which != 0 else cells - LANES
        count = blocks if which == 1 else 1
        start = (0, 1, blocks + 1)[which]
        for half, names in enumerate(slot_rows(coupled[which])):
            named = jnp.transpose(spread(names, LANES).astype(jnp.float32))
            for b in range(count):
                cell = (lane_iota(LANES) + (first + b * LANES)).astype(jnp.float32)
                picked = jnp.where(named == cell, 1.0, 0.0).astype(jnp.bfloat16)
                lanes = slice((start + b) * LANES, (start + b + 1) * LANES)
                sums[half * LANES : (half + 1) * LANES, lanes] = picked


def node_currents(table, slot, which, capacity):
    peers = table.shape[0]
    owner = row_iota(peers) == slot // capacity
    out = []
    for part in range(2):
        lane = (2 * which + part) * capacity + slot % capacity
        found = jnp.where(owner, lane_gather(table, spread(lane, peers)), 0.0)
        out.append(jnp.sum(found, axis=0, keepdims=True))
    return out


def wave_kernel(
    capacity, step_pairs, dirs,
    spectra, outer, inner, table, node_slot, neighbors, cosine, sine, project, choice, ways, slots,
    own_change,
    spectra_new, rows_out, drift, halos, change_a, change_b,
):
    me = lax.axis_index("mesh")
    freqs, stride = spectra.shape[:2]
    edges = neighbors.shape[0]
    peers = table.shape[0]
    pairs = freqs // 2
    whole = dirs // 8 * 8
    rest = dirs - whole
    base = outer.shape[0] - (pairs * dirs + 7) // 8 * 8

    odd = me % 2 == 1
    slot = node_slot[...]
    row = base - TABLE_ROWS + edges
    halo_slot = jnp.where(
        half_mask(1, odd), outer[row : row + 1, :], inner[row : row + 1, :]
    ).astype(jnp.int32)
    lower = lane_iota(1) < LANES // 2
    currents = table[...]
    own_x, own_y = node_currents(currents, slot, jnp.ones((1, LANES), jnp.int32), capacity)
    halo_x, halo_y = node_currents(currents, halo_slot, jnp.where(lower, 2, 0), capacity)

    target = neighbors[...]
    lane = target % LANES
    inside = target // LANES == me

    def beside(own, halo):
        a = lane_gather(spread(own, edges), lane)
        b = lane_gather(spread(halo, edges), lane)
        return jnp.where(inside, a, b)

    drift[0:edges, :] = (
        0.5 * (own_x + beside(own_x, halo_x)) * cosine[...]
        + 0.5 * (own_y + beside(own_y, halo_y)) * sine[...]
    )
    drifts = [spread(drift[s : s + 1, :], 8) for s in range(edges)]
    from_outer = half_mask(dirs, odd)
    halos[...] = jnp.zeros(halos.shape, jnp.float32)
    ratio = 1.0 / 1.1
    bands = [slice(r, r + 8) for r in range(0, stride, 8)]

    def gather(c, change):
        for i in range(step_pairs):
            g = c * step_pairs + i
            parts = []
            for message in (outer, inner):
                at = base + g * whole
                upper = message[at : at + whole, :]
                at = base + pairs * whole + g * rest
                left = message[at : at + rest, :]
                parts.append(jnp.concatenate([upper, left], axis=0))
            x, y = parts
            at = 2 * i * stride
            halos[at : at + dirs, :] = jnp.where(from_outer, x, y)
            at += stride
            halos[at : at + dirs, :] = pltpu.roll(jnp.where(from_outer, y, x), LANES // 2, 1)
        mixed = jnp.concatenate(split(halos[...]), axis=1)
        change[...] = jnp.dot(
            mixed, choice[2 * LANES : 4 * LANES, :], preferred_element_type=jnp.float32
        )

    def advect(c, change, first_speed, first_slow, total):
        total = list(total)
        speeds = []
        for i in range(step_pairs):
            speeds += [first_speed * ratio**i, first_speed * ratio ** (i + pairs)]
        slowness = []
        for i in range(step_pairs):
            slowness += [first_slow * ratio**-i, first_slow * ratio ** -(i + pairs)]
        relative = [[drift * slow for drift in drifts] for slow in slowness]
        relative_sum = [sum(each[1:], each[0]) for each in relative]
        for k, band in enumerate(bands):
            along = [project[s, band, :] for s in range(edges)]
            along_sum = sum(along[1:], along[0])
            for i in range(step_pairs):
                g = c * step_pairs + i
                for j, f in ((2 * i, g), (2 * i + 1, g + pairs)):
                    own = spectra[f, band, :]
                    at = j * stride + band.start
                    own_at = slice(f * stride + band.start, f * stride + band.stop)
                    flux = (along_sum + relative_sum[j]) * own
                    for s in range(edges):
                        down = jnp.minimum(along[s] + relative[j][s], 0.0)
                        lanes = slice(s * LANES, (s + 1) * LANES)
                        step = change[at : at + 8, lanes] + own_change[own_at, lanes]
                        flux = flux + down * step
                    value = own - speeds[j] * flux
                    spectra_new[f, band, :] = value
                    total[k] = total[k] + value
        return first_speed * ratio**step_pairs, first_slow * ratio**-step_pairs, tuple(total)

    zeros = tuple(jnp.zeros((8, LANES), jnp.float32) for _ in bands)
    chunks = pairs // step_pairs
    buffers = (change_a, change_b)
    carry = (1.0, 1.0, zeros)
    gather(0, change_a)
    for c in range(chunks):
        if c + 1 < chunks:
            gather(c + 1, buffers[(c + 1) % 2])
        carry = advect(c, buffers[c % 2], *carry)
    total = carry[2]
    total = jnp.concatenate(total, axis=0)
    zero = jnp.zeros((stride, LANES), jnp.float32)
    cos_dir, sin_dir = ways[0], ways[1]
    mean = jnp.sum(total, axis=0, keepdims=True) * (1.0 / (freqs * dirs))
    step = jnp.exp((ways[2] - 2.0 * mean) * (1.0 / freqs))
    factor = zero + 1.0
    weighted = zero
    for f in range(freqs):
        factor = factor * step
        evolved = spectra_new[f] * factor
        spectra_new[f] = evolved
        weighted = weighted + ((f + 1) / (freqs * dirs)) * evolved
    drift_x = jnp.sum(weighted * cos_dir, axis=0, keepdims=True)
    drift_y = jnp.sum(weighted * sin_dir, axis=0, keepdims=True)
    node = slots[...] - 1
    pick = jnp.maximum(node, 0)
    first = lane_gather(spread(drift_x, peers), pick)
    second = lane_gather(spread(drift_y, peers), pick)
    part = lane_iota(peers) // capacity % 2
    rows_out[...] = jnp.where(node < 0, 0.0, jnp.where(part == 0, first, second))


def two_parts(values):
    first = values.astype(jnp.bfloat16).astype(jnp.float32)
    pad = jnp.zeros((4, values.shape[1]), jnp.float32)
    return jnp.concatenate([first, values - first, pad], axis=0)


def tracer_kernel(
    capacity, shape,
    outer, inner, table, fields, neighbors, matrices, inside, cosine, sine, scale, sums, spectra,
    tracers_new, spectra_out,
    halo, halo_near, halo_tables, stokes, antiflux, lowered, ratios,
    ratio_pieces, steps_a, steps_b, sem,
):
    dirs = spectra_out.shape[1]
    write = pltpu.make_async_copy(spectra.at[:, 0:dirs, :], spectra_out, sem)
    write.start()
    me = lax.axis_index("mesh")
    tracer_count, layers, edges = shape
    peers = table.shape[0]
    halves = peers * capacity // LANES
    blocks, field_rows, _ = fields.shape
    layer_groups = layers // 8
    tracer_groups = tracer_count * layer_groups
    odd = me % 2 == 1

    for b in range(2):
        x = outer[b * field_rows : (b + 1) * field_rows, :]
        y = inner[b * field_rows : (b + 1) * field_rows, :]
        for side, value in ((0, jnp.where(odd, y, x)), (1, jnp.where(odd, x, y))):
            halo[2 * side + b] = value
    at = 2 * field_rows
    x = outer[at : at + TABLE_ROWS, :]
    y = inner[at : at + TABLE_ROWS, :]
    for side, rows in ((0, jnp.where(odd, y, x)), (1, jnp.where(odd, x, y))):
        w = rows[16 : 16 + edges]
        halo_tables[side, 0, 0:edges, :] = w
        halo_tables[side, 1, 0:edges, :] = w * jnp.cos(rows[8 : 8 + edges])
        halo_tables[side, 2, 0:edges, :] = w * jnp.sin(rows[8 : 8 + edges])
        halo_near[side, 0:edges, :] = rows[0:edges].astype(jnp.int32)

    received = table[...]
    lane_of = lane_iota(peers)
    sections = []
    for which in range(3):
        values = []
        for part in range(2):
            lane = (2 * which + part) * capacity + lane_of % capacity
            found = lane_gather(received, lane)
            row = []
            for half in range(halves):
                mine = row_iota(peers) == (lane_of + half * LANES) // capacity
                row.append(jnp.sum(jnp.where(mine, found, 0.0), axis=0, keepdims=True))
            values.append(jnp.concatenate(row, axis=1))
        sections.append(two_parts(jnp.concatenate(values, axis=0)))
    sections.append(jnp.zeros_like(sections[0]))
    total = jnp.dot(
        jnp.concatenate(sections, axis=0).astype(jnp.bfloat16),
        sums[...],
        preferred_element_type=jnp.float32,
    )
    for b in range(blocks + 2):
        which = 0 if b == 0 else 2 if b == blocks + 1 else 1
        at = 8 * which
        lanes = slice(b * LANES, (b + 1) * LANES)
        stokes[b, 0:2, :] = total[at : at + 2, lanes] + total[at + 2 : at + 4, lanes]

    decay = [
        jnp.exp(-3.0 / layers * (row_iota(8) + 8 * g).astype(jnp.float32))
        for g in range(layer_groups)
    ]

    def low_order(b, value, change, wx, wy, keep):
        slope = wx * stokes[b, 0:1, :] + wy * stokes[b, 1:2, :]
        own = [value(8 * g) for g in range(tracer_groups)]
        zero = jnp.zeros((8, LANES), jnp.float32)
        speed_sum = [zero] * layer_groups
        inflow = [zero] * tracer_groups
        highest = [zero] * tracer_groups
        lowest = [zero] * tracer_groups
        positive = [zero] * tracer_groups
        negative = [zero] * tracer_groups
        for s in range(edges):
            slope8 = spread(slope[s : s + 1, :], 8)
            for lg in range(layer_groups):
                speed = change(8 * (tracer_groups + lg), s) + decay[lg] * slope8
                down = jnp.minimum(speed, 0.0)
                half = 0.5 * speed - down
                speed_sum[lg] = speed_sum[lg] + speed
                for t in range(tracer_count):
                    g = t * layer_groups + lg
                    step = change(8 * g, s)
                    flux = half * step
                    if keep:
                        antiflux[b - 1, s, 8 * g : 8 * g + 8, :] = flux
                    inflow[g] = inflow[g] + down * step
                    highest[g] = jnp.maximum(highest[g], step)
                    lowest[g] = jnp.minimum(lowest[g], step)
                    positive[g] = positive[g] + jnp.maximum(flux, 0.0)
                    negative[g] = negative[g] - jnp.minimum(flux, 0.0)
        plus, minus = [], []
        for g in range(tracer_groups):
            loss = speed_sum[g % layer_groups] * own[g] + inflow[g]
            if keep:
                lowered[b - 1, 8 * g : 8 * g + 8, :] = own[g] - loss
            up = jnp.maximum(highest[g] + loss, 0.0) / (negative[g] + FCT_FLOOR)
            down = jnp.maximum(-loss - lowest[g], 0.0) / (positive[g] + FCT_FLOOR)
            plus.append(jnp.minimum(1.0, up))
            minus.append(jnp.minimum(1.0, down))
        both = jnp.concatenate(plus + minus, axis=0)
        ratios[b] = both
        ratio_pieces[b] = stack_split(both)

    def band(ref, *index):
        return lambda row: ref[(*index, slice(row, row + 8), slice(None))]

    potential_row = tracer_groups * 8

    def within(i):
        return lambda row, s: inside[i, row : row + 8, s * LANES : (s + 1) * LANES]

    def edge(i, side):
        beside = halo.at[1 + side]
        sign = 2 * side - 1

        def change(row, s):
            near = spread(neighbors[s : s + 1, i * LANES : (i + 1) * LANES], 8)
            from_halo = near // LANES - (me * blocks + i) == sign
            picked = lane_gather(beside[row : row + 8, :], near % LANES)
            if row >= potential_row:
                picked = picked * spread(scale[i, s : s + 1, :], 8)
            return within(i)(row, s) + jnp.where(from_halo, picked, 0.0)

        return change

    def outside(side):
        i = side * (blocks - 1)
        low, own, high = (
            (halo.at[0], halo.at[1], fields.at[i]),
            (fields.at[i], halo.at[2], halo.at[3]),
        )[side]

        def change(row, s):
            rows = slice(row, row + 8)
            near = spread(halo_near[side, s : s + 1, :], 8)
            place = near // LANES - (me * blocks + i + 2 * side - 1)
            lane = near % LANES
            mine = own[rows, :]
            middle = lane_gather(mine, lane)
            left = lane_gather(low[rows, :], lane)
            right = lane_gather(high[rows, :], lane)
            out = jnp.where(place == 0, middle, jnp.where(place < 0, left, right)) - mine
            if row >= potential_row:
                out = out * spread(halo_tables[side, 0, s : s + 1, :], 8)
            return out

        return change

    for i in range(1, blocks - 1):
        low_order(i + 1, band(fields, i), within(i), cosine[i], sine[i], True)
    for side in range(2):
        b = side * (blocks + 1)
        tables = (halo_tables[side, 1], halo_tables[side, 2])
        low_order(b, band(halo, 1 + side), outside(side), *tables, False)
        i = side * (blocks - 1)
        low_order(i + 1, band(fields, i), edge(i, side), cosine[i], sine[i], True)

    def products(i, steps):
        mixed = jnp.concatenate([ratio_pieces[i], ratio_pieces[i + 1], ratio_pieces[i + 2]], axis=1)
        steps[...] = jnp.dot(mixed, matrices[i], preferred_element_type=jnp.float32)

    def limit(i, steps):
        out = [lowered[i, 8 * g : 8 * g + 8, :] for g in range(tracer_groups)]
        own = [ratios[i + 1, 8 * g : 8 * g + 8, :] for g in range(2 * tracer_groups)]
        low = 16 * tracer_groups
        for s in range(edges):
            lanes = slice(s * LANES, (s + 1) * LANES)
            beside = [
                own[g]
                + (steps[8 * g : 8 * g + 8, lanes] + steps[low + 8 * g : low + 8 * g + 8, lanes])
                for g in range(2 * tracer_groups)
            ]
            for g in range(tracer_groups):
                m = g + tracer_groups
                flux = antiflux[i, s, 8 * g : 8 * g + 8, :]
                factor = jnp.where(
                    flux >= 0.0, jnp.minimum(own[m], beside[g]), jnp.minimum(own[g], beside[m])
                )
                out[g] = out[g] - factor * flux
        lanes = slice(i * LANES, (i + 1) * LANES)
        for g in range(tracer_groups):
            t, lg = g // layer_groups, g % layer_groups
            tracers_new[t, 8 * lg : 8 * lg + 8, lanes] = out[g]

    buffers = (steps_a, steps_b)
    products(0, steps_a)
    for i in range(blocks):
        if i + 1 < blocks:
            products(i + 1, buffers[(i + 1) % 2])
        limit(i, buffers[i % 2])
    write.wait()


def swap(message, first, peers):
    pairs = []
    for i in range(first, peers - 1, 2):
        pairs += [(i, i + 1), (i + 1, i)]
    return lax.ppermute(message, "mesh", pairs)


def whole_spec():
    return pl.BlockSpec(memory_space=pltpu.VMEM)


def local(
    tracers,
    potential,
    surface_current,
    cell_neighbors,
    cell_normal,
    cell_weight,
    spectra,
    wind_velocity,
    node_neighbors,
    node_normal,
    node_weight,
    send_rows,
    node_slot,
):
    peers, _, capacity = send_rows.shape
    freqs, dirs, nodes = spectra.shape
    tracer_count, layers, cells = tracers.shape
    edges = cell_neighbors.shape[0]
    blocks = cells // LANES
    field_rows = (tracer_count + 1) * layers
    head_rows = 2 * field_rows + TABLE_ROWS
    message_rows = head_rows + (freqs // 2 * dirs + 7) // 8 * 8
    slots = node_slot.reshape(1, nodes)
    params = pltpu.CompilerParams(vmem_limit_bytes=VMEM_LIMIT)
    f32 = jnp.float32

    stored = pl.BlockSpec(memory_space=pltpu.HBM)
    rows = tracer_count * layers
    stride = (dirs + 7) // 8 * 8
    step_pairs = 5 if freqs % 10 == 0 else 1
    step_rows = 2 * step_pairs * stride

    def like(x):
        return jax.ShapeDtypeStruct(x.shape, x.dtype)

    def shaped(*shape, dtype=f32):
        return jax.ShapeDtypeStruct(shape, dtype)

    def call(kernel, name, inputs, outputs, scratch, out_specs=None):
        return pl.pallas_call(
            kernel,
            out_shape=outputs,
            in_specs=[whole_spec()] * len(inputs),
            out_specs=out_specs or (whole_spec(),) * len(outputs),
            scratch_shapes=scratch,
            compiler_params=params,
            name=name,
        )(*inputs)

    inputs = (
        spectra, tracers, potential, cell_neighbors, cell_normal, cell_weight, surface_current,
        send_rows, slots, node_neighbors, node_normal, node_weight, wind_velocity,
    )
    (
        currents, outer, inner, own_spectra, own_slots, near, angle, face, wind,
        own_tracers, own_potential, neighbors, normal, weight, coupled,
    ) = pl.pallas_call(
        pack_kernel,
        out_shape=(
            shaped(peers, LANES),
            shaped(message_rows, LANES),
            shaped(message_rows, LANES),
            shaped(freqs, stride, LANES),
            like(slots),
            like(node_neighbors),
            like(node_normal),
            like(node_weight),
            like(wind_velocity),
            like(tracers),
            like(potential),
            like(cell_neighbors),
            like(cell_normal),
            like(cell_weight),
            shaped(3, peers, capacity, dtype=jnp.int32),
        ),
        in_specs=[stored] * len(inputs),
        out_specs=(whole_spec(),) * 15,
        scratch_shapes=[
            pltpu.VMEM(surface_current.shape, f32),
            pltpu.SemaphoreType.DMA((15,)),
        ],
        compiler_params=params,
        name="pack",
    )(*(pltpu.with_memory_space_constraint(x, pltpu.HBM) for x in inputs))
    outer = swap(outer, 1, peers)
    inner = swap(inner, 0, peers)

    (
        cosine, sine, project, choice, ways, slot_choice, own_change,
        fields, matrices, inside, cell_cosine, cell_sine, cell_scale, sums,
    ) = call(
        functools.partial(prepare_kernel, dirs, step_rows),
        "prepare",
        (
            own_spectra, near, angle, face, wind, own_slots, own_tracers, own_potential,
            neighbors, normal, weight, coupled,
        ),
        (
            like(node_normal),
            like(node_normal),
            shaped(edges, stride, LANES),
            shaped(4 * LANES, edges * LANES, dtype=jnp.bfloat16),
            shaped(3, stride, LANES),
            shaped(peers, LANES, dtype=jnp.int32),
            shaped(freqs * stride, edges * LANES),
            shaped(blocks, field_rows, LANES),
            shaped(blocks, 3 * LANES, edges * LANES, dtype=jnp.bfloat16),
            shaped(blocks, field_rows, edges * LANES),
            shaped(blocks, 8, LANES),
            shaped(blocks, 8, LANES),
            shaped(blocks, 8, LANES),
            shaped(peers * capacity, (blocks + 2) * LANES, dtype=jnp.bfloat16),
        ),
        [pltpu.VMEM((blocks, 2 * field_rows, LANES), jnp.bfloat16)],
    )
    currents, cosine = lax.optimization_barrier((currents, cosine))
    currents = lax.all_to_all(currents, "mesh", 0, 0, tiled=True)

    spectra_new, stokes_rows = call(
        functools.partial(wave_kernel, capacity, step_pairs, dirs),
        "wave",
        (
            own_spectra, outer, inner, currents, own_slots, near,
            cosine, sine, project, choice, ways, slot_choice, own_change,
        ),
        (shaped(freqs, stride, LANES), shaped(peers, LANES)),
        [
            pltpu.VMEM((8, LANES), f32),
            pltpu.VMEM((step_rows, LANES), f32),
            pltpu.VMEM((step_rows, edges * LANES), f32),
            pltpu.VMEM((step_rows, edges * LANES), f32),
        ],
    )
    stokes_all = lax.all_to_all(stokes_rows, "mesh", 0, 0, tiled=True)

    return call(
        functools.partial(tracer_kernel, capacity, (tracer_count, layers, edges)),
        "tracer",
        (
            outer, inner, stokes_all, fields, neighbors, matrices, inside, cell_cosine, cell_sine,
            cell_scale, sums, pltpu.with_memory_space_constraint(spectra_new, pltpu.VMEM),
        ),
        (like(tracers), like(spectra)),
        [
            pltpu.VMEM((4, field_rows, LANES), f32),
            pltpu.VMEM((2, 8, LANES), jnp.int32),
            pltpu.VMEM((2, 3, 8, LANES), f32),
            pltpu.VMEM((blocks + 2, 8, LANES), f32),
            pltpu.VMEM((blocks, edges, rows, LANES), f32),
            pltpu.VMEM((blocks, rows, LANES), f32),
            pltpu.VMEM((blocks + 2, 2 * rows, LANES), f32),
            pltpu.VMEM((blocks + 2, 4 * rows, LANES), jnp.bfloat16),
            pltpu.VMEM((4 * rows, edges * LANES), f32),
            pltpu.VMEM((4 * rows, edges * LANES), f32),
            pltpu.SemaphoreType.DMA(()),
        ],
        out_specs=(whole_spec(), stored),
    )


def solution(mesh):
    return jax.shard_map(
        local,
        mesh=mesh,
        in_specs=(
            P(None, None, ("groups", "mesh")),
            P(None, ("groups", "mesh")),
            P(None, ("groups", "mesh")),
            P(None, "mesh"),
            P(None, "mesh"),
            P(None, "mesh"),
            P(None, None, ("groups", "mesh")),
            P(None, ("groups", "mesh")),
            P(None, "mesh"),
            P(None, "mesh"),
            P(None, "mesh"),
            P(),
            P("mesh"),
        ),
        out_specs=(P(None, None, ("groups", "mesh")), P(None, None, ("groups", "mesh"))),
        check_vma=False,
    )
```

```python
import functools
import math

import jax
import jax.numpy as jnp
from jax import lax
from jax.experimental import pallas as pl
from jax.experimental.pallas import tpu as pltpu
from jax.sharding import PartitionSpec as P

LANES = 128
FCT_FLOOR = 0.001
TABLE_ROWS = 24
VMEM_LIMIT = 32 * 1024 * 1024


def lane_gather(values, index):
    return jnp.take_along_axis(values, index, axis=1, mode="promise_in_bounds")


def spread(row, count):
    return jnp.broadcast_to(row, (count, LANES))


def lane_iota(rows):
    return lax.broadcasted_iota(jnp.int32, (rows, LANES), 1)


def row_iota(rows):
    return lax.broadcasted_iota(jnp.int32, (rows, LANES), 0)


def slot_rows(entry):
    peers, capacity = entry.shape
    wide = jnp.concatenate([entry, jnp.zeros((peers, LANES - capacity), jnp.int32)], axis=1)
    wide = lane_gather(wide, lane_iota(peers) % capacity)
    owner = row_iota(peers)
    out = []
    for half in range(peers * capacity // LANES):
        wanted = (lane_iota(peers) + half * LANES) // capacity
        picked = jnp.where(owner == wanted, wide, 0).astype(jnp.float32)
        out.append(jnp.sum(picked, axis=0, keepdims=True).astype(jnp.int32))
    return out


def half_mask(rows, lower):
    half = lane_iota(rows) // (LANES // 2)
    return half == jnp.where(lower, 0, 1)


def peer_rows(values, peers, capacity):
    lane = lane_iota(peers)
    group = lane // capacity
    block = jnp.clip(row_iota(peers) - 1 + group // 2, 0, peers - 1)
    entry = block * capacity + lane % capacity
    out = jnp.zeros((peers, LANES), jnp.float32)
    for part in range(2):
        for half, row in enumerate(values[part]):
            found = lane_gather(spread(row, peers), entry % LANES)
            wanted = (group < 6) & (group % 2 == part) & (entry // LANES == half)
            out = jnp.where(wanted, found, out)
    return out


def direction(dirs, padded):
    turn = row_iota(padded).astype(jnp.float32) * (2.0 * math.pi / dirs)
    return jnp.cos(turn), jnp.sin(turn)


def node_tables(
    me, dirs, near, angle, face, wind, slot, cosine, sine, project, choice, ways, slots
):
    edges, padded = project.shape[:2]
    cosine[...] = face[...] * jnp.cos(angle[...])
    sine[...] = face[...] * jnp.sin(angle[...])
    cos_dir, sin_dir = direction(dirs, padded)
    ways[0] = cos_dir
    ways[1] = sin_dir
    ways[2] = 0.25 * jnp.maximum(wind[0:1, :] * cos_dir + wind[1:2, :] * sin_dir, 0.0)
    taken = jnp.transpose(spread(slot[...].astype(jnp.float32), LANES))
    for half in range(slots.shape[1] // LANES):
        number = (lane_iota(LANES) + half * LANES).astype(jnp.float32)
        picked = jnp.where(taken == number, 1.0, 0.0).astype(jnp.bfloat16)
        slots[:, half * LANES : (half + 1) * LANES] = picked
    source = row_iota(LANES)
    minus = jnp.where(source == lane_iota(LANES), -1.0, 0.0)
    for s in range(edges):
        project[s] = cos_dir * cosine[s : s + 1, :] + sin_dir * sine[s : s + 1, :]
        target = near[s : s + 1, :]
        inside = target // LANES == me
        lane = target % LANES
        own = jnp.where(source == jnp.where(inside, lane, LANES), 1.0, 0.0) + minus
        halo = jnp.where(source == jnp.where(inside, LANES, lane), 1.0, 0.0)
        lanes = slice(s * LANES, (s + 1) * LANES)
        for k, part in enumerate((own, own, halo, halo)):
            choice[k * LANES : (k + 1) * LANES, lanes] = part.astype(jnp.bfloat16)


def split(x):
    first = x.astype(jnp.bfloat16)
    return first, (x - first.astype(jnp.float32)).astype(jnp.bfloat16)


def spot(refs, counts, head, g, whole, rest):
    for k, count in enumerate(counts):
        if g < count:
            start = head if k == 0 else 0
            return refs[k], start + g * whole, start + count * whole + g * rest
        g -= count


def pack_kernel(
    spectra_in, tracers_in, potential_in, neighbors_in, normal_in, weight_in, current_in,
    send_rows, slot_in, near_in, angle_in, face_in, wind_in,
    rows_out, outer, more, inner, spectra, node_slot, near, angle, face, wind,
    tracers, potential, neighbors, normal, weight, coupled,
    current, sems,
):
    peers, _, capacity = send_rows.shape
    me = lax.axis_index("mesh")
    freqs, dirs = spectra_in.shape[:2]
    if dirs < spectra.shape[1]:
        for f in range(freqs):
            spectra[f, dirs // 8 * 8 :, :] = jnp.zeros((8, LANES), jnp.float32)
    pairs = freqs // 2
    copies = []
    for source, target in (
        (send_rows.at[me], coupled.at[1]),
        (current_in, current),
        (slot_in, node_slot),
        (spectra_in, spectra.at[:, 0:dirs, :]),
        (tracers_in, tracers),
        (potential_in, potential),
        (neighbors_in, neighbors),
        (normal_in, normal),
        (weight_in, weight),
        (send_rows.at[jnp.maximum(me - 1, 0)], coupled.at[0]),
        (send_rows.at[jnp.minimum(me + 1, peers - 1)], coupled.at[2]),
        (near_in, near),
        (angle_in, angle),
        (face_in, face),
        (wind_in, wind),
    ):
        copy = pltpu.make_async_copy(source, target, sems.at[len(copies)])
        copy.start()
        copies.append(copy)
    for copy in copies[:3]:
        copy.wait()
    layers, cells = potential.shape
    blocks = cells // LANES
    field_rows = (tracers.shape[0] + 1) * layers
    stacked = jnp.concatenate(
        [current[:, b * LANES : (b + 1) * LANES] for b in range(blocks)], axis=0
    )
    place = row_iota(2 * blocks)
    halves = slot_rows(coupled[1])
    values = [[], []]
    for cell in halves:
        found = lane_gather(stacked, spread(cell % LANES, 2 * blocks))
        for part in range(2):
            picked = jnp.where(place == 2 * (cell // LANES) + part, found, 0.0)
            values[part].append(jnp.sum(picked, axis=0, keepdims=True))
    rows_out[...] = peer_rows(values, peers, capacity)
    for copy in copies[4:9]:
        copy.wait()
    odd = me % 2 == 1
    for out, upward in ((outer, odd), (inner, jnp.logical_not(odd))):
        for b in range(2):
            high = slice((blocks - 2 + b) * LANES, (blocks - 1 + b) * LANES)
            low = slice(b * LANES, (b + 1) * LANES)
            base = b * field_rows
            for t in range(tracers.shape[0]):
                out[base + t * layers : base + (t + 1) * layers, :] = jnp.where(
                    upward, tracers[t, :, high], tracers[t, :, low]
                )
            out[base + field_rows - layers : base + field_rows, :] = jnp.where(
                upward, potential[:, high], potential[:, low]
            )
        high = slice((blocks - 1) * LANES, blocks * LANES)
        low = slice(0, LANES)
        base = 2 * field_rows
        out[base : base + TABLE_ROWS, :] = jnp.zeros((TABLE_ROWS, LANES), jnp.float32)
        edges = neighbors.shape[0]
        near = jnp.where(upward, neighbors[:, high], neighbors[:, low])
        out[base : base + edges, :] = near.astype(jnp.float32)
        out[base + edges : base + edges + 1, :] = node_slot[...].astype(jnp.float32)
        out[base + 8 : base + 8 + edges, :] = jnp.where(upward, normal[:, high], normal[:, low])
        out[base + 16 : base + 16 + edges, :] = jnp.where(upward, weight[:, high], weight[:, low])
    base = 2 * field_rows + TABLE_ROWS
    whole = dirs // 8 * 8
    rest = dirs - whole
    turns = half_mask(dirs, odd)
    copies[3].wait()
    for g in range(pairs):
        natural = spectra[g, 0:dirs, :]
        turned = pltpu.roll(spectra[g + pairs, 0:dirs, :], LANES // 2, 1)
        for refs, counts, mixed in (
            ((outer, more), (pairs // 2, pairs - pairs // 2), jnp.where(turns, turned, natural)),
            ((inner,), (pairs,), jnp.where(turns, natural, turned)),
        ):
            out, at, left = spot(refs, counts, base, g, whole, rest)
            out[at : at + whole, :] = mixed[:whole]
            out[left : left + rest, :] = mixed[whole:]
    for copy in copies[9:]:
        copy.wait()


def choose(cells, first, lanes, matrix):
    place = (cells - first - LANES).astype(jnp.float32).astype(jnp.bfloat16)
    place = spread(place, LANES)
    one = jnp.ones((LANES, LANES), jnp.bfloat16)
    for k in range(3):
        source = (row_iota(LANES) + (k - 1) * LANES).astype(jnp.float32).astype(jnp.bfloat16)
        part = jnp.where(source == place, one, 0 * one)
        if k == 1:
            own = jnp.where(row_iota(LANES) == lane_iota(LANES), 1.0, 0.0).astype(jnp.bfloat16)
            part = part - own
        matrix[k * LANES : (k + 1) * LANES, lanes] = part


def stack_split(x):
    first, second = split(x)
    return jnp.concatenate([first, second], axis=0)


def differences(parts, matrix):
    mixed = jnp.concatenate(parts, axis=1)
    out = jnp.dot(mixed, matrix, preferred_element_type=jnp.float32)
    rows = out.shape[0] // 2
    return out[:rows] + out[rows:]


def prepare_kernel(
    dirs, step_rows,
    spectra, near, angle, face, wind, slot, tracers, potential, neighbors, normal, weight, coupled,
    cosine, sine, project, choice, ways, slots, own_change,
    fields, matrices, inside, cell_cosine, cell_sine, cell_scale, sums,
    pieces,
):
    me = lax.axis_index("mesh")
    node_tables(
        me, dirs, near, angle, face, wind, slot, cosine, sine, project, choice, ways, slots
    )
    freqs, padded, _ = spectra.shape
    step = step_rows // padded

    for c in range(freqs // step):
        own = spectra[c * step : (c + 1) * step].reshape(step_rows, LANES)
        own_change[c * step_rows : (c + 1) * step_rows, :] = jnp.dot(
            jnp.concatenate(split(own), axis=1),
            choice[0 : 2 * LANES, :],
            preferred_element_type=jnp.float32,
        )
    tracer_count, layers, cells = tracers.shape
    blocks = cells // LANES
    edges = neighbors.shape[0]
    field_rows = (tracer_count + 1) * layers
    for b in range(blocks):
        lanes = slice(b * LANES, (b + 1) * LANES)
        for t in range(tracer_count):
            fields[b, t * layers : (t + 1) * layers, :] = tracers[t, :, lanes]
        fields[b, field_rows - layers : field_rows, :] = potential[:, lanes]
        pieces[b] = stack_split(fields[b])
        w = weight[:, lanes]
        cell_scale[b, 0:edges, :] = w
        cell_cosine[b, 0:edges, :] = w * jnp.cos(normal[:, lanes])
        cell_sine[b, 0:edges, :] = w * jnp.sin(normal[:, lanes])
        for s in range(edges):
            choose(
                neighbors[s : s + 1, lanes],
                (me * blocks + b - 1) * LANES,
                slice(s * LANES, (s + 1) * LANES),
                matrices.at[b],
            )
    for b in range(blocks):
        first, last = max(b - 1, 0), min(b + 1, blocks - 1)
        rows = slice((first - b + 1) * LANES, (last - b + 2) * LANES)
        parts = [pieces[k] for k in range(first, last + 1)]
        change = differences(parts, matrices[b, rows, :])
        last_field = field_rows - layers
        inside[b, 0:last_field, :] = change[:last_field]
        for s in range(edges):
            at = slice(s * LANES, (s + 1) * LANES)
            inside[b, last_field:, at] = change[last_field:, at] * cell_scale[b, s : s + 1, :]
    for which in range(3):
        first = 0 if which != 0 else cells - LANES
        count = blocks if which == 1 else 1
        start = (0, 1, blocks + 1)[which]
        for half, names in enumerate(slot_rows(coupled[which])):
            named = jnp.transpose(spread(names, LANES).astype(jnp.float32))
            for b in range(count):
                cell = (lane_iota(LANES) + (first + b * LANES)).astype(jnp.float32)
                picked = jnp.where(named == cell, 1.0, 0.0).astype(jnp.bfloat16)
                lanes = slice((start + b) * LANES, (start + b + 1) * LANES)
                sums[half * LANES : (half + 1) * LANES, lanes] = picked


def node_currents(table, slot, which, capacity):
    peers = table.shape[0]
    owner = row_iota(peers) == slot // capacity
    out = []
    for part in range(2):
        lane = (2 * which + part) * capacity + slot % capacity
        found = jnp.where(owner, lane_gather(table, spread(lane, peers)), 0.0)
        out.append(jnp.sum(found, axis=0, keepdims=True))
    return out


def wave_kernel(
    capacity, step_pairs, dirs, field_rows,
    spectra, outer, more, inner, table, node_slot, neighbors, cosine, sine, project, choice, ways, slots,
    own_change,
    spectra_new, rows_out, drift, halos, change_a, change_b,
):
    me = lax.axis_index("mesh")
    freqs, stride = spectra.shape[:2]
    edges = neighbors.shape[0]
    peers = table.shape[0]
    halves = peers * capacity // LANES
    pairs = freqs // 2
    whole = dirs // 8 * 8
    rest = dirs - whole
    base = 2 * field_rows + TABLE_ROWS

    odd = me % 2 == 1
    slot = node_slot[...]
    row = base - TABLE_ROWS + edges
    halo_slot = jnp.where(
        half_mask(1, odd), outer[row : row + 1, :], inner[row : row + 1, :]
    ).astype(jnp.int32)
    lower = lane_iota(1) < LANES // 2
    currents = table[...]
    own_x, own_y = node_currents(currents, slot, jnp.ones((1, LANES), jnp.int32), capacity)
    halo_x, halo_y = node_currents(currents, halo_slot, jnp.where(lower, 2, 0), capacity)

    target = neighbors[...]
    lane = target % LANES
    inside = target // LANES == me

    def beside(own, halo):
        a = lane_gather(spread(own, edges), lane)
        b = lane_gather(spread(halo, edges), lane)
        return jnp.where(inside, a, b)

    drift[0:edges, :] = (
        0.5 * (own_x + beside(own_x, halo_x)) * cosine[...]
        + 0.5 * (own_y + beside(own_y, halo_y)) * sine[...]
    )
    drifts = [spread(drift[s : s + 1, :], 8) for s in range(edges)]
    from_outer = half_mask(dirs, odd)
    halos[...] = jnp.zeros(halos.shape, jnp.float32)
    ratio = 1.0 / 1.1
    bands = [slice(r, r + 8) for r in range(0, stride, 8)]

    def gather(c, change):
        for i in range(step_pairs):
            g = c * step_pairs + i
            parts = []
            for refs, counts in (
                ((outer, more), (pairs // 2, pairs - pairs // 2)),
                ((inner,), (pairs,)),
            ):
                message, at, low = spot(refs, counts, base, g, whole, rest)
                upper = message[at : at + whole, :]
                left = message[low : low + rest, :]
                parts.append(jnp.concatenate([upper, left], axis=0))
            x, y = parts
            at = 2 * i * stride
            halos[at : at + dirs, :] = jnp.where(from_outer, x, y)
            at += stride
            halos[at : at + dirs, :] = pltpu.roll(jnp.where(from_outer, y, x), LANES // 2, 1)
        mixed = jnp.concatenate(split(halos[...]), axis=1)
        change[...] = jnp.dot(
            mixed, choice[2 * LANES : 4 * LANES, :], preferred_element_type=jnp.float32
        )

    def advect(c, change, first_speed, first_slow, total):
        total = list(total)
        speeds = []
        for i in range(step_pairs):
            speeds += [first_speed * ratio**i, first_speed * ratio ** (i + pairs)]
        slowness = []
        for i in range(step_pairs):
            slowness += [first_slow * ratio**-i, first_slow * ratio ** -(i + pairs)]
        relative = [[drift * slow for drift in drifts] for slow in slowness]
        relative_sum = [sum(each[1:], each[0]) for each in relative]
        for k, band in enumerate(bands):
            along = [project[s, band, :] for s in range(edges)]
            along_sum = sum(along[1:], along[0])
            for i in range(step_pairs):
                g = c * step_pairs + i
                for j, f in ((2 * i, g), (2 * i + 1, g + pairs)):
                    own = spectra[f, band, :]
                    at = j * stride + band.start
                    own_at = slice(f * stride + band.start, f * stride + band.stop)
                    flux = (along_sum + relative_sum[j]) * own
                    for s in range(edges):
                        down = jnp.minimum(along[s] + relative[j][s], 0.0)
                        lanes = slice(s * LANES, (s + 1) * LANES)
                        step = change[at : at + 8, lanes] + own_change[own_at, lanes]
                        flux = flux + down * step
                    value = own - speeds[j] * flux
                    spectra_new[f, band, :] = value
                    total[k] = total[k] + value
        return first_speed * ratio**step_pairs, first_slow * ratio**-step_pairs, tuple(total)

    zeros = tuple(jnp.zeros((8, LANES), jnp.float32) for _ in bands)
    chunks = pairs // step_pairs
    buffers = (change_a, change_b)
    carry = (1.0, 1.0, zeros)
    gather(0, change_a)
    for c in range(chunks):
        if c + 1 < chunks:
            gather(c + 1, buffers[(c + 1) % 2])
        carry = advect(c, buffers[c % 2], *carry)
    total = carry[2]
    total = jnp.concatenate(total, axis=0)
    zero = jnp.zeros((stride, LANES), jnp.float32)
    cos_dir, sin_dir = ways[0], ways[1]
    mean = jnp.sum(total, axis=0, keepdims=True) * (1.0 / (freqs * dirs))
    step = jnp.exp((ways[2] - 2.0 * mean) * (1.0 / freqs))
    run = 10 if freqs % 10 == 0 else 1

    def grow(c, carry):
        factor, weighted = carry
        for i in range(run):
            f = c * run + i
            factor = factor * step
            evolved = spectra_new[f] * factor
            spectra_new[f] = evolved
            kappa = (f + 1).astype(jnp.float32) * (1.0 / freqs)
            weighted = weighted + kappa * evolved
        return factor, weighted

    _, weighted = lax.fori_loop(0, freqs // run, grow, (zero + 1.0, zero))
    stokes = jnp.concatenate(
        [
            jnp.sum(weighted * cos_dir, axis=0, keepdims=True),
            jnp.sum(weighted * sin_dir, axis=0, keepdims=True),
        ],
        axis=0,
    ) * (1.0 / dirs)
    in_order = jnp.dot(
        three_parts(stokes), slots[...], preferred_element_type=jnp.float32
    )
    in_order = in_order[0:2] + (in_order[2:4] + in_order[4:6])
    values = [
        [in_order[part : part + 1, h * LANES : (h + 1) * LANES] for h in range(halves)]
        for part in range(2)
    ]
    rows_out[...] = peer_rows(values, peers, capacity)


def three_parts(values):
    first = values.astype(jnp.bfloat16).astype(jnp.float32)
    left = values - first
    second = left.astype(jnp.bfloat16).astype(jnp.float32)
    third = left - second
    pad = jnp.zeros((10, values.shape[1]), jnp.float32)
    return jnp.concatenate([first, second, third, pad], axis=0).astype(jnp.bfloat16)


def tracer_kernel(
    capacity, shape,
    outer, inner, table, fields, neighbors, matrices, inside, cosine, sine, scale, sums, spectra,
    tracers_new, spectra_out,
    halo, halo_near, halo_tables, stokes, antiflux, lowered, ratios,
    ratio_pieces, steps_a, steps_b, sem,
):
    dirs = spectra_out.shape[1]
    write = pltpu.make_async_copy(spectra.at[:, 0:dirs, :], spectra_out, sem)
    write.start()
    me = lax.axis_index("mesh")
    tracer_count, layers, edges = shape
    peers = table.shape[0]
    halves = peers * capacity // LANES
    blocks, field_rows, _ = fields.shape
    layer_groups = layers // 8
    tracer_groups = tracer_count * layer_groups
    odd = me % 2 == 1

    for b in range(2):
        x = outer[b * field_rows : (b + 1) * field_rows, :]
        y = inner[b * field_rows : (b + 1) * field_rows, :]
        for side, value in ((0, jnp.where(odd, y, x)), (1, jnp.where(odd, x, y))):
            halo[2 * side + b] = value
    at = 2 * field_rows
    x = outer[at : at + TABLE_ROWS, :]
    y = inner[at : at + TABLE_ROWS, :]
    for side, rows in ((0, jnp.where(odd, y, x)), (1, jnp.where(odd, x, y))):
        w = rows[16 : 16 + edges]
        halo_tables[side, 0, 0:edges, :] = w
        halo_tables[side, 1, 0:edges, :] = w * jnp.cos(rows[8 : 8 + edges])
        halo_tables[side, 2, 0:edges, :] = w * jnp.sin(rows[8 : 8 + edges])
        halo_near[side, 0:edges, :] = rows[0:edges].astype(jnp.int32)

    received = table[...]
    lane_of = lane_iota(peers)
    sections = []
    for which in range(3):
        values = []
        for part in range(2):
            lane = (2 * which + part) * capacity + lane_of % capacity
            found = lane_gather(received, lane)
            row = []
            for half in range(halves):
                mine = row_iota(peers) == (lane_of + half * LANES) // capacity
                row.append(jnp.sum(jnp.where(mine, found, 0.0), axis=0, keepdims=True))
            values.append(jnp.concatenate(row, axis=1))
        sections.append(three_parts(jnp.concatenate(values, axis=0)))
    total = jnp.dot(
        jnp.concatenate(sections, axis=0), sums[...], preferred_element_type=jnp.float32
    )
    for b in range(blocks + 2):
        which = 0 if b == 0 else 2 if b == blocks + 1 else 1
        at = 16 * which
        lanes = slice(b * LANES, (b + 1) * LANES)
        first, second, third = (total[at + k : at + k + 2, lanes] for k in (0, 2, 4))
        stokes[b, 0:2, :] = first + (second + third)

    decay = [
        jnp.exp(-3.0 / layers * (row_iota(8) + 8 * g).astype(jnp.float32))
        for g in range(layer_groups)
    ]

    def low_order(b, value, change, wx, wy, keep):
        slope = wx * stokes[b, 0:1, :] + wy * stokes[b, 1:2, :]
        own = [value(8 * g) for g in range(tracer_groups)]
        zero = jnp.zeros((8, LANES), jnp.float32)
        speed_sum = [zero] * layer_groups
        inflow = [zero] * tracer_groups
        highest = [zero] * tracer_groups
        lowest = [zero] * tracer_groups
        positive = [zero] * tracer_groups
        negative = [zero] * tracer_groups
        for s in range(edges):
            slope8 = spread(slope[s : s + 1, :], 8)
            for lg in range(layer_groups):
                speed = change(8 * (tracer_groups + lg), s) + decay[lg] * slope8
                down = jnp.minimum(speed, 0.0)
                half = 0.5 * speed - down
                speed_sum[lg] = speed_sum[lg] + speed
                for t in range(tracer_count):
                    g = t * layer_groups + lg
                    step = change(8 * g, s)
                    flux = half * step
                    if keep:
                        antiflux[b - 1, s, 8 * g : 8 * g + 8, :] = flux
                    inflow[g] = inflow[g] + down * step
                    highest[g] = jnp.maximum(highest[g], step)
                    lowest[g] = jnp.minimum(lowest[g], step)
                    positive[g] = positive[g] + jnp.maximum(flux, 0.0)
                    negative[g] = negative[g] - jnp.minimum(flux, 0.0)
        plus, minus = [], []
        for g in range(tracer_groups):
            loss = speed_sum[g % layer_groups] * own[g] + inflow[g]
            if keep:
                lowered[b - 1, 8 * g : 8 * g + 8, :] = own[g] - loss
            up = jnp.maximum(highest[g] + loss, 0.0) / (negative[g] + FCT_FLOOR)
            down = jnp.maximum(-loss - lowest[g], 0.0) / (positive[g] + FCT_FLOOR)
            plus.append(jnp.minimum(1.0, up))
            minus.append(jnp.minimum(1.0, down))
        both = jnp.concatenate(plus + minus, axis=0)
        ratios[b] = both
        ratio_pieces[b] = stack_split(both)

    def band(ref, *index):
        return lambda row: ref[(*index, slice(row, row + 8), slice(None))]

    potential_row = tracer_groups * 8

    def within(i):
        return lambda row, s: inside[i, row : row + 8, s * LANES : (s + 1) * LANES]

    def edge(i, side):
        beside = halo.at[1 + side]
        sign = 2 * side - 1

        def change(row, s):
            near = spread(neighbors[s : s + 1, i * LANES : (i + 1) * LANES], 8)
            from_halo = near // LANES - (me * blocks + i) == sign
            picked = lane_gather(beside[row : row + 8, :], near % LANES)
            if row >= potential_row:
                picked = picked * spread(scale[i, s : s + 1, :], 8)
            return within(i)(row, s) + jnp.where(from_halo, picked, 0.0)

        return change

    def outside(side):
        i = side * (blocks - 1)
        low, own, high = (
            (halo.at[0], halo.at[1], fields.at[i]),
            (fields.at[i], halo.at[2], halo.at[3]),
        )[side]

        def change(row, s):
            rows = slice(row, row + 8)
            near = spread(halo_near[side, s : s + 1, :], 8)
            place = near // LANES - (me * blocks + i + 2 * side - 1)
            lane = near % LANES
            mine = own[rows, :]
            middle = lane_gather(mine, lane)
            left = lane_gather(low[rows, :], lane)
            right = lane_gather(high[rows, :], lane)
            out = jnp.where(place == 0, middle, jnp.where(place < 0, left, right)) - mine
            if row >= potential_row:
                out = out * spread(halo_tables[side, 0, s : s + 1, :], 8)
            return out

        return change

    for i in range(1, blocks - 1):
        low_order(i + 1, band(fields, i), within(i), cosine[i], sine[i], True)
    for side in range(2):
        b = side * (blocks + 1)
        tables = (halo_tables[side, 1], halo_tables[side, 2])
        low_order(b, band(halo, 1 + side), outside(side), *tables, False)
        i = side * (blocks - 1)
        low_order(i + 1, band(fields, i), edge(i, side), cosine[i], sine[i], True)

    def products(i, steps):
        mixed = jnp.concatenate([ratio_pieces[i], ratio_pieces[i + 1], ratio_pieces[i + 2]], axis=1)
        steps[...] = jnp.dot(mixed, matrices[i], preferred_element_type=jnp.float32)

    def limit(i, steps):
        out = [lowered[i, 8 * g : 8 * g + 8, :] for g in range(tracer_groups)]
        own = [ratios[i + 1, 8 * g : 8 * g + 8, :] for g in range(2 * tracer_groups)]
        low = 16 * tracer_groups
        for s in range(edges):
            lanes = slice(s * LANES, (s + 1) * LANES)
            beside = [
                own[g]
                + (steps[8 * g : 8 * g + 8, lanes] + steps[low + 8 * g : low + 8 * g + 8, lanes])
                for g in range(2 * tracer_groups)
            ]
            for g in range(tracer_groups):
                m = g + tracer_groups
                flux = antiflux[i, s, 8 * g : 8 * g + 8, :]
                factor = jnp.where(
                    flux >= 0.0, jnp.minimum(own[m], beside[g]), jnp.minimum(own[g], beside[m])
                )
                out[g] = out[g] - factor * flux
        lanes = slice(i * LANES, (i + 1) * LANES)
        for g in range(tracer_groups):
            t, lg = g // layer_groups, g % layer_groups
            tracers_new[t, 8 * lg : 8 * lg + 8, lanes] = out[g]

    buffers = (steps_a, steps_b)
    products(0, steps_a)
    for i in range(blocks):
        if i + 1 < blocks:
            products(i + 1, buffers[(i + 1) % 2])
        limit(i, buffers[i % 2])
    write.wait()


def swap(message, first, peers):
    pairs = []
    for i in range(first, peers - 1, 2):
        pairs += [(i, i + 1), (i + 1, i)]
    return lax.ppermute(message, "mesh", pairs)


def whole_spec():
    return pl.BlockSpec(memory_space=pltpu.VMEM)


def local(
    tracers,
    potential,
    surface_current,
    cell_neighbors,
    cell_normal,
    cell_weight,
    spectra,
    wind_velocity,
    node_neighbors,
    node_normal,
    node_weight,
    send_rows,
    node_slot,
):
    peers, _, capacity = send_rows.shape
    freqs, dirs, nodes = spectra.shape
    tracer_count, layers, cells = tracers.shape
    edges = cell_neighbors.shape[0]
    blocks = cells // LANES
    field_rows = (tracer_count + 1) * layers
    head_rows = 2 * field_rows + TABLE_ROWS
    pairs = freqs // 2
    slots = node_slot.reshape(1, nodes)
    params = pltpu.CompilerParams(vmem_limit_bytes=VMEM_LIMIT)
    f32 = jnp.float32

    stored = pl.BlockSpec(memory_space=pltpu.HBM)
    rows = tracer_count * layers
    stride = (dirs + 7) // 8 * 8
    step_pairs = 5 if freqs % 10 == 0 else 1
    step_rows = 2 * step_pairs * stride

    def like(x):
        return jax.ShapeDtypeStruct(x.shape, x.dtype)

    def shaped(*shape, dtype=f32):
        return jax.ShapeDtypeStruct(shape, dtype)

    def call(kernel, name, inputs, outputs, scratch, out_specs=None):
        return pl.pallas_call(
            kernel,
            out_shape=outputs,
            in_specs=[whole_spec()] * len(inputs),
            out_specs=out_specs or (whole_spec(),) * len(outputs),
            scratch_shapes=scratch,
            compiler_params=params,
            name=name,
        )(*inputs)

    inputs = (
        spectra, tracers, potential, cell_neighbors, cell_normal, cell_weight, surface_current,
        send_rows, slots, node_neighbors, node_normal, node_weight, wind_velocity,
    )
    (
        currents, outer, more, inner, own_spectra, own_slots, near, angle, face, wind,
        own_tracers, own_potential, neighbors, normal, weight, coupled,
    ) = pl.pallas_call(
        pack_kernel,
        out_shape=(
            shaped(peers, LANES),
            shaped(head_rows + (pairs // 2 * dirs + 7) // 8 * 8, LANES),
            shaped(((pairs - pairs // 2) * dirs + 7) // 8 * 8, LANES),
            shaped(head_rows + (pairs * dirs + 7) // 8 * 8, LANES),
            shaped(freqs, stride, LANES),
            like(slots),
            like(node_neighbors),
            like(node_normal),
            like(node_weight),
            like(wind_velocity),
            like(tracers),
            like(potential),
            like(cell_neighbors),
            like(cell_normal),
            like(cell_weight),
            shaped(3, peers, capacity, dtype=jnp.int32),
        ),
        in_specs=[stored] * len(inputs),
        out_specs=(whole_spec(),) * 16,
        scratch_shapes=[
            pltpu.VMEM(surface_current.shape, f32),
            pltpu.SemaphoreType.DMA((15,)),
        ],
        compiler_params=params,
        name="pack",
    )(*(pltpu.with_memory_space_constraint(x, pltpu.HBM) for x in inputs))
    outer = swap(outer, 1, peers)
    more = swap(more, 1, peers)
    inner = swap(inner, 0, peers)

    (
        cosine, sine, project, choice, ways, slot_choice, own_change,
        fields, matrices, inside, cell_cosine, cell_sine, cell_scale, sums,
    ) = call(
        functools.partial(prepare_kernel, dirs, step_rows),
        "prepare",
        (
            own_spectra, near, angle, face, wind, own_slots, own_tracers, own_potential,
            neighbors, normal, weight, coupled,
        ),
        (
            like(node_normal),
            like(node_normal),
            shaped(edges, stride, LANES),
            shaped(4 * LANES, edges * LANES, dtype=jnp.bfloat16),
            shaped(3, stride, LANES),
            shaped(nodes, peers * capacity, dtype=jnp.bfloat16),
            shaped(freqs * stride, edges * LANES),
            shaped(blocks, field_rows, LANES),
            shaped(blocks, 3 * LANES, edges * LANES, dtype=jnp.bfloat16),
            shaped(blocks, field_rows, edges * LANES),
            shaped(blocks, 8, LANES),
            shaped(blocks, 8, LANES),
            shaped(blocks, 8, LANES),
            shaped(peers * capacity, (blocks + 2) * LANES, dtype=jnp.bfloat16),
        ),
        [pltpu.VMEM((blocks, 2 * field_rows, LANES), jnp.bfloat16)],
    )
    currents, cosine = lax.optimization_barrier((currents, cosine))
    currents = lax.all_to_all(currents, "mesh", 0, 0, tiled=True)

    spectra_new, stokes_rows = call(
        functools.partial(wave_kernel, capacity, step_pairs, dirs, field_rows),
        "wave",
        (
            own_spectra, outer, more, inner, currents, own_slots, near,
            cosine, sine, project, choice, ways, slot_choice, own_change,
        ),
        (shaped(freqs, stride, LANES), shaped(peers, LANES)),
        [
            pltpu.VMEM((8, LANES), f32),
            pltpu.VMEM((step_rows, LANES), f32),
            pltpu.VMEM((step_rows, edges * LANES), f32),
            pltpu.VMEM((step_rows, edges * LANES), f32),
        ],
    )
    stokes_all = lax.all_to_all(stokes_rows, "mesh", 0, 0, tiled=True)

    return call(
        functools.partial(tracer_kernel, capacity, (tracer_count, layers, edges)),
        "tracer",
        (
            outer, inner, stokes_all, fields, neighbors, matrices, inside, cell_cosine, cell_sine,
            cell_scale, sums, pltpu.with_memory_space_constraint(spectra_new, pltpu.VMEM),
        ),
        (like(tracers), like(spectra)),
        [
            pltpu.VMEM((4, field_rows, LANES), f32),
            pltpu.VMEM((2, 8, LANES), jnp.int32),
            pltpu.VMEM((2, 3, 8, LANES), f32),
            pltpu.VMEM((blocks + 2, 8, LANES), f32),
            pltpu.VMEM((blocks, edges, rows, LANES), f32),
            pltpu.VMEM((blocks, rows, LANES), f32),
            pltpu.VMEM((blocks + 2, 2 * rows, LANES), f32),
            pltpu.VMEM((blocks + 2, 4 * rows, LANES), jnp.bfloat16),
            pltpu.VMEM((4 * rows, edges * LANES), f32),
            pltpu.VMEM((4 * rows, edges * LANES), f32),
            pltpu.SemaphoreType.DMA(()),
        ],
        out_specs=(whole_spec(), stored),
    )


def solution(mesh):
    return jax.shard_map(
        local,
        mesh=mesh,
        in_specs=(
            P(None, None, ("groups", "mesh")),
            P(None, ("groups", "mesh")),
            P(None, ("groups", "mesh")),
            P(None, "mesh"),
            P(None, "mesh"),
            P(None, "mesh"),
            P(None, None, ("groups", "mesh")),
            P(None, ("groups", "mesh")),
            P(None, "mesh"),
            P(None, "mesh"),
            P(None, "mesh"),
            P(),
            P("mesh"),
        ),
        out_specs=(P(None, None, ("groups", "mesh")), P(None, None, ("groups", "mesh"))),
        check_vma=False,
    )
```

```python
import functools
import math

import jax
import jax.numpy as jnp
from jax import lax
from jax.experimental import pallas as pl
from jax.experimental.pallas import tpu as pltpu
from jax.sharding import PartitionSpec as P

LANES = 128
FCT_FLOOR = 0.001
TABLE_ROWS = 24
VMEM_LIMIT = 32 * 1024 * 1024


def lane_gather(values, index):
    return jnp.take_along_axis(values, index, axis=1, mode="promise_in_bounds")


def spread(row, count):
    return jnp.broadcast_to(row, (count, LANES))


def lane_iota(rows):
    return lax.broadcasted_iota(jnp.int32, (rows, LANES), 1)


def row_iota(rows):
    return lax.broadcasted_iota(jnp.int32, (rows, LANES), 0)


def slot_rows(entry):
    peers, capacity = entry.shape
    wide = jnp.concatenate([entry, jnp.zeros((peers, LANES - capacity), jnp.int32)], axis=1)
    wide = lane_gather(wide, lane_iota(peers) % capacity)
    owner = row_iota(peers)
    out = []
    for half in range(peers * capacity // LANES):
        wanted = (lane_iota(peers) + half * LANES) // capacity
        picked = jnp.where(owner == wanted, wide, 0).astype(jnp.float32)
        out.append(jnp.sum(picked, axis=0, keepdims=True).astype(jnp.int32))
    return out


def half_mask(rows, lower):
    half = lane_iota(rows) // (LANES // 2)
    return half == jnp.where(lower, 0, 1)


def peer_rows(values, peers, capacity):
    lane = lane_iota(peers)
    group = lane // capacity
    block = jnp.clip(row_iota(peers) - 1 + group // 2, 0, peers - 1)
    entry = block * capacity + lane % capacity
    out = jnp.zeros((peers, LANES), jnp.float32)
    for part in range(2):
        for half, row in enumerate(values[part]):
            found = lane_gather(spread(row, peers), entry % LANES)
            wanted = (group < 6) & (group % 2 == part) & (entry // LANES == half)
            out = jnp.where(wanted, found, out)
    return out


def direction(dirs, padded):
    turn = row_iota(padded).astype(jnp.float32) * (2.0 * math.pi / dirs)
    return jnp.cos(turn), jnp.sin(turn)


def node_tables(
    me, dirs, near, angle, face, wind, slot, cosine, sine, project, choice, ways, slots
):
    edges, padded = project.shape[:2]
    cosine[...] = face[...] * jnp.cos(angle[...])
    sine[...] = face[...] * jnp.sin(angle[...])
    cos_dir, sin_dir = direction(dirs, padded)
    ways[0] = cos_dir
    ways[1] = sin_dir
    ways[2] = 0.25 * jnp.maximum(wind[0:1, :] * cos_dir + wind[1:2, :] * sin_dir, 0.0)
    taken = jnp.transpose(spread(slot[...].astype(jnp.float32), LANES))
    for half in range(slots.shape[1] // LANES):
        number = (lane_iota(LANES) + half * LANES).astype(jnp.float32)
        picked = jnp.where(taken == number, 1.0, 0.0).astype(jnp.bfloat16)
        slots[:, half * LANES : (half + 1) * LANES] = picked
    source = row_iota(LANES)
    minus = jnp.where(source == lane_iota(LANES), -1.0, 0.0)
    for s in range(edges):
        project[s] = cos_dir * cosine[s : s + 1, :] + sin_dir * sine[s : s + 1, :]
        target = near[s : s + 1, :]
        inside = target // LANES == me
        lane = target % LANES
        own = jnp.where(source == jnp.where(inside, lane, LANES), 1.0, 0.0) + minus
        halo = jnp.where(source == jnp.where(inside, LANES, lane), 1.0, 0.0)
        lanes = slice(s * LANES, (s + 1) * LANES)
        for k, part in enumerate((own, own, halo, halo)):
            choice[k * LANES : (k + 1) * LANES, lanes] = part.astype(jnp.bfloat16)


def split(x):
    first = x.astype(jnp.bfloat16)
    return first, (x - first.astype(jnp.float32)).astype(jnp.bfloat16)


def pack_kernel(
    spectra_in, tracers_in, potential_in, neighbors_in, normal_in, weight_in, current_in,
    send_rows, slot_in, near_in, angle_in, face_in, wind_in,
    rows_out, outer, inner, spectra, node_slot, near, angle, face, wind,
    tracers, potential, neighbors, normal, weight, coupled,
    current, sems,
):
    peers, _, capacity = send_rows.shape
    me = lax.axis_index("mesh")
    freqs, dirs = spectra_in.shape[:2]
    if dirs < spectra.shape[1]:
        for f in range(freqs):
            spectra[f, dirs // 8 * 8 :, :] = jnp.zeros((8, LANES), jnp.float32)
    pairs = freqs // 2
    copies = []
    for source, target in (
        (send_rows.at[me], coupled.at[1]),
        (current_in, current),
        (slot_in, node_slot),
        (spectra_in, spectra.at[:, 0:dirs, :]),
        (tracers_in, tracers),
        (potential_in, potential),
        (neighbors_in, neighbors),
        (normal_in, normal),
        (weight_in, weight),
        (send_rows.at[jnp.maximum(me - 1, 0)], coupled.at[0]),
        (send_rows.at[jnp.minimum(me + 1, peers - 1)], coupled.at[2]),
        (near_in, near),
        (angle_in, angle),
        (face_in, face),
        (wind_in, wind),
    ):
        copy = pltpu.make_async_copy(source, target, sems.at[len(copies)])
        copy.start()
        copies.append(copy)
    for copy in copies[:3]:
        copy.wait()
    layers, cells = potential.shape
    blocks = cells // LANES
    field_rows = (tracers.shape[0] + 1) * layers
    stacked = jnp.concatenate(
        [current[:, b * LANES : (b + 1) * LANES] for b in range(blocks)], axis=0
    )
    place = row_iota(2 * blocks)
    halves = slot_rows(coupled[1])
    values = [[], []]
    for cell in halves:
        found = lane_gather(stacked, spread(cell % LANES, 2 * blocks))
        for part in range(2):
            picked = jnp.where(place == 2 * (cell // LANES) + part, found, 0.0)
            values[part].append(jnp.sum(picked, axis=0, keepdims=True))
    rows_out[...] = peer_rows(values, peers, capacity)
    for copy in copies[4:9]:
        copy.wait()
    odd = me % 2 == 1
    for out, upward in ((outer, odd), (inner, jnp.logical_not(odd))):
        for b in range(2):
            high = slice((blocks - 2 + b) * LANES, (blocks - 1 + b) * LANES)
            low = slice(b * LANES, (b + 1) * LANES)
            base = b * field_rows
            for t in range(tracers.shape[0]):
                out[base + t * layers : base + (t + 1) * layers, :] = jnp.where(
                    upward, tracers[t, :, high], tracers[t, :, low]
                )
            out[base + field_rows - layers : base + field_rows, :] = jnp.where(
                upward, potential[:, high], potential[:, low]
            )
        high = slice((blocks - 1) * LANES, blocks * LANES)
        low = slice(0, LANES)
        base = 2 * field_rows
        out[base : base + TABLE_ROWS, :] = jnp.zeros((TABLE_ROWS, LANES), jnp.float32)
        edges = neighbors.shape[0]
        near = jnp.where(upward, neighbors[:, high], neighbors[:, low])
        out[base : base + edges, :] = near.astype(jnp.float32)
        out[base + edges : base + edges + 1, :] = node_slot[...].astype(jnp.float32)
        out[base + 8 : base + 8 + edges, :] = jnp.where(upward, normal[:, high], normal[:, low])
        out[base + 16 : base + 16 + edges, :] = jnp.where(upward, weight[:, high], weight[:, low])
    base = 2 * field_rows + TABLE_ROWS
    whole = dirs // 8 * 8
    rest = dirs - whole
    turns = half_mask(dirs, odd)
    copies[3].wait()
    for g in range(pairs):
        natural = spectra[g, 0:dirs, :]
        turned = pltpu.roll(spectra[g + pairs, 0:dirs, :], LANES // 2, 1)
        for out, mixed in (
            (outer, jnp.where(turns, turned, natural)),
            (inner, jnp.where(turns, natural, turned)),
        ):
            at = base + g * whole
            out[at : at + whole, :] = mixed[:whole]
            at = base + pairs * whole + g * rest
            out[at : at + rest, :] = mixed[whole:]
    at = base + pairs * dirs
    if at < outer.shape[0]:
        for out in (outer, inner):
            out[at:, :] = jnp.zeros((outer.shape[0] - at, LANES), jnp.float32)
    for copy in copies[9:]:
        copy.wait()


def choose(cells, first, lanes, matrix):
    place = (cells - first - LANES).astype(jnp.float32).astype(jnp.bfloat16)
    place = spread(place, LANES)
    one = jnp.ones((LANES, LANES), jnp.bfloat16)
    for k in range(3):
        source = (row_iota(LANES) + (k - 1) * LANES).astype(jnp.float32).astype(jnp.bfloat16)
        part = jnp.where(source == place, one, 0 * one)
        if k == 1:
            own = jnp.where(row_iota(LANES) == lane_iota(LANES), 1.0, 0.0).astype(jnp.bfloat16)
            part = part - own
        matrix[k * LANES : (k + 1) * LANES, lanes] = part


def stack_split(x):
    first, second = split(x)
    return jnp.concatenate([first, second], axis=0)


def differences(parts, matrix):
    mixed = jnp.concatenate(parts, axis=1)
    out = jnp.dot(mixed, matrix, preferred_element_type=jnp.float32)
    rows = out.shape[0] // 2
    return out[:rows] + out[rows:]


def prepare_kernel(
    dirs, step_rows,
    spectra, near, angle, face, wind, slot, tracers, potential, neighbors, normal, weight, coupled,
    cosine, sine, project, choice, ways, slots, own_parts,
    fields, matrices, inside, cell_cosine, cell_sine, cell_scale, sums,
    pieces,
):
    me = lax.axis_index("mesh")
    node_tables(
        me, dirs, near, angle, face, wind, slot, cosine, sine, project, choice, ways, slots
    )
    freqs, padded, _ = spectra.shape
    step = step_rows // padded // 2
    pairs = freqs // 2
    for c in range(pairs // step):
        rows = []
        for g in range(c * step, (c + 1) * step):
            rows += [spectra[g], spectra[g + pairs]]
        mixed = jnp.concatenate(split(jnp.concatenate(rows, axis=0)), axis=1)
        own_parts[c * step_rows : (c + 1) * step_rows, :] = mixed
    tracer_count, layers, cells = tracers.shape
    blocks = cells // LANES
    edges = neighbors.shape[0]
    field_rows = (tracer_count + 1) * layers
    for b in range(blocks):
        lanes = slice(b * LANES, (b + 1) * LANES)
        for t in range(tracer_count):
            fields[b, t * layers : (t + 1) * layers, :] = tracers[t, :, lanes]
        fields[b, field_rows - layers : field_rows, :] = potential[:, lanes]
        pieces[b] = stack_split(fields[b])
        w = weight[:, lanes]
        cell_scale[b, 0:edges, :] = w
        cell_cosine[b, 0:edges, :] = w * jnp.cos(normal[:, lanes])
        cell_sine[b, 0:edges, :] = w * jnp.sin(normal[:, lanes])
        for s in range(edges):
            choose(
                neighbors[s : s + 1, lanes],
                (me * blocks + b - 1) * LANES,
                slice(s * LANES, (s + 1) * LANES),
                matrices.at[b],
            )
    for b in range(blocks):
        first, last = max(b - 1, 0), min(b + 1, blocks - 1)
        rows = slice((first - b + 1) * LANES, (last - b + 2) * LANES)
        parts = [pieces[k] for k in range(first, last + 1)]
        change = differences(parts, matrices[b, rows, :])
        last_field = field_rows - layers
        inside[b, 0:last_field, :] = change[:last_field]
        for s in range(edges):
            at = slice(s * LANES, (s + 1) * LANES)
            inside[b, last_field:, at] = change[last_field:, at] * cell_scale[b, s : s + 1, :]
    for which in range(3):
        first = 0 if which != 0 else cells - LANES
        count = blocks if which == 1 else 1
        start = (0, 1, blocks + 1)[which]
        for half, names in enumerate(slot_rows(coupled[which])):
            named = jnp.transpose(spread(names, LANES).astype(jnp.float32))
            for b in range(count):
                cell = (lane_iota(LANES) + (first + b * LANES)).astype(jnp.float32)
                picked = jnp.where(named == cell, 1.0, 0.0).astype(jnp.bfloat16)
                lanes = slice((start + b) * LANES, (start + b + 1) * LANES)
                sums[half * LANES : (half + 1) * LANES, lanes] = picked


def node_currents(table, slot, which, capacity):
    peers = table.shape[0]
    owner = row_iota(peers) == slot // capacity
    out = []
    for part in range(2):
        lane = (2 * which + part) * capacity + slot % capacity
        found = jnp.where(owner, lane_gather(table, spread(lane, peers)), 0.0)
        out.append(jnp.sum(found, axis=0, keepdims=True))
    return out


def wave_kernel(
    capacity, step_pairs, dirs,
    spectra, outer, inner, table, node_slot, neighbors, cosine, sine, project, choice, ways, slots,
    own_parts,
    spectra_new, rows_out, drift, halos, change_a, change_b,
):
    me = lax.axis_index("mesh")
    freqs, stride = spectra.shape[:2]
    edges = neighbors.shape[0]
    peers = table.shape[0]
    halves = peers * capacity // LANES
    pairs = freqs // 2
    whole = dirs // 8 * 8
    rest = dirs - whole
    base = outer.shape[0] - (pairs * dirs + 7) // 8 * 8

    odd = me % 2 == 1
    slot = node_slot[...]
    row = base - TABLE_ROWS + edges
    halo_slot = jnp.where(
        half_mask(1, odd), outer[row : row + 1, :], inner[row : row + 1, :]
    ).astype(jnp.int32)
    lower = lane_iota(1) < LANES // 2
    currents = table[...]
    own_x, own_y = node_currents(currents, slot, jnp.ones((1, LANES), jnp.int32), capacity)
    halo_x, halo_y = node_currents(currents, halo_slot, jnp.where(lower, 2, 0), capacity)

    target = neighbors[...]
    lane = target % LANES
    inside = target // LANES == me

    def beside(own, halo):
        a = lane_gather(spread(own, edges), lane)
        b = lane_gather(spread(halo, edges), lane)
        return jnp.where(inside, a, b)

    drift[0:edges, :] = (
        0.5 * (own_x + beside(own_x, halo_x)) * cosine[...]
        + 0.5 * (own_y + beside(own_y, halo_y)) * sine[...]
    )
    drifts = [spread(drift[s : s + 1, :], 8) for s in range(edges)]
    from_outer = half_mask(dirs, odd)
    step_rows = halos.shape[0]
    halos[...] = jnp.zeros(halos.shape, jnp.float32)
    ratio = 1.0 / 1.1
    bands = [slice(r, r + 8) for r in range(0, stride, 8)]

    def gather(c, change):
        for i in range(step_pairs):
            g = c * step_pairs + i
            parts = []
            for message in (outer, inner):
                at = base + g * whole
                upper = message[at : at + whole, :]
                at = base + pairs * whole + g * rest
                left = message[at : at + rest, :]
                parts.append(jnp.concatenate([upper, left], axis=0))
            x, y = parts
            at = 2 * i * stride
            halos[at : at + dirs, :] = jnp.where(from_outer, x, y)
            at += stride
            halos[at : at + dirs, :] = pltpu.roll(jnp.where(from_outer, y, x), LANES // 2, 1)
        own = own_parts[c * step_rows : (c + 1) * step_rows, :]
        mixed = jnp.concatenate([own, *split(halos[...])], axis=1)
        change[...] = jnp.dot(mixed, choice[...], preferred_element_type=jnp.float32)

    def advect(c, change, first_speed, first_slow, total):
        total = list(total)
        speeds = []
        for i in range(step_pairs):
            speeds += [first_speed * ratio**i, first_speed * ratio ** (i + pairs)]
        slowness = []
        for i in range(step_pairs):
            slowness += [first_slow * ratio**-i, first_slow * ratio ** -(i + pairs)]
        relative = [[drift * slow for drift in drifts] for slow in slowness]
        relative_sum = [sum(each[1:], each[0]) for each in relative]
        for k, band in enumerate(bands):
            along = [project[s, band, :] for s in range(edges)]
            along_sum = sum(along[1:], along[0])
            for i in range(step_pairs):
                g = c * step_pairs + i
                for j, f in ((2 * i, g), (2 * i + 1, g + pairs)):
                    own = spectra[f, band, :]
                    at = j * stride + band.start
                    flux = (along_sum + relative_sum[j]) * own
                    for s in range(edges):
                        down = jnp.minimum(along[s] + relative[j][s], 0.0)
                        lanes = slice(s * LANES, (s + 1) * LANES)
                        flux = flux + down * change[at : at + 8, lanes]
                    value = own - speeds[j] * flux
                    spectra_new[f, band, :] = value
                    total[k] = total[k] + value
        return first_speed * ratio**step_pairs, first_slow * ratio**-step_pairs, tuple(total)

    zeros = tuple(jnp.zeros((8, LANES), jnp.float32) for _ in bands)
    chunks = pairs // step_pairs
    buffers = (change_a, change_b)
    carry = (1.0, 1.0, zeros)
    gather(0, change_a)
    for c in range(chunks):
        if c + 1 < chunks:
            gather(c + 1, buffers[(c + 1) % 2])
        carry = advect(c, buffers[c % 2], *carry)
    total = carry[2]
    total = jnp.concatenate(total, axis=0)
    zero = jnp.zeros((stride, LANES), jnp.float32)
    cos_dir, sin_dir = ways[0], ways[1]
    mean = jnp.sum(total, axis=0, keepdims=True) * (1.0 / (freqs * dirs))
    step = jnp.exp((ways[2] - 2.0 * mean) * (1.0 / freqs))
    run = 10 if freqs % 10 == 0 else 1

    def grow(c, carry):
        factor, weighted = carry
        for i in range(run):
            f = c * run + i
            factor = factor * step
            evolved = spectra_new[f] * factor
            spectra_new[f] = evolved
            kappa = (f + 1).astype(jnp.float32) * (1.0 / freqs)
            weighted = weighted + kappa * evolved
        return factor, weighted

    _, weighted = lax.fori_loop(0, freqs // run, grow, (zero + 1.0, zero))
    stokes = jnp.concatenate(
        [
            jnp.sum(weighted * cos_dir, axis=0, keepdims=True),
            jnp.sum(weighted * sin_dir, axis=0, keepdims=True),
        ],
        axis=0,
    ) * (1.0 / dirs)
    in_order = jnp.dot(
        three_parts(stokes), slots[...], preferred_element_type=jnp.float32
    )
    in_order = in_order[0:2] + (in_order[2:4] + in_order[4:6])
    values = [
        [in_order[part : part + 1, h * LANES : (h + 1) * LANES] for h in range(halves)]
        for part in range(2)
    ]
    rows_out[...] = peer_rows(values, peers, capacity)


def three_parts(values):
    first = values.astype(jnp.bfloat16).astype(jnp.float32)
    left = values - first
    second = left.astype(jnp.bfloat16).astype(jnp.float32)
    third = left - second
    pad = jnp.zeros((10, values.shape[1]), jnp.float32)
    return jnp.concatenate([first, second, third, pad], axis=0).astype(jnp.bfloat16)


def tracer_kernel(
    capacity, shape,
    outer, inner, table, fields, neighbors, matrices, inside, cosine, sine, scale, sums, spectra,
    tracers_new, spectra_out,
    halo, halo_near, halo_tables, stokes, antiflux, lowered, ratios,
    ratio_pieces, steps_a, steps_b, sem,
):
    dirs = spectra_out.shape[1]
    write = pltpu.make_async_copy(spectra.at[:, 0:dirs, :], spectra_out, sem)
    write.start()
    me = lax.axis_index("mesh")
    tracer_count, layers, edges = shape
    peers = table.shape[0]
    halves = peers * capacity // LANES
    blocks, field_rows, _ = fields.shape
    layer_groups = layers // 8
    tracer_groups = tracer_count * layer_groups
    odd = me % 2 == 1

    for b in range(2):
        x = outer[b * field_rows : (b + 1) * field_rows, :]
        y = inner[b * field_rows : (b + 1) * field_rows, :]
        for side, value in ((0, jnp.where(odd, y, x)), (1, jnp.where(odd, x, y))):
            halo[2 * side + b] = value
    at = 2 * field_rows
    x = outer[at : at + TABLE_ROWS, :]
    y = inner[at : at + TABLE_ROWS, :]
    for side, rows in ((0, jnp.where(odd, y, x)), (1, jnp.where(odd, x, y))):
        w = rows[16 : 16 + edges]
        halo_tables[side, 0, 0:edges, :] = w
        halo_tables[side, 1, 0:edges, :] = w * jnp.cos(rows[8 : 8 + edges])
        halo_tables[side, 2, 0:edges, :] = w * jnp.sin(rows[8 : 8 + edges])
        halo_near[side, 0:edges, :] = rows[0:edges].astype(jnp.int32)

    received = table[...]
    lane_of = lane_iota(peers)
    sections = []
    for which in range(3):
        values = []
        for part in range(2):
            lane = (2 * which + part) * capacity + lane_of % capacity
            found = lane_gather(received, lane)
            row = []
            for half in range(halves):
                mine = row_iota(peers) == (lane_of + half * LANES) // capacity
                row.append(jnp.sum(jnp.where(mine, found, 0.0), axis=0, keepdims=True))
            values.append(jnp.concatenate(row, axis=1))
        sections.append(three_parts(jnp.concatenate(values, axis=0)))
    total = jnp.dot(
        jnp.concatenate(sections, axis=0), sums[...], preferred_element_type=jnp.float32
    )
    for b in range(blocks + 2):
        which = 0 if b == 0 else 2 if b == blocks + 1 else 1
        at = 16 * which
        lanes = slice(b * LANES, (b + 1) * LANES)
        first, second, third = (total[at + k : at + k + 2, lanes] for k in (0, 2, 4))
        stokes[b, 0:2, :] = first + (second + third)

    decay = [
        jnp.exp(-3.0 / layers * (row_iota(8) + 8 * g).astype(jnp.float32))
        for g in range(layer_groups)
    ]

    def low_order(b, value, change, wx, wy, keep):
        slope = wx * stokes[b, 0:1, :] + wy * stokes[b, 1:2, :]
        own = [value(8 * g) for g in range(tracer_groups)]
        zero = jnp.zeros((8, LANES), jnp.float32)
        speed_sum = [zero] * layer_groups
        inflow = [zero] * tracer_groups
        highest = [zero] * tracer_groups
        lowest = [zero] * tracer_groups
        positive = [zero] * tracer_groups
        negative = [zero] * tracer_groups
        for s in range(edges):
            slope8 = spread(slope[s : s + 1, :], 8)
            for lg in range(layer_groups):
                speed = change(8 * (tracer_groups + lg), s) + decay[lg] * slope8
                down = jnp.minimum(speed, 0.0)
                half = 0.5 * speed - down
                speed_sum[lg] = speed_sum[lg] + speed
                for t in range(tracer_count):
                    g = t * layer_groups + lg
                    step = change(8 * g, s)
                    flux = half * step
                    if keep:
                        antiflux[b - 1, s, 8 * g : 8 * g + 8, :] = flux
                    inflow[g] = inflow[g] + down * step
                    highest[g] = jnp.maximum(highest[g], step)
                    lowest[g] = jnp.minimum(lowest[g], step)
                    positive[g] = positive[g] + jnp.maximum(flux, 0.0)
                    negative[g] = negative[g] - jnp.minimum(flux, 0.0)
        plus, minus = [], []
        for g in range(tracer_groups):
            loss = speed_sum[g % layer_groups] * own[g] + inflow[g]
            if keep:
                lowered[b - 1, 8 * g : 8 * g + 8, :] = own[g] - loss
            up = jnp.maximum(highest[g] + loss, 0.0) / (negative[g] + FCT_FLOOR)
            down = jnp.maximum(-loss - lowest[g], 0.0) / (positive[g] + FCT_FLOOR)
            plus.append(jnp.minimum(1.0, up))
            minus.append(jnp.minimum(1.0, down))
        both = jnp.concatenate(plus + minus, axis=0)
        ratios[b] = both
        ratio_pieces[b] = stack_split(both)

    def band(ref, *index):
        return lambda row: ref[(*index, slice(row, row + 8), slice(None))]

    potential_row = tracer_groups * 8

    def within(i):
        return lambda row, s: inside[i, row : row + 8, s * LANES : (s + 1) * LANES]

    def edge(i, side):
        beside = halo.at[1 + side]
        sign = 2 * side - 1

        def change(row, s):
            near = spread(neighbors[s : s + 1, i * LANES : (i + 1) * LANES], 8)
            from_halo = near // LANES - (me * blocks + i) == sign
            picked = lane_gather(beside[row : row + 8, :], near % LANES)
            if row >= potential_row:
                picked = picked * spread(scale[i, s : s + 1, :], 8)
            return within(i)(row, s) + jnp.where(from_halo, picked, 0.0)

        return change

    def outside(side):
        i = side * (blocks - 1)
        low, own, high = (
            (halo.at[0], halo.at[1], fields.at[i]),
            (fields.at[i], halo.at[2], halo.at[3]),
        )[side]

        def change(row, s):
            rows = slice(row, row + 8)
            near = spread(halo_near[side, s : s + 1, :], 8)
            place = near // LANES - (me * blocks + i + 2 * side - 1)
            lane = near % LANES
            mine = own[rows, :]
            middle = lane_gather(mine, lane)
            left = lane_gather(low[rows, :], lane)
            right = lane_gather(high[rows, :], lane)
            out = jnp.where(place == 0, middle, jnp.where(place < 0, left, right)) - mine
            if row >= potential_row:
                out = out * spread(halo_tables[side, 0, s : s + 1, :], 8)
            return out

        return change

    for i in range(1, blocks - 1):
        low_order(i + 1, band(fields, i), within(i), cosine[i], sine[i], True)
    for side in range(2):
        b = side * (blocks + 1)
        tables = (halo_tables[side, 1], halo_tables[side, 2])
        low_order(b, band(halo, 1 + side), outside(side), *tables, False)
        i = side * (blocks - 1)
        low_order(i + 1, band(fields, i), edge(i, side), cosine[i], sine[i], True)

    def products(i, steps):
        mixed = jnp.concatenate([ratio_pieces[i], ratio_pieces[i + 1], ratio_pieces[i + 2]], axis=1)
        steps[...] = jnp.dot(mixed, matrices[i], preferred_element_type=jnp.float32)

    def limit(i, steps):
        out = [lowered[i, 8 * g : 8 * g + 8, :] for g in range(tracer_groups)]
        own = [ratios[i + 1, 8 * g : 8 * g + 8, :] for g in range(2 * tracer_groups)]
        low = 16 * tracer_groups
        for s in range(edges):
            lanes = slice(s * LANES, (s + 1) * LANES)
            beside = [
                own[g]
                + (steps[8 * g : 8 * g + 8, lanes] + steps[low + 8 * g : low + 8 * g + 8, lanes])
                for g in range(2 * tracer_groups)
            ]
            for g in range(tracer_groups):
                m = g + tracer_groups
                flux = antiflux[i, s, 8 * g : 8 * g + 8, :]
                factor = jnp.where(
                    flux >= 0.0, jnp.minimum(own[m], beside[g]), jnp.minimum(own[g], beside[m])
                )
                out[g] = out[g] - factor * flux
        lanes = slice(i * LANES, (i + 1) * LANES)
        for g in range(tracer_groups):
            t, lg = g // layer_groups, g % layer_groups
            tracers_new[t, 8 * lg : 8 * lg + 8, lanes] = out[g]

    buffers = (steps_a, steps_b)
    products(0, steps_a)
    for i in range(blocks):
        if i + 1 < blocks:
            products(i + 1, buffers[(i + 1) % 2])
        limit(i, buffers[i % 2])
    write.wait()


def swap(message, first, peers):
    pairs = []
    for i in range(first, peers - 1, 2):
        pairs += [(i, i + 1), (i + 1, i)]
    return lax.ppermute(message, "mesh", pairs)


def whole_spec():
    return pl.BlockSpec(memory_space=pltpu.VMEM)


def local(
    tracers,
    potential,
    surface_current,
    cell_neighbors,
    cell_normal,
    cell_weight,
    spectra,
    wind_velocity,
    node_neighbors,
    node_normal,
    node_weight,
    send_rows,
    node_slot,
):
    peers, _, capacity = send_rows.shape
    freqs, dirs, nodes = spectra.shape
    tracer_count, layers, cells = tracers.shape
    edges = cell_neighbors.shape[0]
    blocks = cells // LANES
    field_rows = (tracer_count + 1) * layers
    head_rows = 2 * field_rows + TABLE_ROWS
    message_rows = head_rows + (freqs // 2 * dirs + 7) // 8 * 8
    slots = node_slot.reshape(1, nodes)
    params = pltpu.CompilerParams(vmem_limit_bytes=VMEM_LIMIT)
    f32 = jnp.float32

    stored = pl.BlockSpec(memory_space=pltpu.HBM)
    rows = tracer_count * layers
    stride = (dirs + 7) // 8 * 8
    step_pairs = 5 if freqs % 10 == 0 else 1
    step_rows = 2 * step_pairs * stride

    def like(x):
        return jax.ShapeDtypeStruct(x.shape, x.dtype)

    def shaped(*shape, dtype=f32):
        return jax.ShapeDtypeStruct(shape, dtype)

    def call(kernel, name, inputs, outputs, scratch, out_specs=None):
        return pl.pallas_call(
            kernel,
            out_shape=outputs,
            in_specs=[whole_spec()] * len(inputs),
            out_specs=out_specs or (whole_spec(),) * len(outputs),
            scratch_shapes=scratch,
            compiler_params=params,
            name=name,
        )(*inputs)

    inputs = (
        spectra, tracers, potential, cell_neighbors, cell_normal, cell_weight, surface_current,
        send_rows, slots, node_neighbors, node_normal, node_weight, wind_velocity,
    )
    (
        currents, outer, inner, own_spectra, own_slots, near, angle, face, wind,
        own_tracers, own_potential, neighbors, normal, weight, coupled,
    ) = pl.pallas_call(
        pack_kernel,
        out_shape=(
            shaped(peers, LANES),
            shaped(message_rows, LANES),
            shaped(message_rows, LANES),
            shaped(freqs, stride, LANES),
            like(slots),
            like(node_neighbors),
            like(node_normal),
            like(node_weight),
            like(wind_velocity),
            like(tracers),
            like(potential),
            like(cell_neighbors),
            like(cell_normal),
            like(cell_weight),
            shaped(3, peers, capacity, dtype=jnp.int32),
        ),
        in_specs=[stored] * len(inputs),
        out_specs=(whole_spec(),) * 15,
        scratch_shapes=[
            pltpu.VMEM(surface_current.shape, f32),
            pltpu.SemaphoreType.DMA((15,)),
        ],
        compiler_params=params,
        name="pack",
    )(*(pltpu.with_memory_space_constraint(x, pltpu.HBM) for x in inputs))
    outer = swap(outer, 1, peers)
    inner = swap(inner, 0, peers)

    (
        cosine, sine, project, choice, ways, slot_choice, own_parts,
        fields, matrices, inside, cell_cosine, cell_sine, cell_scale, sums,
    ) = call(
        functools.partial(prepare_kernel, dirs, step_rows),
        "prepare",
        (
            own_spectra, near, angle, face, wind, own_slots, own_tracers, own_potential,
            neighbors, normal, weight, coupled,
        ),
        (
            like(node_normal),
            like(node_normal),
            shaped(edges, stride, LANES),
            shaped(4 * LANES, edges * LANES, dtype=jnp.bfloat16),
            shaped(3, stride, LANES),
            shaped(nodes, peers * capacity, dtype=jnp.bfloat16),
            shaped(freqs * stride, 2 * LANES, dtype=jnp.bfloat16),
            shaped(blocks, field_rows, LANES),
            shaped(blocks, 3 * LANES, edges * LANES, dtype=jnp.bfloat16),
            shaped(blocks, field_rows, edges * LANES),
            shaped(blocks, 8, LANES),
            shaped(blocks, 8, LANES),
            shaped(blocks, 8, LANES),
            shaped(peers * capacity, (blocks + 2) * LANES, dtype=jnp.bfloat16),
        ),
        [pltpu.VMEM((blocks, 2 * field_rows, LANES), jnp.bfloat16)],
    )
    currents, cosine = lax.optimization_barrier((currents, cosine))
    currents = lax.all_to_all(currents, "mesh", 0, 0, tiled=True)

    spectra_new, stokes_rows = call(
        functools.partial(wave_kernel, capacity, step_pairs, dirs),
        "wave",
        (
            own_spectra, outer, inner, currents, own_slots, near,
            cosine, sine, project, choice, ways, slot_choice, own_parts,
        ),
        (shaped(freqs, stride, LANES), shaped(peers, LANES)),
        [
            pltpu.VMEM((8, LANES), f32),
            pltpu.VMEM((step_rows, LANES), f32),
            pltpu.VMEM((step_rows, edges * LANES), f32),
            pltpu.VMEM((step_rows, edges * LANES), f32),
        ],
    )
    stokes_all = lax.all_to_all(stokes_rows, "mesh", 0, 0, tiled=True)

    return call(
        functools.partial(tracer_kernel, capacity, (tracer_count, layers, edges)),
        "tracer",
        (
            outer, inner, stokes_all, fields, neighbors, matrices, inside, cell_cosine, cell_sine,
            cell_scale, sums, pltpu.with_memory_space_constraint(spectra_new, pltpu.VMEM),
        ),
        (like(tracers), like(spectra)),
        [
            pltpu.VMEM((4, field_rows, LANES), f32),
            pltpu.VMEM((2, 8, LANES), jnp.int32),
            pltpu.VMEM((2, 3, 8, LANES), f32),
            pltpu.VMEM((blocks + 2, 8, LANES), f32),
            pltpu.VMEM((blocks, edges, rows, LANES), f32),
            pltpu.VMEM((blocks, rows, LANES), f32),
            pltpu.VMEM((blocks + 2, 2 * rows, LANES), f32),
            pltpu.VMEM((blocks + 2, 4 * rows, LANES), jnp.bfloat16),
            pltpu.VMEM((4 * rows, edges * LANES), f32),
            pltpu.VMEM((4 * rows, edges * LANES), f32),
            pltpu.SemaphoreType.DMA(()),
        ],
        out_specs=(whole_spec(), stored),
    )


def solution(mesh):
    return jax.shard_map(
        local,
        mesh=mesh,
        in_specs=(
            P(None, None, ("groups", "mesh")),
            P(None, ("groups", "mesh")),
            P(None, ("groups", "mesh")),
            P(None, "mesh"),
            P(None, "mesh"),
            P(None, "mesh"),
            P(None, None, ("groups", "mesh")),
            P(None, ("groups", "mesh")),
            P(None, "mesh"),
            P(None, "mesh"),
            P(None, "mesh"),
            P(),
            P("mesh"),
        ),
        out_specs=(P(None, None, ("groups", "mesh")), P(None, None, ("groups", "mesh"))),
        check_vma=False,
    )
```

```python
import functools
import math

import jax
import jax.numpy as jnp
from jax import lax
from jax.experimental import pallas as pl
from jax.experimental.pallas import tpu as pltpu
from jax.sharding import PartitionSpec as P

LANES = 128
FCT_FLOOR = 0.001
TABLE_ROWS = 24
VMEM_LIMIT = 32 * 1024 * 1024


def lane_gather(values, index):
    return jnp.take_along_axis(values, index, axis=1, mode="promise_in_bounds")


def spread(row, count):
    return jnp.broadcast_to(row, (count, LANES))


def lane_iota(rows):
    return lax.broadcasted_iota(jnp.int32, (rows, LANES), 1)


def row_iota(rows):
    return lax.broadcasted_iota(jnp.int32, (rows, LANES), 0)


def slot_rows(entry):
    peers, capacity = entry.shape
    wide = jnp.concatenate([entry, jnp.zeros((peers, LANES - capacity), jnp.int32)], axis=1)
    wide = lane_gather(wide, lane_iota(peers) % capacity)
    owner = row_iota(peers)
    out = []
    for half in range(peers * capacity // LANES):
        wanted = (lane_iota(peers) + half * LANES) // capacity
        picked = jnp.where(owner == wanted, wide, 0).astype(jnp.float32)
        out.append(jnp.sum(picked, axis=0, keepdims=True).astype(jnp.int32))
    return out


def half_mask(rows, lower):
    half = lane_iota(rows) // (LANES // 2)
    return half == jnp.where(lower, 0, 1)


def peer_rows(values, peers, capacity):
    lane = lane_iota(peers)
    group = lane // capacity
    block = jnp.clip(row_iota(peers) - 1 + group // 2, 0, peers - 1)
    entry = block * capacity + lane % capacity
    out = jnp.zeros((peers, LANES), jnp.float32)
    for part in range(2):
        for half, row in enumerate(values[part]):
            found = lane_gather(spread(row, peers), entry % LANES)
            wanted = (group < 6) & (group % 2 == part) & (entry // LANES == half)
            out = jnp.where(wanted, found, out)
    return out


def direction(dirs, padded):
    turn = row_iota(padded).astype(jnp.float32) * (2.0 * math.pi / dirs)
    return jnp.cos(turn), jnp.sin(turn)


def node_tables(
    me, dirs, near, angle, face, wind, slot, cosine, sine, project, choice, ways, slots
):
    edges, padded = project.shape[:2]
    cosine[...] = face[...] * jnp.cos(angle[...])
    sine[...] = face[...] * jnp.sin(angle[...])
    cos_dir, sin_dir = direction(dirs, padded)
    ways[0] = cos_dir
    ways[1] = sin_dir
    ways[2] = 0.25 * jnp.maximum(wind[0:1, :] * cos_dir + wind[1:2, :] * sin_dir, 0.0)
    taken = jnp.transpose(spread(slot[...].astype(jnp.float32), LANES))
    for half in range(slots.shape[1] // LANES):
        number = (lane_iota(LANES) + half * LANES).astype(jnp.float32)
        picked = jnp.where(taken == number, 1.0, 0.0).astype(jnp.bfloat16)
        slots[:, half * LANES : (half + 1) * LANES] = picked
    source = row_iota(LANES)
    minus = jnp.where(source == lane_iota(LANES), -1.0, 0.0)
    for s in range(edges):
        project[s] = cos_dir * cosine[s : s + 1, :] + sin_dir * sine[s : s + 1, :]
        target = near[s : s + 1, :]
        inside = target // LANES == me
        lane = target % LANES
        own = jnp.where(source == jnp.where(inside, lane, LANES), 1.0, 0.0) + minus
        halo = jnp.where(source == jnp.where(inside, LANES, lane), 1.0, 0.0)
        lanes = slice(s * LANES, (s + 1) * LANES)
        for k, part in enumerate((own, own, halo, halo)):
            choice[k * LANES : (k + 1) * LANES, lanes] = part.astype(jnp.bfloat16)


def split(x):
    first = x.astype(jnp.bfloat16)
    return first, (x - first.astype(jnp.float32)).astype(jnp.bfloat16)


def pack_kernel(
    spectra_in, tracers_in, potential_in, neighbors_in, normal_in, weight_in, slot_in,
    outer, inner, spectra, tracers, potential, neighbors, normal, weight, node_slot,
    sems,
):
    me = lax.axis_index("mesh")
    freqs, dirs = spectra_in.shape[:2]
    if dirs < spectra.shape[1]:
        for f in range(freqs):
            spectra[f, dirs // 8 * 8 :, :] = jnp.zeros((8, LANES), jnp.float32)
    pairs = freqs // 2
    early = pairs // 2
    copies = []
    for source, target in (
        (spectra_in.at[0:early], spectra.at[0:early, 0:dirs, :]),
        (spectra_in.at[pairs : pairs + early], spectra.at[pairs : pairs + early, 0:dirs, :]),
        (tracers_in, tracers),
        (potential_in, potential),
        (neighbors_in, neighbors),
        (normal_in, normal),
        (weight_in, weight),
        (slot_in, node_slot),
        (spectra_in.at[early:pairs], spectra.at[early:pairs, 0:dirs, :]),
        (spectra_in.at[pairs + early :], spectra.at[pairs + early :, 0:dirs, :]),
    ):
        copy = pltpu.make_async_copy(source, target, sems.at[len(copies)])
        copy.start()
        copies.append(copy)
    layers, cells = potential.shape
    blocks = cells // LANES
    field_rows = (tracers.shape[0] + 1) * layers
    for copy in copies[2:8]:
        copy.wait()
    odd = me % 2 == 1
    for out, upward in ((outer, odd), (inner, jnp.logical_not(odd))):
        for b in range(2):
            high = slice((blocks - 2 + b) * LANES, (blocks - 1 + b) * LANES)
            low = slice(b * LANES, (b + 1) * LANES)
            base = b * field_rows
            for t in range(tracers.shape[0]):
                out[base + t * layers : base + (t + 1) * layers, :] = jnp.where(
                    upward, tracers[t, :, high], tracers[t, :, low]
                )
            out[base + field_rows - layers : base + field_rows, :] = jnp.where(
                upward, potential[:, high], potential[:, low]
            )
        high = slice((blocks - 1) * LANES, blocks * LANES)
        low = slice(0, LANES)
        base = 2 * field_rows
        out[base : base + TABLE_ROWS, :] = jnp.zeros((TABLE_ROWS, LANES), jnp.float32)
        edges = neighbors.shape[0]
        near = jnp.where(upward, neighbors[:, high], neighbors[:, low])
        out[base : base + edges, :] = near.astype(jnp.float32)
        out[base + edges : base + edges + 1, :] = node_slot[...].astype(jnp.float32)
        out[base + 8 : base + 8 + edges, :] = jnp.where(upward, normal[:, high], normal[:, low])
        out[base + 16 : base + 16 + edges, :] = jnp.where(upward, weight[:, high], weight[:, low])
    base = 2 * field_rows + TABLE_ROWS
    whole = dirs // 8 * 8
    rest = dirs - whole
    turns = half_mask(dirs, odd)
    for g in range(pairs):
        if g in (0, early):
            at = 0 if g == 0 else 8
            copies[at].wait()
            copies[at + 1].wait()
        natural = spectra[g, 0:dirs, :]
        turned = pltpu.roll(spectra[g + pairs, 0:dirs, :], LANES // 2, 1)
        for out, mixed in (
            (outer, jnp.where(turns, turned, natural)),
            (inner, jnp.where(turns, natural, turned)),
        ):
            at = base + g * whole
            out[at : at + whole, :] = mixed[:whole]
            at = base + pairs * whole + g * rest
            out[at : at + rest, :] = mixed[whole:]
    at = base + pairs * dirs
    if at < outer.shape[0]:
        for out in (outer, inner):
            out[at:, :] = jnp.zeros((outer.shape[0] - at, LANES), jnp.float32)


def current_rows(current, coupled, rows_out):
    peers, capacity = coupled.shape[1:]
    blocks = current.shape[1] // LANES
    stacked = jnp.concatenate(
        [current[:, b * LANES : (b + 1) * LANES] for b in range(blocks)], axis=0
    )
    place = row_iota(2 * blocks)
    values = [[], []]
    for cell in slot_rows(coupled[1]):
        found = lane_gather(stacked, spread(cell % LANES, 2 * blocks))
        for part in range(2):
            picked = jnp.where(place == 2 * (cell // LANES) + part, found, 0.0)
            values[part].append(jnp.sum(picked, axis=0, keepdims=True))
    rows_out[...] = peer_rows(values, peers, capacity)


def choose(cells, first, lanes, matrix):
    place = (cells - first - LANES).astype(jnp.float32).astype(jnp.bfloat16)
    place = spread(place, LANES)
    one = jnp.ones((LANES, LANES), jnp.bfloat16)
    for k in range(3):
        source = (row_iota(LANES) + (k - 1) * LANES).astype(jnp.float32).astype(jnp.bfloat16)
        part = jnp.where(source == place, one, 0 * one)
        if k == 1:
            own = jnp.where(row_iota(LANES) == lane_iota(LANES), 1.0, 0.0).astype(jnp.bfloat16)
            part = part - own
        matrix[k * LANES : (k + 1) * LANES, lanes] = part


def stack_split(x):
    first, second = split(x)
    return jnp.concatenate([first, second], axis=0)


def differences(parts, matrix):
    mixed = jnp.concatenate(parts, axis=1)
    out = jnp.dot(mixed, matrix, preferred_element_type=jnp.float32)
    rows = out.shape[0] // 2
    return out[:rows] + out[rows:]


def prepare_kernel(
    dirs, step_rows,
    spectra, slot, tracers, potential, neighbors, normal, weight,
    near_in, angle_in, face_in, wind_in, send_rows, current_in,
    near, rows_out, cosine, sine, project, choice, ways, slots, own_parts,
    fields, matrices, inside, cell_cosine, cell_sine, cell_scale, sums,
    pieces, angle, face, wind, coupled, current, sems,
):
    me = lax.axis_index("mesh")
    peers = send_rows.shape[0]
    copies = []
    for source, target in (
        (near_in, near),
        (angle_in, angle),
        (face_in, face),
        (wind_in, wind),
        (current_in, current),
        (send_rows.at[jnp.maximum(me - 1, 0)], coupled.at[0]),
        (send_rows.at[me], coupled.at[1]),
        (send_rows.at[jnp.minimum(me + 1, peers - 1)], coupled.at[2]),
    ):
        copy = pltpu.make_async_copy(source, target, sems.at[len(copies)])
        copy.start()
        copies.append(copy)
    tracer_count, layers, cells = tracers.shape
    blocks = cells // LANES
    edges = neighbors.shape[0]
    field_rows = (tracer_count + 1) * layers
    for b in range(blocks):
        lanes = slice(b * LANES, (b + 1) * LANES)
        for t in range(tracer_count):
            fields[b, t * layers : (t + 1) * layers, :] = tracers[t, :, lanes]
        fields[b, field_rows - layers : field_rows, :] = potential[:, lanes]
        pieces[b] = stack_split(fields[b])
        w = weight[:, lanes]
        cell_scale[b, 0:edges, :] = w
        cell_cosine[b, 0:edges, :] = w * jnp.cos(normal[:, lanes])
        cell_sine[b, 0:edges, :] = w * jnp.sin(normal[:, lanes])
        for s in range(edges):
            choose(
                neighbors[s : s + 1, lanes],
                (me * blocks + b - 1) * LANES,
                slice(s * LANES, (s + 1) * LANES),
                matrices.at[b],
            )
    for b in range(blocks):
        first, last = max(b - 1, 0), min(b + 1, blocks - 1)
        rows = slice((first - b + 1) * LANES, (last - b + 2) * LANES)
        parts = [pieces[k] for k in range(first, last + 1)]
        change = differences(parts, matrices[b, rows, :])
        last_field = field_rows - layers
        inside[b, 0:last_field, :] = change[:last_field]
        for s in range(edges):
            at = slice(s * LANES, (s + 1) * LANES)
            inside[b, last_field:, at] = change[last_field:, at] * cell_scale[b, s : s + 1, :]
    for copy in copies:
        copy.wait()
    current_rows(current, coupled, rows_out)
    node_tables(
        me, dirs, near, angle, face, wind, slot, cosine, sine, project, choice, ways, slots
    )
    freqs, padded, _ = spectra.shape
    step = step_rows // padded // 2
    pairs = freqs // 2
    for c in range(pairs // step):
        rows = []
        for g in range(c * step, (c + 1) * step):
            rows += [spectra[g], spectra[g + pairs]]
        mixed = jnp.concatenate(split(jnp.concatenate(rows, axis=0)), axis=1)
        own_parts[c * step_rows : (c + 1) * step_rows, :] = mixed
    for which in range(3):
        first = 0 if which != 0 else cells - LANES
        count = blocks if which == 1 else 1
        start = (0, 1, blocks + 1)[which]
        for half, names in enumerate(slot_rows(coupled[which])):
            named = jnp.transpose(spread(names, LANES).astype(jnp.float32))
            for b in range(count):
                cell = (lane_iota(LANES) + (first + b * LANES)).astype(jnp.float32)
                picked = jnp.where(named == cell, 1.0, 0.0).astype(jnp.bfloat16)
                lanes = slice((start + b) * LANES, (start + b + 1) * LANES)
                sums[half * LANES : (half + 1) * LANES, lanes] = picked


def node_currents(table, slot, which, capacity):
    peers = table.shape[0]
    owner = row_iota(peers) == slot // capacity
    out = []
    for part in range(2):
        lane = (2 * which + part) * capacity + slot % capacity
        found = jnp.where(owner, lane_gather(table, spread(lane, peers)), 0.0)
        out.append(jnp.sum(found, axis=0, keepdims=True))
    return out


def wave_kernel(
    capacity, step_pairs, dirs,
    spectra, outer, inner, table, node_slot, neighbors, cosine, sine, project, choice, ways, slots,
    own_parts,
    spectra_new, rows_out, drift, halos, change_a, change_b,
):
    me = lax.axis_index("mesh")
    freqs, stride = spectra.shape[:2]
    edges = neighbors.shape[0]
    peers = table.shape[0]
    halves = peers * capacity // LANES
    pairs = freqs // 2
    whole = dirs // 8 * 8
    rest = dirs - whole
    base = outer.shape[0] - (pairs * dirs + 7) // 8 * 8

    odd = me % 2 == 1
    slot = node_slot[...]
    row = base - TABLE_ROWS + edges
    halo_slot = jnp.where(
        half_mask(1, odd), outer[row : row + 1, :], inner[row : row + 1, :]
    ).astype(jnp.int32)
    lower = lane_iota(1) < LANES // 2
    currents = table[...]
    own_x, own_y = node_currents(currents, slot, jnp.ones((1, LANES), jnp.int32), capacity)
    halo_x, halo_y = node_currents(currents, halo_slot, jnp.where(lower, 2, 0), capacity)

    target = neighbors[...]
    lane = target % LANES
    inside = target // LANES == me

    def beside(own, halo):
        a = lane_gather(spread(own, edges), lane)
        b = lane_gather(spread(halo, edges), lane)
        return jnp.where(inside, a, b)

    drift[0:edges, :] = (
        0.5 * (own_x + beside(own_x, halo_x)) * cosine[...]
        + 0.5 * (own_y + beside(own_y, halo_y)) * sine[...]
    )
    drifts = [spread(drift[s : s + 1, :], 8) for s in range(edges)]
    from_outer = half_mask(dirs, odd)
    step_rows = halos.shape[0]
    halos[...] = jnp.zeros(halos.shape, jnp.float32)
    ratio = 1.0 / 1.1
    bands = [slice(r, r + 8) for r in range(0, stride, 8)]

    def gather(c, change):
        for i in range(step_pairs):
            g = c * step_pairs + i
            parts = []
            for message in (outer, inner):
                at = base + g * whole
                upper = message[at : at + whole, :]
                at = base + pairs * whole + g * rest
                left = message[at : at + rest, :]
                parts.append(jnp.concatenate([upper, left], axis=0))
            x, y = parts
            at = 2 * i * stride
            halos[at : at + dirs, :] = jnp.where(from_outer, x, y)
            at += stride
            halos[at : at + dirs, :] = pltpu.roll(jnp.where(from_outer, y, x), LANES // 2, 1)
        own = own_parts[c * step_rows : (c + 1) * step_rows, :]
        mixed = jnp.concatenate([own, *split(halos[...])], axis=1)
        change[...] = jnp.dot(mixed, choice[...], preferred_element_type=jnp.float32)

    def advect(c, change, first_speed, first_slow, total):
        total = list(total)
        speeds = []
        for i in range(step_pairs):
            speeds += [first_speed * ratio**i, first_speed * ratio ** (i + pairs)]
        slowness = []
        for i in range(step_pairs):
            slowness += [first_slow * ratio**-i, first_slow * ratio ** -(i + pairs)]
        relative = [[drift * slow for drift in drifts] for slow in slowness]
        relative_sum = [sum(each[1:], each[0]) for each in relative]
        for k, band in enumerate(bands):
            along = [project[s, band, :] for s in range(edges)]
            along_sum = sum(along[1:], along[0])
            for i in range(step_pairs):
                g = c * step_pairs + i
                for j, f in ((2 * i, g), (2 * i + 1, g + pairs)):
                    own = spectra[f, band, :]
                    at = j * stride + band.start
                    flux = (along_sum + relative_sum[j]) * own
                    for s in range(edges):
                        down = jnp.minimum(along[s] + relative[j][s], 0.0)
                        lanes = slice(s * LANES, (s + 1) * LANES)
                        flux = flux + down * change[at : at + 8, lanes]
                    value = own - speeds[j] * flux
                    spectra_new[f, band, :] = value
                    total[k] = total[k] + value
        return first_speed * ratio**step_pairs, first_slow * ratio**-step_pairs, tuple(total)

    zeros = tuple(jnp.zeros((8, LANES), jnp.float32) for _ in bands)
    chunks = pairs // step_pairs
    buffers = (change_a, change_b)
    carry = (1.0, 1.0, zeros)
    gather(0, change_a)
    for c in range(chunks):
        if c + 1 < chunks:
            gather(c + 1, buffers[(c + 1) % 2])
        carry = advect(c, buffers[c % 2], *carry)
    total = carry[2]
    total = jnp.concatenate(total, axis=0)
    zero = jnp.zeros((stride, LANES), jnp.float32)
    cos_dir, sin_dir = ways[0], ways[1]
    mean = jnp.sum(total, axis=0, keepdims=True) * (1.0 / (freqs * dirs))
    step = jnp.exp((ways[2] - 2.0 * mean) * (1.0 / freqs))
    run = 10 if freqs % 10 == 0 else 1

    def grow(c, carry):
        factor, weighted = carry
        for i in range(run):
            f = c * run + i
            factor = factor * step
            evolved = spectra_new[f] * factor
            spectra_new[f] = evolved
            kappa = (f + 1).astype(jnp.float32) * (1.0 / freqs)
            weighted = weighted + kappa * evolved
        return factor, weighted

    _, weighted = lax.fori_loop(0, freqs // run, grow, (zero + 1.0, zero))
    stokes = jnp.concatenate(
        [
            jnp.sum(weighted * cos_dir, axis=0, keepdims=True),
            jnp.sum(weighted * sin_dir, axis=0, keepdims=True),
        ],
        axis=0,
    ) * (1.0 / dirs)
    in_order = jnp.dot(
        three_parts(stokes), slots[...], preferred_element_type=jnp.float32
    )
    in_order = in_order[0:2] + (in_order[2:4] + in_order[4:6])
    values = [
        [in_order[part : part + 1, h * LANES : (h + 1) * LANES] for h in range(halves)]
        for part in range(2)
    ]
    rows_out[...] = peer_rows(values, peers, capacity)


def three_parts(values):
    first = values.astype(jnp.bfloat16).astype(jnp.float32)
    left = values - first
    second = left.astype(jnp.bfloat16).astype(jnp.float32)
    third = left - second
    pad = jnp.zeros((10, values.shape[1]), jnp.float32)
    return jnp.concatenate([first, second, third, pad], axis=0).astype(jnp.bfloat16)


def tracer_kernel(
    capacity, shape,
    outer, inner, table, fields, neighbors, matrices, inside, cosine, sine, scale, sums, spectra,
    tracers_new, spectra_out,
    halo, halo_near, halo_tables, stokes, antiflux, lowered, ratios,
    ratio_pieces, steps_a, steps_b, sem,
):
    dirs = spectra_out.shape[1]
    write = pltpu.make_async_copy(spectra.at[:, 0:dirs, :], spectra_out, sem)
    write.start()
    me = lax.axis_index("mesh")
    tracer_count, layers, edges = shape
    peers = table.shape[0]
    halves = peers * capacity // LANES
    blocks, field_rows, _ = fields.shape
    layer_groups = layers // 8
    tracer_groups = tracer_count * layer_groups
    odd = me % 2 == 1

    for b in range(2):
        x = outer[b * field_rows : (b + 1) * field_rows, :]
        y = inner[b * field_rows : (b + 1) * field_rows, :]
        for side, value in ((0, jnp.where(odd, y, x)), (1, jnp.where(odd, x, y))):
            halo[2 * side + b] = value
    at = 2 * field_rows
    x = outer[at : at + TABLE_ROWS, :]
    y = inner[at : at + TABLE_ROWS, :]
    for side, rows in ((0, jnp.where(odd, y, x)), (1, jnp.where(odd, x, y))):
        w = rows[16 : 16 + edges]
        halo_tables[side, 0, 0:edges, :] = w
        halo_tables[side, 1, 0:edges, :] = w * jnp.cos(rows[8 : 8 + edges])
        halo_tables[side, 2, 0:edges, :] = w * jnp.sin(rows[8 : 8 + edges])
        halo_near[side, 0:edges, :] = rows[0:edges].astype(jnp.int32)

    received = table[...]
    lane_of = lane_iota(peers)
    sections = []
    for which in range(3):
        values = []
        for part in range(2):
            lane = (2 * which + part) * capacity + lane_of % capacity
            found = lane_gather(received, lane)
            row = []
            for half in range(halves):
                mine = row_iota(peers) == (lane_of + half * LANES) // capacity
                row.append(jnp.sum(jnp.where(mine, found, 0.0), axis=0, keepdims=True))
            values.append(jnp.concatenate(row, axis=1))
        sections.append(three_parts(jnp.concatenate(values, axis=0)))
    total = jnp.dot(
        jnp.concatenate(sections, axis=0), sums[...], preferred_element_type=jnp.float32
    )
    for b in range(blocks + 2):
        which = 0 if b == 0 else 2 if b == blocks + 1 else 1
        at = 16 * which
        lanes = slice(b * LANES, (b + 1) * LANES)
        first, second, third = (total[at + k : at + k + 2, lanes] for k in (0, 2, 4))
        stokes[b, 0:2, :] = first + (second + third)

    decay = [
        jnp.exp(-3.0 / layers * (row_iota(8) + 8 * g).astype(jnp.float32))
        for g in range(layer_groups)
    ]

    def low_order(b, value, change, wx, wy, keep):
        slope = wx * stokes[b, 0:1, :] + wy * stokes[b, 1:2, :]
        own = [value(8 * g) for g in range(tracer_groups)]
        zero = jnp.zeros((8, LANES), jnp.float32)
        speed_sum = [zero] * layer_groups
        inflow = [zero] * tracer_groups
        highest = [zero] * tracer_groups
        lowest = [zero] * tracer_groups
        positive = [zero] * tracer_groups
        negative = [zero] * tracer_groups
        for s in range(edges):
            slope8 = spread(slope[s : s + 1, :], 8)
            for lg in range(layer_groups):
                speed = change(8 * (tracer_groups + lg), s) + decay[lg] * slope8
                down = jnp.minimum(speed, 0.0)
                half = 0.5 * speed - down
                speed_sum[lg] = speed_sum[lg] + speed
                for t in range(tracer_count):
                    g = t * layer_groups + lg
                    step = change(8 * g, s)
                    flux = half * step
                    if keep:
                        antiflux[b - 1, s, 8 * g : 8 * g + 8, :] = flux
                    inflow[g] = inflow[g] + down * step
                    highest[g] = jnp.maximum(highest[g], step)
                    lowest[g] = jnp.minimum(lowest[g], step)
                    positive[g] = positive[g] + jnp.maximum(flux, 0.0)
                    negative[g] = negative[g] - jnp.minimum(flux, 0.0)
        plus, minus = [], []
        for g in range(tracer_groups):
            loss = speed_sum[g % layer_groups] * own[g] + inflow[g]
            if keep:
                lowered[b - 1, 8 * g : 8 * g + 8, :] = own[g] - loss
            up = jnp.maximum(highest[g] + loss, 0.0) / (negative[g] + FCT_FLOOR)
            down = jnp.maximum(-loss - lowest[g], 0.0) / (positive[g] + FCT_FLOOR)
            plus.append(jnp.minimum(1.0, up))
            minus.append(jnp.minimum(1.0, down))
        both = jnp.concatenate(plus + minus, axis=0)
        ratios[b] = both
        ratio_pieces[b] = stack_split(both)

    def band(ref, *index):
        return lambda row: ref[(*index, slice(row, row + 8), slice(None))]

    potential_row = tracer_groups * 8

    def within(i):
        return lambda row, s: inside[i, row : row + 8, s * LANES : (s + 1) * LANES]

    def edge(i, side):
        beside = halo.at[1 + side]
        sign = 2 * side - 1

        def change(row, s):
            near = spread(neighbors[s : s + 1, i * LANES : (i + 1) * LANES], 8)
            from_halo = near // LANES - (me * blocks + i) == sign
            picked = lane_gather(beside[row : row + 8, :], near % LANES)
            if row >= potential_row:
                picked = picked * spread(scale[i, s : s + 1, :], 8)
            return within(i)(row, s) + jnp.where(from_halo, picked, 0.0)

        return change

    def outside(side):
        i = side * (blocks - 1)
        low, own, high = (
            (halo.at[0], halo.at[1], fields.at[i]),
            (fields.at[i], halo.at[2], halo.at[3]),
        )[side]

        def change(row, s):
            rows = slice(row, row + 8)
            near = spread(halo_near[side, s : s + 1, :], 8)
            place = near // LANES - (me * blocks + i + 2 * side - 1)
            lane = near % LANES
            mine = own[rows, :]
            middle = lane_gather(mine, lane)
            left = lane_gather(low[rows, :], lane)
            right = lane_gather(high[rows, :], lane)
            out = jnp.where(place == 0, middle, jnp.where(place < 0, left, right)) - mine
            if row >= potential_row:
                out = out * spread(halo_tables[side, 0, s : s + 1, :], 8)
            return out

        return change

    for i in range(1, blocks - 1):
        low_order(i + 1, band(fields, i), within(i), cosine[i], sine[i], True)
    for side in range(2):
        b = side * (blocks + 1)
        tables = (halo_tables[side, 1], halo_tables[side, 2])
        low_order(b, band(halo, 1 + side), outside(side), *tables, False)
        i = side * (blocks - 1)
        low_order(i + 1, band(fields, i), edge(i, side), cosine[i], sine[i], True)

    def products(i, steps):
        mixed = jnp.concatenate([ratio_pieces[i], ratio_pieces[i + 1], ratio_pieces[i + 2]], axis=1)
        steps[...] = jnp.dot(mixed, matrices[i], preferred_element_type=jnp.float32)

    def limit(i, steps):
        out = [lowered[i, 8 * g : 8 * g + 8, :] for g in range(tracer_groups)]
        own = [ratios[i + 1, 8 * g : 8 * g + 8, :] for g in range(2 * tracer_groups)]
        low = 16 * tracer_groups
        for s in range(edges):
            lanes = slice(s * LANES, (s + 1) * LANES)
            beside = [
                own[g]
                + (steps[8 * g : 8 * g + 8, lanes] + steps[low + 8 * g : low + 8 * g + 8, lanes])
                for g in range(2 * tracer_groups)
            ]
            for g in range(tracer_groups):
                m = g + tracer_groups
                flux = antiflux[i, s, 8 * g : 8 * g + 8, :]
                factor = jnp.where(
                    flux >= 0.0, jnp.minimum(own[m], beside[g]), jnp.minimum(own[g], beside[m])
                )
                out[g] = out[g] - factor * flux
        lanes = slice(i * LANES, (i + 1) * LANES)
        for g in range(tracer_groups):
            t, lg = g // layer_groups, g % layer_groups
            tracers_new[t, 8 * lg : 8 * lg + 8, lanes] = out[g]

    buffers = (steps_a, steps_b)
    products(0, steps_a)
    for i in range(blocks):
        if i + 1 < blocks:
            products(i + 1, buffers[(i + 1) % 2])
        limit(i, buffers[i % 2])
    write.wait()


def swap(message, first, peers):
    pairs = []
    for i in range(first, peers - 1, 2):
        pairs += [(i, i + 1), (i + 1, i)]
    return lax.ppermute(message, "mesh", pairs)


def whole_spec():
    return pl.BlockSpec(memory_space=pltpu.VMEM)


def local(
    tracers,
    potential,
    surface_current,
    cell_neighbors,
    cell_normal,
    cell_weight,
    spectra,
    wind_velocity,
    node_neighbors,
    node_normal,
    node_weight,
    send_rows,
    node_slot,
):
    peers, _, capacity = send_rows.shape
    freqs, dirs, nodes = spectra.shape
    tracer_count, layers, cells = tracers.shape
    edges = cell_neighbors.shape[0]
    blocks = cells // LANES
    field_rows = (tracer_count + 1) * layers
    head_rows = 2 * field_rows + TABLE_ROWS
    message_rows = head_rows + (freqs // 2 * dirs + 7) // 8 * 8
    slots = node_slot.reshape(1, nodes)
    params = pltpu.CompilerParams(vmem_limit_bytes=VMEM_LIMIT)
    f32 = jnp.float32

    stored = pl.BlockSpec(memory_space=pltpu.HBM)
    rows = tracer_count * layers
    stride = (dirs + 7) // 8 * 8
    step_pairs = 5 if freqs % 10 == 0 else 1
    step_rows = 2 * step_pairs * stride

    def like(x):
        return jax.ShapeDtypeStruct(x.shape, x.dtype)

    def shaped(*shape, dtype=f32):
        return jax.ShapeDtypeStruct(shape, dtype)

    def call(kernel, name, inputs, outputs, scratch, in_specs=None, out_specs=None):
        return pl.pallas_call(
            kernel,
            out_shape=outputs,
            in_specs=in_specs or [whole_spec()] * len(inputs),
            out_specs=out_specs or (whole_spec(),) * len(outputs),
            scratch_shapes=scratch,
            compiler_params=params,
            name=name,
        )(*inputs)

    inputs = (
        spectra, tracers, potential, cell_neighbors, cell_normal, cell_weight, slots,
    )
    (
        outer, inner, own_spectra, own_tracers, own_potential, neighbors, normal, weight, own_slots,
    ) = pl.pallas_call(
        pack_kernel,
        out_shape=(
            shaped(message_rows, LANES),
            shaped(message_rows, LANES),
            shaped(freqs, stride, LANES),
            *(like(x) for x in inputs[1:]),
        ),
        in_specs=[stored] * len(inputs),
        out_specs=(whole_spec(),) * 9,
        scratch_shapes=[pltpu.SemaphoreType.DMA((10,))],
        compiler_params=params,
        name="pack",
    )(*(pltpu.with_memory_space_constraint(x, pltpu.HBM) for x in inputs))
    outer = swap(outer, 1, peers)
    inner = swap(inner, 0, peers)

    (
        near, currents, cosine, sine, project, choice, ways, slot_choice, own_parts,
        fields, matrices, inside, cell_cosine, cell_sine, cell_scale, sums,
    ) = call(
        functools.partial(prepare_kernel, dirs, step_rows),
        "prepare",
        (
            own_spectra, own_slots, own_tracers, own_potential, neighbors, normal, weight,
            *(
                pltpu.with_memory_space_constraint(x, pltpu.HBM)
                for x in (
                    node_neighbors, node_normal, node_weight, wind_velocity, send_rows,
                    surface_current,
                )
            ),
        ),
        (
            like(node_neighbors),
            shaped(peers, LANES),
            like(node_normal),
            like(node_normal),
            shaped(edges, stride, LANES),
            shaped(4 * LANES, edges * LANES, dtype=jnp.bfloat16),
            shaped(3, stride, LANES),
            shaped(nodes, peers * capacity, dtype=jnp.bfloat16),
            shaped(freqs * stride, 2 * LANES, dtype=jnp.bfloat16),
            shaped(blocks, field_rows, LANES),
            shaped(blocks, 3 * LANES, edges * LANES, dtype=jnp.bfloat16),
            shaped(blocks, field_rows, edges * LANES),
            shaped(blocks, 8, LANES),
            shaped(blocks, 8, LANES),
            shaped(blocks, 8, LANES),
            shaped(peers * capacity, (blocks + 2) * LANES, dtype=jnp.bfloat16),
        ),
        [
            pltpu.VMEM((blocks, 2 * field_rows, LANES), jnp.bfloat16),
            pltpu.VMEM(node_normal.shape, f32),
            pltpu.VMEM(node_weight.shape, f32),
            pltpu.VMEM(wind_velocity.shape, f32),
            pltpu.VMEM((3, peers, capacity), jnp.int32),
            pltpu.VMEM(surface_current.shape, f32),
            pltpu.SemaphoreType.DMA((8,)),
        ],
        in_specs=[whole_spec()] * 7 + [stored] * 6,
    )
    currents = lax.all_to_all(currents, "mesh", 0, 0, tiled=True)

    spectra_new, stokes_rows = call(
        functools.partial(wave_kernel, capacity, step_pairs, dirs),
        "wave",
        (
            own_spectra, outer, inner, currents, own_slots, near,
            cosine, sine, project, choice, ways, slot_choice, own_parts,
        ),
        (shaped(freqs, stride, LANES), shaped(peers, LANES)),
        [
            pltpu.VMEM((8, LANES), f32),
            pltpu.VMEM((step_rows, LANES), f32),
            pltpu.VMEM((step_rows, edges * LANES), f32),
            pltpu.VMEM((step_rows, edges * LANES), f32),
        ],
    )
    stokes_all = lax.all_to_all(stokes_rows, "mesh", 0, 0, tiled=True)

    return call(
        functools.partial(tracer_kernel, capacity, (tracer_count, layers, edges)),
        "tracer",
        (
            outer, inner, stokes_all, fields, neighbors, matrices, inside, cell_cosine, cell_sine,
            cell_scale, sums, pltpu.with_memory_space_constraint(spectra_new, pltpu.VMEM),
        ),
        (like(tracers), like(spectra)),
        [
            pltpu.VMEM((4, field_rows, LANES), f32),
            pltpu.VMEM((2, 8, LANES), jnp.int32),
            pltpu.VMEM((2, 3, 8, LANES), f32),
            pltpu.VMEM((blocks + 2, 8, LANES), f32),
            pltpu.VMEM((blocks, edges, rows, LANES), f32),
            pltpu.VMEM((blocks, rows, LANES), f32),
            pltpu.VMEM((blocks + 2, 2 * rows, LANES), f32),
            pltpu.VMEM((blocks + 2, 4 * rows, LANES), jnp.bfloat16),
            pltpu.VMEM((4 * rows, edges * LANES), f32),
            pltpu.VMEM((4 * rows, edges * LANES), f32),
            pltpu.SemaphoreType.DMA(()),
        ],
        out_specs=(whole_spec(), stored),
    )


def solution(mesh):
    return jax.shard_map(
        local,
        mesh=mesh,
        in_specs=(
            P(None, None, ("groups", "mesh")),
            P(None, ("groups", "mesh")),
            P(None, ("groups", "mesh")),
            P(None, "mesh"),
            P(None, "mesh"),
            P(None, "mesh"),
            P(None, None, ("groups", "mesh")),
            P(None, ("groups", "mesh")),
            P(None, "mesh"),
            P(None, "mesh"),
            P(None, "mesh"),
            P(),
            P("mesh"),
        ),
        out_specs=(P(None, None, ("groups", "mesh")), P(None, None, ("groups", "mesh"))),
        check_vma=False,
    )
```

```python
import functools
import math

import jax
import jax.numpy as jnp
from jax import lax
from jax.experimental import pallas as pl
from jax.experimental.pallas import tpu as pltpu
from jax.sharding import PartitionSpec as P

LANES = 128
FCT_FLOOR = 0.001
TABLE_ROWS = 24
VMEM_LIMIT = 32 * 1024 * 1024


def lane_gather(values, index):
    return jnp.take_along_axis(values, index, axis=1, mode="promise_in_bounds")


def spread(row, count):
    return jnp.broadcast_to(row, (count, LANES))


def lane_iota(rows):
    return lax.broadcasted_iota(jnp.int32, (rows, LANES), 1)


def row_iota(rows):
    return lax.broadcasted_iota(jnp.int32, (rows, LANES), 0)


def slot_rows(entry):
    peers, capacity = entry.shape
    wide = jnp.concatenate([entry, jnp.zeros((peers, LANES - capacity), jnp.int32)], axis=1)
    wide = lane_gather(wide, lane_iota(peers) % capacity)
    owner = row_iota(peers)
    out = []
    for half in range(peers * capacity // LANES):
        wanted = (lane_iota(peers) + half * LANES) // capacity
        picked = jnp.where(owner == wanted, wide, 0).astype(jnp.float32)
        out.append(jnp.sum(picked, axis=0, keepdims=True).astype(jnp.int32))
    return out


def half_mask(rows, lower):
    half = lane_iota(rows) // (LANES // 2)
    return half == jnp.where(lower, 0, 1)


def peer_rows(values, peers, capacity):
    lane = lane_iota(peers)
    group = lane // capacity
    block = jnp.clip(row_iota(peers) - 1 + group // 2, 0, peers - 1)
    entry = block * capacity + lane % capacity
    out = jnp.zeros((peers, LANES), jnp.float32)
    for part in range(2):
        for half, row in enumerate(values[part]):
            found = lane_gather(spread(row, peers), entry % LANES)
            wanted = (group < 6) & (group % 2 == part) & (entry // LANES == half)
            out = jnp.where(wanted, found, out)
    return out


def direction(dirs, padded):
    turn = row_iota(padded).astype(jnp.float32) * (2.0 * math.pi / dirs)
    return jnp.cos(turn), jnp.sin(turn)


def node_tables(
    me, dirs, near, angle, face, wind, slot, cosine, sine, project, choice, ways, slots
):
    edges, padded = project.shape[:2]
    cosine[...] = face[...] * jnp.cos(angle[...])
    sine[...] = face[...] * jnp.sin(angle[...])
    cos_dir, sin_dir = direction(dirs, padded)
    ways[0] = cos_dir
    ways[1] = sin_dir
    ways[2] = 0.25 * jnp.maximum(wind[0:1, :] * cos_dir + wind[1:2, :] * sin_dir, 0.0)
    taken = jnp.transpose(spread(slot[...].astype(jnp.float32), LANES))
    for half in range(slots.shape[1] // LANES):
        number = (lane_iota(LANES) + half * LANES).astype(jnp.float32)
        picked = jnp.where(taken == number, 1.0, 0.0).astype(jnp.bfloat16)
        slots[:, half * LANES : (half + 1) * LANES] = picked
    source = row_iota(LANES)
    minus = jnp.where(source == lane_iota(LANES), -1.0, 0.0)
    for s in range(edges):
        project[s] = cos_dir * cosine[s : s + 1, :] + sin_dir * sine[s : s + 1, :]
        target = near[s : s + 1, :]
        inside = target // LANES == me
        lane = target % LANES
        own = jnp.where(source == jnp.where(inside, lane, LANES), 1.0, 0.0) + minus
        halo = jnp.where(source == jnp.where(inside, LANES, lane), 1.0, 0.0)
        lanes = slice(s * LANES, (s + 1) * LANES)
        for k, part in enumerate((own, own, halo, halo)):
            choice[k * LANES : (k + 1) * LANES, lanes] = part.astype(jnp.bfloat16)


def split(x):
    first = x.astype(jnp.bfloat16)
    return first, (x - first.astype(jnp.float32)).astype(jnp.bfloat16)


def pack_kernel(
    spectra_in, tracers_in, potential_in, neighbors_in, normal_in, weight_in, current_in,
    send_rows, slot_in, near_in, angle_in, face_in, wind_in,
    rows_out, outer, inner, spectra, node_slot, near, angle, face, wind,
    tracers, potential, neighbors, normal, weight, coupled,
    current, sems,
):
    peers, _, capacity = send_rows.shape
    me = lax.axis_index("mesh")
    freqs, dirs = spectra_in.shape[:2]
    if dirs < spectra.shape[1]:
        for f in range(freqs):
            spectra[f, dirs // 8 * 8 :, :] = jnp.zeros((8, LANES), jnp.float32)
    pairs = freqs // 2
    copies = []
    for source, target in (
        (send_rows.at[me], coupled.at[1]),
        (current_in, current),
        (slot_in, node_slot),
        (spectra_in, spectra.at[:, 0:dirs, :]),
        (tracers_in, tracers),
        (potential_in, potential),
        (neighbors_in, neighbors),
        (normal_in, normal),
        (weight_in, weight),
        (send_rows.at[jnp.maximum(me - 1, 0)], coupled.at[0]),
        (send_rows.at[jnp.minimum(me + 1, peers - 1)], coupled.at[2]),
        (near_in, near),
        (angle_in, angle),
        (face_in, face),
        (wind_in, wind),
    ):
        copy = pltpu.make_async_copy(source, target, sems.at[len(copies)])
        copy.start()
        copies.append(copy)
    for copy in copies[:3]:
        copy.wait()
    layers, cells = potential.shape
    blocks = cells // LANES
    field_rows = (tracers.shape[0] + 1) * layers
    stacked = jnp.concatenate(
        [current[:, b * LANES : (b + 1) * LANES] for b in range(blocks)], axis=0
    )
    place = row_iota(2 * blocks)
    halves = slot_rows(coupled[1])
    values = [[], []]
    for cell in halves:
        found = lane_gather(stacked, spread(cell % LANES, 2 * blocks))
        for part in range(2):
            picked = jnp.where(place == 2 * (cell // LANES) + part, found, 0.0)
            values[part].append(jnp.sum(picked, axis=0, keepdims=True))
    rows_out[...] = peer_rows(values, peers, capacity)
    for copy in copies[4:9]:
        copy.wait()
    odd = me % 2 == 1
    for out, upward in ((outer, odd), (inner, jnp.logical_not(odd))):
        for b in range(2):
            high = slice((blocks - 2 + b) * LANES, (blocks - 1 + b) * LANES)
            low = slice(b * LANES, (b + 1) * LANES)
            base = b * field_rows
            for t in range(tracers.shape[0]):
                out[base + t * layers : base + (t + 1) * layers, :] = jnp.where(
                    upward, tracers[t, :, high], tracers[t, :, low]
                )
            out[base + field_rows - layers : base + field_rows, :] = jnp.where(
                upward, potential[:, high], potential[:, low]
            )
        high = slice((blocks - 1) * LANES, blocks * LANES)
        low = slice(0, LANES)
        base = 2 * field_rows
        out[base : base + TABLE_ROWS, :] = jnp.zeros((TABLE_ROWS, LANES), jnp.float32)
        edges = neighbors.shape[0]
        near = jnp.where(upward, neighbors[:, high], neighbors[:, low])
        out[base : base + edges, :] = near.astype(jnp.float32)
        out[base + edges : base + edges + 1, :] = node_slot[...].astype(jnp.float32)
        out[base + 8 : base + 8 + edges, :] = jnp.where(upward, normal[:, high], normal[:, low])
        out[base + 16 : base + 16 + edges, :] = jnp.where(upward, weight[:, high], weight[:, low])
    base = 2 * field_rows + TABLE_ROWS
    whole = dirs // 8 * 8
    rest = dirs - whole
    turns = half_mask(dirs, odd)
    copies[3].wait()
    for g in range(pairs):
        natural = spectra[g, 0:dirs, :]
        turned = pltpu.roll(spectra[g + pairs, 0:dirs, :], LANES // 2, 1)
        for out, mixed in (
            (outer, jnp.where(turns, turned, natural)),
            (inner, jnp.where(turns, natural, turned)),
        ):
            at = base + g * whole
            out[at : at + whole, :] = mixed[:whole]
            at = base + pairs * whole + g * rest
            out[at : at + rest, :] = mixed[whole:]
    at = base + pairs * dirs
    if at < outer.shape[0]:
        for out in (outer, inner):
            out[at:, :] = jnp.zeros((outer.shape[0] - at, LANES), jnp.float32)
    for copy in copies[9:]:
        copy.wait()


def choose(cells, first, lanes, matrix):
    place = (cells - first - LANES).astype(jnp.float32).astype(jnp.bfloat16)
    place = spread(place, LANES)
    one = jnp.ones((LANES, LANES), jnp.bfloat16)
    for k in range(3):
        source = (row_iota(LANES) + (k - 1) * LANES).astype(jnp.float32).astype(jnp.bfloat16)
        part = jnp.where(source == place, one, 0 * one)
        if k == 1:
            own = jnp.where(row_iota(LANES) == lane_iota(LANES), 1.0, 0.0).astype(jnp.bfloat16)
            part = part - own
        matrix[k * LANES : (k + 1) * LANES, lanes] = part


def stack_split(x):
    first, second = split(x)
    return jnp.concatenate([first, second], axis=0)


def differences(parts, matrix):
    mixed = jnp.concatenate(parts, axis=1)
    out = jnp.dot(mixed, matrix, preferred_element_type=jnp.float32)
    rows = out.shape[0] // 2
    return out[:rows] + out[rows:]


def prepare_kernel(
    dirs, step_rows,
    spectra, near, angle, face, wind, slot, tracers, potential, neighbors, normal, weight, coupled,
    cosine, sine, project, choice, ways, slots, own_change,
    fields, matrices, inside, cell_cosine, cell_sine, cell_scale, sums,
    pieces,
):
    me = lax.axis_index("mesh")
    node_tables(
        me, dirs, near, angle, face, wind, slot, cosine, sine, project, choice, ways, slots
    )
    freqs, padded, _ = spectra.shape
    step = step_rows // padded

    for c in range(freqs // step):
        own = spectra[c * step : (c + 1) * step].reshape(step_rows, LANES)
        own_change[c * step_rows : (c + 1) * step_rows, :] = jnp.dot(
            jnp.concatenate(split(own), axis=1),
            choice[0 : 2 * LANES, :],
            preferred_element_type=jnp.float32,
        )
    tracer_count, layers, cells = tracers.shape
    blocks = cells // LANES
    edges = neighbors.shape[0]
    field_rows = (tracer_count + 1) * layers
    for b in range(blocks):
        lanes = slice(b * LANES, (b + 1) * LANES)
        for t in range(tracer_count):
            fields[b, t * layers : (t + 1) * layers, :] = tracers[t, :, lanes]
        fields[b, field_rows - layers : field_rows, :] = potential[:, lanes]
        pieces[b] = stack_split(fields[b])
        w = weight[:, lanes]
        cell_scale[b, 0:edges, :] = w
        cell_cosine[b, 0:edges, :] = w * jnp.cos(normal[:, lanes])
        cell_sine[b, 0:edges, :] = w * jnp.sin(normal[:, lanes])
        for s in range(edges):
            choose(
                neighbors[s : s + 1, lanes],
                (me * blocks + b - 1) * LANES,
                slice(s * LANES, (s + 1) * LANES),
                matrices.at[b],
            )
    for b in range(blocks):
        first, last = max(b - 1, 0), min(b + 1, blocks - 1)
        rows = slice((first - b + 1) * LANES, (last - b + 2) * LANES)
        parts = [pieces[k] for k in range(first, last + 1)]
        change = differences(parts, matrices[b, rows, :])
        last_field = field_rows - layers
        inside[b, 0:last_field, :] = change[:last_field]
        for s in range(edges):
            at = slice(s * LANES, (s + 1) * LANES)
            inside[b, last_field:, at] = change[last_field:, at] * cell_scale[b, s : s + 1, :]
    for which in range(3):
        first = 0 if which != 0 else cells - LANES
        count = blocks if which == 1 else 1
        start = (0, 1, blocks + 1)[which]
        for half, names in enumerate(slot_rows(coupled[which])):
            named = jnp.transpose(spread(names, LANES).astype(jnp.float32))
            for b in range(count):
                cell = (lane_iota(LANES) + (first + b * LANES)).astype(jnp.float32)
                picked = jnp.where(named == cell, 1.0, 0.0).astype(jnp.bfloat16)
                lanes = slice((start + b) * LANES, (start + b + 1) * LANES)
                sums[half * LANES : (half + 1) * LANES, lanes] = picked


def node_currents(table, slot, which, capacity):
    peers = table.shape[0]
    owner = row_iota(peers) == slot // capacity
    out = []
    for part in range(2):
        lane = (2 * which + part) * capacity + slot % capacity
        found = jnp.where(owner, lane_gather(table, spread(lane, peers)), 0.0)
        out.append(jnp.sum(found, axis=0, keepdims=True))
    return out


def halo_tasks(
    layers, outer, inner, fields, neighbors, inside, scale,
    halo, tables, edge_change, halo_change, near_cells,
):
    me = lax.axis_index("mesh")
    odd = me % 2 == 1
    blocks, field_rows, _ = fields.shape
    edges = neighbors.shape[0]
    for b in range(2):
        x = outer[b * field_rows : (b + 1) * field_rows, :]
        y = inner[b * field_rows : (b + 1) * field_rows, :]
        halo[b] = jnp.where(odd, y, x)
        halo[2 + b] = jnp.where(odd, x, y)
    at = 2 * field_rows
    x = outer[at : at + TABLE_ROWS, :]
    y = inner[at : at + TABLE_ROWS, :]
    for side, rows in ((0, jnp.where(odd, y, x)), (1, jnp.where(odd, x, y))):
        w = rows[16 : 16 + edges]
        tables[side, 0, 0:edges, :] = w
        tables[side, 1, 0:edges, :] = w * jnp.cos(rows[8 : 8 + edges])
        tables[side, 2, 0:edges, :] = w * jnp.sin(rows[8 : 8 + edges])
        near_cells[side, 0:edges, :] = rows[0:edges].astype(jnp.int32)

    def task(side, s):
        i = side * (blocks - 1)
        lanes = slice(s * LANES, (s + 1) * LANES)
        low, own, high = (
            (halo.at[0], halo.at[1], fields.at[i]),
            (fields.at[i], halo.at[2], halo.at[3]),
        )[side]
        near = spread(neighbors[s : s + 1, i * LANES : (i + 1) * LANES], 8)
        from_halo = near // LANES - (me * blocks + i) == 2 * side - 1
        lane = near % LANES
        far = spread(near_cells[side, s : s + 1, :], 8)
        place = far // LANES - (me * blocks + i + 2 * side - 1)
        far_lane = far % LANES
        for row in range(0, field_rows, 8):
            rows = slice(row, row + 8)
            mine = own[rows, :]
            picked = lane_gather(mine, lane)
            middle = lane_gather(mine, far_lane)
            left = lane_gather(low[rows, :], far_lane)
            right = lane_gather(high[rows, :], far_lane)
            out = jnp.where(place == 0, middle, jnp.where(place < 0, left, right)) - mine
            if row >= field_rows - layers:
                picked = picked * spread(scale[i, s : s + 1, :], 8)
                out = out * spread(tables[side, 0, s : s + 1, :], 8)
            halo_change[side, rows, lanes] = out
            edge_change[side, rows, lanes] = inside[i, rows, lanes] + jnp.where(
                from_halo, picked, 0.0
            )

    return [functools.partial(task, side, s) for s in range(edges) for side in range(2)]


def chunk_sizes(pairs):
    first = min(2, pairs)
    left = pairs - first
    parts = -(-left // 6)
    sizes = [first] + [left * (k + 1) // parts - left * k // parts for k in range(parts)]
    return [(sum(sizes[:k]), size) for k, size in enumerate(sizes)]


def wave_kernel(
    capacity, sizes, dirs, layers,
    spectra, outer, inner, table, node_slot, neighbors, cosine, sine, project, choice, ways, slots,
    own_change, fields, cell_neighbors, cell_inside, scale,
    spectra_new, rows_out, halo, tables, edge_change, halo_change,
    drift, halos, change_a, change_b, near_cells,
):
    me = lax.axis_index("mesh")
    freqs, stride = spectra.shape[:2]
    edges = neighbors.shape[0]
    peers = table.shape[0]
    halves = peers * capacity // LANES
    pairs = freqs // 2
    whole = dirs // 8 * 8
    rest = dirs - whole
    base = outer.shape[0] - (pairs * dirs + 7) // 8 * 8

    odd = me % 2 == 1
    slot = node_slot[...]
    row = base - TABLE_ROWS + edges
    halo_slot = jnp.where(
        half_mask(1, odd), outer[row : row + 1, :], inner[row : row + 1, :]
    ).astype(jnp.int32)
    lower = lane_iota(1) < LANES // 2
    currents = table[...]
    own_x, own_y = node_currents(currents, slot, jnp.ones((1, LANES), jnp.int32), capacity)
    halo_x, halo_y = node_currents(currents, halo_slot, jnp.where(lower, 2, 0), capacity)

    target = neighbors[...]
    lane = target % LANES
    inside = target // LANES == me

    def beside(own, halo):
        a = lane_gather(spread(own, edges), lane)
        b = lane_gather(spread(halo, edges), lane)
        return jnp.where(inside, a, b)

    drift[0:edges, :] = (
        0.5 * (own_x + beside(own_x, halo_x)) * cosine[...]
        + 0.5 * (own_y + beside(own_y, halo_y)) * sine[...]
    )
    drifts = [spread(drift[s : s + 1, :], 8) for s in range(edges)]
    from_outer = half_mask(dirs, odd)
    halos[...] = jnp.zeros(halos.shape, jnp.float32)
    ratio = 1.0 / 1.1
    bands = [slice(r, r + 8) for r in range(0, stride, 8)]

    def gather(c, change):
        start, count = sizes[c]
        for i in range(count):
            g = start + i
            parts = []
            for message in (outer, inner):
                at = base + g * whole
                upper = message[at : at + whole, :]
                at = base + pairs * whole + g * rest
                left = message[at : at + rest, :]
                parts.append(jnp.concatenate([upper, left], axis=0))
            x, y = parts
            at = 2 * i * stride
            halos[at : at + dirs, :] = jnp.where(from_outer, x, y)
            at += stride
            halos[at : at + dirs, :] = pltpu.roll(jnp.where(from_outer, y, x), LANES // 2, 1)
        rows = 2 * count * stride
        mixed = jnp.concatenate(split(halos[0:rows, :]), axis=1)
        change[0:rows, :] = jnp.dot(
            mixed, choice[2 * LANES : 4 * LANES, :], preferred_element_type=jnp.float32
        )

    def advect(c, change, total):
        total = list(total)
        start, count = sizes[c]
        order = [f for i in range(count) for f in (start + i, start + i + pairs)]
        speeds = [ratio**f for f in order]
        slowness = [ratio**-f for f in order]
        relative = [[drift * slow for drift in drifts] for slow in slowness]
        relative_sum = [sum(each[1:], each[0]) for each in relative]
        for k, band in enumerate(bands):
            along = [project[s, band, :] for s in range(edges)]
            along_sum = sum(along[1:], along[0])
            for j, f in enumerate(order):
                own = spectra[f, band, :]
                at = j * stride + band.start
                own_at = slice(f * stride + band.start, f * stride + band.stop)
                flux = (along_sum + relative_sum[j]) * own
                for s in range(edges):
                    down = jnp.minimum(along[s] + relative[j][s], 0.0)
                    lanes = slice(s * LANES, (s + 1) * LANES)
                    step = change[at : at + 8, lanes] + own_change[own_at, lanes]
                    flux = flux + down * step
                value = own - speeds[j] * flux
                spectra_new[f, band, :] = value
                total[k] = total[k] + value
        return tuple(total)

    zeros = tuple(jnp.zeros((8, LANES), jnp.float32) for _ in bands)
    buffers = (change_a, change_b)
    total = zeros
    gather(0, change_a)
    tasks = halo_tasks(
        layers, outer, inner, fields, cell_neighbors, cell_inside, scale,
        halo, tables, edge_change, halo_change, near_cells,
    )
    chunks = len(sizes)
    for c in range(chunks):
        if c + 1 < chunks:
            gather(c + 1, buffers[(c + 1) % 2])
        for task in tasks[c * len(tasks) // chunks : (c + 1) * len(tasks) // chunks]:
            task()
        total = advect(c, buffers[c % 2], total)
    total = jnp.concatenate(total, axis=0)
    zero = jnp.zeros((stride, LANES), jnp.float32)
    cos_dir, sin_dir = ways[0], ways[1]
    mean = jnp.sum(total, axis=0, keepdims=True) * (1.0 / (freqs * dirs))
    step = jnp.exp((ways[2] - 2.0 * mean) * (1.0 / freqs))
    factor = zero + 1.0
    weighted = zero
    for f in range(freqs):
        factor = factor * step
        evolved = spectra_new[f] * factor
        spectra_new[f] = evolved
        weighted = weighted + ((f + 1) / freqs) * evolved
    stokes = jnp.concatenate(
        [
            jnp.sum(weighted * cos_dir, axis=0, keepdims=True),
            jnp.sum(weighted * sin_dir, axis=0, keepdims=True),
        ],
        axis=0,
    ) * (1.0 / dirs)
    in_order = jnp.dot(
        three_parts(stokes), slots[...], preferred_element_type=jnp.float32
    )
    in_order = in_order[0:2] + (in_order[2:4] + in_order[4:6])
    values = [
        [in_order[part : part + 1, h * LANES : (h + 1) * LANES] for h in range(halves)]
        for part in range(2)
    ]
    rows_out[...] = peer_rows(values, peers, capacity)


def three_parts(values):
    first = values.astype(jnp.bfloat16).astype(jnp.float32)
    left = values - first
    second = left.astype(jnp.bfloat16).astype(jnp.float32)
    third = left - second
    pad = jnp.zeros((10, values.shape[1]), jnp.float32)
    return jnp.concatenate([first, second, third, pad], axis=0).astype(jnp.bfloat16)


def tracer_kernel(
    capacity, shape,
    halo, halo_tables, edge_change, halo_change, table, fields, matrices, inside, cosine, sine,
    sums, spectra,
    tracers_new, spectra_out,
    stokes, antiflux, lowered, ratios,
    ratio_pieces, steps_a, steps_b, sem,
):
    dirs = spectra_out.shape[1]
    write = pltpu.make_async_copy(spectra.at[:, 0:dirs, :], spectra_out, sem)
    write.start()
    tracer_count, layers, edges = shape
    peers = table.shape[0]
    halves = peers * capacity // LANES
    blocks, field_rows, _ = fields.shape
    layer_groups = layers // 8
    tracer_groups = tracer_count * layer_groups

    received = table[...]
    lane_of = lane_iota(peers)
    sections = []
    for which in range(3):
        values = []
        for part in range(2):
            lane = (2 * which + part) * capacity + lane_of % capacity
            found = lane_gather(received, lane)
            row = []
            for half in range(halves):
                mine = row_iota(peers) == (lane_of + half * LANES) // capacity
                row.append(jnp.sum(jnp.where(mine, found, 0.0), axis=0, keepdims=True))
            values.append(jnp.concatenate(row, axis=1))
        sections.append(three_parts(jnp.concatenate(values, axis=0)))
    total = jnp.dot(
        jnp.concatenate(sections, axis=0), sums[...], preferred_element_type=jnp.float32
    )
    for b in range(blocks + 2):
        which = 0 if b == 0 else 2 if b == blocks + 1 else 1
        at = 16 * which
        lanes = slice(b * LANES, (b + 1) * LANES)
        first, second, third = (total[at + k : at + k + 2, lanes] for k in (0, 2, 4))
        stokes[b, 0:2, :] = first + (second + third)

    decay = [
        jnp.exp(-3.0 / layers * (row_iota(8) + 8 * g).astype(jnp.float32))
        for g in range(layer_groups)
    ]

    def low_order(b, value, change, wx, wy, keep):
        slope = wx * stokes[b, 0:1, :] + wy * stokes[b, 1:2, :]
        own = [value(8 * g) for g in range(tracer_groups)]
        zero = jnp.zeros((8, LANES), jnp.float32)
        speed_sum = [zero] * layer_groups
        inflow = [zero] * tracer_groups
        highest = [zero] * tracer_groups
        lowest = [zero] * tracer_groups
        positive = [zero] * tracer_groups
        negative = [zero] * tracer_groups
        for s in range(edges):
            slope8 = spread(slope[s : s + 1, :], 8)
            for lg in range(layer_groups):
                speed = change(8 * (tracer_groups + lg), s) + decay[lg] * slope8
                down = jnp.minimum(speed, 0.0)
                half = 0.5 * speed - down
                speed_sum[lg] = speed_sum[lg] + speed
                for t in range(tracer_count):
                    g = t * layer_groups + lg
                    step = change(8 * g, s)
                    flux = half * step
                    if keep:
                        antiflux[b - 1, s, 8 * g : 8 * g + 8, :] = flux
                    inflow[g] = inflow[g] + down * step
                    highest[g] = jnp.maximum(highest[g], step)
                    lowest[g] = jnp.minimum(lowest[g], step)
                    positive[g] = positive[g] + jnp.maximum(flux, 0.0)
                    negative[g] = negative[g] - jnp.minimum(flux, 0.0)
        plus, minus = [], []
        for g in range(tracer_groups):
            loss = speed_sum[g % layer_groups] * own[g] + inflow[g]
            if keep:
                lowered[b - 1, 8 * g : 8 * g + 8, :] = own[g] - loss
            up = jnp.maximum(highest[g] + loss, 0.0) / (negative[g] + FCT_FLOOR)
            down = jnp.maximum(-loss - lowest[g], 0.0) / (positive[g] + FCT_FLOOR)
            plus.append(jnp.minimum(1.0, up))
            minus.append(jnp.minimum(1.0, down))
        both = jnp.concatenate(plus + minus, axis=0)
        ratios[b] = both
        ratio_pieces[b] = stack_split(both)

    def band(ref, *index):
        return lambda row: ref[(*index, slice(row, row + 8), slice(None))]

    def column(ref, index):
        return lambda row, s: ref[index, row : row + 8, s * LANES : (s + 1) * LANES]

    for side in range(2):
        b = side * (blocks + 1)
        normals = (halo_tables[side, 1], halo_tables[side, 2])
        low_order(b, band(halo, 1 + side), column(halo_change, side), *normals, False)
    for i in range(blocks):
        change = column(inside, i)
        if i in (0, blocks - 1):
            change = column(edge_change, min(i, 1))
        low_order(i + 1, band(fields, i), change, cosine[i], sine[i], True)

    def products(i, steps):
        mixed = jnp.concatenate([ratio_pieces[i], ratio_pieces[i + 1], ratio_pieces[i + 2]], axis=1)
        steps[...] = jnp.dot(mixed, matrices[i], preferred_element_type=jnp.float32)

    def limit(i, steps):
        out = [lowered[i, 8 * g : 8 * g + 8, :] for g in range(tracer_groups)]
        own = [ratios[i + 1, 8 * g : 8 * g + 8, :] for g in range(2 * tracer_groups)]
        low = 16 * tracer_groups
        for s in range(edges):
            lanes = slice(s * LANES, (s + 1) * LANES)
            beside = [
                own[g]
                + (steps[8 * g : 8 * g + 8, lanes] + steps[low + 8 * g : low + 8 * g + 8, lanes])
                for g in range(2 * tracer_groups)
            ]
            for g in range(tracer_groups):
                m = g + tracer_groups
                flux = antiflux[i, s, 8 * g : 8 * g + 8, :]
                factor = jnp.where(
                    flux >= 0.0, jnp.minimum(own[m], beside[g]), jnp.minimum(own[g], beside[m])
                )
                out[g] = out[g] - factor * flux
        lanes = slice(i * LANES, (i + 1) * LANES)
        for g in range(tracer_groups):
            t, lg = g // layer_groups, g % layer_groups
            tracers_new[t, 8 * lg : 8 * lg + 8, lanes] = out[g]

    buffers = (steps_a, steps_b)
    products(0, steps_a)
    for i in range(blocks):
        if i + 1 < blocks:
            products(i + 1, buffers[(i + 1) % 2])
        limit(i, buffers[i % 2])
    write.wait()


def swap(message, first, peers):
    pairs = []
    for i in range(first, peers - 1, 2):
        pairs += [(i, i + 1), (i + 1, i)]
    return lax.ppermute(message, "mesh", pairs)


def whole_spec():
    return pl.BlockSpec(memory_space=pltpu.VMEM)


def local(
    tracers,
    potential,
    surface_current,
    cell_neighbors,
    cell_normal,
    cell_weight,
    spectra,
    wind_velocity,
    node_neighbors,
    node_normal,
    node_weight,
    send_rows,
    node_slot,
):
    peers, _, capacity = send_rows.shape
    freqs, dirs, nodes = spectra.shape
    tracer_count, layers, cells = tracers.shape
    edges = cell_neighbors.shape[0]
    blocks = cells // LANES
    field_rows = (tracer_count + 1) * layers
    head_rows = 2 * field_rows + TABLE_ROWS
    message_rows = head_rows + (freqs // 2 * dirs + 7) // 8 * 8
    slots = node_slot.reshape(1, nodes)
    params = pltpu.CompilerParams(vmem_limit_bytes=VMEM_LIMIT)
    f32 = jnp.float32

    stored = pl.BlockSpec(memory_space=pltpu.HBM)
    rows = tracer_count * layers
    stride = (dirs + 7) // 8 * 8
    step_pairs = 5 if freqs % 10 == 0 else 1
    step_rows = 2 * step_pairs * stride

    def like(x):
        return jax.ShapeDtypeStruct(x.shape, x.dtype)

    def shaped(*shape, dtype=f32):
        return jax.ShapeDtypeStruct(shape, dtype)

    def call(kernel, name, inputs, outputs, scratch, out_specs=None):
        return pl.pallas_call(
            kernel,
            out_shape=outputs,
            in_specs=[whole_spec()] * len(inputs),
            out_specs=out_specs or (whole_spec(),) * len(outputs),
            scratch_shapes=scratch,
            compiler_params=params,
            name=name,
        )(*inputs)

    inputs = (
        spectra, tracers, potential, cell_neighbors, cell_normal, cell_weight, surface_current,
        send_rows, slots, node_neighbors, node_normal, node_weight, wind_velocity,
    )
    (
        currents, outer, inner, own_spectra, own_slots, near, angle, face, wind,
        own_tracers, own_potential, neighbors, normal, weight, coupled,
    ) = pl.pallas_call(
        pack_kernel,
        out_shape=(
            shaped(peers, LANES),
            shaped(message_rows, LANES),
            shaped(message_rows, LANES),
            shaped(freqs, stride, LANES),
            like(slots),
            like(node_neighbors),
            like(node_normal),
            like(node_weight),
            like(wind_velocity),
            like(tracers),
            like(potential),
            like(cell_neighbors),
            like(cell_normal),
            like(cell_weight),
            shaped(3, peers, capacity, dtype=jnp.int32),
        ),
        in_specs=[stored] * len(inputs),
        out_specs=(whole_spec(),) * 15,
        scratch_shapes=[
            pltpu.VMEM(surface_current.shape, f32),
            pltpu.SemaphoreType.DMA((15,)),
        ],
        compiler_params=params,
        name="pack",
    )(*(pltpu.with_memory_space_constraint(x, pltpu.HBM) for x in inputs))
    outer = swap(outer, 1, peers)
    inner = swap(inner, 0, peers)

    (
        cosine, sine, project, choice, ways, slot_choice, own_change,
        fields, matrices, inside, cell_cosine, cell_sine, cell_scale, sums,
    ) = call(
        functools.partial(prepare_kernel, dirs, step_rows),
        "prepare",
        (
            own_spectra, near, angle, face, wind, own_slots, own_tracers, own_potential,
            neighbors, normal, weight, coupled,
        ),
        (
            like(node_normal),
            like(node_normal),
            shaped(edges, stride, LANES),
            shaped(4 * LANES, edges * LANES, dtype=jnp.bfloat16),
            shaped(3, stride, LANES),
            shaped(nodes, peers * capacity, dtype=jnp.bfloat16),
            shaped(freqs * stride, edges * LANES),
            shaped(blocks, field_rows, LANES),
            shaped(blocks, 3 * LANES, edges * LANES, dtype=jnp.bfloat16),
            shaped(blocks, field_rows, edges * LANES),
            shaped(blocks, 8, LANES),
            shaped(blocks, 8, LANES),
            shaped(blocks, 8, LANES),
            shaped(peers * capacity, (blocks + 2) * LANES, dtype=jnp.bfloat16),
        ),
        [pltpu.VMEM((blocks, 2 * field_rows, LANES), jnp.bfloat16)],
    )
    currents, cosine = lax.optimization_barrier((currents, cosine))
    currents = lax.all_to_all(currents, "mesh", 0, 0, tiled=True)

    spectra_new, stokes_rows, halo, halo_tables, edge_change, halo_change = call(
        functools.partial(wave_kernel, capacity, chunk_sizes(freqs // 2), dirs, layers),
        "wave",
        (
            own_spectra, outer, inner, currents, own_slots, near,
            cosine, sine, project, choice, ways, slot_choice, own_change,
            fields, neighbors, inside, cell_scale,
        ),
        (
            shaped(freqs, stride, LANES),
            shaped(peers, LANES),
            shaped(4, field_rows, LANES),
            shaped(2, 3, 8, LANES),
            shaped(2, field_rows, edges * LANES),
            shaped(2, field_rows, edges * LANES),
        ),
        [
            pltpu.VMEM((8, LANES), f32),
            pltpu.VMEM((12 * stride, LANES), f32),
            pltpu.VMEM((12 * stride, edges * LANES), f32),
            pltpu.VMEM((12 * stride, edges * LANES), f32),
            pltpu.VMEM((2, 8, LANES), jnp.int32),
        ],
    )
    stokes_all = lax.all_to_all(stokes_rows, "mesh", 0, 0, tiled=True)

    return call(
        functools.partial(tracer_kernel, capacity, (tracer_count, layers, edges)),
        "tracer",
        (
            halo, halo_tables, edge_change, halo_change, stokes_all, fields, matrices, inside,
            cell_cosine, cell_sine, sums, pltpu.with_memory_space_constraint(spectra_new, pltpu.VMEM),
        ),
        (like(tracers), like(spectra)),
        [
            pltpu.VMEM((blocks + 2, 8, LANES), f32),
            pltpu.VMEM((blocks, edges, rows, LANES), f32),
            pltpu.VMEM((blocks, rows, LANES), f32),
            pltpu.VMEM((blocks + 2, 2 * rows, LANES), f32),
            pltpu.VMEM((blocks + 2, 4 * rows, LANES), jnp.bfloat16),
            pltpu.VMEM((4 * rows, edges * LANES), f32),
            pltpu.VMEM((4 * rows, edges * LANES), f32),
            pltpu.SemaphoreType.DMA(()),
        ],
        out_specs=(whole_spec(), stored),
    )


def solution(mesh):
    return jax.shard_map(
        local,
        mesh=mesh,
        in_specs=(
            P(None, None, ("groups", "mesh")),
            P(None, ("groups", "mesh")),
            P(None, ("groups", "mesh")),
            P(None, "mesh"),
            P(None, "mesh"),
            P(None, "mesh"),
            P(None, None, ("groups", "mesh")),
            P(None, ("groups", "mesh")),
            P(None, "mesh"),
            P(None, "mesh"),
            P(None, "mesh"),
            P(),
            P("mesh"),
        ),
        out_specs=(P(None, None, ("groups", "mesh")), P(None, None, ("groups", "mesh"))),
        check_vma=False,
    )
```
